32 devices in a mesh: grp: 2 (over y), patch: 4 (over z), head: 2 (over x), sub: 2 (over core).
Axes of the slice: x: 2, y: 2, z: 4, core: 2. Of those that a mesh axis runs over, the one named last changes fastest.
Arguments:
- queries: bfloat16 [2048, 4096], P(('grp', 'patch'), ('head', 'sub')), parts along dimension 0, may hold values from -140 to 140
- fresh_kv: bfloat16 [2, 2048, 4096], P(None, ('grp', 'patch'), ('head', 'sub')), parts along dimension 1, may hold values from -9 to 9
- cached_kv: bfloat16 [2, 2048, 4096], P(None, 'grp', ('head', 'sub')), parts along dimension 1, may hold values from -5 to 5
- exponents: int32 [2, 16, 32], P(None, ('grp', 'patch'), ('head', 'sub')), parts along dimension 1, may hold values from -10 to -7
- out_weight: bfloat16 [4096, 5120], P(('head', 'sub'), 'patch'), may hold values from -0.09375 to 0.09375
- hidden_in: bfloat16 [2048, 5120], P(('grp', 'patch', 'head', 'sub')), parts along dimension 0, may hold values from -6 to 6
- attn_gate: float32 [5120], replicated, may hold values from 0.25 to 1.75
Outputs:
- mixed: bfloat16 [2048, 5120], P(('grp', 'patch', 'head', 'sub')), parts along dimension 0
The draws below stay inside these ranges and needn't reach their ends.
There are 2 independent parts, one for each index of `grp`. The reference program is written for one: setup_inputs(seed, part) draws one part's arguments, and reference() takes and returns one part's arrays. A program takes and returns all parts, laid end to end along the dimension named above; an argument that names none is the same for every part. Nothing has to cross between parts.
All inputs are finite; a program needn't handle non-finite values.
Results may differ from the reference program's by a relative error of at most 0.0095.
Values may be sent and summed in bfloat16 or wider, within the bound.
No kernel may reach another device: no remote copies, remote signals or barrier semaphores. Data moves between devices by JAX's collectives and lax.ppermute only.
A program may use at most 128 MiB of HBM per device.

```python
import jax
import jax.numpy as jnp
from jax import lax

WIDTH = 5120
HEADS = 32
HEAD_DIM = 128
SCALE_ROWS = 128
TOKENS = 1024
HEAD_DEV = 8
N_HEAD = 2
N_SUB = 2


def base_fields(key):
    shape = (2, TOKENS, HEADS * HEAD_DIM)
    cached = jnp.clip(jax.random.normal(jax.random.fold_in(key, 11), shape, jnp.float32), -4.8, 4.8)
    noise = jnp.clip(jax.random.normal(jax.random.fold_in(key, 12), shape, jnp.float32), -5.0, 5.0)
    return (cached, noise)


def draw_cached_kv(key, part):
    cached, noise = base_fields(key)
    return cached.astype(jnp.bfloat16)


def draw_fresh_kv(key, part):
    cached, noise = base_fields(key)
    fresh = cached + 0.7 * noise
    return fresh.astype(jnp.bfloat16)


def draw_queries(key, part):
    key = jax.random.fold_in(key, 3)
    shape = (TOKENS, HEADS * HEAD_DIM)
    return (2.5 * jnp.clip(jax.random.normal(key, shape, jnp.float32), -5.0, 5.0)).astype(jnp.bfloat16)


def with_ends(result, key, smallest, top_value):
    longest = result.shape.index(max(result.shape))
    spots = []
    for shift in (0, 1):
        where = [jax.random.randint(jax.random.fold_in(key, axis), (), 0, length) for axis, length in enumerate(result.shape)]
        where[longest] = (where[longest] + shift) % result.shape[longest]
        spots.append(tuple(where))
    return result.at[spots[0]].set(smallest).at[spots[1]].set(top_value)


def block_levels(rng, shape, cuts, low, high):
    def one(axis_at, shards_of):
        heights = jax.random.uniform(jax.random.fold_in(jax.random.fold_in(rng, 6), axis_at), (shards_of,), jnp.float32, low / len(cuts), high / len(cuts))
        return jnp.repeat(jnp.exp(heights), shape[axis_at] // shards_of).reshape((-1,) + (1,) * (len(shape) - axis_at - 1))

    gain = one(*cuts[0])
    for cut in cuts[1:]:
        gain = gain * one(*cut)
    return gain


def bell_draw(stream_key, dims, scale, most, shards=(), kind=jnp.bfloat16):
    entries = scale * jax.random.normal(stream_key, dims, jnp.float32)
    if shards:
        entries = entries * block_levels(stream_key, dims, shards, -0.22, 0.18)
    return jnp.clip(entries, -most, most).astype(kind)


def setup_inputs(seed: int = 0, part: int = 0) -> dict:
    seeds = jax.random.split(jax.random.key(seed), 8)
    part_splits = jax.random.split(jax.random.fold_in(seeds[7], part), 8)
    queries = draw_queries(jax.random.fold_in(jax.random.fold_in(seeds[7], part), 71), part)
    fresh_kv = draw_fresh_kv(jax.random.fold_in(jax.random.fold_in(seeds[7], part), 71), part)
    cached_kv = draw_cached_kv(jax.random.fold_in(jax.random.fold_in(seeds[7], part), 71), part)
    exponents = with_ends(jax.random.randint(part_splits[3], (2, TOKENS // SCALE_ROWS, HEADS), -10, -6), jax.random.fold_in(part_splits[3], 1), -10, (-6) - 1).astype(jnp.int32)
    out_weight = bell_draw(seeds[4], (HEADS * HEAD_DIM, WIDTH), (HEADS * HEAD_DIM) ** -0.5, 0.09375, ((0, 4), (1, 4)))
    hidden_in = bell_draw(part_splits[5], (TOKENS, WIDTH), 1.0, 6.0, ((0, 16),))
    attn_gate = jnp.clip(1.0 + 0.15 * jax.random.normal(seeds[6], (WIDTH,), jnp.float32), 0.25, 1.75)
    return dict(queries=queries, fresh_kv=fresh_kv, cached_kv=cached_kv, exponents=exponents, out_weight=out_weight, hidden_in=hidden_in, attn_gate=attn_gate)


SATURATION = 448.0


def expand_scale(exps_float):
    grown = jnp.repeat(exps_float, SCALE_ROWS, axis=1)
    return jnp.exp2(jnp.repeat(grown, HEAD_DIM, axis=2))


def decode_all(fresh_kv, cached_kv, exponents):
    exps_float = exponents.astype(jnp.float32)
    cached = cached_kv.astype(jnp.float32)
    residual = fresh_kv.astype(jnp.float32) - cached
    codes = jnp.clip(residual * expand_scale(-exps_float), -SATURATION, SATURATION).astype(jnp.bfloat16)
    codes = lax.optimization_barrier(codes)
    return (cached + codes.astype(jnp.float32) * expand_scale(exps_float)).astype(jnp.bfloat16)


def head_attention(triple):
    query_head, key_head, value_head = triple
    scores = jnp.dot(query_head, key_head.T, preferred_element_type=jnp.float32) * (HEAD_DIM ** -0.5)
    peak = jnp.max(scores, axis=1, keepdims=True)
    expo = jnp.exp(scores - peak)
    weights = (expo / jnp.sum(expo, axis=1, keepdims=True)).astype(jnp.bfloat16)
    return jnp.dot(weights, value_head, preferred_element_type=jnp.float32).astype(jnp.bfloat16)


def reference(queries, fresh_kv, cached_kv, exponents, out_weight, hidden_in, attn_gate):
    decoded = decode_all(fresh_kv, cached_kv, exponents)
    query_heads = queries.reshape(TOKENS, HEADS, HEAD_DIM).transpose(1, 0, 2)
    key_heads = decoded[0].reshape(TOKENS, HEADS, HEAD_DIM).transpose(1, 0, 2)
    value_heads = decoded[1].reshape(TOKENS, HEADS, HEAD_DIM).transpose(1, 0, 2)
    attended = lax.map(head_attention, (query_heads, key_heads, value_heads))
    attended = attended.transpose(1, 0, 2).reshape(TOKENS, HEADS * HEAD_DIM)
    groups = N_HEAD * N_SUB
    span = HEAD_DEV * HEAD_DIM
    att_groups = attended.reshape(TOKENS, groups, span).transpose(1, 0, 2)
    weight_groups = out_weight.reshape(groups, span, WIDTH)

    def add_group(running, pair):
        partial_term = jnp.dot(pair[0], pair[1], preferred_element_type=jnp.float32).astype(jnp.bfloat16)
        partial_term = lax.optimization_barrier(partial_term)
        return running + partial_term.astype(jnp.float32), None

    projected, unused = lax.scan(add_group, jnp.zeros((TOKENS, WIDTH), jnp.float32), (att_groups, weight_groups))
    return (hidden_in.astype(jnp.float32) + attn_gate * projected).astype(jnp.bfloat16)
```

```python
import functools
import math

import jax
import jax.numpy as jnp
from jax import lax
from jax.experimental import pallas as pl
from jax.experimental.pallas import tpu as pltpu
from jax.sharding import PartitionSpec as P

HEAD_DIM = 128
SCALE_ROWS = 128
SATURATION = 448.0
VMEM_BYTES = 48 * 1024 * 1024


def shift_pairs(groups, step):
    pairs = []
    for group in groups:
        count = len(group)
        pairs += [(group[at], group[(at + step) % count]) for at in range(count)]
    return pairs


def pack_kernel(split, where_ref, exps_ref, q_ref, fresh_ref, cached_ref, *outs):
    tok = q_ref.shape[0]
    feat = q_ref.shape[1] // split
    for rel in range(split):
        dest = lax.rem(where_ref[1] + rel, split)
        cols = pl.ds(pl.multiple_of(dest * feat, HEAD_DIM), feat)
        outs[rel][0] = q_ref[:, cols]
        for stacked in range(2):
            for head in range(feat // HEAD_DIM):
                head_at = dest * (feat // HEAD_DIM) + head
                lanes = pl.ds(pl.multiple_of(head_at * HEAD_DIM, HEAD_DIM), HEAD_DIM)
                for block in range(tok // SCALE_ROWS):
                    rows = pl.ds(block * SCALE_ROWS, SCALE_ROWS)
                    power = jnp.full(
                        (1, HEAD_DIM), exps_ref[stacked, block, head_at].astype(jnp.float32)
                    )
                    cached = cached_ref[stacked, rows, lanes].astype(jnp.float32)
                    residual = fresh_ref[stacked, rows, lanes].astype(jnp.float32) - cached
                    codes = jnp.clip(
                        residual * jnp.exp2(-power), -SATURATION, SATURATION
                    ).astype(jnp.bfloat16)
                    decoded = cached + codes.astype(jnp.float32) * jnp.exp2(power)
                    outs[rel][
                        1 + stacked, rows, pl.ds(head * HEAD_DIM, HEAD_DIM)
                    ] = decoded.astype(jnp.bfloat16)


def pack(split, where, exponents, queries, fresh_kv, cached_kv):
    tok, channels = queries.shape
    feat = channels // split
    piece = jax.ShapeDtypeStruct((3, tok, feat), jnp.bfloat16)
    return pl.pallas_call(
        functools.partial(pack_kernel, split),
        out_shape=[piece] * split,
        grid_spec=pltpu.PrefetchScalarGridSpec(
            num_scalar_prefetch=1,
            grid=(1,),
            in_specs=[
                pl.BlockSpec(memory_space=pltpu.SMEM),
                pl.BlockSpec((tok, channels), lambda i, w: (0, 0)),
                pl.BlockSpec((2, tok, channels), lambda i, w: (0, 0, 0)),
                pl.BlockSpec((2, tok, channels), lambda i, w: (0, w[0], 0)),
            ],
            out_specs=[pl.BlockSpec((3, tok, feat), lambda i, w: (0, 0, 0))] * split,
        ),
        compiler_params=pltpu.CompilerParams(vmem_limit_bytes=VMEM_BYTES),
        name="pack",
    )(where, exponents, queries, fresh_kv, cached_kv)


def attend_kernel(split, count, where_ref, *refs):
    out_ref = refs[-1]
    q_refs, kv_refs = refs[:split], refs[split:-1]
    tok = q_refs[0].shape[1]
    feat = q_refs[0].shape[2]
    factor = HEAD_DIM**-0.5 * math.log2(math.e)
    for head in range(feat // HEAD_DIM):
        lanes = pl.ds(head * HEAD_DIM, HEAD_DIM)
        keys = jnp.concatenate([ref[1, :, lanes] for ref in kv_refs], axis=0)
        values = jnp.concatenate([ref[2, :, lanes] for ref in kv_refs], axis=0)
        for rel in range(split):
            scores = lax.dot_general(
                q_refs[rel][0, :, lanes],
                keys,
                (((1,), (1,)), ((), ())),
                preferred_element_type=jnp.float32,
            )
            peak = jnp.max(scores, axis=1, keepdims=True)
            expo = jnp.exp2((scores - peak) * factor)
            total = jnp.sum(expo, axis=1, keepdims=True)
            mix = jnp.dot(
                expo.astype(jnp.bfloat16), values, preferred_element_type=jnp.float32
            )
            source = lax.rem(where_ref[1] + split - rel, split)
            out_ref[source, :, lanes] = (mix / total).astype(jnp.bfloat16)


def attend(where, pieces, kv_pieces):
    split = len(pieces)
    _, tok, feat = pieces[0].shape
    whole = pl.BlockSpec((3, tok, feat), lambda i, w: (0, 0, 0))
    return pl.pallas_call(
        functools.partial(attend_kernel, split, len(kv_pieces)),
        out_shape=jax.ShapeDtypeStruct((split, tok, feat), jnp.bfloat16),
        grid_spec=pltpu.PrefetchScalarGridSpec(
            num_scalar_prefetch=1,
            grid=(1,),
            in_specs=[whole] * (split + len(kv_pieces)),
            out_specs=pl.BlockSpec((split, tok, feat), lambda i, w: (0, 0, 0)),
        ),
        compiler_params=pltpu.CompilerParams(vmem_limit_bytes=VMEM_BYTES),
        name="attend",
    )(where, *pieces, *kv_pieces)


def project_kernel(where_ref, att_ref, weight_ref, *refs):
    outs, acc_ref = refs[:-1], refs[-1]
    n_head, n_sub, rows, cols = acc_ref.shape
    split, _, tok, feat = att_ref.shape
    acc = jnp.dot(att_ref[0, 0], weight_ref[:feat], preferred_element_type=jnp.float32)
    for at in range(1, split):
        acc += jnp.dot(
            att_ref[at, 0],
            weight_ref[at * feat : (at + 1) * feat],
            preferred_element_type=jnp.float32,
        )
    acc_ref[...] = acc.reshape(n_head, n_sub, rows, cols)
    for sub_rel in range(n_sub):
        sub_at = lax.rem(where_ref[3] + sub_rel, n_sub)
        for head_rel in range(n_head):
            head_at = lax.rem(where_ref[2] + head_rel, n_head)
            outs[sub_rel][head_rel, 0] = acc_ref[head_at, sub_at].astype(jnp.bfloat16)


def project(where, gathered, weight, n_head, n_sub):
    n_patch, split, tok, feat = gathered.shape
    cols = weight.shape[1]
    rows = tok // (n_head * n_sub)
    shape = jax.ShapeDtypeStruct((n_head, n_patch, rows, cols), jnp.bfloat16)
    return pl.pallas_call(
        project_kernel,
        out_shape=[shape] * n_sub,
        grid_spec=pltpu.PrefetchScalarGridSpec(
            num_scalar_prefetch=1,
            grid=(n_patch,),
            in_specs=[
                pl.BlockSpec(
                    (split, 1, tok, feat),
                    lambda i, w: (lax.div(i, split), lax.rem(i, split), 0, 0),
                ),
                pl.BlockSpec(weight.shape, lambda i, w: (0, 0)),
            ],
            out_specs=[
                pl.BlockSpec(
                    (n_head, 1, rows, cols),
                    lambda i, w: (0, lax.rem(i + n_patch - w[0], n_patch), 0, 0),
                )
            ]
            * n_sub,
            scratch_shapes=[pltpu.VMEM((n_head, n_sub, rows, cols), jnp.float32)],
        ),
        compiler_params=pltpu.CompilerParams(vmem_limit_bytes=VMEM_BYTES),
        name="project",
    )(where, gathered, weight)


def body(sizes, queries, fresh_kv, cached_kv, exponents, out_weight, hidden_in, attn_gate):
    n_patch, n_head, n_sub = sizes["patch"], sizes["head"], sizes["sub"]
    tok, channels = queries.shape
    split = math.gcd(channels // HEAD_DIM, n_patch)
    patch_at = lax.axis_index("patch")
    where = jnp.stack(
        [patch_at, lax.rem(patch_at, split), lax.axis_index("head"), lax.axis_index("sub")]
    ).astype(jnp.int32)

    sent = pack(split, where, exponents, queries, fresh_kv, cached_kv)
    near = [list(range(at, at + split)) for at in range(0, n_patch, split)]
    pieces = [sent[0]] + [
        lax.ppermute(sent[rel], "patch", shift_pairs(near, rel)) for rel in range(1, split)
    ]
    kv_pieces = list(pieces)
    far = [list(range(at, n_patch, split)) for at in range(split)]
    for rel in range(1, n_patch // split):
        kv_pieces += [lax.ppermute(x, "patch", shift_pairs(far, rel)) for x in pieces]

    attended = attend(where, pieces, kv_pieces)
    gathered = lax.all_gather(attended, "patch", axis=0)

    terms = project(where, gathered, out_weight, n_head, n_sub)
    partial = terms[0].astype(jnp.float32)
    ring = [list(range(n_sub))]
    for rel in range(1, n_sub):
        partial += lax.ppermute(terms[rel], "sub", shift_pairs(ring, rel)).astype(jnp.float32)
    ring = [list(range(n_head))]
    total = partial[0]
    for rel in range(1, n_head):
        arrived = lax.ppermute(partial[rel].astype(jnp.bfloat16), "head", shift_pairs(ring, rel))
        total += arrived.astype(jnp.float32)
    ring = [list(range(n_patch))]
    total = total.astype(jnp.bfloat16)
    blocks = [total[0]] + [
        lax.ppermute(total[rel], "patch", shift_pairs(ring, rel)) for rel in range(1, n_patch)
    ]
    order = jnp.roll(jnp.stack([blocks[-at % n_patch] for at in range(n_patch)]), patch_at, axis=0)
    projected = order.transpose(1, 0, 2).reshape(hidden_in.shape).astype(jnp.float32)
    return (hidden_in.astype(jnp.float32) + attn_gate * projected).astype(jnp.bfloat16)


def solution(mesh):
    in_specs = (
        P(("grp", "patch"), ("head", "sub")),
        P(None, ("grp", "patch"), ("head", "sub")),
        P(None, "grp", ("head", "sub")),
        P(None, ("grp", "patch"), ("head", "sub")),
        P(("head", "sub"), "patch"),
        P(("grp", "patch", "head", "sub"), None),
        P(),
    )
    out_specs = P(("grp", "patch", "head", "sub"), None)
    sizes = dict(mesh.shape)
    return jax.shard_map(
        functools.partial(body, sizes),
        mesh=mesh,
        in_specs=in_specs,
        out_specs=out_specs,
        check_vma=False,
    )
```

```python
import functools
import math

import jax
import jax.numpy as jnp
from jax import lax
from jax.experimental import pallas as pl
from jax.experimental.pallas import tpu as pltpu
from jax.sharding import PartitionSpec as P

HEAD_DIM = 128
SCALE_ROWS = 128
SATURATION = 448.0
VMEM_BYTES = 60 * 1024 * 1024


def spec(shape):
    return pl.BlockSpec(shape, lambda i, w: (0,) * len(shape))


def call(kernel, name, out_shape, grid, in_specs, out_specs, scratch=(), cost=None):
    return pl.pallas_call(
        kernel,
        out_shape=out_shape,
        grid_spec=pltpu.PrefetchScalarGridSpec(
            num_scalar_prefetch=1,
            grid=(grid,),
            in_specs=in_specs,
            out_specs=out_specs,
            scratch_shapes=list(scratch),
        ),
        compiler_params=pltpu.CompilerParams(vmem_limit_bytes=VMEM_BYTES),
        cost_estimate=cost,
        name=name,
    )


def swap(x, axes, count, mask, only=None):
    pairs = [(at, at ^ mask) for at in range(count) if only is None or at in only]
    return lax.ppermute(x, axes, pairs)


def pack_kernel(split, per, chunk, where_ref, exps_ref, q_ref, fresh_ref, cached_ref, *outs):
    step = pl.program_id(0)
    tok = q_ref.shape[0]
    head_at = (where_ref[1] ^ step) * per + chunk
    for rel in range(split):

        @pl.when(step == rel)
        def fill(out=outs[rel]):
            out[0] = q_ref[...]
            for stacked in range(2):
                for block in range(tok // SCALE_ROWS):
                    rows = pl.ds(block * SCALE_ROWS, SCALE_ROWS)
                    power = jnp.full(
                        (1, HEAD_DIM), exps_ref[stacked, block, head_at].astype(jnp.float32)
                    )
                    cached = cached_ref[stacked, rows].astype(jnp.float32)
                    residual = fresh_ref[stacked, rows].astype(jnp.float32) - cached
                    codes = jnp.clip(
                        residual * jnp.exp2(-power), -SATURATION, SATURATION
                    ).astype(jnp.bfloat16)
                    decoded = cached + codes.astype(jnp.float32) * jnp.exp2(power)
                    out[1 + stacked, rows] = decoded.astype(jnp.bfloat16)


def pack(split, per, chunk, where, exponents, queries, fresh_kv, cached_kv):
    tok = queries.shape[0]
    piece = jax.ShapeDtypeStruct((3, tok, HEAD_DIM), jnp.bfloat16)

    def column(i, w):
        return (w[1] ^ i) * per + chunk

    return call(
        functools.partial(pack_kernel, split, per, chunk),
        "pack",
        [piece] * split,
        split,
        [
            pl.BlockSpec(memory_space=pltpu.SMEM),
            pl.BlockSpec((tok, HEAD_DIM), lambda i, w: (0, column(i, w))),
            pl.BlockSpec((2, tok, HEAD_DIM), lambda i, w: (0, 0, column(i, w))),
            pl.BlockSpec((2, tok, HEAD_DIM), lambda i, w: (0, w[0], column(i, w))),
        ],
        [spec(piece.shape)] * split,
    )(where, exponents, queries, fresh_kv, cached_kv)


def attend_kernel(split, n_kv, where_ref, *refs):
    q_refs, kv_refs = refs[:split], refs[split : split + n_kv]
    outs, mix_ref = refs[split + n_kv : -1], refs[-1]
    tok = q_refs[0].shape[1]
    factor = HEAD_DIM**-0.5 * math.log2(math.e)
    keys = jnp.concatenate([ref[1] for ref in kv_refs], axis=0)
    values = jnp.concatenate([ref[2] for ref in kv_refs], axis=0)
    values = jnp.concatenate([values, jnp.ones_like(values)], axis=1)
    for rel in range(split):
        scores = lax.dot_general(
            q_refs[rel][0], keys, (((1,), (1,)), ((), ())), preferred_element_type=jnp.float32
        )
        peak = jnp.max(scores, axis=1, keepdims=True)
        expo = jnp.exp2((scores - peak) * factor).astype(jnp.bfloat16)
        mix = jnp.dot(expo, values, preferred_element_type=jnp.float32)
        mix = mix[:, :HEAD_DIM] / mix[:, HEAD_DIM:]
        mix_ref[...] = mix.reshape(mix_ref.shape)
        for at, out in enumerate(outs):
            out[where_ref[1] ^ rel] = mix_ref[where_ref[2] ^ at].astype(jnp.bfloat16)


def attend(where, n_rel, pieces, kv_pieces):
    split = len(pieces)
    _, tok, feat = pieces[0].shape
    rows = tok // n_rel
    out = jax.ShapeDtypeStruct((split, rows, feat), jnp.bfloat16)
    return call(
        functools.partial(attend_kernel, split, len(kv_pieces)),
        "attend",
        [out] * n_rel,
        1,
        [spec(pieces[0].shape)] * (split + len(kv_pieces)),
        [spec(out.shape)] * n_rel,
        [pltpu.VMEM((n_rel, rows, feat), jnp.float32)],
    )(where, *pieces, *kv_pieces)


def project_kernel(plan, n_slots, n_weights, with_acc, last, where_ref, *refs):
    slots, refs = refs[:n_slots], refs[n_slots:]
    weights, refs = refs[:n_weights], refs[n_weights:]
    acc_in, refs = (refs[0], refs[1:]) if with_acc else (None, refs)
    if last:
        outs, held_ref, acc_ref = refs[:-2], refs[-2], refs[-1]
    else:
        outs, held_ref = refs[:-1], refs[-1]
    split = held_ref.shape[0]

    @pl.when(pl.program_id(0) == 0)
    def arrange():
        rows = slots[0].shape[0]
        for at, slot in enumerate(slots):
            group, near = divmod(at, split)
            held_ref[where_ref[1] ^ near, group * rows : (group + 1) * rows] = slot[...]

    acc = acc_in[...] if with_acc else None
    for head, lanes, parts in plan:
        place = head(where_ref) if callable(head) else head
        weight = [weights[index][part, 0] if part is not None else weights[index][0] for index, part in parts]
        weight = jnp.concatenate(weight, axis=0) if len(weight) > 1 else weight[0]
        term = jnp.dot(
            held_ref[place, :, lanes * HEAD_DIM : (lanes + len(parts)) * HEAD_DIM],
            weight,
            preferred_element_type=jnp.float32,
        )
        acc = term if acc is None else acc + term
    if not last:
        outs[0][...] = acc
    else:
        acc_ref[...] = acc.reshape(acc_ref.shape)
        for at, out in enumerate(outs):
            group, near = divmod(at, split)
            out[...] = acc_ref[group, where_ref[1] ^ near].astype(jnp.bfloat16)


def project(plan, split, chunk, where, slots, weights, acc, last):
    rows, lanes = slots[0].shape
    total = rows * len(slots) // split
    cols = weights[0].shape[-1]
    wide = 256 if cols % 256 == 0 else cols
    specs = [spec(slots[0].shape)] * len(slots)
    for weight in weights:
        if weight.ndim == 4:
            specs.append(
                pl.BlockSpec((weight.shape[0], 1, HEAD_DIM, wide), lambda i, w: (0, chunk, 0, i))
            )
        else:
            specs.append(pl.BlockSpec((1, HEAD_DIM, wide), lambda i, w: (chunk, 0, i)))
    whole = pl.BlockSpec((total, wide), lambda i, w: (0, i))
    if acc is not None:
        specs.append(whole)
    scratch = [pltpu.VMEM((split, total, lanes), jnp.bfloat16)]
    if last:
        piece = rows // split
        out_shape = [jax.ShapeDtypeStruct((piece, cols), jnp.bfloat16)] * len(slots)
        out_specs = [pl.BlockSpec((piece, wide), lambda i, w: (0, i))] * len(slots)
        scratch.append(pltpu.VMEM((len(slots) // split, split, piece, wide), jnp.float32))
    else:
        out_shape = [jax.ShapeDtypeStruct((total, cols), jnp.float32)]
        out_specs = [whole]
    kernel = functools.partial(
        project_kernel, plan, len(slots), len(weights), acc is not None, last
    )
    operands = [*slots, *weights] + ([] if acc is None else [acc])
    return call(kernel, "project", out_shape, cols // wide, specs, out_specs, scratch)(
        where, *operands
    )


def mix_kernel(n_patch, where_ref, hidden_ref, gate_ref, *refs):
    out_ref = refs[-1]
    cols = refs[0].shape[1]
    for rel in range(n_patch):
        lanes = pl.ds(pl.multiple_of((where_ref[0] ^ rel) * cols, HEAD_DIM), cols)
        mixed = hidden_ref[:, lanes].astype(jnp.float32) + gate_ref[:, lanes] * refs[rel][
            ...
        ].astype(jnp.float32)
        out_ref[:, lanes] = mixed.astype(jnp.bfloat16)


def mix(where, hidden_in, attn_gate, blocks):
    rows, width = hidden_in.shape
    n_patch = len(blocks)
    if blocks[0].shape[1] % HEAD_DIM:
        order = jnp.stack(blocks)[where[0] ^ jnp.arange(n_patch)]
        projected = order.transpose(1, 0, 2).reshape(rows, width).astype(jnp.float32)
        return (hidden_in.astype(jnp.float32) + attn_gate * projected).astype(jnp.bfloat16)
    return call(
        functools.partial(mix_kernel, n_patch),
        "mix",
        jax.ShapeDtypeStruct((rows, width), jnp.bfloat16),
        1,
        [spec((rows, width)), spec((1, width))] + [spec(blocks[0].shape)] * n_patch,
        spec((rows, width)),
    )(where, hidden_in, attn_gate[None], *blocks)


def share_weight(sizes, split, per, out_weight, where):
    n_head, n_sub = sizes["head"], sizes["sub"]
    n_rel = n_head * n_sub
    cols = out_weight.shape[1]
    own = out_weight.reshape(split, per, HEAD_DIM, cols)
    if (n_head, n_sub, sizes["grp"], split) != (2, 2, 2, 4):
        weights = [own] + [swap(own, ("head", "sub"), n_rel, rel) for rel in range(1, n_rel)]
        plan = []
        for at in range(split):
            for rel in range(0, n_rel, 2):
                plan.append((at, rel, [(rel, at), (rel + 1, at)]))
        return weights, plan
    across = []
    for half in range(2):
        mine = lax.dynamic_index_in_dim(own, 2 * where[3] + half, 0, keepdims=False)
        across.append(swap(mine, "head", 2, 1))
    passed = [swap(x, "grp", 2, 1) for x in across]
    weights = [own, swap(own, "sub", 2, 1)]
    for x in across + passed:
        weights += [x, swap(x, "sub", 2, 1)]
    plan = [(at, 0, [(0, at), (1, at)]) for at in range(4)]
    for flip in range(2):
        for half in range(2):
            index = 2 + 2 * (2 * flip + half)

            def head(where_ref, flip=flip, half=half):
                return 2 * (where_ref[3] ^ flip) + half

            plan.append((head, 2, [(index, None), (index + 1, None)]))
    return weights, plan


def gather(x, where, n_patch):
    if n_patch != 4:
        return [x] + [swap(x, "patch", n_patch, rel) for rel in range(1, n_patch)]
    far = swap(x, "patch", 4, 2)
    next_to = swap(x, "patch", 4, 1)
    middle = swap(x, "patch", 4, 3, (1, 2))
    ends = lax.ppermute(far, "patch", [(1, 0), (2, 3)])
    inner = (where[0] == 1) | (where[0] == 2)
    return [x, next_to, far, jnp.where(inner, middle, ends)]


def body(sizes, queries, fresh_kv, cached_kv, exponents, out_weight, hidden_in, attn_gate):
    n_patch, n_rel = sizes["patch"], sizes["head"] * sizes["sub"]
    heads = queries.shape[1] // HEAD_DIM
    split = math.gcd(heads, n_patch)
    per = heads // split
    patch_at = lax.axis_index("patch")
    where = jnp.stack(
        [
            patch_at,
            patch_at % split,
            lax.axis_index("head") * sizes["sub"] + lax.axis_index("sub"),
            lax.axis_index("grp"),
        ]
    ).astype(jnp.int32)

    arrived = []
    for chunk in range(per):
        sent = pack(split, per, chunk, where, exponents, queries, fresh_kv, cached_kv)
        pieces = [sent[0]] + [
            swap(sent[rel], "patch", n_patch, rel) for rel in range(1, split)
        ]
        arrived.append(pieces)
    weights, plan = share_weight(sizes, split, per, out_weight, where)

    slots = []
    for pieces in arrived:
        kv_pieces = list(pieces)
        for rel in range(split, n_patch, split):
            kv_pieces += [swap(x, "patch", n_patch, rel) for x in pieces]
        out = attend(where, n_rel, pieces, kv_pieces)
        out = [out[0]] + [swap(out[rel], ("head", "sub"), n_rel, rel) for rel in range(1, n_rel)]
        flat = [x.reshape(-1, HEAD_DIM) for x in out]
        slots.append(gather(jnp.concatenate(flat, axis=1), where, n_patch))

    acc = None
    for chunk in range(per):
        acc = project(plan, split, chunk, where, slots[chunk], weights, acc, chunk == per - 1)
        if chunk < per - 1:
            acc = acc[0]
    blocks = [acc[0]] + [swap(acc[rel], "patch", n_patch, rel) for rel in range(1, n_patch)]
    return mix(where, hidden_in, attn_gate, blocks)


def solution(mesh):
    in_specs = (
        P(("grp", "patch"), ("head", "sub")),
        P(None, ("grp", "patch"), ("head", "sub")),
        P(None, "grp", ("head", "sub")),
        P(None, ("grp", "patch"), ("head", "sub")),
        P(("head", "sub"), "patch"),
        P(("grp", "patch", "head", "sub"), None),
        P(),
    )
    out_specs = P(("grp", "patch", "head", "sub"), None)
    return jax.shard_map(
        functools.partial(body, dict(mesh.shape)),
        mesh=mesh,
        in_specs=in_specs,
        out_specs=out_specs,
        check_vma=False,
    )
```

```python
import functools
import math

import jax
import jax.numpy as jnp
from jax import lax
from jax.experimental import pallas as pl
from jax.experimental.pallas import tpu as pltpu
from jax.sharding import PartitionSpec as P

HEAD_DIM = 128
SCALE_ROWS = 128
SATURATION = 448.0
VMEM_BYTES = 32 * 1024 * 1024


def spec(shape):
    return pl.BlockSpec(shape, lambda i, w: (0,) * len(shape))


def call(kernel, name, out_shape, grid, in_specs, out_specs, scratch=(), cost=None):
    return pl.pallas_call(
        kernel,
        out_shape=out_shape,
        grid_spec=pltpu.PrefetchScalarGridSpec(
            num_scalar_prefetch=1,
            grid=(grid,),
            in_specs=in_specs,
            out_specs=out_specs,
            scratch_shapes=list(scratch),
        ),
        compiler_params=pltpu.CompilerParams(vmem_limit_bytes=VMEM_BYTES),
        cost_estimate=cost,
        name=name,
    )


def swap(x, axes, count, mask, only=None):
    pairs = [(at, at ^ mask) for at in range(count) if only is None or at in only]
    return lax.ppermute(x, axes, pairs)


def pack_kernel(split, per, where_ref, exps_ref, q_ref, fresh_ref, cached_ref, *outs):
    rows = q_ref.shape[0]
    block = pl.program_id(0) * rows // SCALE_ROWS
    for dest in range(split):
        for chunk in range(per):
            head = dest * per + chunk
            lanes = slice(head * HEAD_DIM, (head + 1) * HEAD_DIM)
            outs[chunk][dest, 0] = q_ref[:, lanes]
            for stacked in range(2):
                power = jnp.full((1, HEAD_DIM), exps_ref[stacked, block, head].astype(jnp.float32))
                cached = cached_ref[stacked, :, lanes].astype(jnp.float32)
                residual = fresh_ref[stacked, :, lanes].astype(jnp.float32) - cached
                codes = jnp.clip(
                    residual * jnp.exp2(-power), -SATURATION, SATURATION
                ).astype(jnp.bfloat16)
                decoded = cached + codes.astype(jnp.float32) * jnp.exp2(power)
                outs[chunk][dest, 1 + stacked] = decoded.astype(jnp.bfloat16)


def pack(split, per, where, exponents, queries, fresh_kv, cached_kv):
    tok, channels = queries.shape
    rows = SCALE_ROWS // 2
    steps = tok // rows
    out = jax.ShapeDtypeStruct((split, 3, tok, HEAD_DIM), jnp.bfloat16)
    return call(
        functools.partial(pack_kernel, split, per),
        "pack",
        [out] * per,
        steps,
        [
            pl.BlockSpec(memory_space=pltpu.SMEM),
            pl.BlockSpec((rows, channels), lambda i, w: (i, 0)),
            pl.BlockSpec((2, rows, channels), lambda i, w: (0, i, 0)),
            pl.BlockSpec((2, rows, channels), lambda i, w: (0, w[0] * steps + i, 0)),
        ],
        [pl.BlockSpec((split, 3, rows, HEAD_DIM), lambda i, w: (0, 0, i, 0))] * per,
    )(where, exponents, queries, fresh_kv, cached_kv)


def attend_kernel(where_ref, q_ref, kv_ref, out_ref):
    split = q_ref.shape[0]
    n_rel, _, rows, _ = out_ref.shape
    factor = HEAD_DIM**-0.5 * math.log2(math.e)
    keys = kv_ref[:, 1].reshape(-1, HEAD_DIM)
    values = kv_ref[:, 2].reshape(-1, HEAD_DIM)
    values = jnp.concatenate([values, jnp.ones_like(values)], axis=1)
    for at in range(split):
        scores = lax.dot_general(
            q_ref[at, 0], keys, (((1,), (1,)), ((), ())), preferred_element_type=jnp.float32
        )
        peak = jnp.max(scores, axis=1, keepdims=True)
        expo = jnp.exp2((scores - peak) * factor).astype(jnp.bfloat16)
        mix = jnp.dot(expo, values, preferred_element_type=jnp.float32)
        mix = (mix[:, :HEAD_DIM] / mix[:, HEAD_DIM:]).astype(jnp.bfloat16)
        for rel in range(n_rel):
            out_ref[rel, at] = mix[rel * rows : (rel + 1) * rows]


def attend(where, n_rel, arrived, everyone):
    split, _, tok, feat = arrived.shape
    out = jax.ShapeDtypeStruct((n_rel, split, tok // n_rel, feat), jnp.bfloat16)
    return call(
        attend_kernel,
        "attend",
        out,
        1,
        [spec(arrived.shape), spec(everyone.shape)],
        spec(out.shape),
    )(where, arrived, everyone)


def project_kernel(split, n_slots, with_acc, last, where_ref, *refs):
    slots, weight_ref, refs = refs[:n_slots], refs[n_slots], refs[n_slots + 1 :]
    acc_ref, refs = (refs[0], refs[1:]) if with_acc else (None, refs)
    out_ref, held_ref = refs
    n_rel, rows, _ = slots[0].shape

    @pl.when(pl.program_id(0) == 0)
    def arrange():
        for at, slot in enumerate(slots):
            group, near = divmod(at, split)
            for rel in range(n_rel):
                lane = (rel * split + (where_ref[1] ^ near)) * HEAD_DIM
                held_ref[
                    group * rows : (group + 1) * rows,
                    pl.ds(pl.multiple_of(lane, HEAD_DIM), HEAD_DIM),
                ] = slot[rel]

    acc = jnp.dot(held_ref[...], weight_ref[0], preferred_element_type=jnp.float32)
    if with_acc:
        acc += acc_ref[...]
    if not last:
        out_ref[...] = acc
    else:
        piece = rows // split
        for group in range(n_slots // split):
            for at in range(split):
                start = group * rows + at * piece
                out_ref[(where_ref[2] ^ group) * split + at] = acc[start : start + piece].astype(
                    jnp.bfloat16
                )


def project(split, where, slots, weight_at, acc, last):
    weight, index = weight_at
    n_rel, rows, _ = slots[0].shape
    total = rows * len(slots) // split
    _, depth, cols = weight.shape
    wide = 256 if cols % 256 == 0 else cols
    whole = pl.BlockSpec((total, wide), lambda i, w: (0, i))
    specs = [spec(slots[0].shape)] * len(slots)
    specs.append(pl.BlockSpec((1, depth, wide), lambda i, w: (index, 0, i)))
    if acc is not None:
        specs.append(whole)
    if last:
        piece = rows // split
        out = jax.ShapeDtypeStruct((len(slots), piece, cols), jnp.bfloat16)
        out_spec = pl.BlockSpec((len(slots), piece, wide), lambda i, w: (0, 0, i))
    else:
        out = jax.ShapeDtypeStruct((total, cols), jnp.float32)
        out_spec = whole
    operands = [*slots, weight] + ([] if acc is None else [acc])
    return call(
        functools.partial(project_kernel, split, len(slots), acc is not None, last),
        "project",
        out,
        cols // wide,
        specs,
        out_spec,
        [pltpu.VMEM((total, depth), jnp.bfloat16)],
    )(where, *operands)


def mix_kernel(where_ref, hidden_ref, gate_ref, block_ref, out_ref):
    mixed = hidden_ref[...].astype(jnp.float32) + gate_ref[...] * block_ref[0].astype(jnp.float32)
    out_ref[...] = mixed.astype(jnp.bfloat16)


def mix(where, hidden_in, attn_gate, blocks):
    rows, width = hidden_in.shape
    n_patch, _, cols = blocks.shape
    if cols % HEAD_DIM:
        projected = blocks.transpose(1, 0, 2).reshape(rows, width).astype(jnp.float32)
        return (hidden_in.astype(jnp.float32) + attn_gate * projected).astype(jnp.bfloat16)
    return call(
        mix_kernel,
        "mix",
        jax.ShapeDtypeStruct((rows, width), jnp.bfloat16),
        n_patch,
        [
            pl.BlockSpec((rows, cols), lambda i, w: (0, i)),
            pl.BlockSpec((1, cols), lambda i, w: (0, i)),
            pl.BlockSpec((1, rows, cols), lambda i, w: (i, 0, 0)),
        ],
        pl.BlockSpec((rows, cols), lambda i, w: (0, i)),
    )(where, hidden_in, attn_gate[None], blocks)


def share_weight(sizes, split, per, out_weight):
    cols = out_weight.shape[1]
    own = out_weight.reshape(split, per, HEAD_DIM, cols)
    if per == sizes["grp"]:
        mine = lax.dynamic_index_in_dim(own, lax.axis_index("grp"), 1, keepdims=False)
        shared = lax.all_gather(mine, ("grp", "head", "sub"), axis=0, tiled=True)
        shared = shared.reshape(per, -1, cols)
        return [(shared, chunk) for chunk in range(per)]
    return [
        (
            lax.all_gather(own[:, chunk], ("head", "sub"), axis=0, tiled=True).reshape(1, -1, cols),
            0,
        )
        for chunk in range(per)
    ]


def gather(x, where, n_patch):
    if n_patch != 4:
        return [x] + [swap(x, "patch", n_patch, rel) for rel in range(1, n_patch)]
    far = swap(x, "patch", 4, 2)
    next_to = swap(x, "patch", 4, 1)
    middle = swap(x, "patch", 4, 3, (1, 2))
    ends = lax.ppermute(far, "patch", [(1, 0), (2, 3)])
    inner = (where[0] == 1) | (where[0] == 2)
    return [x, next_to, far, jnp.where(inner, middle, ends)]


def body(sizes, queries, fresh_kv, cached_kv, exponents, out_weight, hidden_in, attn_gate):
    n_patch, n_rel = sizes["patch"], sizes["head"] * sizes["sub"]
    heads = queries.shape[1] // HEAD_DIM
    split = math.gcd(heads, n_patch)
    per = heads // split
    patch_at = lax.axis_index("patch")
    where = jnp.stack([patch_at, patch_at % split, patch_at // split]).astype(jnp.int32)
    near, far = None, None
    if split < n_patch:
        near = [list(range(at, at + split)) for at in range(0, n_patch, split)]
        far = [list(range(at, n_patch, split)) for at in range(split)]

    weights = share_weight(sizes, split, per, out_weight)
    sent = pack(split, per, where, exponents, queries, fresh_kv, cached_kv)
    arrived = [lax.all_to_all(x, "patch", 0, 0, axis_index_groups=near) for x in sent]
    slots = []
    for x in arrived:
        everyone = x if far is None else lax.all_gather(
            x, "patch", axis=0, tiled=True, axis_index_groups=far
        )
        out = lax.all_to_all(attend(where, n_rel, x, everyone), ("head", "sub"), 0, 0)
        slots.append(gather(out.reshape(n_rel, -1, HEAD_DIM), where, n_patch))
    acc = None
    for chunk in range(per):
        acc = project(split, where, slots[chunk], weights[chunk], acc, chunk == per - 1)
    return mix(where, hidden_in, attn_gate, lax.all_to_all(acc, "patch", 0, 0))


def solution(mesh):
    in_specs = (
        P(("grp", "patch"), ("head", "sub")),
        P(None, ("grp", "patch"), ("head", "sub")),
        P(None, "grp", ("head", "sub")),
        P(None, ("grp", "patch"), ("head", "sub")),
        P(("head", "sub"), "patch"),
        P(("grp", "patch", "head", "sub"), None),
        P(),
    )
    out_specs = P(("grp", "patch", "head", "sub"), None)
    return jax.shard_map(
        functools.partial(body, dict(mesh.shape)),
        mesh=mesh,
        in_specs=in_specs,
        out_specs=out_specs,
        check_vma=False,
    )
```

```python
import functools
import math

import jax
import jax.numpy as jnp
from jax import lax
from jax.experimental import pallas as pl
from jax.experimental.pallas import tpu as pltpu
from jax.sharding import PartitionSpec as P

HEAD_DIM = 128
SCALE_ROWS = 128
SATURATION = 448.0
VMEM_BYTES = 32 * 1024 * 1024
ATTEND_FLOPS = 20_000_000_000
PACK_VMEM_BYTES = 60 * 1024 * 1024


def spec(shape):
    return pl.BlockSpec(shape, lambda i, w: (0,) * len(shape))


def call(kernel, name, out_shape, grid, in_specs, out_specs, scratch=(), cost=None, vmem=VMEM_BYTES):
    return pl.pallas_call(
        kernel,
        out_shape=out_shape,
        grid_spec=pltpu.PrefetchScalarGridSpec(
            num_scalar_prefetch=1,
            grid=(grid,),
            in_specs=in_specs,
            out_specs=out_specs,
            scratch_shapes=list(scratch),
        ),
        compiler_params=pltpu.CompilerParams(vmem_limit_bytes=vmem),
        cost_estimate=cost,
        name=name,
    )


def swap(x, axes, count, mask, only=None):
    pairs = [(at, at ^ mask) for at in range(count) if only is None or at in only]
    return lax.ppermute(x, axes, pairs)


def piece_place(split, per, rel, chunk):
    if rel < 2:
        return rel, chunk
    return 2 + chunk * (split - 2) + rel - 2, 0


def pack_kernel(split, per, where_ref, exps_ref, q_ref, fresh_ref, cached_ref, *outs):
    rows = q_ref.shape[0]
    block = pl.program_id(0) * rows // SCALE_ROWS
    for chunk in range(per):
        for rel in range(split):
            number, index = piece_place(split, per, rel, chunk)
            out = outs[number].at[index]
            head = (where_ref[1] ^ rel) * per + chunk
            lanes = pl.ds(pl.multiple_of(head * HEAD_DIM, HEAD_DIM), HEAD_DIM)
            out[0] = q_ref[:, lanes]
            for stacked in range(2):
                power = jnp.full((1, HEAD_DIM), exps_ref[stacked, block, head].astype(jnp.float32))
                cached = cached_ref[stacked, :, lanes].astype(jnp.float32)
                residual = fresh_ref[stacked, :, lanes].astype(jnp.float32) - cached
                codes = jnp.clip(
                    residual * jnp.exp2(-power), -SATURATION, SATURATION
                ).astype(jnp.bfloat16)
                decoded = cached + codes.astype(jnp.float32) * jnp.exp2(power)
                out[1 + stacked] = decoded.astype(jnp.bfloat16)


def pack(split, per, where, exponents, queries, fresh_kv, cached_kv):
    tok, channels = queries.shape
    rows = SCALE_ROWS // 2
    steps = tok // rows
    sizes = [per] * 2 + [1] * (per * (split - 2))
    return call(
        functools.partial(pack_kernel, split, per),
        "pack",
        [jax.ShapeDtypeStruct((size, 3, tok, HEAD_DIM), jnp.bfloat16) for size in sizes],
        steps,
        [
            pl.BlockSpec(memory_space=pltpu.SMEM),
            pl.BlockSpec((rows, channels), lambda i, w: (i, 0)),
            pl.BlockSpec((2, rows, channels), lambda i, w: (0, i, 0)),
            pl.BlockSpec((2, rows, channels), lambda i, w: (0, w[0] * steps + i, 0)),
        ],
        [pl.BlockSpec((size, 3, rows, HEAD_DIM), lambda i, w: (0, 0, i, 0)) for size in sizes],
        vmem=PACK_VMEM_BYTES,
    )(where, exponents, queries, fresh_kv, cached_kv)


def attend_kernel(split, n_kv, where_ref, *refs):
    q_refs, kv_refs, outs = refs[:split], refs[split : split + n_kv], refs[split + n_kv : -1]
    mix_ref = refs[-1]
    factor = HEAD_DIM**-0.5 * math.log2(math.e)
    keys = jnp.concatenate([ref[0, 1] for ref in kv_refs], axis=0)
    values = jnp.concatenate([ref[0, 2] for ref in kv_refs], axis=0)
    values = jnp.concatenate([values, jnp.ones_like(values)], axis=1)
    for rel in range(split):
        scores = lax.dot_general(
            q_refs[rel][0, 0], keys, (((1,), (1,)), ((), ())), preferred_element_type=jnp.float32
        )
        peak = jnp.max(scores, axis=1, keepdims=True)
        expo = jnp.exp2((scores - peak) * factor).astype(jnp.bfloat16)
        mix = jnp.dot(expo, values, preferred_element_type=jnp.float32)
        mix = mix[:, :HEAD_DIM] / mix[:, HEAD_DIM:]
        mix_ref[rel] = mix.reshape(mix_ref.shape[1:])
        for at, out in enumerate(outs):
            out[where_ref[1] ^ rel] = mix_ref[rel, where_ref[3] ^ at].astype(jnp.bfloat16)


def attend(where, n_rel, pieces, kv_pieces):
    split = len(pieces)
    _, _, tok, feat = pieces[0][0].shape
    rows = tok // n_rel
    out = jax.ShapeDtypeStruct((split, rows, feat), jnp.bfloat16)
    return call(
        functools.partial(attend_kernel, split, len(kv_pieces)),
        "attend",
        [out] * n_rel,
        1,
        [
            pl.BlockSpec((1, 3, tok, feat), lambda i, w, at=at: (at, 0, 0, 0))
            for _, at in pieces + kv_pieces
        ],
        [spec(out.shape)] * n_rel,
        [pltpu.VMEM((split, n_rel, rows, feat), jnp.float32)],
        pl.CostEstimate(flops=ATTEND_FLOPS, bytes_accessed=0, transcendentals=0),
    )(where, *[x for x, _ in pieces + kv_pieces])


def project_kernel(split, n_slots, with_acc, last, where_ref, *refs):
    slots, weight_ref, refs = refs[:n_slots], refs[n_slots], refs[n_slots + 1 :]
    acc_ref, refs = (refs[0], refs[1:]) if with_acc else (None, refs)
    outs, held_ref = refs[:-2], refs[-2]
    out_ref = outs[0]
    n_rel, rows, _ = slots[0].shape

    @pl.when(pl.program_id(0) == 0)
    def arrange():
        for at, slot in enumerate(slots):
            group, near = divmod(at, split)
            for rel in range(n_rel):
                lane = ((where_ref[3] ^ rel) * split + (where_ref[1] ^ near)) * HEAD_DIM
                held_ref[
                    group * rows : (group + 1) * rows,
                    pl.ds(pl.multiple_of(lane, HEAD_DIM), HEAD_DIM),
                ] = slot[rel]

    acc = jnp.dot(held_ref[...], weight_ref[0], preferred_element_type=jnp.float32)
    if with_acc:
        acc += acc_ref[...]
    if not last:
        out_ref[...] = acc
    else:
        full_ref = refs[-1]
        full_ref[...] = acc.reshape(full_ref.shape)
        for at, out in enumerate(outs):
            group, near = divmod(at, split)
            out[...] = full_ref[group, where_ref[1] ^ near].astype(jnp.bfloat16)


def project(split, where, slots, weight_at, acc, last):
    weight, index = weight_at
    n_rel, rows, _ = slots[0].shape
    total = rows * len(slots) // split
    _, depth, cols = weight.shape
    wide = 256 if cols % 256 == 0 else cols
    whole = pl.BlockSpec((total, wide), lambda i, w: (0, i))
    specs = [spec(slots[0].shape)] * len(slots)
    specs.append(pl.BlockSpec((1, depth, wide), lambda i, w: (index, 0, i)))
    if acc is not None:
        specs.append(whole)
    scratch = [pltpu.VMEM((total, depth), jnp.bfloat16)]
    if last:
        piece = rows // split
        out = [jax.ShapeDtypeStruct((piece, cols), jnp.bfloat16)] * len(slots)
        out_spec = [pl.BlockSpec((piece, wide), lambda i, w: (0, i))] * len(slots)
        scratch.append(pltpu.VMEM((len(slots) // split, split, piece, wide), jnp.float32))
    else:
        out = jax.ShapeDtypeStruct((total, cols), jnp.float32)
        out_spec = whole
        scratch.append(pltpu.VMEM((8, HEAD_DIM), jnp.float32))
    operands = [*slots, weight] + ([] if acc is None else [acc])
    return call(
        functools.partial(project_kernel, split, len(slots), acc is not None, last),
        "project",
        out,
        cols // wide,
        specs,
        out_spec,
        scratch,
    )(where, *operands)


def mix_kernel(n_patch, where_ref, hidden_ref, gate_ref, *refs):
    out_ref = refs[-1]
    cols = refs[0].shape[1]
    for rel in range(n_patch):
        lanes = pl.ds(pl.multiple_of((where_ref[0] ^ rel) * cols, HEAD_DIM), cols)
        mixed = hidden_ref[:, lanes].astype(jnp.float32) + gate_ref[:, lanes] * refs[rel][
            ...
        ].astype(jnp.float32)
        out_ref[:, lanes] = mixed.astype(jnp.bfloat16)


def mix(where, hidden_in, attn_gate, blocks):
    rows, width = hidden_in.shape
    n_patch, cols = len(blocks), blocks[0].shape[1]
    if cols % HEAD_DIM:
        order = jnp.stack(blocks)[where[0] ^ jnp.arange(n_patch)]
        projected = order.transpose(1, 0, 2).reshape(rows, width).astype(jnp.float32)
        return (hidden_in.astype(jnp.float32) + attn_gate * projected).astype(jnp.bfloat16)
    return call(
        functools.partial(mix_kernel, n_patch),
        "mix",
        jax.ShapeDtypeStruct((rows, width), jnp.bfloat16),
        1,
        [spec((rows, width)), spec((1, width))] + [spec(blocks[0].shape)] * n_patch,
        spec((rows, width)),
    )(where, hidden_in, attn_gate[None], *blocks)


def share_weight(sizes, split, per, out_weight):
    cols = out_weight.shape[1]
    own = out_weight.reshape(split, per, HEAD_DIM, cols)
    if per == sizes["grp"]:
        mine = lax.dynamic_index_in_dim(own, lax.axis_index("grp"), 1, keepdims=False)
        shared = lax.all_gather(mine, ("grp", "head", "sub"), axis=0, tiled=True)
        shared = shared.reshape(per, -1, cols)
        return [(shared, chunk) for chunk in range(per)]
    return [
        (
            lax.all_gather(own[:, chunk], ("head", "sub"), axis=0, tiled=True).reshape(1, -1, cols),
            0,
        )
        for chunk in range(per)
    ]


def gather(x, where, n_patch):
    if n_patch != 4:
        return [x] + [swap(x, "patch", n_patch, rel) for rel in range(1, n_patch)]
    far = swap(x, "patch", 4, 2)
    next_to = swap(x, "patch", 4, 1)
    middle = swap(x, "patch", 4, 3, (1, 2))
    far, next_to = lax.optimization_barrier((far, next_to))
    ends = lax.ppermute(far, "patch", [(1, 0), (2, 3)])
    inner = (where[0] == 1) | (where[0] == 2)
    return [x, next_to, far, jnp.where(inner, middle, ends)]


def body(sizes, queries, fresh_kv, cached_kv, exponents, out_weight, hidden_in, attn_gate):
    n_patch, n_rel = sizes["patch"], sizes["head"] * sizes["sub"]
    heads = queries.shape[1] // HEAD_DIM
    split = math.gcd(heads, n_patch)
    per = heads // split
    patch_at = lax.axis_index("patch")
    rel_at = lax.axis_index("head") * sizes["sub"] + lax.axis_index("sub")
    where = jnp.stack([patch_at, patch_at % split, patch_at // split, rel_at]).astype(jnp.int32)

    sent = pack(split, per, where, exponents, queries, fresh_kv, cached_kv)
    sent, out_weight = lax.optimization_barrier((sent, out_weight))
    arrived = [sent[0], swap(sent[1], "patch", n_patch, 1)]
    for at, x in enumerate(sent[2:]):
        arrived.append(swap(x, "patch", n_patch, 2 + at % (split - 2)))
    weights = share_weight(sizes, split, per, out_weight)
    slots = []
    for chunk in range(per):
        pieces = []
        for rel in range(split):
            number, index = piece_place(split, per, rel, chunk)
            pieces.append((arrived[number], index))
        kv_pieces = list(pieces)
        for rel in range(split, n_patch, split):
            kv_pieces += [(swap(x, "patch", n_patch, rel), at) for x, at in pieces]
        out = attend(where, n_rel, pieces, kv_pieces)
        out = [out[0]] + [swap(out[rel], ("head", "sub"), n_rel, rel) for rel in range(1, n_rel)]
        joined = jnp.stack([x.reshape(-1, HEAD_DIM) for x in out])
        slots.append(gather(joined, where, n_patch))
    acc = None
    for chunk in range(per):
        acc = project(split, where, slots[chunk], weights[chunk], acc, chunk == per - 1)
    blocks = [acc[0]] + [swap(acc[rel], "patch", n_patch, rel) for rel in range(1, n_patch)]
    return mix(where, hidden_in, attn_gate, blocks)


def solution(mesh):
    in_specs = (
        P(("grp", "patch"), ("head", "sub")),
        P(None, ("grp", "patch"), ("head", "sub")),
        P(None, "grp", ("head", "sub")),
        P(None, ("grp", "patch"), ("head", "sub")),
        P(("head", "sub"), "patch"),
        P(("grp", "patch", "head", "sub"), None),
        P(),
    )
    out_specs = P(("grp", "patch", "head", "sub"), None)
    return jax.shard_map(
        functools.partial(body, dict(mesh.shape)),
        mesh=mesh,
        in_specs=in_specs,
        out_specs=out_specs,
        check_vma=False,
    )
```

```python
import functools
import math

import jax
import jax.numpy as jnp
from jax import lax
from jax.experimental import pallas as pl
from jax.experimental.pallas import tpu as pltpu
from jax.sharding import PartitionSpec as P

HEAD_DIM = 128
SCALE_ROWS = 128
SATURATION = 448.0
VMEM_BYTES = 32 * 1024 * 1024
PACK_VMEM_BYTES = 60 * 1024 * 1024
ATTEND_FLOPS = 5_000_000_000
PROJECT_FLOPS = 5_000_000_000

PATCH, NEAR, HEAD, SUB, INNER = range(5)


def spec(shape):
    return pl.BlockSpec(shape, lambda i, w: (0,) * len(shape))


def call(kernel, name, out_shape, grid, in_specs, out_specs, scratch=(), flops=0, vmem=VMEM_BYTES):
    return pl.pallas_call(
        kernel,
        out_shape=out_shape,
        grid_spec=pltpu.PrefetchScalarGridSpec(
            num_scalar_prefetch=1,
            grid=(grid,),
            in_specs=in_specs,
            out_specs=out_specs,
            scratch_shapes=list(scratch),
        ),
        compiler_params=pltpu.CompilerParams(vmem_limit_bytes=vmem),
        cost_estimate=pl.CostEstimate(flops=flops, bytes_accessed=0, transcendentals=0),
        name=name,
    )


def swap(x, axes, count, mask, only=None):
    pairs = [(at, at ^ mask) for at in range(count) if only is None or at in only]
    return lax.ppermute(x, axes, pairs)


def pack_kernel(split, per, where_ref, exps_ref, q_ref, fresh_ref, cached_ref, *outs):
    rows = q_ref.shape[0]
    block = pl.program_id(0) * rows // SCALE_ROWS
    for rel in range(split):
        for chunk in range(per):
            head = (where_ref[NEAR] ^ rel) * per + chunk
            lanes = pl.ds(pl.multiple_of(head * HEAD_DIM, HEAD_DIM), HEAD_DIM)
            here = pl.ds(chunk * HEAD_DIM, HEAD_DIM)
            outs[rel][0, :, here] = q_ref[:, lanes]
            for stacked in range(2):
                power = jnp.full((1, HEAD_DIM), exps_ref[stacked, block, head].astype(jnp.float32))
                cached = cached_ref[stacked, :, lanes].astype(jnp.float32)
                residual = fresh_ref[stacked, :, lanes].astype(jnp.float32) - cached
                codes = jnp.clip(
                    residual * jnp.exp2(-power), -SATURATION, SATURATION
                ).astype(jnp.bfloat16)
                decoded = cached + codes.astype(jnp.float32) * jnp.exp2(power)
                outs[rel][1 + stacked, :, here] = decoded.astype(jnp.bfloat16)


def pack(split, per, where, exponents, queries, fresh_kv, cached_kv):
    tok, channels = queries.shape
    feat = channels // split
    rows = SCALE_ROWS // 2
    steps = tok // rows
    return call(
        functools.partial(pack_kernel, split, per),
        "pack",
        [jax.ShapeDtypeStruct((3, tok, feat), jnp.bfloat16)] * split,
        steps,
        [
            pl.BlockSpec(memory_space=pltpu.SMEM),
            pl.BlockSpec((rows, channels), lambda i, w: (i, 0)),
            pl.BlockSpec((2, rows, channels), lambda i, w: (0, i, 0)),
            pl.BlockSpec((2, rows, channels), lambda i, w: (0, w[PATCH] * steps + i, 0)),
        ],
        [pl.BlockSpec((3, rows, feat), lambda i, w: (0, i, 0))] * split,
        vmem=PACK_VMEM_BYTES,
    )(where, exponents, queries, fresh_kv, cached_kv)


def attend_kernel(split, part, parts, where_ref, *refs):
    q_refs, kv_refs, out_ref = refs[:split], refs[:-1], refs[-1]
    factor = HEAD_DIM**-0.5 * math.log2(math.e)
    tok, feat = q_refs[0].shape[1:]
    count = out_ref.shape[1] // part[1]
    starts = [at * (tok // count) + part[0] for at in range(count)]
    for head in range(feat // HEAD_DIM):
        lanes = pl.ds(head * HEAD_DIM, HEAD_DIM)
        keys = jnp.concatenate([ref[1, :, lanes] for ref in kv_refs], axis=0)
        values = jnp.concatenate([ref[2, :, lanes] for ref in kv_refs], axis=0)
        values = jnp.concatenate([values, jnp.ones_like(values)], axis=1)
        for rel in range(split):
            rows = [q_refs[rel][0, start : start + part[1], lanes] for start in starts]
            query = jnp.concatenate(rows, axis=0) if len(rows) > 1 else rows[0]
            scores = lax.dot_general(
                query, keys, (((1,), (1,)), ((), ())), preferred_element_type=jnp.float32
            )
            peak = jnp.max(scores, axis=1, keepdims=True)
            expo = jnp.exp2((scores - peak) * factor).astype(jnp.bfloat16)
            mix = jnp.dot(expo, values, preferred_element_type=jnp.float32)
            mix = mix[:, :HEAD_DIM] / mix[:, HEAD_DIM:]
            out_ref[where_ref[NEAR] ^ rel, :, lanes] = mix.astype(jnp.bfloat16)


def attend(where, part, count, pieces, kv_pieces):
    split = len(pieces)
    _, tok, feat = pieces[0].shape
    out = jax.ShapeDtypeStruct((split, count * part[1], feat), jnp.bfloat16)
    return call(
        functools.partial(attend_kernel, split, part, count),
        "attend",
        out,
        1,
        [spec((3, tok, feat))] * len(kv_pieces),
        spec(out.shape),
        flops=ATTEND_FLOPS,
    )(where, *kv_pieces)


def project_kernel(split, n_slots, n_more, where_ref, *refs):
    slots, refs = refs[:n_slots], refs[n_slots:]
    more, weight_ref, refs = refs[:n_more], refs[n_more], refs[n_more + 1 :]
    outs, held_ref, acc_ref = refs[:-2], refs[-2], refs[-1]
    rows, feat = slots[0].shape
    n_sub, n_head = acc_ref.shape[3], acc_ref.shape[2]

    @pl.when(pl.program_id(0) == 0)
    def arrange():
        for at, slot in enumerate(slots):
            group, near = divmod(at, split)
            lane = (where_ref[NEAR] ^ near) * feat
            block = slot[...]
            if more and at == n_slots - 1:
                block = jnp.where(where_ref[INNER] == 1, block, more[0][...])
            held_ref[
                group * rows : (group + 1) * rows, pl.ds(pl.multiple_of(lane, HEAD_DIM), feat)
            ] = block

    acc = jnp.dot(held_ref[...], weight_ref[...], preferred_element_type=jnp.float32)
    acc_ref[...] = acc.reshape(acc_ref.shape)
    for sub in range(n_sub):
        for head in range(n_head):
            for at in range(n_slots):
                group, near = divmod(at, split)
                outs[sub][head, at] = acc_ref[
                    group, where_ref[NEAR] ^ near, where_ref[HEAD] ^ head, where_ref[SUB] ^ sub
                ].astype(jnp.bfloat16)


def project(split, where, slots, more, weight, n_head, n_sub):
    rows, feat = slots[0].shape
    n_patch = len(slots)
    total = rows * n_patch // split
    depth, cols = weight.shape
    wide = 640 if cols % 640 == 0 else cols
    piece = rows // (split * n_head * n_sub)
    return call(
        functools.partial(project_kernel, split, n_patch, len(more)),
        "project",
        [jax.ShapeDtypeStruct((n_head, n_patch, piece, cols), jnp.bfloat16)] * n_sub,
        cols // wide,
        [spec((rows, feat))] * (n_patch + len(more))
        + [pl.BlockSpec((depth, wide), lambda i, w: (0, i))],
        [pl.BlockSpec((n_head, n_patch, piece, wide), lambda i, w: (0, 0, 0, i))] * n_sub,
        [
            pltpu.VMEM((total, depth), jnp.bfloat16),
            pltpu.VMEM((n_patch // split, split, n_head, n_sub, piece, wide), jnp.float32),
        ],
        flops=PROJECT_FLOPS,
    )(where, *slots, *more, weight)


def mix_kernel(n_patch, where_ref, hidden_ref, gate_ref, *refs):
    blocks, out_ref = refs[:-1], refs[-1]
    piece, cols = blocks[0].shape
    for part in range(len(blocks) // n_patch):
        rows = pl.ds(part * piece, piece)
        for rel in range(n_patch):
            lanes = pl.ds(pl.multiple_of((where_ref[PATCH] ^ rel) * cols, HEAD_DIM), cols)
            mixed = hidden_ref[rows, lanes].astype(jnp.float32) + gate_ref[:, lanes] * blocks[
                part * n_patch + rel
            ][...].astype(jnp.float32)
            out_ref[rows, lanes] = mixed.astype(jnp.bfloat16)


def mix(where, hidden_in, attn_gate, blocks):
    rows, width = hidden_in.shape
    n_patch = len(blocks[0])
    piece, cols = blocks[0][0].shape
    if cols % HEAD_DIM:
        order = jnp.concatenate([jnp.stack(x) for x in blocks], axis=1)
        order = order[where[PATCH] ^ jnp.arange(n_patch)]
        projected = order.transpose(1, 0, 2).reshape(rows, width).astype(jnp.float32)
        return (hidden_in.astype(jnp.float32) + attn_gate * projected).astype(jnp.bfloat16)
    flat = [x for part in blocks for x in part]
    return call(
        functools.partial(mix_kernel, n_patch),
        "mix",
        jax.ShapeDtypeStruct((rows, width), jnp.bfloat16),
        1,
        [spec((rows, width)), spec((1, width))] + [spec((piece, cols))] * len(flat),
        spec((rows, width)),
    )(where, hidden_in, attn_gate[None], *flat)


def gather(x, n_patch):
    if n_patch != 4:
        return [x] + [swap(x, "patch", n_patch, rel) for rel in range(1, n_patch)], []
    far = swap(x, "patch", 4, 2)
    next_to = swap(x, "patch", 4, 1)
    middle = swap(x, "patch", 4, 3, (1, 2))
    far, next_to = lax.optimization_barrier((far, next_to))
    ends = lax.ppermute(far, "patch", [(1, 0), (2, 3)])
    return [x, next_to, far, middle], [ends]


def add_sub_kernel(n_sub, where_ref, *refs):
    terms, kept_ref, outs = refs[:n_sub], refs[n_sub], refs[n_sub + 1 :]
    for head in range(len(outs) + 1):
        total = terms[0][head].astype(jnp.float32)
        for term in terms[1:]:
            total += term[head].astype(jnp.float32)
        if head == 0:
            kept_ref[...] = total
        else:
            outs[head - 1][...] = total.astype(jnp.bfloat16)


def add_head_kernel(n_more, where_ref, kept_ref, *refs):
    for at, out in enumerate(refs[n_more:]):
        total = kept_ref[at]
        for term in refs[:n_more]:
            total += term[at].astype(jnp.float32)
        out[...] = total.astype(jnp.bfloat16)


def reduce_sub(sizes, where, terms):
    n_sub, n_head = sizes["sub"], sizes["head"]
    terms = [terms[0]] + [swap(terms[rel], "sub", n_sub, rel) for rel in range(1, n_sub)]
    shape = terms[0].shape[1:]
    return call(
        functools.partial(add_sub_kernel, n_sub),
        "add_sub",
        [jax.ShapeDtypeStruct(shape, jnp.float32)]
        + [jax.ShapeDtypeStruct(shape, jnp.bfloat16)] * (n_head - 1),
        1,
        [spec(terms[0].shape)] * n_sub,
        [spec(shape)] * n_head,
    )(where, *terms)


def reduce_head(sizes, where, sums):
    n_head = sizes["head"]
    shape = sums[0].shape
    sums = [sums[0]] + [swap(sums[rel], "head", n_head, rel) for rel in range(1, n_head)]
    return call(
        functools.partial(add_head_kernel, n_head - 1),
        "add_head",
        [jax.ShapeDtypeStruct(shape[1:], jnp.bfloat16)] * shape[0],
        1,
        [spec(shape)] * n_head,
        [spec(shape[1:])] * shape[0],
    )(where, *sums)


def body(sizes, queries, fresh_kv, cached_kv, exponents, out_weight, hidden_in, attn_gate):
    n_patch, n_head, n_sub = sizes["patch"], sizes["head"], sizes["sub"]
    tok, channels = queries.shape
    heads = channels // HEAD_DIM
    split = math.gcd(heads, n_patch)
    patch_at = lax.axis_index("patch")
    inner = (patch_at > 0) & (patch_at < n_patch - 1)
    where = jnp.stack(
        [patch_at, patch_at % split, lax.axis_index("head"), lax.axis_index("sub"), inner]
    ).astype(jnp.int32)

    sent = pack(split, heads // split, where, exponents, queries, fresh_kv, cached_kv)
    pieces = [sent[0]] + [swap(sent[rel], "patch", n_patch, rel) for rel in range(1, split)]
    kv_pieces = list(pieces)
    for rel in range(split, n_patch, split):
        kv_pieces += [swap(x, "patch", n_patch, rel) for x in pieces]

    count = n_head * n_sub
    piece = tok // count
    parts = 2 if piece % 32 == 0 else 1
    slots = []
    for part in range(parts):
        rows = (part * (piece // parts), piece // parts)
        attended = attend(where, rows, count, pieces, kv_pieces)
        attended = attended.reshape(-1, attended.shape[2])
        slots.append(gather(attended, n_patch))
    blocks = []
    for part in range(parts):
        terms = project(split, where, *slots[part], out_weight, n_head, n_sub)
        sums = reduce_sub(sizes, where, terms)
        if part + 1 < parts:
            sums, slots[part + 1] = lax.optimization_barrier((sums, slots[part + 1]))
        total = reduce_head(sizes, where, sums)
        blocks.append(
            [total[0]] + [swap(total[rel], "patch", n_patch, rel) for rel in range(1, n_patch)]
        )
    return mix(where, hidden_in, attn_gate, blocks)


def solution(mesh):
    in_specs = (
        P(("grp", "patch"), ("head", "sub")),
        P(None, ("grp", "patch"), ("head", "sub")),
        P(None, "grp", ("head", "sub")),
        P(None, ("grp", "patch"), ("head", "sub")),
        P(("head", "sub"), "patch"),
        P(("grp", "patch", "head", "sub"), None),
        P(),
    )
    out_specs = P(("grp", "patch", "head", "sub"), None)
    return jax.shard_map(
        functools.partial(body, dict(mesh.shape)),
        mesh=mesh,
        in_specs=in_specs,
        out_specs=out_specs,
        check_vma=False,
    )
```

```python
import functools
import math

import jax
import jax.numpy as jnp
from jax import lax
from jax.experimental import pallas as pl
from jax.experimental.pallas import tpu as pltpu
from jax.sharding import PartitionSpec as P

HEAD_DIM = 128
SCALE_ROWS = 128
SATURATION = 448.0
VMEM_BYTES = 32 * 1024 * 1024
PACK_VMEM_BYTES = 60 * 1024 * 1024
ATTEND_FLOPS = 1
PROJECT_FLOPS = 1

PATCH, NEAR, HEAD, SUB, INNER = range(5)


def spec(shape):
    return pl.BlockSpec(shape, lambda i, w: (0,) * len(shape))


def call(kernel, name, out_shape, grid, in_specs, out_specs, scratch=(), flops=1, vmem=VMEM_BYTES):
    return pl.pallas_call(
        kernel,
        out_shape=out_shape,
        grid_spec=pltpu.PrefetchScalarGridSpec(
            num_scalar_prefetch=1,
            grid=(grid,),
            in_specs=in_specs,
            out_specs=out_specs,
            scratch_shapes=list(scratch),
        ),
        compiler_params=pltpu.CompilerParams(vmem_limit_bytes=vmem),
        cost_estimate=pl.CostEstimate(flops=flops, bytes_accessed=0, transcendentals=0),
        name=name,
    )


def swap(x, axes, count, mask, only=None):
    pairs = [(at, at ^ mask) for at in range(count) if only is None or at in only]
    return lax.ppermute(x, axes, pairs)


def pack_kernel(span, per, upper, where_ref, exps_ref, q_ref, fresh_ref, cached_ref, *outs):
    rows = q_ref.shape[0]
    block = pl.program_id(0) * rows // SCALE_ROWS
    half = (where_ref[NEAR] // span) ^ upper
    for rel in range(span):
        for chunk in range(per):
            head = ((where_ref[NEAR] % span) ^ rel) * per + chunk
            lanes = pl.ds(pl.multiple_of(head * HEAD_DIM, HEAD_DIM), HEAD_DIM)
            here = pl.ds(chunk * HEAD_DIM, HEAD_DIM)
            outs[rel][0, :, here] = q_ref[:, lanes]
            for stacked in range(2):
                exponent = exps_ref[stacked, block, half * span * per + head]
                power = jnp.full((1, HEAD_DIM), exponent.astype(jnp.float32))
                cached = cached_ref[stacked, :, lanes].astype(jnp.float32)
                residual = fresh_ref[stacked, :, lanes].astype(jnp.float32) - cached
                codes = jnp.clip(
                    residual * jnp.exp2(-power), -SATURATION, SATURATION
                ).astype(jnp.bfloat16)
                decoded = cached + codes.astype(jnp.float32) * jnp.exp2(power)
                outs[rel][1 + stacked, :, here] = decoded.astype(jnp.bfloat16)


def pack(split, per, upper, where, exponents, queries, fresh_kv, cached_kv):
    tok, channels = queries.shape
    span = split // 2
    wide, feat = channels // 2, channels // split
    rows = SCALE_ROWS
    steps = tok // rows

    def half(w):
        return (w[NEAR] // span) ^ upper

    return call(
        functools.partial(pack_kernel, span, per, upper),
        "pack",
        [jax.ShapeDtypeStruct((3, tok, feat), jnp.bfloat16)] * span,
        steps,
        [
            pl.BlockSpec(memory_space=pltpu.SMEM),
            pl.BlockSpec((rows, wide), lambda i, w: (i, half(w))),
            pl.BlockSpec((2, rows, wide), lambda i, w: (0, i, half(w))),
            pl.BlockSpec((2, rows, wide), lambda i, w: (0, w[PATCH] * steps + i, half(w))),
        ],
        [pl.BlockSpec((3, rows, feat), lambda i, w: (0, i, 0))] * span,
        vmem=PACK_VMEM_BYTES,
    )(where, exponents, queries, fresh_kv, cached_kv)


def attend_kernel(split, part, parts, where_ref, *refs):
    q_refs, kv_refs, out_ref = refs[:split], refs[:-1], refs[-1]
    factor = HEAD_DIM**-0.5 * math.log2(math.e)
    tok, feat = q_refs[0].shape[1:]
    count = out_ref.shape[1] // part[1]
    starts = [at * (tok // count) + part[0] for at in range(count)]
    for head in range(feat // HEAD_DIM):
        lanes = pl.ds(head * HEAD_DIM, HEAD_DIM)
        keys = jnp.concatenate([ref[1, :, lanes] for ref in kv_refs], axis=0)
        values = jnp.concatenate([ref[2, :, lanes] for ref in kv_refs], axis=0)
        values = jnp.concatenate([values, jnp.ones_like(values)], axis=1)
        for rel in range(split):
            rows = [q_refs[rel][0, start : start + part[1], lanes] for start in starts]
            query = jnp.concatenate(rows, axis=0) if len(rows) > 1 else rows[0]
            scores = lax.dot_general(
                query, keys, (((1,), (1,)), ((), ())), preferred_element_type=jnp.float32
            )
            peak = jnp.max(scores, axis=1, keepdims=True)
            expo = jnp.exp2((scores - peak) * factor).astype(jnp.bfloat16)
            mix = jnp.dot(expo, values, preferred_element_type=jnp.float32)
            mix = mix[:, :HEAD_DIM] / mix[:, HEAD_DIM:]
            out_ref[where_ref[NEAR] ^ rel, :, lanes] = mix.astype(jnp.bfloat16)


def attend(where, part, count, pieces, kv_pieces):
    split = len(pieces)
    _, tok, feat = pieces[0].shape
    out = jax.ShapeDtypeStruct((split, count * part[1], feat), jnp.bfloat16)
    return call(
        functools.partial(attend_kernel, split, part, count),
        "attend",
        out,
        1,
        [spec((3, tok, feat))] * len(kv_pieces),
        spec(out.shape),
        flops=ATTEND_FLOPS,
    )(where, *kv_pieces)


def project_kernel(split, n_slots, n_more, where_ref, *refs):
    slots, refs = refs[:n_slots], refs[n_slots:]
    more, weight_ref, refs = refs[:n_more], refs[n_more], refs[n_more + 1 :]
    outs, held_ref, acc_ref = refs[:-2], refs[-2], refs[-1]
    rows, feat = slots[0].shape
    n_sub, n_head = acc_ref.shape[3], acc_ref.shape[2]

    @pl.when(pl.program_id(0) == 0)
    def arrange():
        for at, slot in enumerate(slots):
            group, near = divmod(at, split)
            lane = (where_ref[NEAR] ^ near) * feat
            block = slot[...]
            if more and at == n_slots - 1:
                block = jnp.where(where_ref[INNER] == 1, block, more[0][...])
            held_ref[
                group * rows : (group + 1) * rows, pl.ds(pl.multiple_of(lane, HEAD_DIM), feat)
            ] = block

    acc = jnp.dot(held_ref[...], weight_ref[...], preferred_element_type=jnp.float32)
    acc_ref[...] = acc.reshape(acc_ref.shape)
    for sub in range(n_sub):
        for head in range(n_head):
            for at in range(n_slots):
                group, near = divmod(at, split)
                outs[sub][head, at] = acc_ref[
                    group, where_ref[NEAR] ^ near, where_ref[HEAD] ^ head, where_ref[SUB] ^ sub
                ].astype(jnp.bfloat16)


def project(split, where, slots, more, weight, n_head, n_sub):
    rows, feat = slots[0].shape
    n_patch = len(slots)
    total = rows * n_patch // split
    depth, cols = weight.shape
    wide = 640 if cols % 640 == 0 else cols
    piece = rows // (split * n_head * n_sub)
    return call(
        functools.partial(project_kernel, split, n_patch, len(more)),
        "project",
        [jax.ShapeDtypeStruct((n_head, n_patch, piece, cols), jnp.bfloat16)] * n_sub,
        cols // wide,
        [spec((rows, feat))] * (n_patch + len(more))
        + [pl.BlockSpec((depth, wide), lambda i, w: (0, i))],
        [pl.BlockSpec((n_head, n_patch, piece, wide), lambda i, w: (0, 0, 0, i))] * n_sub,
        [
            pltpu.VMEM((total, depth), jnp.bfloat16),
            pltpu.VMEM((n_patch // split, split, n_head, n_sub, piece, wide), jnp.float32),
        ],
        flops=PROJECT_FLOPS,
    )(where, *slots, *more, weight)


def mix_kernel(n_patch, where_ref, hidden_ref, gate_ref, *refs):
    blocks, out_ref = refs[:-1], refs[-1]
    piece, cols = blocks[0].shape
    for part in range(len(blocks) // n_patch):
        rows = pl.ds(part * piece, piece)
        for rel in range(n_patch):
            lanes = pl.ds(pl.multiple_of((where_ref[PATCH] ^ rel) * cols, HEAD_DIM), cols)
            mixed = hidden_ref[rows, lanes].astype(jnp.float32) + gate_ref[:, lanes] * blocks[
                part * n_patch + rel
            ][...].astype(jnp.float32)
            out_ref[rows, lanes] = mixed.astype(jnp.bfloat16)


def mix(where, hidden_in, attn_gate, blocks):
    rows, width = hidden_in.shape
    n_patch = len(blocks[0])
    piece, cols = blocks[0][0].shape
    if cols % HEAD_DIM:
        order = jnp.concatenate([jnp.stack(x) for x in blocks], axis=1)
        order = order[where[PATCH] ^ jnp.arange(n_patch)]
        projected = order.transpose(1, 0, 2).reshape(rows, width).astype(jnp.float32)
        return (hidden_in.astype(jnp.float32) + attn_gate * projected).astype(jnp.bfloat16)
    flat = [x for part in blocks for x in part]
    return call(
        functools.partial(mix_kernel, n_patch),
        "mix",
        jax.ShapeDtypeStruct((rows, width), jnp.bfloat16),
        1,
        [spec((rows, width)), spec((1, width))] + [spec((piece, cols))] * len(flat),
        spec((rows, width)),
    )(where, hidden_in, attn_gate[None], *flat)


def gather(parts, n_patch):
    if n_patch != 4:
        return [
            ([x] + [swap(x, "patch", n_patch, rel) for rel in range(1, n_patch)], [])
            for x in parts
        ]
    far = [swap(x, "patch", 4, 2) for x in parts]
    next_to = [swap(x, "patch", 4, 1) for x in parts]
    middle = [swap(x, "patch", 4, 3, (1, 2)) for x in parts]
    out = []
    for at, x in enumerate(parts):
        far[at], next_to[at], parts = lax.optimization_barrier((far[at], next_to[at], parts))
        ends = lax.ppermute(far[at], "patch", [(1, 0), (2, 3)])
        if at + 1 < len(parts):
            ends, far[at + 1], next_to[at + 1] = lax.optimization_barrier(
                (ends, far[at + 1], next_to[at + 1])
            )
        out.append(([x, next_to[at], far[at], middle[at]], [ends]))
    return out


def add_sub_kernel(n_sub, where_ref, *refs):
    terms, kept_ref, outs = refs[:n_sub], refs[n_sub], refs[n_sub + 1 :]
    for head in range(len(outs) + 1):
        total = terms[0][head].astype(jnp.float32)
        for term in terms[1:]:
            total += term[head].astype(jnp.float32)
        if head == 0:
            kept_ref[...] = total
        else:
            outs[head - 1][...] = total.astype(jnp.bfloat16)


def add_head_kernel(n_more, where_ref, kept_ref, *refs):
    for at, out in enumerate(refs[n_more:]):
        total = kept_ref[at]
        for term in refs[:n_more]:
            total += term[at].astype(jnp.float32)
        out[...] = total.astype(jnp.bfloat16)


def reduce_sub(sizes, where, terms):
    n_sub, n_head = sizes["sub"], sizes["head"]
    terms = [terms[0]] + [swap(terms[rel], "sub", n_sub, rel) for rel in range(1, n_sub)]
    shape = terms[0].shape[1:]
    return call(
        functools.partial(add_sub_kernel, n_sub),
        "add_sub",
        [jax.ShapeDtypeStruct(shape, jnp.float32)]
        + [jax.ShapeDtypeStruct(shape, jnp.bfloat16)] * (n_head - 1),
        1,
        [spec(terms[0].shape)] * n_sub,
        [spec(shape)] * n_head,
    )(where, *terms)


def reduce_head(sizes, where, sums):
    n_head = sizes["head"]
    shape = sums[0].shape
    sums = [sums[0]] + [swap(sums[rel], "head", n_head, rel) for rel in range(1, n_head)]
    return call(
        functools.partial(add_head_kernel, n_head - 1),
        "add_head",
        [jax.ShapeDtypeStruct(shape[1:], jnp.bfloat16)] * shape[0],
        1,
        [spec(shape)] * n_head,
        [spec(shape[1:])] * shape[0],
    )(where, *sums)


def body(sizes, queries, fresh_kv, cached_kv, exponents, out_weight, hidden_in, attn_gate):
    n_patch, n_head, n_sub = sizes["patch"], sizes["head"], sizes["sub"]
    tok, channels = queries.shape
    heads = channels // HEAD_DIM
    split = math.gcd(heads, n_patch)
    patch_at = lax.axis_index("patch")
    inner = (patch_at > 0) & (patch_at < n_patch - 1)
    where = jnp.stack(
        [patch_at, patch_at % split, lax.axis_index("head"), lax.axis_index("sub"), inner]
    ).astype(jnp.int32)

    arrays = (exponents, queries, fresh_kv, cached_kv)
    upper = pack(split, heads // split, 1, where, *arrays)
    upper, where = lax.optimization_barrier((upper, where))
    sent = [*pack(split, heads // split, 0, where, *arrays), *upper]
    pieces = [sent[0]] + [swap(sent[rel], "patch", n_patch, rel) for rel in range(1, split)]
    kv_pieces = list(pieces)
    for rel in range(split, n_patch, split):
        kv_pieces += [swap(x, "patch", n_patch, rel) for x in pieces]

    count = n_head * n_sub
    piece = tok // count
    parts = 2 if piece % 32 == 0 else 1
    attended = []
    for part in range(parts):
        rows = (part * (piece // parts), piece // parts)
        x = attend(where, rows, count, pieces, kv_pieces)
        attended.append(x.reshape(-1, x.shape[2]))
    slots = gather(attended, n_patch)
    blocks = []
    for part in range(parts):
        terms = project(split, where, *slots[part], out_weight, n_head, n_sub)
        sums = reduce_sub(sizes, where, terms)
        if part + 1 < parts:
            sums, slots[part + 1] = lax.optimization_barrier((sums, slots[part + 1]))
        total = reduce_head(sizes, where, sums)
        blocks.append(
            [total[0]] + [swap(total[rel], "patch", n_patch, rel) for rel in range(1, n_patch)]
        )
    return mix(where, hidden_in, attn_gate, blocks)


def solution(mesh):
    in_specs = (
        P(("grp", "patch"), ("head", "sub")),
        P(None, ("grp", "patch"), ("head", "sub")),
        P(None, "grp", ("head", "sub")),
        P(None, ("grp", "patch"), ("head", "sub")),
        P(("head", "sub"), "patch"),
        P(("grp", "patch", "head", "sub"), None),
        P(),
    )
    out_specs = P(("grp", "patch", "head", "sub"), None)
    return jax.shard_map(
        functools.partial(body, dict(mesh.shape)),
        mesh=mesh,
        in_specs=in_specs,
        out_specs=out_specs,
        check_vma=False,
    )
```

```python
import functools
import math

import jax
import jax.numpy as jnp
from jax import lax
from jax.experimental import pallas as pl
from jax.experimental.pallas import tpu as pltpu
from jax.sharding import PartitionSpec as P

HEAD_DIM = 128
SCALE_ROWS = 128
SATURATION = 448.0
VMEM_BYTES = 32 * 1024 * 1024
PACK_VMEM_BYTES = 60 * 1024 * 1024
ATTEND_FLOPS = 1
PROJECT_FLOPS = 1

PATCH, NEAR, HEAD, SUB, INNER = range(5)


def spec(shape):
    return pl.BlockSpec(shape, lambda i, w: (0,) * len(shape))


def call(kernel, name, out_shape, grid, in_specs, out_specs, scratch=(), flops=1, vmem=VMEM_BYTES):
    return pl.pallas_call(
        kernel,
        out_shape=out_shape,
        grid_spec=pltpu.PrefetchScalarGridSpec(
            num_scalar_prefetch=1,
            grid=(grid,),
            in_specs=in_specs,
            out_specs=out_specs,
            scratch_shapes=list(scratch),
        ),
        compiler_params=pltpu.CompilerParams(vmem_limit_bytes=vmem),
        cost_estimate=pl.CostEstimate(flops=flops, bytes_accessed=0, transcendentals=0),
        name=name,
    )


def swap(x, axes, count, mask, only=None):
    pairs = [(at, at ^ mask) for at in range(count) if only is None or at in only]
    return lax.ppermute(x, axes, pairs)


def decode(fresh, cached, exponent):
    power = jnp.full((1, HEAD_DIM), exponent.astype(jnp.float32))
    cached = cached.astype(jnp.float32)
    residual = fresh.astype(jnp.float32) - cached
    codes = jnp.clip(residual * jnp.exp2(-power), -SATURATION, SATURATION).astype(jnp.bfloat16)
    return (cached + codes.astype(jnp.float32) * jnp.exp2(power)).astype(jnp.bfloat16)


def pack_kernel(split, per, exps_ref, q_ref, fresh_ref, cached_ref, *refs):
    outs, (q_buf, fresh_buf, cached_buf, sems) = refs[:-4], refs[-4:]
    patch = lax.axis_index("patch")
    near = lax.rem(patch, split)
    tok = q_buf.shape[0]
    copies = []
    for block in range(tok // SCALE_ROWS):
        rows = pl.ds(block * SCALE_ROWS, SCALE_ROWS)
        there = pl.ds(pl.multiple_of(patch * tok + block * SCALE_ROWS, SCALE_ROWS), SCALE_ROWS)
        copies.append(
            [
                pltpu.make_async_copy(q_ref.at[rows], q_buf.at[rows], sems.at[block, 0]),
                pltpu.make_async_copy(fresh_ref.at[:, rows], fresh_buf.at[:, rows], sems.at[block, 1]),
                pltpu.make_async_copy(cached_ref.at[:, there], cached_buf.at[:, rows], sems.at[block, 2]),
            ]
        )
        for copy in copies[-1]:
            copy.start()
    for block in range(tok // SCALE_ROWS):
        rows = pl.ds(block * SCALE_ROWS, SCALE_ROWS)
        for copy in copies[block]:
            copy.wait()
        for rel in range(1, split):
            out = outs[rel - 1]
            for chunk in range(per):
                head = (near ^ rel) * per + chunk
                lanes = pl.ds(pl.multiple_of(head * HEAD_DIM, HEAD_DIM), HEAD_DIM)
                here = pl.ds(chunk * HEAD_DIM, HEAD_DIM)
                out[0, rows, here] = q_buf[rows, lanes]
                for stacked in range(2):
                    out[1 + stacked, rows, here] = decode(
                        fresh_buf[stacked, rows, lanes],
                        cached_buf[stacked, rows, lanes],
                        exps_ref[stacked, block, head],
                    )


def pack(split, exponents, queries, fresh_kv, cached_kv):
    tok, channels = queries.shape
    feat = channels // split
    blocks = tok // SCALE_ROWS
    hbm = pl.BlockSpec(memory_space=pltpu.HBM)
    return pl.pallas_call(
        functools.partial(pack_kernel, split, feat // HEAD_DIM),
        out_shape=[jax.ShapeDtypeStruct((3, tok, feat), jnp.bfloat16)] * (split - 1),
        in_specs=[pl.BlockSpec(memory_space=pltpu.SMEM), hbm, hbm, hbm],
        out_specs=[pl.BlockSpec(memory_space=pltpu.VMEM)] * (split - 1),
        scratch_shapes=[
            pltpu.VMEM((tok, channels), jnp.bfloat16),
            pltpu.VMEM((2, tok, channels), jnp.bfloat16),
            pltpu.VMEM((2, tok, channels), jnp.bfloat16),
            pltpu.SemaphoreType.DMA((blocks, 3)),
        ],
        compiler_params=pltpu.CompilerParams(vmem_limit_bytes=PACK_VMEM_BYTES),
        name="pack",
    )(exponents, queries, fresh_kv, cached_kv)


def own_kernel(per, where_ref, exps_ref, q_ref, fresh_ref, cached_ref, out_ref):
    out_ref[0] = q_ref[...]
    for chunk in range(per):
        lanes = pl.ds(chunk * HEAD_DIM, HEAD_DIM)
        for block in range(q_ref.shape[0] // SCALE_ROWS):
            rows = pl.ds(block * SCALE_ROWS, SCALE_ROWS)
            for stacked in range(2):
                out_ref[1 + stacked, rows, lanes] = decode(
                    fresh_ref[stacked, rows, lanes],
                    cached_ref[stacked, rows, lanes],
                    exps_ref[stacked, block, where_ref[NEAR] * per + chunk],
                )


def pack_own(split, where, exponents, queries, fresh_kv, cached_kv):
    tok, channels = queries.shape
    feat = channels // split
    out = jax.ShapeDtypeStruct((3, tok, feat), jnp.bfloat16)
    return call(
        functools.partial(own_kernel, feat // HEAD_DIM),
        "own",
        out,
        1,
        [
            pl.BlockSpec(memory_space=pltpu.SMEM),
            pl.BlockSpec((tok, feat), lambda i, w: (0, w[NEAR])),
            pl.BlockSpec((2, tok, feat), lambda i, w: (0, 0, w[NEAR])),
            pl.BlockSpec((2, tok, feat), lambda i, w: (0, w[PATCH], w[NEAR])),
        ],
        spec(out.shape),
        vmem=PACK_VMEM_BYTES,
    )(where, exponents, queries, fresh_kv, cached_kv)


def attend_kernel(split, part, where_ref, *refs):
    q_refs, kv_refs, out_ref = (refs[0], *refs[split - 1 : 0 : -1]), refs[:-1], refs[-1]
    factor = HEAD_DIM**-0.5 * math.log2(math.e)
    tok, feat = q_refs[0].shape[1:]
    count = out_ref.shape[1] // part[1]
    starts = [at * (tok // count) + part[0] for at in range(count)]
    for head in range(feat // HEAD_DIM):
        lanes = pl.ds(head * HEAD_DIM, HEAD_DIM)
        keys = jnp.concatenate([ref[1, :, lanes] for ref in kv_refs], axis=0)
        values = jnp.concatenate([ref[2, :, lanes] for ref in kv_refs], axis=0)
        values = jnp.concatenate([values, jnp.ones_like(values)], axis=1)
        for rel in range(split):
            rows = [q_refs[rel][0, start : start + part[1], lanes] for start in starts]
            query = jnp.concatenate(rows, axis=0) if len(rows) > 1 else rows[0]
            scores = lax.dot_general(
                query, keys, (((1,), (1,)), ((), ())), preferred_element_type=jnp.float32
            )
            peak = jnp.max(scores, axis=1, keepdims=True)
            expo = jnp.exp2((scores - peak) * factor).astype(jnp.bfloat16)
            mix = jnp.dot(expo, values, preferred_element_type=jnp.float32)
            mix = mix[:, :HEAD_DIM] / mix[:, HEAD_DIM:]
            out_ref[where_ref[NEAR] ^ rel, :, lanes] = mix.astype(jnp.bfloat16)


def attend(where, part, count, pieces, kv_pieces):
    split = len(pieces)
    _, tok, feat = pieces[0].shape
    out = jax.ShapeDtypeStruct((split, count * part[1], feat), jnp.bfloat16)
    return call(
        functools.partial(attend_kernel, split, part),
        "attend",
        out,
        1,
        [spec((3, tok, feat))] * len(kv_pieces),
        spec(out.shape),
        flops=ATTEND_FLOPS,
    )(where, *kv_pieces)


def project_kernel(split, n_slots, n_more, where_ref, *refs):
    slots, refs = refs[:n_slots], refs[n_slots:]
    more, weight_ref, refs = refs[:n_more], refs[n_more], refs[n_more + 1 :]
    outs, held_ref, acc_ref = refs[:-2], refs[-2], refs[-1]
    rows, feat = slots[0].shape
    n_sub, n_head = acc_ref.shape[3], acc_ref.shape[2]

    @pl.when(pl.program_id(0) == 0)
    def arrange():
        for at, slot in enumerate(slots):
            group, near = divmod(at, split)
            lane = (where_ref[NEAR] ^ near) * feat
            block = slot[...]
            if more and at == n_slots - 1:
                block = jnp.where(where_ref[INNER] == 1, block, more[0][...])
            held_ref[
                group * rows : (group + 1) * rows, pl.ds(pl.multiple_of(lane, HEAD_DIM), feat)
            ] = block

    acc = jnp.dot(held_ref[...], weight_ref[...], preferred_element_type=jnp.float32)
    acc_ref[...] = acc.reshape(acc_ref.shape)
    for sub in range(n_sub):
        for head in range(n_head):
            for at in range(n_slots):
                group, near = divmod(at, split)
                outs[sub][head, at] = acc_ref[
                    group, where_ref[NEAR] ^ near, where_ref[HEAD] ^ head, where_ref[SUB] ^ sub
                ].astype(jnp.bfloat16)


def project(split, where, slots, more, weight, n_head, n_sub):
    rows, feat = slots[0].shape
    n_patch = len(slots)
    total = rows * n_patch // split
    depth, cols = weight.shape
    wide = 640 if cols % 640 == 0 else cols
    piece = rows // (split * n_head * n_sub)
    return call(
        functools.partial(project_kernel, split, n_patch, len(more)),
        "project",
        [jax.ShapeDtypeStruct((n_head, n_patch, piece, cols), jnp.bfloat16)] * n_sub,
        cols // wide,
        [spec((rows, feat))] * (n_patch + len(more))
        + [pl.BlockSpec((depth, wide), lambda i, w: (0, i))],
        [pl.BlockSpec((n_head, n_patch, piece, wide), lambda i, w: (0, 0, 0, i))] * n_sub,
        [
            pltpu.VMEM((total, depth), jnp.bfloat16),
            pltpu.VMEM((n_patch // split, split, n_head, n_sub, piece, wide), jnp.float32),
        ],
        flops=PROJECT_FLOPS,
    )(where, *slots, *more, weight)


def mix_kernel(n_patch, where_ref, hidden_ref, gate_ref, *refs):
    blocks, out_ref = refs[:-1], refs[-1]
    piece, cols = blocks[0].shape
    for part in range(len(blocks) // n_patch):
        rows = pl.ds(part * piece, piece)
        for rel in range(n_patch):
            lanes = pl.ds(pl.multiple_of((where_ref[PATCH] ^ rel) * cols, HEAD_DIM), cols)
            mixed = hidden_ref[rows, lanes].astype(jnp.float32) + gate_ref[:, lanes] * blocks[
                part * n_patch + rel
            ][...].astype(jnp.float32)
            out_ref[rows, lanes] = mixed.astype(jnp.bfloat16)


def mix(where, hidden_in, attn_gate, blocks):
    rows, width = hidden_in.shape
    n_patch = len(blocks[0])
    piece, cols = blocks[0][0].shape
    if cols % HEAD_DIM:
        order = jnp.concatenate([jnp.stack(x) for x in blocks], axis=1)
        order = order[where[PATCH] ^ jnp.arange(n_patch)]
        projected = order.transpose(1, 0, 2).reshape(rows, width).astype(jnp.float32)
        return (hidden_in.astype(jnp.float32) + attn_gate * projected).astype(jnp.bfloat16)
    flat = [x for part in blocks for x in part]
    return call(
        functools.partial(mix_kernel, n_patch),
        "mix",
        jax.ShapeDtypeStruct((rows, width), jnp.bfloat16),
        1,
        [spec((rows, width)), spec((1, width))] + [spec((piece, cols))] * len(flat),
        spec((rows, width)),
    )(where, hidden_in, attn_gate[None], *flat)


def gather(parts, n_patch):
    if n_patch != 4:
        return [
            ([x] + [swap(x, "patch", n_patch, rel) for rel in range(1, n_patch)], [])
            for x in parts
        ]
    far = [swap(x, "patch", 4, 2) for x in parts]
    next_to = [swap(x, "patch", 4, 1) for x in parts]
    out = []
    for at, x in enumerate(parts):
        far[at], next_to[at], parts = lax.optimization_barrier((far[at], next_to[at], parts))
        middle = swap(parts[at], "patch", 4, 3, (1, 2))
        ends = lax.ppermute(far[at], "patch", [(1, 0), (2, 3)])
        if at + 1 < len(parts):
            ends, far[at + 1], next_to[at + 1] = lax.optimization_barrier(
                (ends, far[at + 1], next_to[at + 1])
            )
        out.append(([x, next_to[at], far[at], middle], [ends]))
    return out


def add_sub_kernel(n_sub, where_ref, *refs):
    terms, kept_ref, outs = refs[:n_sub], refs[n_sub], refs[n_sub + 1 :]
    for head in range(len(outs) + 1):
        total = terms[0][head].astype(jnp.float32)
        for term in terms[1:]:
            total += term[head].astype(jnp.float32)
        if head == 0:
            kept_ref[...] = total
        else:
            outs[head - 1][...] = total.astype(jnp.bfloat16)


def add_head_kernel(n_more, where_ref, kept_ref, *refs):
    for at, out in enumerate(refs[n_more:]):
        total = kept_ref[at]
        for term in refs[:n_more]:
            total += term[at].astype(jnp.float32)
        out[...] = total.astype(jnp.bfloat16)


def reduce_sub(sizes, where, terms):
    n_sub, n_head = sizes["sub"], sizes["head"]
    terms = [terms[0]] + [swap(terms[rel], "sub", n_sub, rel) for rel in range(1, n_sub)]
    shape = terms[0].shape[1:]
    return call(
        functools.partial(add_sub_kernel, n_sub),
        "add_sub",
        [jax.ShapeDtypeStruct(shape, jnp.float32)]
        + [jax.ShapeDtypeStruct(shape, jnp.bfloat16)] * (n_head - 1),
        1,
        [spec(terms[0].shape)] * n_sub,
        [spec(shape)] * n_head,
    )(where, *terms)


def reduce_head(sizes, where, sums):
    n_head = sizes["head"]
    shape = sums[0].shape
    sums = [sums[0]] + [swap(sums[rel], "head", n_head, rel) for rel in range(1, n_head)]
    return call(
        functools.partial(add_head_kernel, n_head - 1),
        "add_head",
        [jax.ShapeDtypeStruct(shape[1:], jnp.bfloat16)] * shape[0],
        1,
        [spec(shape)] * n_head,
        [spec(shape[1:])] * shape[0],
    )(where, *sums)


def body(sizes, queries, fresh_kv, cached_kv, exponents, out_weight, hidden_in, attn_gate):
    n_patch, n_head, n_sub = sizes["patch"], sizes["head"], sizes["sub"]
    tok, channels = queries.shape
    heads = channels // HEAD_DIM
    split = math.gcd(heads, n_patch)
    patch_at = lax.axis_index("patch")
    inner = (patch_at > 0) & (patch_at < n_patch - 1)
    where = jnp.stack(
        [patch_at, patch_at % split, lax.axis_index("head"), lax.axis_index("sub"), inner]
    ).astype(jnp.int32)

    arrays = (exponents, queries, fresh_kv, cached_kv)
    sent = pack(split, *arrays)
    far_first = [swap(sent[rel - 1], "patch", n_patch, rel) for rel in range(split - 1, 0, -1)]
    where, sent = lax.optimization_barrier((where, sent))
    pieces = [pack_own(split, where, *arrays), *far_first]
    kv_pieces = list(pieces)
    for rel in range(split, n_patch, split):
        kv_pieces += [swap(x, "patch", n_patch, rel) for x in pieces]

    count = n_head * n_sub
    piece = tok // count
    parts = 2 if piece % 32 == 0 else 1
    attended = []
    for part in range(parts):
        rows = (part * (piece // parts), piece // parts)
        x = attend(where, rows, count, pieces, kv_pieces)
        attended.append(x.reshape(-1, x.shape[2]))
    slots = gather(attended, n_patch)
    blocks = []
    for part in range(parts):
        terms = project(split, where, *slots[part], out_weight, n_head, n_sub)
        total = reduce_head(sizes, where, reduce_sub(sizes, where, terms))
        blocks.append(
            [total[0]] + [swap(total[rel], "patch", n_patch, rel) for rel in range(1, n_patch)]
        )
    return mix(where, hidden_in, attn_gate, blocks)


def solution(mesh):
    in_specs = (
        P(("grp", "patch"), ("head", "sub")),
        P(None, ("grp", "patch"), ("head", "sub")),
        P(None, "grp", ("head", "sub")),
        P(None, ("grp", "patch"), ("head", "sub")),
        P(("head", "sub"), "patch"),
        P(("grp", "patch", "head", "sub"), None),
        P(),
    )
    out_specs = P(("grp", "patch", "head", "sub"), None)
    return jax.shard_map(
        functools.partial(body, dict(mesh.shape)),
        mesh=mesh,
        in_specs=in_specs,
        out_specs=out_specs,
        check_vma=False,
    )
```

```python
import functools
import math

import jax
import jax.numpy as jnp
from jax import lax
from jax.experimental import pallas as pl
from jax.experimental.pallas import tpu as pltpu
from jax.sharding import PartitionSpec as P

HEAD_DIM = 128
SCALE_ROWS = 128
SATURATION = 448.0
VMEM_BYTES = 32 * 1024 * 1024
PACK_VMEM_BYTES = 60 * 1024 * 1024
ATTEND_FLOPS = 1
PROJECT_FLOPS = 1

PATCH, NEAR, HEAD, SUB, INNER, GRP = range(6)


def spec(shape):
    return pl.BlockSpec(shape, lambda i, w: (0,) * len(shape))


def call(kernel, name, out_shape, grid, in_specs, out_specs, scratch=(), flops=1, vmem=VMEM_BYTES):
    return pl.pallas_call(
        kernel,
        out_shape=out_shape,
        grid_spec=pltpu.PrefetchScalarGridSpec(
            num_scalar_prefetch=1,
            grid=(grid,),
            in_specs=in_specs,
            out_specs=out_specs,
            scratch_shapes=list(scratch),
        ),
        compiler_params=pltpu.CompilerParams(vmem_limit_bytes=vmem),
        cost_estimate=pl.CostEstimate(flops=flops, bytes_accessed=0, transcendentals=0),
        name=name,
    )


def swap(x, axes, count, mask, only=None):
    pairs = [(at, at ^ mask) for at in range(count) if only is None or at in only]
    return lax.ppermute(x, axes, pairs)


def decode(fresh, cached, exponent):
    power = jnp.full((1, HEAD_DIM), exponent.astype(jnp.float32))
    cached = cached.astype(jnp.float32)
    residual = fresh.astype(jnp.float32) - cached
    codes = jnp.clip(residual * jnp.exp2(-power), -SATURATION, SATURATION).astype(jnp.bfloat16)
    return (cached + codes.astype(jnp.float32) * jnp.exp2(power)).astype(jnp.bfloat16)


def pack_kernel(split, per, exps_ref, q_ref, fresh_ref, cached_ref, *refs):
    outs, (q_buf, fresh_buf, cached_buf, sems) = refs[:-4], refs[-4:]
    patch = lax.axis_index("patch")
    near = lax.rem(patch, split)
    tok = q_buf.shape[0]
    copies = []
    for block in range(tok // SCALE_ROWS):
        rows = pl.ds(block * SCALE_ROWS, SCALE_ROWS)
        there = pl.ds(pl.multiple_of(patch * tok + block * SCALE_ROWS, SCALE_ROWS), SCALE_ROWS)
        copies.append(
            [
                pltpu.make_async_copy(q_ref.at[rows], q_buf.at[rows], sems.at[block, 0]),
                pltpu.make_async_copy(fresh_ref.at[:, rows], fresh_buf.at[:, rows], sems.at[block, 1]),
                pltpu.make_async_copy(cached_ref.at[:, there], cached_buf.at[:, rows], sems.at[block, 2]),
            ]
        )
        for copy in copies[-1]:
            copy.start()
    for block in range(tok // SCALE_ROWS):
        rows = pl.ds(block * SCALE_ROWS, SCALE_ROWS)
        for copy in copies[block]:
            copy.wait()
        for rel in range(1, split):
            out = outs[rel - 1]
            for chunk in range(per):
                head = (near ^ rel) * per + chunk
                lanes = pl.ds(pl.multiple_of(head * HEAD_DIM, HEAD_DIM), HEAD_DIM)
                here = pl.ds(chunk * HEAD_DIM, HEAD_DIM)
                out[0, rows, here] = q_buf[rows, lanes]
                for stacked in range(2):
                    out[1 + stacked, rows, here] = decode(
                        fresh_buf[stacked, rows, lanes],
                        cached_buf[stacked, rows, lanes],
                        exps_ref[stacked, block, head],
                    )


def pack(split, exponents, queries, fresh_kv, cached_kv):
    tok, channels = queries.shape
    feat = channels // split
    blocks = tok // SCALE_ROWS
    hbm = pl.BlockSpec(memory_space=pltpu.HBM)
    return pl.pallas_call(
        functools.partial(pack_kernel, split, feat // HEAD_DIM),
        out_shape=[jax.ShapeDtypeStruct((3, tok, feat), jnp.bfloat16)] * (split - 1),
        in_specs=[pl.BlockSpec(memory_space=pltpu.SMEM), hbm, hbm, hbm],
        out_specs=[pl.BlockSpec(memory_space=pltpu.VMEM)] * (split - 1),
        scratch_shapes=[
            pltpu.VMEM((tok, channels), jnp.bfloat16),
            pltpu.VMEM((2, tok, channels), jnp.bfloat16),
            pltpu.VMEM((2, tok, channels), jnp.bfloat16),
            pltpu.SemaphoreType.DMA((blocks, 3)),
        ],
        compiler_params=pltpu.CompilerParams(vmem_limit_bytes=PACK_VMEM_BYTES),
        name="pack",
    )(exponents, queries, fresh_kv, cached_kv)


def own_kernel(per, where_ref, exps_ref, q_ref, fresh_ref, cached_ref, out_ref):
    out_ref[0] = q_ref[...]
    for chunk in range(per):
        lanes = pl.ds(chunk * HEAD_DIM, HEAD_DIM)
        for block in range(q_ref.shape[0] // SCALE_ROWS):
            rows = pl.ds(block * SCALE_ROWS, SCALE_ROWS)
            for stacked in range(2):
                out_ref[1 + stacked, rows, lanes] = decode(
                    fresh_ref[stacked, rows, lanes],
                    cached_ref[stacked, rows, lanes],
                    exps_ref[stacked, block, where_ref[NEAR] * per + chunk],
                )


def pack_own(split, where, exponents, queries, fresh_kv, cached_kv):
    tok, channels = queries.shape
    feat = channels // split
    out = jax.ShapeDtypeStruct((3, tok, feat), jnp.bfloat16)
    return call(
        functools.partial(own_kernel, feat // HEAD_DIM),
        "own",
        out,
        1,
        [
            pl.BlockSpec(memory_space=pltpu.SMEM),
            pl.BlockSpec((tok, feat), lambda i, w: (0, w[NEAR])),
            pl.BlockSpec((2, tok, feat), lambda i, w: (0, 0, w[NEAR])),
            pl.BlockSpec((2, tok, feat), lambda i, w: (0, w[PATCH], w[NEAR])),
        ],
        spec(out.shape),
    )(where, exponents, queries, fresh_kv, cached_kv)


def attend_kernel(split, part, where_ref, *refs):
    q_refs, kv_refs, out_ref = (refs[0], *refs[split - 1 : 0 : -1]), refs[:-1], refs[-1]
    factor = HEAD_DIM**-0.5 * math.log2(math.e)
    tok, feat = q_refs[0].shape[1:]
    count = out_ref.shape[1] // part[1]
    starts = [at * (tok // count) + part[0] for at in range(count)]
    for head in range(feat // HEAD_DIM):
        lanes = pl.ds(head * HEAD_DIM, HEAD_DIM)
        keys = jnp.concatenate([ref[1, :, lanes] for ref in kv_refs], axis=0)
        values = jnp.concatenate([ref[2, :, lanes] for ref in kv_refs], axis=0)
        values = jnp.concatenate([values, jnp.ones_like(values)], axis=1)
        for rel in range(split):
            rows = [q_refs[rel][0, start : start + part[1], lanes] for start in starts]
            query = jnp.concatenate(rows, axis=0) if len(rows) > 1 else rows[0]
            scores = lax.dot_general(
                query, keys, (((1,), (1,)), ((), ())), preferred_element_type=jnp.float32
            )
            peak = jnp.max(scores, axis=1, keepdims=True)
            expo = jnp.exp2((scores - peak) * factor).astype(jnp.bfloat16)
            mix = jnp.dot(expo, values, preferred_element_type=jnp.float32)
            mix = mix[:, :HEAD_DIM] / mix[:, HEAD_DIM:]
            out_ref[where_ref[NEAR] ^ rel, :, lanes] = mix.astype(jnp.bfloat16)


def attend(where, part, count, pieces, kv_pieces):
    split = len(pieces)
    _, tok, feat = pieces[0].shape
    out = jax.ShapeDtypeStruct((split, count * part[1], feat), jnp.bfloat16)
    return call(
        functools.partial(attend_kernel, split, part),
        "attend",
        out,
        1,
        [spec((3, tok, feat))] * len(kv_pieces),
        spec(out.shape),
        flops=ATTEND_FLOPS,
    )(where, *kv_pieces)


def project_kernel(split, n_slots, n_more, where_ref, *refs):
    slots, refs = refs[:n_slots], refs[n_slots:]
    more, weight_ref, refs = refs[:n_more], refs[n_more], refs[n_more + 1 :]
    outs, held_ref, acc_ref = refs[:-2], refs[-2], refs[-1]
    rows, feat = slots[0].shape
    n_sub, n_head = acc_ref.shape[3], acc_ref.shape[2]

    @pl.when(pl.program_id(0) == 0)
    def arrange():
        for at, slot in enumerate(slots):
            group, near = divmod(at, split)
            lane = (where_ref[NEAR] ^ near) * feat
            block = slot[...]
            if more and at == n_slots - 1:
                block = jnp.where(where_ref[INNER] == 1, block, more[0][...])
            held_ref[
                group * rows : (group + 1) * rows, pl.ds(pl.multiple_of(lane, HEAD_DIM), feat)
            ] = block

    acc = jnp.dot(held_ref[...], weight_ref[...], preferred_element_type=jnp.float32)
    acc_ref[...] = acc.reshape(acc_ref.shape)
    for sub in range(n_sub):
        for head in range(n_head):
            for at in range(n_slots):
                group, near = divmod(at, split)
                outs[sub][head, at] = acc_ref[
                    group, where_ref[NEAR] ^ near, where_ref[HEAD] ^ head, where_ref[SUB] ^ sub
                ].astype(jnp.bfloat16)


def project(split, where, slots, more, weight, n_head, n_sub):
    rows, feat = slots[0].shape
    n_patch = len(slots)
    total = rows * n_patch // split
    depth, cols = weight.shape
    wide = 640 if cols % 640 == 0 else cols
    piece = rows // (split * n_head * n_sub)
    return call(
        functools.partial(project_kernel, split, n_patch, len(more)),
        "project",
        [jax.ShapeDtypeStruct((n_head, n_patch, piece, cols), jnp.bfloat16)] * n_sub,
        cols // wide,
        [spec((rows, feat))] * (n_patch + len(more))
        + [pl.BlockSpec((depth, wide), lambda i, w: (0, i))],
        [pl.BlockSpec((n_head, n_patch, piece, wide), lambda i, w: (0, 0, 0, i))] * n_sub,
        [
            pltpu.VMEM((total, depth), jnp.bfloat16),
            pltpu.VMEM((n_patch // split, split, n_head, n_sub, piece, wide), jnp.float32),
        ],
        flops=PROJECT_FLOPS,
    )(where, *slots, *more, weight)


def mix_kernel(n_patch, where_ref, hidden_ref, gate_ref, *refs):
    blocks, out_ref = refs[:-1], refs[-1]
    piece, cols = blocks[0].shape
    for part in range(len(blocks) // n_patch):
        rows = pl.ds(part * piece, piece)
        for rel in range(n_patch):
            lanes = pl.ds(pl.multiple_of((where_ref[PATCH] ^ rel) * cols, HEAD_DIM), cols)
            mixed = hidden_ref[rows, lanes].astype(jnp.float32) + gate_ref[:, lanes] * blocks[
                part * n_patch + rel
            ][...].astype(jnp.float32)
            out_ref[rows, lanes] = mixed.astype(jnp.bfloat16)


def mix(where, hidden_in, attn_gate, blocks):
    rows, width = hidden_in.shape
    n_patch = len(blocks[0])
    piece, cols = blocks[0][0].shape
    if cols % HEAD_DIM:
        order = jnp.concatenate([jnp.stack(x) for x in blocks], axis=1)
        order = order[where[PATCH] ^ jnp.arange(n_patch)]
        projected = order.transpose(1, 0, 2).reshape(rows, width).astype(jnp.float32)
        return (hidden_in.astype(jnp.float32) + attn_gate * projected).astype(jnp.bfloat16)
    flat = [x for part in blocks for x in part]
    return call(
        functools.partial(mix_kernel, n_patch),
        "mix",
        jax.ShapeDtypeStruct((rows, width), jnp.bfloat16),
        1,
        [spec((rows, width)), spec((1, width))] + [spec((piece, cols))] * len(flat),
        spec((rows, width)),
    )(where, hidden_in, attn_gate[None], *flat)


def gather(parts, n_patch):
    if n_patch != 4:
        return [
            ([x] + [swap(x, "patch", n_patch, rel) for rel in range(1, n_patch)], [])
            for x in parts
        ]
    far = [swap(x, "patch", 4, 2) for x in parts]
    next_to = [swap(x, "patch", 4, 1) for x in parts]
    out = []
    for at, x in enumerate(parts):
        far[at], next_to[at], parts = lax.optimization_barrier((far[at], next_to[at], parts))
        middle = swap(parts[at], "patch", 4, 3, (1, 2))
        ends = lax.ppermute(far[at], "patch", [(1, 0), (2, 3)])
        if at + 1 < len(parts):
            ends, far[at + 1], next_to[at + 1] = lax.optimization_barrier(
                (ends, far[at + 1], next_to[at + 1])
            )
        out.append(([x, next_to[at], far[at], middle], [ends]))
    return out


def add_sub_kernel(n_sub, where_ref, *refs):
    terms, kept_ref, outs = refs[:n_sub], refs[n_sub], refs[n_sub + 1 :]
    for head in range(len(outs) + 1):
        total = terms[0][head].astype(jnp.float32)
        for term in terms[1:]:
            total += term[head].astype(jnp.float32)
        if head == 0:
            kept_ref[...] = total
        else:
            outs[head - 1][...] = total.astype(jnp.bfloat16)


def add_head_kernel(n_more, where_ref, kept_ref, *refs):
    for at, out in enumerate(refs[n_more:]):
        total = kept_ref[at]
        for term in refs[:n_more]:
            total += term[at].astype(jnp.float32)
        out[...] = total.astype(jnp.bfloat16)


def reduce_sub(sizes, where, terms):
    n_sub, n_head = sizes["sub"], sizes["head"]
    terms = [terms[0]] + [swap(terms[rel], "sub", n_sub, rel) for rel in range(1, n_sub)]
    shape = terms[0].shape[1:]
    return call(
        functools.partial(add_sub_kernel, n_sub),
        "add_sub",
        [jax.ShapeDtypeStruct(shape, jnp.float32)]
        + [jax.ShapeDtypeStruct(shape, jnp.bfloat16)] * (n_head - 1),
        1,
        [spec(terms[0].shape)] * n_sub,
        [spec(shape)] * n_head,
    )(where, *terms)


def reduce_head(sizes, where, sums):
    n_head = sizes["head"]
    shape = sums[0].shape
    sums = [sums[0]] + [swap(sums[rel], "head", n_head, rel) for rel in range(1, n_head)]
    return call(
        functools.partial(add_head_kernel, n_head - 1),
        "add_head",
        [jax.ShapeDtypeStruct(shape[1:], jnp.bfloat16)] * shape[0],
        1,
        [spec(shape)] * n_head,
        [spec(shape[1:])] * shape[0],
    )(where, *sums)


def sum_tail(sizes, where, pieces, kv_pieces, out_weight, hidden_in, attn_gate):
    n_patch, n_head, n_sub = sizes["patch"], sizes["head"], sizes["sub"]
    split, tok = len(pieces), pieces[0].shape[1]
    count = n_head * n_sub
    piece = tok // count
    parts = 2 if piece % 32 == 0 else 1
    attended = []
    for part in range(parts):
        rows = (part * (piece // parts), piece // parts)
        x = attend(where, rows, count, pieces, kv_pieces)
        attended.append(x.reshape(-1, x.shape[2]))
    slots = gather(attended, n_patch)
    blocks = []
    for part in range(parts):
        terms = project(split, where, *slots[part], out_weight, n_head, n_sub)
        total = reduce_head(sizes, where, reduce_sub(sizes, where, terms))
        blocks.append(
            [total[0]] + [swap(total[rel], "patch", n_patch, rel) for rel in range(1, n_patch)]
        )
    return mix(where, hidden_in, attn_gate, blocks)


def attend_halves_kernel(where_ref, *refs):
    pieces, outs = refs[:-2], refs[-2:]
    split = len(pieces)
    rels = [0, *range(split - 1, 0, -1)]
    factor = HEAD_DIM**-0.5 * math.log2(math.e)
    rows, feat = outs[0].shape[1:]
    for head in range(feat // HEAD_DIM):
        lanes = pl.ds(head * HEAD_DIM, HEAD_DIM)
        keys = jnp.concatenate([ref[1, :, lanes] for ref in pieces], axis=0)
        values = jnp.concatenate([ref[2, :, lanes] for ref in pieces], axis=0)
        values = jnp.concatenate([values, jnp.ones_like(values)], axis=1)
        for half, out in enumerate(outs):
            start = pl.multiple_of((where_ref[HEAD] ^ half) * rows, rows)
            query = jnp.concatenate([ref[0, pl.ds(start, rows), lanes] for ref in pieces], axis=0)
            scores = lax.dot_general(
                query, keys, (((1,), (1,)), ((), ())), preferred_element_type=jnp.float32
            )
            peak = jnp.max(scores, axis=1, keepdims=True)
            expo = jnp.exp2((scores - peak) * factor).astype(jnp.bfloat16)
            mix = jnp.dot(expo, values, preferred_element_type=jnp.float32)
            mix = (mix[:, :HEAD_DIM] / mix[:, HEAD_DIM:]).astype(jnp.bfloat16)
            for at, rel in enumerate(rels):
                out[where_ref[NEAR] ^ rel, :, lanes] = mix[at * rows : (at + 1) * rows]


def attend_halves(where, pieces):
    split = len(pieces)
    _, tok, feat = pieces[0].shape
    out = jax.ShapeDtypeStruct((split, tok // 2, feat), jnp.bfloat16)
    outs = call(
        attend_halves_kernel,
        "attend",
        [out] * 2,
        1,
        [spec((3, tok, feat))] * split,
        [spec(out.shape)] * 2,
    )(where, *pieces)
    return [x.reshape(-1, feat) for x in outs]


def hold_slots(slots, more, held_ref, where_ref, place):
    feat = slots[0].shape[1]
    for at, slot in enumerate(slots):
        block = slot[...]
        if at == len(slots) - 1:
            block = jnp.where(where_ref[INNER] == 1, block, more[...])
        lane = place(where_ref[NEAR] ^ at) * feat
        held_ref[:, pl.ds(pl.multiple_of(lane, HEAD_DIM), feat)] = block


def first_kernel(where_ref, *refs):
    slots, (more, weight_ref, out_ref, held_ref) = refs[:4], refs[4:]

    @pl.when(pl.program_id(0) == 0)
    def arrange():
        hold_slots(slots, more, held_ref, where_ref, lambda at: at)

    out_ref[...] = jnp.dot(held_ref[...], weight_ref[...], preferred_element_type=jnp.float32)


def first_product(where, slots, more, weight):
    rows, feat = slots[0].shape
    depth, cols = weight.shape
    wide = cols // 2
    return call(
        first_kernel,
        "first",
        jax.ShapeDtypeStruct((rows, cols), jnp.float32),
        2,
        [spec((rows, feat))] * 5 + [pl.BlockSpec((depth, wide), lambda i, w: (0, i))],
        pl.BlockSpec((rows, wide), lambda i, w: (0, i)),
        [pltpu.VMEM((rows, depth), jnp.bfloat16)],
    )(where, *slots, *more, weight)


def second_kernel(where_ref, *refs):
    slots, more, weights, (acc_in, keep_ref, send_ref, held_ref, acc_ref) = (
        refs[:4],
        refs[4],
        refs[5:7],
        refs[7:],
    )

    def place(at):
        return 2 * ((at // 2) ^ where_ref[GRP]) + at % 2

    hold_slots(slots, more, held_ref, where_ref, place)
    depth = weights[0].shape[0]
    acc = acc_in[...]
    for at, weight in enumerate(weights):
        acc += jnp.dot(
            held_ref[:, at * depth : (at + 1) * depth],
            weight[...],
            preferred_element_type=jnp.float32,
        )
    acc_ref[...] = acc.reshape(acc_ref.shape)
    for sub, out in enumerate((keep_ref, send_ref)):
        for at in range(4):
            out[at] = acc_ref[where_ref[NEAR] ^ at, where_ref[SUB] ^ sub].astype(jnp.bfloat16)


def second_product(where, chunk, slots, more, weights, acc):
    rows, feat = slots[0].shape
    depth, cols = weights[0].shape
    wide = cols // 2
    out = jax.ShapeDtypeStruct((4, rows // 8, wide), jnp.bfloat16)
    return call(
        second_kernel,
        "second",
        [out] * 2,
        1,
        [spec((rows, feat))] * 5
        + [pl.BlockSpec((depth, wide), lambda i, w: (0, chunk))] * 2
        + [pl.BlockSpec((rows, wide), lambda i, w: (0, chunk))],
        [spec(out.shape)] * 2,
        [
            pltpu.VMEM((rows, 2 * depth), jnp.bfloat16),
            pltpu.VMEM((4, 2, rows // 8, wide), jnp.float32),
        ],
    )(where, *slots, *more, *weights, acc)


def add_kernel(where_ref, keep_ref, term_ref, *outs):
    for at, out in enumerate(outs):
        total = keep_ref[at].astype(jnp.float32) + term_ref[at].astype(jnp.float32)
        out[...] = total.astype(jnp.bfloat16)


def add(where, keep, term):
    return call(
        add_kernel,
        "add",
        [jax.ShapeDtypeStruct(keep.shape[1:], jnp.bfloat16)] * keep.shape[0],
        1,
        [spec(keep.shape)] * 2,
        [spec(keep.shape[1:])] * keep.shape[0],
    )(where, keep, term)


def share_tail(sizes, where, pieces, kv_pieces, out_weight, hidden_in, attn_gate):
    half = out_weight.shape[0] // 2
    out_weight, where = lax.optimization_barrier((out_weight, where))
    start = lax.axis_index("grp") * half
    fetched = swap(lax.dynamic_slice_in_dim(out_weight, start, half, 0), "head", 2, 1)
    pieces, fetched = lax.optimization_barrier((pieces, fetched))
    passed = swap(fetched, "grp", 2, 1)

    mine, other = attend_halves(where, pieces)
    other = swap(other, "head", 2, 1)
    slots = []
    for at, x in enumerate((mine, other)):
        far, next_to = swap(x, "patch", 4, 2), swap(x, "patch", 4, 1)
        far, next_to, other, x = lax.optimization_barrier((far, next_to, other, x))
        if at == 1:
            far, x, passed = lax.optimization_barrier((far, x, passed))
        middle = swap(x, "patch", 4, 3, (1, 2))
        ends = lax.ppermute(far, "patch", [(1, 0), (2, 3)])
        slots.append(([x, next_to, far, middle], [ends]))
    acc = first_product(where, *slots[0], out_weight)
    terms = [second_product(where, at, *slots[1], [fetched, passed], acc) for at in range(2)]
    blocks = []
    for keep, send in terms:
        total = add(where, keep, swap(send, "sub", 2, 1))
        blocks.append([total[0]] + [swap(total[rel], "patch", 4, rel) for rel in range(1, 4)])
    return mix_columns(where, hidden_in, attn_gate, blocks)


def mix_columns_kernel(where_ref, hidden_ref, gate_ref, *refs):
    blocks, out_ref = refs[:-1], refs[-1]
    cols = blocks[0].shape[1]
    for chunk in range(2):
        for rel in range(4):
            start = (2 * (where_ref[PATCH] ^ rel) + chunk) * cols
            lanes = pl.ds(pl.multiple_of(start, HEAD_DIM), cols)
            mixed = hidden_ref[:, lanes].astype(jnp.float32) + gate_ref[:, lanes] * blocks[
                4 * chunk + rel
            ][...].astype(jnp.float32)
            out_ref[:, lanes] = mixed.astype(jnp.bfloat16)


def mix_columns(where, hidden_in, attn_gate, blocks):
    rows, width = hidden_in.shape
    flat = [x for chunk in blocks for x in chunk]
    return call(
        mix_columns_kernel,
        "mix",
        jax.ShapeDtypeStruct((rows, width), jnp.bfloat16),
        1,
        [spec((rows, width)), spec((1, width))] + [spec(flat[0].shape)] * len(flat),
        spec((rows, width)),
    )(where, hidden_in, attn_gate[None], *flat)


def body(sizes, queries, fresh_kv, cached_kv, exponents, out_weight, hidden_in, attn_gate):
    n_patch, n_head, n_sub = sizes["patch"], sizes["head"], sizes["sub"]
    tok, channels = queries.shape
    heads = channels // HEAD_DIM
    split = math.gcd(heads, n_patch)
    patch_at = lax.axis_index("patch")
    inner = (patch_at > 0) & (patch_at < n_patch - 1)
    where = jnp.stack(
        [
            patch_at,
            patch_at % split,
            lax.axis_index("head"),
            lax.axis_index("sub"),
            inner,
            lax.axis_index("grp"),
        ]
    ).astype(jnp.int32)

    arrays = (exponents, queries, fresh_kv, cached_kv)
    sent = pack(split, *arrays)
    far_first = [swap(sent[rel - 1], "patch", n_patch, rel) for rel in range(split - 1, 0, -1)]
    where, sent = lax.optimization_barrier((where, sent))
    pieces = [pack_own(split, where, *arrays), *far_first]
    kv_pieces = list(pieces)
    for rel in range(split, n_patch, split):
        kv_pieces += [swap(x, "patch", n_patch, rel) for x in pieces]

    tail = (sizes, where, pieces, kv_pieces, out_weight, hidden_in, attn_gate)
    if (sizes["grp"], n_head, split, n_patch) == (2, 2, 4, 4):
        return share_tail(*tail)
    return sum_tail(*tail)


def solution(mesh):
    in_specs = (
        P(("grp", "patch"), ("head", "sub")),
        P(None, ("grp", "patch"), ("head", "sub")),
        P(None, "grp", ("head", "sub")),
        P(None, ("grp", "patch"), ("head", "sub")),
        P(("head", "sub"), "patch"),
        P(("grp", "patch", "head", "sub"), None),
        P(),
    )
    out_specs = P(("grp", "patch", "head", "sub"), None)
    return jax.shard_map(
        functools.partial(body, dict(mesh.shape)),
        mesh=mesh,
        in_specs=in_specs,
        out_specs=out_specs,
        check_vma=False,
    )
```

```python
import functools
import math

import jax
import jax.numpy as jnp
from jax import lax
from jax.experimental import pallas as pl
from jax.experimental.pallas import tpu as pltpu
from jax.sharding import PartitionSpec as P

HEAD_DIM = 128
SCALE_ROWS = 128
SATURATION = 448.0
VMEM_BYTES = 32 * 1024 * 1024
PACK_VMEM_BYTES = 60 * 1024 * 1024
ATTEND_FLOPS = 1
PROJECT_FLOPS = 1

PATCH, NEAR, HEAD, SUB, INNER, GRP = range(6)


def spec(shape):
    return pl.BlockSpec(shape, lambda i, w: (0,) * len(shape))


def call(kernel, name, out_shape, grid, in_specs, out_specs, scratch=(), flops=1, vmem=VMEM_BYTES):
    return pl.pallas_call(
        kernel,
        out_shape=out_shape,
        grid_spec=pltpu.PrefetchScalarGridSpec(
            num_scalar_prefetch=1,
            grid=(grid,),
            in_specs=in_specs,
            out_specs=out_specs,
            scratch_shapes=list(scratch),
        ),
        compiler_params=pltpu.CompilerParams(vmem_limit_bytes=vmem),
        cost_estimate=pl.CostEstimate(flops=flops, bytes_accessed=0, transcendentals=0),
        name=name,
    )


def swap(x, axes, count, mask, only=None):
    pairs = [(at, at ^ mask) for at in range(count) if only is None or at in only]
    return lax.ppermute(x, axes, pairs)


def decode(fresh, cached, exponent):
    power = jnp.full((1, HEAD_DIM), exponent.astype(jnp.float32))
    cached = cached.astype(jnp.float32)
    residual = fresh.astype(jnp.float32) - cached
    codes = jnp.clip(residual * jnp.exp2(-power), -SATURATION, SATURATION).astype(jnp.bfloat16)
    return (cached + codes.astype(jnp.float32) * jnp.exp2(power)).astype(jnp.bfloat16)


def pack_kernel(split, per, exps_ref, q_ref, fresh_ref, cached_ref, *refs):
    outs, (q_buf, fresh_buf, cached_buf, sems) = refs[:-4], refs[-4:]
    patch = lax.axis_index("patch")
    near = lax.rem(patch, split)
    tok = q_buf.shape[0]
    copies = []
    for block in range(tok // SCALE_ROWS):
        rows = pl.ds(block * SCALE_ROWS, SCALE_ROWS)
        there = pl.ds(pl.multiple_of(patch * tok + block * SCALE_ROWS, SCALE_ROWS), SCALE_ROWS)
        copies.append(
            [
                pltpu.make_async_copy(q_ref.at[rows], q_buf.at[rows], sems.at[block, 0]),
                pltpu.make_async_copy(fresh_ref.at[:, rows], fresh_buf.at[:, rows], sems.at[block, 1]),
                pltpu.make_async_copy(cached_ref.at[:, there], cached_buf.at[:, rows], sems.at[block, 2]),
            ]
        )
        for copy in copies[-1]:
            copy.start()
    for block in range(tok // SCALE_ROWS):
        rows = pl.ds(block * SCALE_ROWS, SCALE_ROWS)
        for copy in copies[block]:
            copy.wait()
        for rel in range(1, split):
            out = outs[rel - 1]
            for chunk in range(per):
                head = (near ^ rel) * per + chunk
                lanes = pl.ds(pl.multiple_of(head * HEAD_DIM, HEAD_DIM), HEAD_DIM)
                here = pl.ds(chunk * HEAD_DIM, HEAD_DIM)
                out[0, rows, here] = q_buf[rows, lanes]
                for stacked in range(2):
                    out[1 + stacked, rows, here] = decode(
                        fresh_buf[stacked, rows, lanes],
                        cached_buf[stacked, rows, lanes],
                        exps_ref[stacked, block, head],
                    )


def pack(split, exponents, queries, fresh_kv, cached_kv):
    tok, channels = queries.shape
    feat = channels // split
    blocks = tok // SCALE_ROWS
    hbm = pl.BlockSpec(memory_space=pltpu.HBM)
    return pl.pallas_call(
        functools.partial(pack_kernel, split, feat // HEAD_DIM),
        out_shape=[jax.ShapeDtypeStruct((3, tok, feat), jnp.bfloat16)] * (split - 1),
        in_specs=[pl.BlockSpec(memory_space=pltpu.SMEM), hbm, hbm, hbm],
        out_specs=[pl.BlockSpec(memory_space=pltpu.VMEM)] * (split - 1),
        scratch_shapes=[
            pltpu.VMEM((tok, channels), jnp.bfloat16),
            pltpu.VMEM((2, tok, channels), jnp.bfloat16),
            pltpu.VMEM((2, tok, channels), jnp.bfloat16),
            pltpu.SemaphoreType.DMA((blocks, 3)),
        ],
        compiler_params=pltpu.CompilerParams(vmem_limit_bytes=PACK_VMEM_BYTES),
        name="pack",
    )(exponents, queries, fresh_kv, cached_kv)


def own_kernel(per, where_ref, exps_ref, q_ref, fresh_ref, cached_ref, out_ref):
    out_ref[0] = q_ref[...]
    for chunk in range(per):
        lanes = pl.ds(chunk * HEAD_DIM, HEAD_DIM)
        for block in range(q_ref.shape[0] // SCALE_ROWS):
            rows = pl.ds(block * SCALE_ROWS, SCALE_ROWS)
            for stacked in range(2):
                out_ref[1 + stacked, rows, lanes] = decode(
                    fresh_ref[stacked, rows, lanes],
                    cached_ref[stacked, rows, lanes],
                    exps_ref[stacked, block, where_ref[NEAR] * per + chunk],
                )


def pack_own(split, where, exponents, queries, fresh_kv, cached_kv):
    tok, channels = queries.shape
    feat = channels // split
    out = jax.ShapeDtypeStruct((3, tok, feat), jnp.bfloat16)
    return call(
        functools.partial(own_kernel, feat // HEAD_DIM),
        "own",
        out,
        1,
        [
            pl.BlockSpec(memory_space=pltpu.SMEM),
            pl.BlockSpec((tok, feat), lambda i, w: (0, w[NEAR])),
            pl.BlockSpec((2, tok, feat), lambda i, w: (0, 0, w[NEAR])),
            pl.BlockSpec((2, tok, feat), lambda i, w: (0, w[PATCH], w[NEAR])),
        ],
        spec(out.shape),
    )(where, exponents, queries, fresh_kv, cached_kv)


def attend_kernel(split, part, where_ref, *refs):
    q_refs, kv_refs, out_ref = (refs[0], *refs[split - 1 : 0 : -1]), refs[:-1], refs[-1]
    factor = HEAD_DIM**-0.5 * math.log2(math.e)
    tok, feat = q_refs[0].shape[1:]
    count = out_ref.shape[1] // part[1]
    starts = [at * (tok // count) + part[0] for at in range(count)]
    for head in range(feat // HEAD_DIM):
        lanes = pl.ds(head * HEAD_DIM, HEAD_DIM)
        keys = jnp.concatenate([ref[1, :, lanes] for ref in kv_refs], axis=0)
        values = jnp.concatenate([ref[2, :, lanes] for ref in kv_refs], axis=0)
        values = jnp.concatenate([values, jnp.ones_like(values)], axis=1)
        for rel in range(split):
            rows = [q_refs[rel][0, start : start + part[1], lanes] for start in starts]
            query = jnp.concatenate(rows, axis=0) if len(rows) > 1 else rows[0]
            scores = lax.dot_general(
                query, keys, (((1,), (1,)), ((), ())), preferred_element_type=jnp.float32
            )
            peak = jnp.max(scores, axis=1, keepdims=True)
            expo = jnp.exp2((scores - peak) * factor).astype(jnp.bfloat16)
            mix = jnp.dot(expo, values, preferred_element_type=jnp.float32)
            mix = mix[:, :HEAD_DIM] / mix[:, HEAD_DIM:]
            out_ref[where_ref[NEAR] ^ rel, :, lanes] = mix.astype(jnp.bfloat16)


def attend(where, part, count, pieces, kv_pieces):
    split = len(pieces)
    _, tok, feat = pieces[0].shape
    out = jax.ShapeDtypeStruct((split, count * part[1], feat), jnp.bfloat16)
    return call(
        functools.partial(attend_kernel, split, part),
        "attend",
        out,
        1,
        [spec((3, tok, feat))] * len(kv_pieces),
        spec(out.shape),
        flops=ATTEND_FLOPS,
    )(where, *kv_pieces)


def project_kernel(split, n_slots, n_more, where_ref, *refs):
    slots, refs = refs[:n_slots], refs[n_slots:]
    more, weight_ref, refs = refs[:n_more], refs[n_more], refs[n_more + 1 :]
    outs, held_ref, acc_ref = refs[:-2], refs[-2], refs[-1]
    rows, feat = slots[0].shape
    n_sub, n_head = acc_ref.shape[3], acc_ref.shape[2]

    @pl.when(pl.program_id(0) == 0)
    def arrange():
        for at, slot in enumerate(slots):
            group, near = divmod(at, split)
            lane = (where_ref[NEAR] ^ near) * feat
            block = slot[...]
            if more and at == n_slots - 1:
                block = jnp.where(where_ref[INNER] == 1, block, more[0][...])
            held_ref[
                group * rows : (group + 1) * rows, pl.ds(pl.multiple_of(lane, HEAD_DIM), feat)
            ] = block

    acc = jnp.dot(held_ref[...], weight_ref[...], preferred_element_type=jnp.float32)
    acc_ref[...] = acc.reshape(acc_ref.shape)
    for sub in range(n_sub):
        for head in range(n_head):
            for at in range(n_slots):
                group, near = divmod(at, split)
                outs[sub][head, at] = acc_ref[
                    group, where_ref[NEAR] ^ near, where_ref[HEAD] ^ head, where_ref[SUB] ^ sub
                ].astype(jnp.bfloat16)


def project(split, where, slots, more, weight, n_head, n_sub):
    rows, feat = slots[0].shape
    n_patch = len(slots)
    total = rows * n_patch // split
    depth, cols = weight.shape
    wide = 640 if cols % 640 == 0 else cols
    piece = rows // (split * n_head * n_sub)
    return call(
        functools.partial(project_kernel, split, n_patch, len(more)),
        "project",
        [jax.ShapeDtypeStruct((n_head, n_patch, piece, cols), jnp.bfloat16)] * n_sub,
        cols // wide,
        [spec((rows, feat))] * (n_patch + len(more))
        + [pl.BlockSpec((depth, wide), lambda i, w: (0, i))],
        [pl.BlockSpec((n_head, n_patch, piece, wide), lambda i, w: (0, 0, 0, i))] * n_sub,
        [
            pltpu.VMEM((total, depth), jnp.bfloat16),
            pltpu.VMEM((n_patch // split, split, n_head, n_sub, piece, wide), jnp.float32),
        ],
        flops=PROJECT_FLOPS,
    )(where, *slots, *more, weight)


def mix_kernel(n_patch, where_ref, hidden_ref, gate_ref, *refs):
    blocks, out_ref = refs[:-1], refs[-1]
    piece, cols = blocks[0].shape
    for part in range(len(blocks) // n_patch):
        rows = pl.ds(part * piece, piece)
        for rel in range(n_patch):
            lanes = pl.ds(pl.multiple_of((where_ref[PATCH] ^ rel) * cols, HEAD_DIM), cols)
            mixed = hidden_ref[rows, lanes].astype(jnp.float32) + gate_ref[:, lanes] * blocks[
                part * n_patch + rel
            ][...].astype(jnp.float32)
            out_ref[rows, lanes] = mixed.astype(jnp.bfloat16)


def mix(where, hidden_in, attn_gate, blocks):
    rows, width = hidden_in.shape
    n_patch = len(blocks[0])
    piece, cols = blocks[0][0].shape
    if cols % HEAD_DIM:
        order = jnp.concatenate([jnp.stack(x) for x in blocks], axis=1)
        order = order[where[PATCH] ^ jnp.arange(n_patch)]
        projected = order.transpose(1, 0, 2).reshape(rows, width).astype(jnp.float32)
        return (hidden_in.astype(jnp.float32) + attn_gate * projected).astype(jnp.bfloat16)
    flat = [x for part in blocks for x in part]
    return call(
        functools.partial(mix_kernel, n_patch),
        "mix",
        jax.ShapeDtypeStruct((rows, width), jnp.bfloat16),
        1,
        [spec((rows, width)), spec((1, width))] + [spec((piece, cols))] * len(flat),
        spec((rows, width)),
    )(where, hidden_in, attn_gate[None], *flat)


def gather(parts, n_patch):
    if n_patch != 4:
        return [
            ([x] + [swap(x, "patch", n_patch, rel) for rel in range(1, n_patch)], [])
            for x in parts
        ]
    far = [swap(x, "patch", 4, 2) for x in parts]
    next_to = [swap(x, "patch", 4, 1) for x in parts]
    out = []
    for at, x in enumerate(parts):
        far[at], next_to[at], parts = lax.optimization_barrier((far[at], next_to[at], parts))
        middle = swap(parts[at], "patch", 4, 3, (1, 2))
        ends = lax.ppermute(far[at], "patch", [(1, 0), (2, 3)])
        if at + 1 < len(parts):
            ends, far[at + 1], next_to[at + 1] = lax.optimization_barrier(
                (ends, far[at + 1], next_to[at + 1])
            )
        out.append(([x, next_to[at], far[at], middle], [ends]))
    return out


def add_sub_kernel(n_sub, where_ref, *refs):
    terms, kept_ref, outs = refs[:n_sub], refs[n_sub], refs[n_sub + 1 :]
    for head in range(len(outs) + 1):
        total = terms[0][head].astype(jnp.float32)
        for term in terms[1:]:
            total += term[head].astype(jnp.float32)
        if head == 0:
            kept_ref[...] = total
        else:
            outs[head - 1][...] = total.astype(jnp.bfloat16)


def add_head_kernel(n_more, where_ref, kept_ref, *refs):
    for at, out in enumerate(refs[n_more:]):
        total = kept_ref[at]
        for term in refs[:n_more]:
            total += term[at].astype(jnp.float32)
        out[...] = total.astype(jnp.bfloat16)


def reduce_sub(sizes, where, terms):
    n_sub, n_head = sizes["sub"], sizes["head"]
    terms = [terms[0]] + [swap(terms[rel], "sub", n_sub, rel) for rel in range(1, n_sub)]
    shape = terms[0].shape[1:]
    return call(
        functools.partial(add_sub_kernel, n_sub),
        "add_sub",
        [jax.ShapeDtypeStruct(shape, jnp.float32)]
        + [jax.ShapeDtypeStruct(shape, jnp.bfloat16)] * (n_head - 1),
        1,
        [spec(terms[0].shape)] * n_sub,
        [spec(shape)] * n_head,
    )(where, *terms)


def reduce_head(sizes, where, sums):
    n_head = sizes["head"]
    shape = sums[0].shape
    sums = [sums[0]] + [swap(sums[rel], "head", n_head, rel) for rel in range(1, n_head)]
    return call(
        functools.partial(add_head_kernel, n_head - 1),
        "add_head",
        [jax.ShapeDtypeStruct(shape[1:], jnp.bfloat16)] * shape[0],
        1,
        [spec(shape)] * n_head,
        [spec(shape[1:])] * shape[0],
    )(where, *sums)


def sum_tail(sizes, where, pieces, kv_pieces, out_weight, hidden_in, attn_gate):
    n_patch, n_head, n_sub = sizes["patch"], sizes["head"], sizes["sub"]
    split, tok = len(pieces), pieces[0].shape[1]
    count = n_head * n_sub
    piece = tok // count
    parts = 2 if piece % 32 == 0 else 1
    attended = []
    for part in range(parts):
        rows = (part * (piece // parts), piece // parts)
        x = attend(where, rows, count, pieces, kv_pieces)
        attended.append(x.reshape(-1, x.shape[2]))
    slots = gather(attended, n_patch)
    blocks = []
    for part in range(parts):
        terms = project(split, where, *slots[part], out_weight, n_head, n_sub)
        total = reduce_head(sizes, where, reduce_sub(sizes, where, terms))
        blocks.append(
            [total[0]] + [swap(total[rel], "patch", n_patch, rel) for rel in range(1, n_patch)]
        )
    return mix(where, hidden_in, attn_gate, blocks)


def attend_halves_kernel(where_ref, *refs):
    pieces, outs = refs[:-2], refs[-2:]
    split = len(pieces)
    rels = [0, *range(split - 1, 0, -1)]
    factor = HEAD_DIM**-0.5 * math.log2(math.e)
    rows, feat = outs[0].shape[1:]
    for head in range(feat // HEAD_DIM):
        lanes = pl.ds(head * HEAD_DIM, HEAD_DIM)
        keys = jnp.concatenate([ref[1, :, lanes] for ref in pieces], axis=0)
        values = jnp.concatenate([ref[2, :, lanes] for ref in pieces], axis=0)
        values = jnp.concatenate([values, jnp.ones_like(values)], axis=1)
        for half, out in enumerate(outs):
            start = pl.multiple_of((where_ref[HEAD] ^ half) * rows, rows)
            query = jnp.concatenate([ref[0, pl.ds(start, rows), lanes] for ref in pieces], axis=0)
            scores = lax.dot_general(
                query, keys, (((1,), (1,)), ((), ())), preferred_element_type=jnp.float32
            )
            peak = jnp.max(scores, axis=1, keepdims=True)
            expo = jnp.exp2((scores - peak) * factor).astype(jnp.bfloat16)
            mix = jnp.dot(expo, values, preferred_element_type=jnp.float32)
            mix = (mix[:, :HEAD_DIM] / mix[:, HEAD_DIM:]).astype(jnp.bfloat16)
            for at, rel in enumerate(rels):
                out[where_ref[NEAR] ^ rel, :, lanes] = mix[at * rows : (at + 1) * rows]


def attend_halves(where, pieces):
    split = len(pieces)
    _, tok, feat = pieces[0].shape
    out = jax.ShapeDtypeStruct((split, tok // 2, feat), jnp.bfloat16)
    outs = call(
        attend_halves_kernel,
        "attend",
        [out] * 2,
        1,
        [spec((3, tok, feat))] * split,
        [spec(out.shape)] * 2,
    )(where, *pieces)
    return [x.reshape(-1, feat) for x in outs]


def first_kernel(where_ref, *refs):
    slots, (more, own_ref, fetched_ref, passed_ref, out_ref, held_ref) = refs[:7], refs[7:]
    feat = slots[0].shape[1]

    @pl.when(pl.program_id(0) == 0)
    def arrange():
        for at, slot in enumerate(slots):
            block = slot[...]
            if at == 3:
                block = jnp.where(where_ref[INNER] == 1, block, more[...])
            place = where_ref[NEAR] ^ (at % 4)
            if at >= 4:
                place = 4 + (2 * ((place // 2) ^ where_ref[GRP]) + place % 2)
            held_ref[:, pl.ds(pl.multiple_of(place * feat, HEAD_DIM), feat)] = block
        place = where_ref[NEAR] ^ 3
        place = 4 + (2 * ((place // 2) ^ where_ref[GRP]) + place % 2)
        held_ref[:, pl.ds(pl.multiple_of(place * feat, HEAD_DIM), feat)] = jnp.zeros(
            (slots[0].shape[0], feat), jnp.bfloat16
        )

    depth = 4 * feat
    acc = jnp.dot(held_ref[:, :depth], own_ref[...], preferred_element_type=jnp.float32)
    half = depth // 2
    for at, weight in enumerate((fetched_ref, passed_ref)):
        acc += jnp.dot(
            held_ref[:, depth + at * half : depth + (at + 1) * half],
            weight[...],
            preferred_element_type=jnp.float32,
        )
    out_ref[...] = acc


def first_product(where, slots, more, weights):
    rows, feat = slots[0].shape
    cols = weights[0].shape[1]
    wide = cols // 2
    return call(
        first_kernel,
        "first",
        jax.ShapeDtypeStruct((rows, cols), jnp.float32),
        2,
        [spec((rows, feat))] * 8
        + [pl.BlockSpec((x.shape[0], wide), lambda i, w: (0, i)) for x in weights],
        pl.BlockSpec((rows, wide), lambda i, w: (0, i)),
        [pltpu.VMEM((rows, 8 * feat), jnp.bfloat16)],
    )(where, *slots, more, *weights)


def second_kernel(where_ref, slot, more, fetched_ref, passed_ref, acc_in, keep_ref, send_ref, acc_ref):
    feat = slot.shape[1]
    place = where_ref[NEAR] ^ 3
    rows = pl.ds(pl.multiple_of((place % 2) * feat, HEAD_DIM), feat)
    weight = jnp.where(
        (place // 2) == where_ref[GRP], fetched_ref[rows, :], passed_ref[rows, :]
    )
    block = jnp.where(where_ref[INNER] == 1, slot[...], more[...])
    acc = acc_in[...] + jnp.dot(block, weight, preferred_element_type=jnp.float32)
    acc_ref[...] = acc.reshape(acc_ref.shape)
    for sub, out in enumerate((keep_ref, send_ref)):
        for at in range(4):
            out[at] = acc_ref[where_ref[NEAR] ^ at, where_ref[SUB] ^ sub].astype(jnp.bfloat16)


def second_product(where, slot, more, weights, acc):
    rows, feat = slot.shape
    depth, cols = weights[0].shape
    wide = cols // 2
    out = jax.ShapeDtypeStruct((4, rows // 8, cols), jnp.bfloat16)
    return call(
        second_kernel,
        "second",
        [out] * 2,
        2,
        [spec((rows, feat))] * 2
        + [pl.BlockSpec((depth, wide), lambda i, w: (0, i))] * 2
        + [pl.BlockSpec((rows, wide), lambda i, w: (0, i))],
        [pl.BlockSpec((4, rows // 8, wide), lambda i, w: (0, 0, i))] * 2,
        [pltpu.VMEM((4, 2, rows // 8, wide), jnp.float32)],
    )(where, slot, more, *weights, acc)


def add_kernel(where_ref, keep_ref, term_ref, *outs):
    for at, out in enumerate(outs):
        total = keep_ref[at].astype(jnp.float32) + term_ref[at].astype(jnp.float32)
        out[...] = total.astype(jnp.bfloat16)


def add(where, keep, term):
    return call(
        add_kernel,
        "add",
        [jax.ShapeDtypeStruct(keep.shape[1:], jnp.bfloat16)] * keep.shape[0],
        1,
        [spec(keep.shape)] * 2,
        [spec(keep.shape[1:])] * keep.shape[0],
    )(where, keep, term)


def share_tail(sizes, where, pieces, kv_pieces, out_weight, hidden_in, attn_gate):
    half = out_weight.shape[0] // 2
    out_weight, where = lax.optimization_barrier((out_weight, where))
    start = lax.axis_index("grp") * half
    fetched = swap(lax.dynamic_slice_in_dim(out_weight, start, half, 0), "head", 2, 1)
    pieces, fetched = lax.optimization_barrier((pieces, fetched))
    passed = swap(fetched, "grp", 2, 1)

    mine, other = attend_halves(where, pieces)
    other = swap(other, "head", 2, 1)
    slots = []
    for at, x in enumerate((mine, other)):
        far, next_to = swap(x, "patch", 4, 2), swap(x, "patch", 4, 1)
        far, next_to, other, x, passed = lax.optimization_barrier((far, next_to, other, x, passed))
        middle = swap(x, "patch", 4, 3, (1, 2))
        ends = lax.ppermute(far, "patch", [(1, 0), (2, 3)])
        slots.append([x, next_to, far, middle, ends])
    first = [*slots[0][:4], *slots[1][:3]]
    acc = first_product(where, first, slots[0][4], [out_weight, fetched, passed])
    keep, send = second_product(where, *slots[1][3:], [fetched, passed], acc)
    total = add(where, keep, swap(send, "sub", 2, 1))
    blocks = [total[0]] + [swap(total[rel], "patch", 4, rel) for rel in range(3, 0, -1)]
    return mix(where, hidden_in, attn_gate, [[blocks[0], *blocks[:0:-1]]])


def body(sizes, queries, fresh_kv, cached_kv, exponents, out_weight, hidden_in, attn_gate):
    n_patch, n_head, n_sub = sizes["patch"], sizes["head"], sizes["sub"]
    tok, channels = queries.shape
    heads = channels // HEAD_DIM
    split = math.gcd(heads, n_patch)
    patch_at = lax.axis_index("patch")
    inner = (patch_at > 0) & (patch_at < n_patch - 1)
    where = jnp.stack(
        [
            patch_at,
            patch_at % split,
            lax.axis_index("head"),
            lax.axis_index("sub"),
            inner,
            lax.axis_index("grp"),
        ]
    ).astype(jnp.int32)

    arrays = (exponents, queries, fresh_kv, cached_kv)
    sent = pack(split, *arrays)
    far_first = [swap(sent[rel - 1], "patch", n_patch, rel) for rel in range(split - 1, 0, -1)]
    where, sent = lax.optimization_barrier((where, sent))
    pieces = [pack_own(split, where, *arrays), *far_first]
    kv_pieces = list(pieces)
    for rel in range(split, n_patch, split):
        kv_pieces += [swap(x, "patch", n_patch, rel) for x in pieces]

    tail = (sizes, where, pieces, kv_pieces, out_weight, hidden_in, attn_gate)
    if (sizes["grp"], n_head, split, n_patch) == (2, 2, 4, 4):
        return share_tail(*tail)
    return sum_tail(*tail)


def solution(mesh):
    in_specs = (
        P(("grp", "patch"), ("head", "sub")),
        P(None, ("grp", "patch"), ("head", "sub")),
        P(None, "grp", ("head", "sub")),
        P(None, ("grp", "patch"), ("head", "sub")),
        P(("head", "sub"), "patch"),
        P(("grp", "patch", "head", "sub"), None),
        P(),
    )
    out_specs = P(("grp", "patch", "head", "sub"), None)
    return jax.shard_map(
        functools.partial(body, dict(mesh.shape)),
        mesh=mesh,
        in_specs=in_specs,
        out_specs=out_specs,
        check_vma=False,
    )
```

```python
import functools
import math

import jax
import jax.numpy as jnp
from jax import lax
from jax.experimental import pallas as pl
from jax.experimental.pallas import tpu as pltpu
from jax.sharding import PartitionSpec as P

HEAD_DIM = 128
SCALE_ROWS = 128
SATURATION = 448.0
VMEM_BYTES = 32 * 1024 * 1024
PACK_VMEM_BYTES = 60 * 1024 * 1024
ATTEND_FLOPS = 1
PROJECT_FLOPS = 1

PATCH, NEAR, HEAD, SUB, INNER, GRP = range(6)


def spec(shape):
    return pl.BlockSpec(shape, lambda i, w: (0,) * len(shape))


def call(kernel, name, out_shape, grid, in_specs, out_specs, scratch=(), flops=1, vmem=VMEM_BYTES):
    return pl.pallas_call(
        kernel,
        out_shape=out_shape,
        grid_spec=pltpu.PrefetchScalarGridSpec(
            num_scalar_prefetch=1,
            grid=(grid,),
            in_specs=in_specs,
            out_specs=out_specs,
            scratch_shapes=list(scratch),
        ),
        compiler_params=pltpu.CompilerParams(vmem_limit_bytes=vmem),
        cost_estimate=pl.CostEstimate(flops=flops, bytes_accessed=0, transcendentals=0),
        name=name,
    )


def swap(x, axes, count, mask, only=None):
    pairs = [(at, at ^ mask) for at in range(count) if only is None or at in only]
    return lax.ppermute(x, axes, pairs)


def decode(fresh, cached, exponent):
    power = jnp.full((1, HEAD_DIM), exponent.astype(jnp.float32))
    cached = cached.astype(jnp.float32)
    residual = fresh.astype(jnp.float32) - cached
    codes = jnp.clip(residual * jnp.exp2(-power), -SATURATION, SATURATION).astype(jnp.bfloat16)
    return (cached + codes.astype(jnp.float32) * jnp.exp2(power)).astype(jnp.bfloat16)


def pack_kernel(split, per, exps_ref, q_ref, fresh_ref, cached_ref, *refs):
    outs, (q_buf, fresh_buf, cached_buf, sems) = refs[:-4], refs[-4:]
    patch = lax.axis_index("patch")
    near = lax.rem(patch, split)
    tok = q_buf.shape[0]
    copies = []
    for block in range(tok // SCALE_ROWS):
        rows = pl.ds(block * SCALE_ROWS, SCALE_ROWS)
        there = pl.ds(pl.multiple_of(patch * tok + block * SCALE_ROWS, SCALE_ROWS), SCALE_ROWS)
        copies.append(
            [
                pltpu.make_async_copy(q_ref.at[rows], q_buf.at[rows], sems.at[block, 0]),
                pltpu.make_async_copy(fresh_ref.at[:, rows], fresh_buf.at[:, rows], sems.at[block, 1]),
                pltpu.make_async_copy(cached_ref.at[:, there], cached_buf.at[:, rows], sems.at[block, 2]),
            ]
        )
        for copy in copies[-1]:
            copy.start()
    for block in range(tok // SCALE_ROWS):
        rows = pl.ds(block * SCALE_ROWS, SCALE_ROWS)
        for copy in copies[block]:
            copy.wait()
        for rel in range(1, split):
            out = outs[rel - 1]
            for chunk in range(per):
                head = (near ^ rel) * per + chunk
                lanes = pl.ds(pl.multiple_of(head * HEAD_DIM, HEAD_DIM), HEAD_DIM)
                here = pl.ds(chunk * HEAD_DIM, HEAD_DIM)
                out[0, rows, here] = q_buf[rows, lanes]
                for stacked in range(2):
                    out[1 + stacked, rows, here] = decode(
                        fresh_buf[stacked, rows, lanes],
                        cached_buf[stacked, rows, lanes],
                        exps_ref[stacked, block, head],
                    )


def pack(split, exponents, queries, fresh_kv, cached_kv):
    tok, channels = queries.shape
    feat = channels // split
    blocks = tok // SCALE_ROWS
    hbm = pl.BlockSpec(memory_space=pltpu.HBM)
    return pl.pallas_call(
        functools.partial(pack_kernel, split, feat // HEAD_DIM),
        out_shape=[jax.ShapeDtypeStruct((3, tok, feat), jnp.bfloat16)] * (split - 1),
        in_specs=[pl.BlockSpec(memory_space=pltpu.SMEM), hbm, hbm, hbm],
        out_specs=[pl.BlockSpec(memory_space=pltpu.VMEM)] * (split - 1),
        scratch_shapes=[
            pltpu.VMEM((tok, channels), jnp.bfloat16),
            pltpu.VMEM((2, tok, channels), jnp.bfloat16),
            pltpu.VMEM((2, tok, channels), jnp.bfloat16),
            pltpu.SemaphoreType.DMA((blocks, 3)),
        ],
        compiler_params=pltpu.CompilerParams(vmem_limit_bytes=PACK_VMEM_BYTES),
        name="pack",
    )(exponents, queries, fresh_kv, cached_kv)


def own_kernel(per, where_ref, exps_ref, q_ref, fresh_ref, cached_ref, out_ref):
    out_ref[0] = q_ref[...]
    for chunk in range(per):
        lanes = pl.ds(chunk * HEAD_DIM, HEAD_DIM)
        for block in range(q_ref.shape[0] // SCALE_ROWS):
            rows = pl.ds(block * SCALE_ROWS, SCALE_ROWS)
            for stacked in range(2):
                out_ref[1 + stacked, rows, lanes] = decode(
                    fresh_ref[stacked, rows, lanes],
                    cached_ref[stacked, rows, lanes],
                    exps_ref[stacked, block, where_ref[NEAR] * per + chunk],
                )


def pack_own(split, where, exponents, queries, fresh_kv, cached_kv):
    tok, channels = queries.shape
    feat = channels // split
    out = jax.ShapeDtypeStruct((3, tok, feat), jnp.bfloat16)
    return call(
        functools.partial(own_kernel, feat // HEAD_DIM),
        "own",
        out,
        1,
        [
            pl.BlockSpec(memory_space=pltpu.SMEM),
            pl.BlockSpec((tok, feat), lambda i, w: (0, w[NEAR])),
            pl.BlockSpec((2, tok, feat), lambda i, w: (0, 0, w[NEAR])),
            pl.BlockSpec((2, tok, feat), lambda i, w: (0, w[PATCH], w[NEAR])),
        ],
        spec(out.shape),
    )(where, exponents, queries, fresh_kv, cached_kv)


def attend_kernel(split, part, where_ref, *refs):
    q_refs, kv_refs, out_ref = (refs[0], *refs[split - 1 : 0 : -1]), refs[:-1], refs[-1]
    factor = HEAD_DIM**-0.5 * math.log2(math.e)
    tok, feat = q_refs[0].shape[1:]
    count = out_ref.shape[1] // part[1]
    starts = [at * (tok // count) + part[0] for at in range(count)]
    for head in range(feat // HEAD_DIM):
        lanes = pl.ds(head * HEAD_DIM, HEAD_DIM)
        keys = jnp.concatenate([ref[1, :, lanes] for ref in kv_refs], axis=0)
        values = jnp.concatenate([ref[2, :, lanes] for ref in kv_refs], axis=0)
        values = jnp.concatenate([values, jnp.ones_like(values)], axis=1)
        for rel in range(split):
            rows = [q_refs[rel][0, start : start + part[1], lanes] for start in starts]
            query = jnp.concatenate(rows, axis=0) if len(rows) > 1 else rows[0]
            scores = lax.dot_general(
                query, keys, (((1,), (1,)), ((), ())), preferred_element_type=jnp.float32
            )
            peak = jnp.max(scores, axis=1, keepdims=True)
            expo = jnp.exp2((scores - peak) * factor).astype(jnp.bfloat16)
            mix = jnp.dot(expo, values, preferred_element_type=jnp.float32)
            mix = mix[:, :HEAD_DIM] / mix[:, HEAD_DIM:]
            out_ref[where_ref[NEAR] ^ rel, :, lanes] = mix.astype(jnp.bfloat16)


def attend(where, part, count, pieces, kv_pieces):
    split = len(pieces)
    _, tok, feat = pieces[0].shape
    out = jax.ShapeDtypeStruct((split, count * part[1], feat), jnp.bfloat16)
    return call(
        functools.partial(attend_kernel, split, part),
        "attend",
        out,
        1,
        [spec((3, tok, feat))] * len(kv_pieces),
        spec(out.shape),
        flops=ATTEND_FLOPS,
    )(where, *kv_pieces)


def project_kernel(split, n_slots, n_more, where_ref, *refs):
    slots, refs = refs[:n_slots], refs[n_slots:]
    more, weight_ref, refs = refs[:n_more], refs[n_more], refs[n_more + 1 :]
    outs, held_ref, acc_ref = refs[:-2], refs[-2], refs[-1]
    rows, feat = slots[0].shape
    n_sub, n_head = acc_ref.shape[3], acc_ref.shape[2]

    @pl.when(pl.program_id(0) == 0)
    def arrange():
        for at, slot in enumerate(slots):
            group, near = divmod(at, split)
            lane = (where_ref[NEAR] ^ near) * feat
            block = slot[...]
            if more and at == n_slots - 1:
                block = jnp.where(where_ref[INNER] == 1, block, more[0][...])
            held_ref[
                group * rows : (group + 1) * rows, pl.ds(pl.multiple_of(lane, HEAD_DIM), feat)
            ] = block

    acc = jnp.dot(held_ref[...], weight_ref[...], preferred_element_type=jnp.float32)
    acc_ref[...] = acc.reshape(acc_ref.shape)
    for sub in range(n_sub):
        for head in range(n_head):
            for at in range(n_slots):
                group, near = divmod(at, split)
                outs[sub][head, at] = acc_ref[
                    group, where_ref[NEAR] ^ near, where_ref[HEAD] ^ head, where_ref[SUB] ^ sub
                ].astype(jnp.bfloat16)


def project(split, where, slots, more, weight, n_head, n_sub):
    rows, feat = slots[0].shape
    n_patch = len(slots)
    total = rows * n_patch // split
    depth, cols = weight.shape
    wide = 640 if cols % 640 == 0 else cols
    piece = rows // (split * n_head * n_sub)
    return call(
        functools.partial(project_kernel, split, n_patch, len(more)),
        "project",
        [jax.ShapeDtypeStruct((n_head, n_patch, piece, cols), jnp.bfloat16)] * n_sub,
        cols // wide,
        [spec((rows, feat))] * (n_patch + len(more))
        + [pl.BlockSpec((depth, wide), lambda i, w: (0, i))],
        [pl.BlockSpec((n_head, n_patch, piece, wide), lambda i, w: (0, 0, 0, i))] * n_sub,
        [
            pltpu.VMEM((total, depth), jnp.bfloat16),
            pltpu.VMEM((n_patch // split, split, n_head, n_sub, piece, wide), jnp.float32),
        ],
        flops=PROJECT_FLOPS,
    )(where, *slots, *more, weight)


def mix_kernel(rels, where_ref, hidden_ref, gate_ref, *refs):
    blocks, out_ref = refs[:-1], refs[-1]
    piece, cols = blocks[0].shape
    for part in range(len(blocks) // len(rels)):
        rows = pl.ds(part * piece, piece)
        for at, rel in enumerate(rels):
            lanes = pl.ds(pl.multiple_of((where_ref[PATCH] ^ rel) * cols, HEAD_DIM), cols)
            mixed = hidden_ref[rows, lanes].astype(jnp.float32) + gate_ref[:, lanes] * blocks[
                part * len(rels) + at
            ][...].astype(jnp.float32)
            out_ref[rows, lanes] = mixed.astype(jnp.bfloat16)


def mix(where, hidden_in, attn_gate, blocks):
    rows, width = hidden_in.shape
    n_patch = len(blocks[0])
    piece, cols = blocks[0][0].shape
    if cols % HEAD_DIM:
        order = jnp.concatenate([jnp.stack(x) for x in blocks], axis=1)
        order = order[where[PATCH] ^ jnp.arange(n_patch)]
        projected = order.transpose(1, 0, 2).reshape(rows, width).astype(jnp.float32)
        return (hidden_in.astype(jnp.float32) + attn_gate * projected).astype(jnp.bfloat16)
    rels = [0, *range(n_patch - 1, 0, -1)]
    flat = [part[rel] for part in blocks for rel in rels]
    return call(
        functools.partial(mix_kernel, rels),
        "mix",
        jax.ShapeDtypeStruct((rows, width), jnp.bfloat16),
        1,
        [spec((rows, width)), spec((1, width))] + [spec((piece, cols))] * len(flat),
        spec((rows, width)),
    )(where, hidden_in, attn_gate[None], *flat)


def gather(parts, n_patch):
    if n_patch != 4:
        return [
            ([x] + [swap(x, "patch", n_patch, rel) for rel in range(1, n_patch)], [])
            for x in parts
        ]
    far = [swap(x, "patch", 4, 2) for x in parts]
    next_to = [swap(x, "patch", 4, 1) for x in parts]
    out = []
    for at, x in enumerate(parts):
        far[at], next_to[at], parts = lax.optimization_barrier((far[at], next_to[at], parts))
        middle = swap(parts[at], "patch", 4, 3, (1, 2))
        ends = lax.ppermute(far[at], "patch", [(1, 0), (2, 3)])
        if at + 1 < len(parts):
            ends, far[at + 1], next_to[at + 1] = lax.optimization_barrier(
                (ends, far[at + 1], next_to[at + 1])
            )
        out.append(([x, next_to[at], far[at], middle], [ends]))
    return out


def add_sub_kernel(n_sub, where_ref, *refs):
    terms, kept_ref, outs = refs[:n_sub], refs[n_sub], refs[n_sub + 1 :]
    for head in range(len(outs) + 1):
        total = terms[0][head].astype(jnp.float32)
        for term in terms[1:]:
            total += term[head].astype(jnp.float32)
        if head == 0:
            kept_ref[...] = total
        else:
            outs[head - 1][...] = total.astype(jnp.bfloat16)


def add_head_kernel(n_more, where_ref, kept_ref, *refs):
    for at, out in enumerate(refs[n_more:]):
        total = kept_ref[at]
        for term in refs[:n_more]:
            total += term[at].astype(jnp.float32)
        out[...] = total.astype(jnp.bfloat16)


def reduce_sub(sizes, where, terms):
    n_sub, n_head = sizes["sub"], sizes["head"]
    terms = [terms[0]] + [swap(terms[rel], "sub", n_sub, rel) for rel in range(1, n_sub)]
    shape = terms[0].shape[1:]
    return call(
        functools.partial(add_sub_kernel, n_sub),
        "add_sub",
        [jax.ShapeDtypeStruct(shape, jnp.float32)]
        + [jax.ShapeDtypeStruct(shape, jnp.bfloat16)] * (n_head - 1),
        1,
        [spec(terms[0].shape)] * n_sub,
        [spec(shape)] * n_head,
    )(where, *terms)


def reduce_head(sizes, where, sums):
    n_head = sizes["head"]
    shape = sums[0].shape
    sums = [sums[0]] + [swap(sums[rel], "head", n_head, rel) for rel in range(1, n_head)]
    return call(
        functools.partial(add_head_kernel, n_head - 1),
        "add_head",
        [jax.ShapeDtypeStruct(shape[1:], jnp.bfloat16)] * shape[0],
        1,
        [spec(shape)] * n_head,
        [spec(shape[1:])] * shape[0],
    )(where, *sums)


def sum_tail(sizes, where, pieces, kv_pieces, out_weight, hidden_in, attn_gate):
    n_patch, n_head, n_sub = sizes["patch"], sizes["head"], sizes["sub"]
    split, tok = len(pieces), pieces[0].shape[1]
    count = n_head * n_sub
    piece = tok // count
    parts = 2 if piece % 32 == 0 else 1
    attended = []
    for part in range(parts):
        rows = (part * (piece // parts), piece // parts)
        x = attend(where, rows, count, pieces, kv_pieces)
        attended.append(x.reshape(-1, x.shape[2]))
    slots = gather(attended, n_patch)
    blocks = []
    for part in range(parts):
        terms = project(split, where, *slots[part], out_weight, n_head, n_sub)
        total = reduce_head(sizes, where, reduce_sub(sizes, where, terms))
        blocks.append(
            [total[0]] + [swap(total[rel], "patch", n_patch, rel) for rel in range(1, n_patch)]
        )
    return mix(where, hidden_in, attn_gate, blocks)


def attend_halves_kernel(where_ref, *refs):
    pieces, outs = refs[:-2], refs[-2:]
    split = len(pieces)
    rels = [0, *range(split - 1, 0, -1)]
    factor = HEAD_DIM**-0.5 * math.log2(math.e)
    rows, feat = outs[0].shape[1:]
    for head in range(feat // HEAD_DIM):
        lanes = pl.ds(head * HEAD_DIM, HEAD_DIM)
        keys = jnp.concatenate([ref[1, :, lanes] for ref in pieces], axis=0)
        values = jnp.concatenate([ref[2, :, lanes] for ref in pieces], axis=0)
        values = jnp.concatenate([values, jnp.ones_like(values)], axis=1)
        for half, out in enumerate(outs):
            start = pl.multiple_of((where_ref[HEAD] ^ half) * rows, rows)
            query = jnp.concatenate([ref[0, pl.ds(start, rows), lanes] for ref in pieces], axis=0)
            scores = lax.dot_general(
                query, keys, (((1,), (1,)), ((), ())), preferred_element_type=jnp.float32
            )
            peak = jnp.max(scores, axis=1, keepdims=True)
            expo = jnp.exp2((scores - peak) * factor).astype(jnp.bfloat16)
            mix = jnp.dot(expo, values, preferred_element_type=jnp.float32)
            mix = (mix[:, :HEAD_DIM] / mix[:, HEAD_DIM:]).astype(jnp.bfloat16)
            for at, rel in enumerate(rels):
                out[where_ref[NEAR] ^ rel, :, lanes] = mix[at * rows : (at + 1) * rows]


def attend_halves(where, pieces):
    split = len(pieces)
    _, tok, feat = pieces[0].shape
    out = jax.ShapeDtypeStruct((split, tok // 2, feat), jnp.bfloat16)
    outs = call(
        attend_halves_kernel,
        "attend",
        [out] * 2,
        1,
        [spec((3, tok, feat))] * split,
        [spec(out.shape)] * 2,
    )(where, *pieces)
    return [x.reshape(-1, feat) for x in outs]


def first_kernel(where_ref, *refs):
    slots, (more, own_ref, fetched_ref, passed_ref, out_ref, held_ref) = refs[:7], refs[7:]
    feat = slots[0].shape[1]

    @pl.when(pl.program_id(0) == 0)
    def arrange():
        for at, slot in enumerate(slots):
            block = slot[...]
            if at == 3:
                block = jnp.where(where_ref[INNER] == 1, block, more[...])
            place = where_ref[NEAR] ^ (at % 4)
            if at >= 4:
                place = 4 + (2 * ((place // 2) ^ where_ref[GRP]) + place % 2)
            held_ref[:, pl.ds(pl.multiple_of(place * feat, HEAD_DIM), feat)] = block
        place = where_ref[NEAR] ^ 3
        place = 4 + (2 * ((place // 2) ^ where_ref[GRP]) + place % 2)
        held_ref[:, pl.ds(pl.multiple_of(place * feat, HEAD_DIM), feat)] = jnp.zeros(
            (slots[0].shape[0], feat), jnp.bfloat16
        )

    depth = 4 * feat
    acc = jnp.dot(held_ref[:, :depth], own_ref[...], preferred_element_type=jnp.float32)
    half = depth // 2
    for at, weight in enumerate((fetched_ref, passed_ref)):
        acc += jnp.dot(
            held_ref[:, depth + at * half : depth + (at + 1) * half],
            weight[...],
            preferred_element_type=jnp.float32,
        )
    out_ref[...] = acc


def first_product(where, slots, more, weights):
    rows, feat = slots[0].shape
    cols = weights[0].shape[1]
    wide = cols // 2
    return call(
        first_kernel,
        "first",
        jax.ShapeDtypeStruct((rows, cols), jnp.float32),
        2,
        [spec((rows, feat))] * 8
        + [pl.BlockSpec((x.shape[0], wide), lambda i, w: (0, i)) for x in weights],
        pl.BlockSpec((rows, wide), lambda i, w: (0, i)),
        [pltpu.VMEM((rows, 8 * feat), jnp.bfloat16)],
    )(where, *slots, more, *weights)


def second_kernel(where_ref, slot, more, fetched_ref, passed_ref, acc_in, keep_ref, send_ref, acc_ref):
    feat = slot.shape[1]
    place = where_ref[NEAR] ^ 3
    rows = pl.ds(pl.multiple_of((place % 2) * feat, HEAD_DIM), feat)
    weight = jnp.where(
        (place // 2) == where_ref[GRP], fetched_ref[rows, :], passed_ref[rows, :]
    )
    block = jnp.where(where_ref[INNER] == 1, slot[...], more[...])
    acc = acc_in[...] + jnp.dot(block, weight, preferred_element_type=jnp.float32)
    acc_ref[...] = acc.reshape(acc_ref.shape)
    for sub, out in enumerate((keep_ref, send_ref)):
        for at in range(4):
            out[at] = acc_ref[where_ref[NEAR] ^ at, where_ref[SUB] ^ sub].astype(jnp.bfloat16)


def second_product(where, slot, more, weights, acc):
    rows, feat = slot.shape
    depth, cols = weights[0].shape
    wide = cols // 2
    out = jax.ShapeDtypeStruct((4, rows // 8, cols), jnp.bfloat16)
    return call(
        second_kernel,
        "second",
        [out] * 2,
        2,
        [spec((rows, feat))] * 2
        + [pl.BlockSpec((depth, wide), lambda i, w: (0, i))] * 2
        + [pl.BlockSpec((rows, wide), lambda i, w: (0, i))],
        [pl.BlockSpec((4, rows // 8, wide), lambda i, w: (0, 0, i))] * 2,
        [pltpu.VMEM((4, 2, rows // 8, wide), jnp.float32)],
    )(where, slot, more, *weights, acc)


def add_kernel(where_ref, keep_ref, term_ref, *outs):
    for at, out in enumerate(outs):
        total = keep_ref[at].astype(jnp.float32) + term_ref[at].astype(jnp.float32)
        out[...] = total.astype(jnp.bfloat16)


def add(where, keep, term):
    return call(
        add_kernel,
        "add",
        [jax.ShapeDtypeStruct(keep.shape[1:], jnp.bfloat16)] * keep.shape[0],
        1,
        [spec(keep.shape)] * 2,
        [spec(keep.shape[1:])] * keep.shape[0],
    )(where, keep, term)


def share_tail(sizes, where, pieces, kv_pieces, out_weight, hidden_in, attn_gate):
    half = out_weight.shape[0] // 2
    out_weight, where = lax.optimization_barrier((out_weight, where))
    start = lax.axis_index("grp") * half
    fetched = swap(lax.dynamic_slice_in_dim(out_weight, start, half, 0), "head", 2, 1)
    pieces, fetched = lax.optimization_barrier((pieces, fetched))
    passed = swap(fetched, "grp", 2, 1)

    mine, other = attend_halves(where, pieces)
    other = swap(other, "head", 2, 1)
    slots = []
    for at, x in enumerate((mine, other)):
        far, next_to = swap(x, "patch", 4, 2), swap(x, "patch", 4, 1)
        far, next_to, other, x = lax.optimization_barrier((far, next_to, other, x))
        if at == 1:
            far, x, passed = lax.optimization_barrier((far, x, passed))
        middle = swap(x, "patch", 4, 3, (1, 2))
        ends = lax.ppermute(far, "patch", [(1, 0), (2, 3)])
        slots.append([x, next_to, far, middle, ends])
    first = [*slots[0][:4], *slots[1][:3]]
    acc = first_product(where, first, slots[0][4], [out_weight, fetched, passed])
    keep, send = second_product(where, *slots[1][3:], [fetched, passed], acc)
    total = add(where, keep, swap(send, "sub", 2, 1))
    blocks = [total[0]] + [swap(total[rel], "patch", 4, rel) for rel in range(3, 0, -1)]
    return mix(where, hidden_in, attn_gate, [[blocks[0], *blocks[:0:-1]]])


def body(sizes, queries, fresh_kv, cached_kv, exponents, out_weight, hidden_in, attn_gate):
    n_patch, n_head, n_sub = sizes["patch"], sizes["head"], sizes["sub"]
    tok, channels = queries.shape
    heads = channels // HEAD_DIM
    split = math.gcd(heads, n_patch)
    patch_at = lax.axis_index("patch")
    inner = (patch_at > 0) & (patch_at < n_patch - 1)
    where = jnp.stack(
        [
            patch_at,
            patch_at % split,
            lax.axis_index("head"),
            lax.axis_index("sub"),
            inner,
            lax.axis_index("grp"),
        ]
    ).astype(jnp.int32)

    arrays = (exponents, queries, fresh_kv, cached_kv)
    sent = pack(split, *arrays)
    far_first = [swap(sent[rel - 1], "patch", n_patch, rel) for rel in range(split - 1, 0, -1)]
    where, sent = lax.optimization_barrier((where, sent))
    pieces = [pack_own(split, where, *arrays), *far_first]
    kv_pieces = list(pieces)
    for rel in range(split, n_patch, split):
        kv_pieces += [swap(x, "patch", n_patch, rel) for x in pieces]

    tail = (sizes, where, pieces, kv_pieces, out_weight, hidden_in, attn_gate)
    if (sizes["grp"], n_head, split, n_patch) == (2, 2, 4, 4):
        return share_tail(*tail)
    return sum_tail(*tail)


def solution(mesh):
    in_specs = (
        P(("grp", "patch"), ("head", "sub")),
        P(None, ("grp", "patch"), ("head", "sub")),
        P(None, "grp", ("head", "sub")),
        P(None, ("grp", "patch"), ("head", "sub")),
        P(("head", "sub"), "patch"),
        P(("grp", "patch", "head", "sub"), None),
        P(),
    )
    out_specs = P(("grp", "patch", "head", "sub"), None)
    return jax.shard_map(
        functools.partial(body, dict(mesh.shape)),
        mesh=mesh,
        in_specs=in_specs,
        out_specs=out_specs,
        check_vma=False,
    )
```

```python
import functools
import math

import jax
import jax.numpy as jnp
from jax import lax
from jax.experimental import pallas as pl
from jax.experimental.pallas import tpu as pltpu
from jax.sharding import PartitionSpec as P

HEAD_DIM = 128
SCALE_ROWS = 128
SATURATION = 448.0
PACK_ROWS = 64
VMEM_BYTES = 32 * 1024 * 1024
PACK_VMEM_BYTES = 60 * 1024 * 1024
ATTEND_FLOPS = 1
PROJECT_FLOPS = 1

PATCH, NEAR, HEAD, SUB, INNER, GRP = range(6)


def spec(shape):
    return pl.BlockSpec(shape, lambda i, w: (0,) * len(shape))


def call(kernel, name, out_shape, grid, in_specs, out_specs, scratch=(), flops=1, vmem=VMEM_BYTES):
    return pl.pallas_call(
        kernel,
        out_shape=out_shape,
        grid_spec=pltpu.PrefetchScalarGridSpec(
            num_scalar_prefetch=1,
            grid=(grid,),
            in_specs=in_specs,
            out_specs=out_specs,
            scratch_shapes=list(scratch),
        ),
        compiler_params=pltpu.CompilerParams(vmem_limit_bytes=vmem),
        cost_estimate=pl.CostEstimate(flops=flops, bytes_accessed=0, transcendentals=0),
        name=name,
    )


def swap(x, axes, count, mask, only=None):
    pairs = [(at, at ^ mask) for at in range(count) if only is None or at in only]
    return lax.ppermute(x, axes, pairs)


def decode(fresh, cached, exponent):
    power = jnp.full((1, HEAD_DIM), exponent.astype(jnp.float32))
    cached = cached.astype(jnp.float32)
    residual = fresh.astype(jnp.float32) - cached
    codes = jnp.clip(residual * jnp.exp2(-power), -SATURATION, SATURATION).astype(jnp.bfloat16)
    return (cached + codes.astype(jnp.float32) * jnp.exp2(power)).astype(jnp.bfloat16)


def pack_kernel(split, per, exps_ref, q_ref, fresh_ref, cached_ref, *refs):
    outs, bufs = refs[: split - 1], refs[split - 1 : 2 * split - 2]
    q_buf, fresh_buf, cached_buf, sems, out_sems = refs[2 * split - 2 :]
    patch = lax.axis_index("patch")
    near = lax.rem(patch, split)
    tok = q_buf.shape[0]
    copies, sent = [], []
    for block in range(tok // PACK_ROWS):
        rows = pl.ds(block * PACK_ROWS, PACK_ROWS)
        there = pl.ds(pl.multiple_of(patch * tok + block * PACK_ROWS, PACK_ROWS), PACK_ROWS)
        copies.append(
            [
                pltpu.make_async_copy(q_ref.at[rows], q_buf.at[rows], sems.at[block, 0]),
                pltpu.make_async_copy(fresh_ref.at[:, rows], fresh_buf.at[:, rows], sems.at[block, 1]),
                pltpu.make_async_copy(cached_ref.at[:, there], cached_buf.at[:, rows], sems.at[block, 2]),
            ]
        )
        for copy in copies[-1]:
            copy.start()
    for block in range(tok // PACK_ROWS):
        rows = pl.ds(block * PACK_ROWS, PACK_ROWS)
        for copy in copies[block]:
            copy.wait()
        for rel in range(split - 1, 0, -1):
            buf = bufs[rel - 1]
            for chunk in range(per):
                head = (near ^ rel) * per + chunk
                lanes = pl.ds(pl.multiple_of(head * HEAD_DIM, HEAD_DIM), HEAD_DIM)
                here = pl.ds(chunk * HEAD_DIM, HEAD_DIM)
                buf[0, rows, here] = q_buf[rows, lanes]
                for stacked in range(2):
                    buf[1 + stacked, rows, here] = decode(
                        fresh_buf[stacked, rows, lanes],
                        cached_buf[stacked, rows, lanes],
                        exps_ref[stacked, block * PACK_ROWS // SCALE_ROWS, head],
                    )
            sent.append(
                pltpu.make_async_copy(
                    buf.at[:, rows], outs[rel - 1].at[:, rows], out_sems.at[block, rel - 1]
                )
            )
            sent[-1].start()
    for copy in sent:
        copy.wait()


def pack(split, exponents, queries, fresh_kv, cached_kv):
    tok, channels = queries.shape
    feat = channels // split
    blocks = tok // PACK_ROWS
    hbm = pl.BlockSpec(memory_space=pltpu.HBM)
    return pl.pallas_call(
        functools.partial(pack_kernel, split, feat // HEAD_DIM),
        out_shape=[jax.ShapeDtypeStruct((3, tok, feat), jnp.bfloat16)] * (split - 1),
        in_specs=[pl.BlockSpec(memory_space=pltpu.SMEM), hbm, hbm, hbm],
        out_specs=[hbm] * (split - 1),
        scratch_shapes=[pltpu.VMEM((3, tok, feat), jnp.bfloat16)] * (split - 1)
        + [
            pltpu.VMEM((tok, channels), jnp.bfloat16),
            pltpu.VMEM((2, tok, channels), jnp.bfloat16),
            pltpu.VMEM((2, tok, channels), jnp.bfloat16),
            pltpu.SemaphoreType.DMA((blocks, 3)),
            pltpu.SemaphoreType.DMA((blocks, split - 1)),
        ],
        compiler_params=pltpu.CompilerParams(vmem_limit_bytes=PACK_VMEM_BYTES),
        name="pack",
    )(exponents, queries, fresh_kv, cached_kv)


def own_kernel(per, where_ref, exps_ref, q_ref, fresh_ref, cached_ref, out_ref):
    out_ref[0] = q_ref[...]
    for chunk in range(per):
        lanes = pl.ds(chunk * HEAD_DIM, HEAD_DIM)
        for block in range(q_ref.shape[0] // SCALE_ROWS):
            rows = pl.ds(block * SCALE_ROWS, SCALE_ROWS)
            for stacked in range(2):
                out_ref[1 + stacked, rows, lanes] = decode(
                    fresh_ref[stacked, rows, lanes],
                    cached_ref[stacked, rows, lanes],
                    exps_ref[stacked, block, where_ref[NEAR] * per + chunk],
                )


def pack_own(split, where, exponents, queries, fresh_kv, cached_kv):
    tok, channels = queries.shape
    feat = channels // split
    out = jax.ShapeDtypeStruct((3, tok, feat), jnp.bfloat16)
    return call(
        functools.partial(own_kernel, feat // HEAD_DIM),
        "own",
        out,
        1,
        [
            pl.BlockSpec(memory_space=pltpu.SMEM),
            pl.BlockSpec((tok, feat), lambda i, w: (0, w[NEAR])),
            pl.BlockSpec((2, tok, feat), lambda i, w: (0, 0, w[NEAR])),
            pl.BlockSpec((2, tok, feat), lambda i, w: (0, w[PATCH], w[NEAR])),
        ],
        spec(out.shape),
    )(where, exponents, queries, fresh_kv, cached_kv)


def attend_kernel(split, part, where_ref, *refs):
    q_refs, kv_refs, out_ref = (refs[0], *refs[split - 1 : 0 : -1]), refs[:-1], refs[-1]
    factor = HEAD_DIM**-0.5 * math.log2(math.e)
    tok, feat = q_refs[0].shape[1:]
    count = out_ref.shape[1] // part[1]
    starts = [at * (tok // count) + part[0] for at in range(count)]
    for head in range(feat // HEAD_DIM):
        lanes = pl.ds(head * HEAD_DIM, HEAD_DIM)
        keys = jnp.concatenate([ref[1, :, lanes] for ref in kv_refs], axis=0)
        values = jnp.concatenate([ref[2, :, lanes] for ref in kv_refs], axis=0)
        values = jnp.concatenate([values, jnp.ones_like(values)], axis=1)
        for rel in range(split):
            rows = [q_refs[rel][0, start : start + part[1], lanes] for start in starts]
            query = jnp.concatenate(rows, axis=0) if len(rows) > 1 else rows[0]
            scores = lax.dot_general(
                query, keys, (((1,), (1,)), ((), ())), preferred_element_type=jnp.float32
            )
            peak = jnp.max(scores, axis=1, keepdims=True)
            expo = jnp.exp2((scores - peak) * factor).astype(jnp.bfloat16)
            mix = jnp.dot(expo, values, preferred_element_type=jnp.float32)
            mix = mix[:, :HEAD_DIM] / mix[:, HEAD_DIM:]
            out_ref[where_ref[NEAR] ^ rel, :, lanes] = mix.astype(jnp.bfloat16)


def attend(where, part, count, pieces, kv_pieces):
    split = len(pieces)
    _, tok, feat = pieces[0].shape
    out = jax.ShapeDtypeStruct((split, count * part[1], feat), jnp.bfloat16)
    return call(
        functools.partial(attend_kernel, split, part),
        "attend",
        out,
        1,
        [spec((3, tok, feat))] * len(kv_pieces),
        spec(out.shape),
        flops=ATTEND_FLOPS,
    )(where, *kv_pieces)


def project_kernel(split, n_slots, n_more, where_ref, *refs):
    slots, refs = refs[:n_slots], refs[n_slots:]
    more, weight_ref, refs = refs[:n_more], refs[n_more], refs[n_more + 1 :]
    outs, held_ref, acc_ref = refs[:-2], refs[-2], refs[-1]
    rows, feat = slots[0].shape
    n_sub, n_head = acc_ref.shape[3], acc_ref.shape[2]

    @pl.when(pl.program_id(0) == 0)
    def arrange():
        for at, slot in enumerate(slots):
            group, near = divmod(at, split)
            lane = (where_ref[NEAR] ^ near) * feat
            block = slot[...]
            if more and at == n_slots - 1:
                block = jnp.where(where_ref[INNER] == 1, block, more[0][...])
            held_ref[
                group * rows : (group + 1) * rows, pl.ds(pl.multiple_of(lane, HEAD_DIM), feat)
            ] = block

    acc = jnp.dot(held_ref[...], weight_ref[...], preferred_element_type=jnp.float32)
    acc_ref[...] = acc.reshape(acc_ref.shape)
    for sub in range(n_sub):
        for head in range(n_head):
            for at in range(n_slots):
                group, near = divmod(at, split)
                outs[sub][head, at] = acc_ref[
                    group, where_ref[NEAR] ^ near, where_ref[HEAD] ^ head, where_ref[SUB] ^ sub
                ].astype(jnp.bfloat16)


def project(split, where, slots, more, weight, n_head, n_sub):
    rows, feat = slots[0].shape
    n_patch = len(slots)
    total = rows * n_patch // split
    depth, cols = weight.shape
    wide = 640 if cols % 640 == 0 else cols
    piece = rows // (split * n_head * n_sub)
    return call(
        functools.partial(project_kernel, split, n_patch, len(more)),
        "project",
        [jax.ShapeDtypeStruct((n_head, n_patch, piece, cols), jnp.bfloat16)] * n_sub,
        cols // wide,
        [spec((rows, feat))] * (n_patch + len(more))
        + [pl.BlockSpec((depth, wide), lambda i, w: (0, i))],
        [pl.BlockSpec((n_head, n_patch, piece, wide), lambda i, w: (0, 0, 0, i))] * n_sub,
        [
            pltpu.VMEM((total, depth), jnp.bfloat16),
            pltpu.VMEM((n_patch // split, split, n_head, n_sub, piece, wide), jnp.float32),
        ],
        flops=PROJECT_FLOPS,
    )(where, *slots, *more, weight)


def mix_kernel(rels, where_ref, hidden_ref, gate_ref, *refs):
    blocks, out_ref = refs[:-1], refs[-1]
    piece, cols = blocks[0].shape
    for part in range(len(blocks) // len(rels)):
        rows = pl.ds(part * piece, piece)
        for at, rel in enumerate(rels):
            lanes = pl.ds(pl.multiple_of((where_ref[PATCH] ^ rel) * cols, HEAD_DIM), cols)
            mixed = hidden_ref[rows, lanes].astype(jnp.float32) + gate_ref[:, lanes] * blocks[
                part * len(rels) + at
            ][...].astype(jnp.float32)
            out_ref[rows, lanes] = mixed.astype(jnp.bfloat16)


def mix(where, hidden_in, attn_gate, blocks):
    rows, width = hidden_in.shape
    n_patch = len(blocks[0])
    piece, cols = blocks[0][0].shape
    if cols % HEAD_DIM:
        order = jnp.concatenate([jnp.stack(x) for x in blocks], axis=1)
        order = order[where[PATCH] ^ jnp.arange(n_patch)]
        projected = order.transpose(1, 0, 2).reshape(rows, width).astype(jnp.float32)
        return (hidden_in.astype(jnp.float32) + attn_gate * projected).astype(jnp.bfloat16)
    rels = [0, *range(n_patch - 1, 0, -1)]
    flat = [part[rel] for part in blocks for rel in rels]
    return call(
        functools.partial(mix_kernel, rels),
        "mix",
        jax.ShapeDtypeStruct((rows, width), jnp.bfloat16),
        1,
        [spec((rows, width)), spec((1, width))] + [spec((piece, cols))] * len(flat),
        spec((rows, width)),
    )(where, hidden_in, attn_gate[None], *flat)


def gather(parts, n_patch):
    if n_patch != 4:
        return [
            ([x] + [swap(x, "patch", n_patch, rel) for rel in range(1, n_patch)], [])
            for x in parts
        ]
    far = [swap(x, "patch", 4, 2) for x in parts]
    next_to = [swap(x, "patch", 4, 1) for x in parts]
    out = []
    for at, x in enumerate(parts):
        far[at], next_to[at], parts = lax.optimization_barrier((far[at], next_to[at], parts))
        middle = swap(parts[at], "patch", 4, 3, (1, 2))
        ends = lax.ppermute(far[at], "patch", [(1, 0), (2, 3)])
        if at + 1 < len(parts):
            ends, far[at + 1], next_to[at + 1] = lax.optimization_barrier(
                (ends, far[at + 1], next_to[at + 1])
            )
        out.append(([x, next_to[at], far[at], middle], [ends]))
    return out


def add_sub_kernel(n_sub, where_ref, *refs):
    terms, kept_ref, outs = refs[:n_sub], refs[n_sub], refs[n_sub + 1 :]
    for head in range(len(outs) + 1):
        total = terms[0][head].astype(jnp.float32)
        for term in terms[1:]:
            total += term[head].astype(jnp.float32)
        if head == 0:
            kept_ref[...] = total
        else:
            outs[head - 1][...] = total.astype(jnp.bfloat16)


def add_head_kernel(n_more, where_ref, kept_ref, *refs):
    for at, out in enumerate(refs[n_more:]):
        total = kept_ref[at]
        for term in refs[:n_more]:
            total += term[at].astype(jnp.float32)
        out[...] = total.astype(jnp.bfloat16)


def reduce_sub(sizes, where, terms):
    n_sub, n_head = sizes["sub"], sizes["head"]
    terms = [terms[0]] + [swap(terms[rel], "sub", n_sub, rel) for rel in range(1, n_sub)]
    shape = terms[0].shape[1:]
    return call(
        functools.partial(add_sub_kernel, n_sub),
        "add_sub",
        [jax.ShapeDtypeStruct(shape, jnp.float32)]
        + [jax.ShapeDtypeStruct(shape, jnp.bfloat16)] * (n_head - 1),
        1,
        [spec(terms[0].shape)] * n_sub,
        [spec(shape)] * n_head,
    )(where, *terms)


def reduce_head(sizes, where, sums):
    n_head = sizes["head"]
    shape = sums[0].shape
    sums = [sums[0]] + [swap(sums[rel], "head", n_head, rel) for rel in range(1, n_head)]
    return call(
        functools.partial(add_head_kernel, n_head - 1),
        "add_head",
        [jax.ShapeDtypeStruct(shape[1:], jnp.bfloat16)] * shape[0],
        1,
        [spec(shape)] * n_head,
        [spec(shape[1:])] * shape[0],
    )(where, *sums)


def sum_tail(sizes, where, pieces, kv_pieces, out_weight, hidden_in, attn_gate):
    n_patch, n_head, n_sub = sizes["patch"], sizes["head"], sizes["sub"]
    split, tok = len(pieces), pieces[0].shape[1]
    count = n_head * n_sub
    piece = tok // count
    parts = 2 if piece % 32 == 0 else 1
    attended = []
    for part in range(parts):
        rows = (part * (piece // parts), piece // parts)
        x = attend(where, rows, count, pieces, kv_pieces)
        attended.append(x.reshape(-1, x.shape[2]))
    slots = gather(attended, n_patch)
    blocks = []
    for part in range(parts):
        terms = project(split, where, *slots[part], out_weight, n_head, n_sub)
        total = reduce_head(sizes, where, reduce_sub(sizes, where, terms))
        blocks.append(
            [total[0]] + [swap(total[rel], "patch", n_patch, rel) for rel in range(1, n_patch)]
        )
    return mix(where, hidden_in, attn_gate, blocks)


def attend_halves_kernel(where_ref, *refs):
    pieces, outs = refs[:-2], refs[-2:]
    split = len(pieces)
    rels = [0, *range(split - 1, 0, -1)]
    factor = HEAD_DIM**-0.5 * math.log2(math.e)
    rows, feat = outs[0].shape[1:]
    for head in range(feat // HEAD_DIM):
        lanes = pl.ds(head * HEAD_DIM, HEAD_DIM)
        keys = jnp.concatenate([ref[1, :, lanes] for ref in pieces], axis=0)
        values = jnp.concatenate([ref[2, :, lanes] for ref in pieces], axis=0)
        values = jnp.concatenate([values, jnp.ones_like(values)], axis=1)
        for half, out in enumerate(outs):
            start = pl.multiple_of((where_ref[HEAD] ^ half) * rows, rows)
            query = jnp.concatenate([ref[0, pl.ds(start, rows), lanes] for ref in pieces], axis=0)
            scores = lax.dot_general(
                query, keys, (((1,), (1,)), ((), ())), preferred_element_type=jnp.float32
            )
            peak = jnp.max(scores, axis=1, keepdims=True)
            expo = jnp.exp2((scores - peak) * factor).astype(jnp.bfloat16)
            mix = jnp.dot(expo, values, preferred_element_type=jnp.float32)
            mix = (mix[:, :HEAD_DIM] / mix[:, HEAD_DIM:]).astype(jnp.bfloat16)
            for at, rel in enumerate(rels):
                out[where_ref[NEAR] ^ rel, :, lanes] = mix[at * rows : (at + 1) * rows]


def attend_halves(where, pieces):
    split = len(pieces)
    _, tok, feat = pieces[0].shape
    out = jax.ShapeDtypeStruct((split, tok // 2, feat), jnp.bfloat16)
    outs = call(
        attend_halves_kernel,
        "attend",
        [out] * 2,
        1,
        [spec((3, tok, feat))] * split,
        [spec(out.shape)] * 2,
    )(where, *pieces)
    return [x.reshape(-1, feat) for x in outs]


def first_kernel(where_ref, *refs):
    slots, (more, own_ref, fetched_ref, passed_ref, out_ref, held_ref) = refs[:7], refs[7:]
    feat = slots[0].shape[1]

    @pl.when(pl.program_id(0) == 0)
    def arrange():
        for at, slot in enumerate(slots):
            block = slot[...]
            if at == 3:
                block = jnp.where(where_ref[INNER] == 1, block, more[...])
            place = where_ref[NEAR] ^ (at % 4)
            if at >= 4:
                place = 4 + (2 * ((place // 2) ^ where_ref[GRP]) + place % 2)
            held_ref[:, pl.ds(pl.multiple_of(place * feat, HEAD_DIM), feat)] = block
        place = where_ref[NEAR] ^ 3
        place = 4 + (2 * ((place // 2) ^ where_ref[GRP]) + place % 2)
        held_ref[:, pl.ds(pl.multiple_of(place * feat, HEAD_DIM), feat)] = jnp.zeros(
            (slots[0].shape[0], feat), jnp.bfloat16
        )

    depth = 4 * feat
    acc = jnp.dot(held_ref[:, :depth], own_ref[...], preferred_element_type=jnp.float32)
    half = depth // 2
    for at, weight in enumerate((fetched_ref, passed_ref)):
        acc += jnp.dot(
            held_ref[:, depth + at * half : depth + (at + 1) * half],
            weight[...],
            preferred_element_type=jnp.float32,
        )
    out_ref[...] = acc


def first_product(where, slots, more, weights):
    rows, feat = slots[0].shape
    cols = weights[0].shape[1]
    wide = cols // 2
    return call(
        first_kernel,
        "first",
        jax.ShapeDtypeStruct((rows, cols), jnp.float32),
        2,
        [spec((rows, feat))] * 8
        + [pl.BlockSpec((x.shape[0], wide), lambda i, w: (0, i)) for x in weights],
        pl.BlockSpec((rows, wide), lambda i, w: (0, i)),
        [pltpu.VMEM((rows, 8 * feat), jnp.bfloat16)],
    )(where, *slots, more, *weights)


def second_kernel(where_ref, slot, more, fetched_ref, passed_ref, acc_in, keep_ref, send_ref, acc_ref):
    feat = slot.shape[1]
    place = where_ref[NEAR] ^ 3
    rows = pl.ds(pl.multiple_of((place % 2) * feat, HEAD_DIM), feat)
    weight = jnp.where(
        (place // 2) == where_ref[GRP], fetched_ref[rows, :], passed_ref[rows, :]
    )
    block = jnp.where(where_ref[INNER] == 1, slot[...], more[...])
    acc = acc_in[...] + jnp.dot(block, weight, preferred_element_type=jnp.float32)
    acc_ref[...] = acc.reshape(acc_ref.shape)
    for sub, out in enumerate((keep_ref, send_ref)):
        for at in range(4):
            out[at] = acc_ref[where_ref[NEAR] ^ at, where_ref[SUB] ^ sub].astype(jnp.bfloat16)


def second_product(where, chunk, slot, more, weights, acc):
    rows, feat = slot.shape
    depth, cols = weights[0].shape
    wide = cols // 2
    out = jax.ShapeDtypeStruct((4, rows // 8, wide), jnp.bfloat16)
    return call(
        second_kernel,
        "second",
        [out] * 2,
        1,
        [spec((rows, feat))] * 2
        + [pl.BlockSpec((depth, wide), lambda i, w: (0, chunk))] * 2
        + [pl.BlockSpec((rows, wide), lambda i, w: (0, chunk))],
        [spec(out.shape)] * 2,
        [pltpu.VMEM((4, 2, rows // 8, wide), jnp.float32)],
    )(where, slot, more, *weights, acc)


def add_kernel(where_ref, keep_ref, term_ref, *outs):
    for at, out in enumerate(outs):
        total = keep_ref[at].astype(jnp.float32) + term_ref[at].astype(jnp.float32)
        out[...] = total.astype(jnp.bfloat16)


def add(where, keep, term):
    return call(
        add_kernel,
        "add",
        [jax.ShapeDtypeStruct(keep.shape[1:], jnp.bfloat16)] * keep.shape[0],
        1,
        [spec(keep.shape)] * 2,
        [spec(keep.shape[1:])] * keep.shape[0],
    )(where, keep, term)


def share_tail(sizes, where, pieces, kv_pieces, out_weight, hidden_in, attn_gate):
    half = out_weight.shape[0] // 2
    out_weight, where = lax.optimization_barrier((out_weight, where))
    start = lax.axis_index("grp") * half
    fetched = swap(lax.dynamic_slice_in_dim(out_weight, start, half, 0), "head", 2, 1)
    pieces, fetched = lax.optimization_barrier((pieces, fetched))
    passed = swap(fetched, "grp", 2, 1)

    mine, other = attend_halves(where, pieces)
    other = swap(other, "head", 2, 1)
    slots = []
    for at, x in enumerate((mine, other)):
        far, next_to = swap(x, "patch", 4, 2), swap(x, "patch", 4, 1)
        far, next_to, other, x = lax.optimization_barrier((far, next_to, other, x))
        if at == 1:
            far, x, passed = lax.optimization_barrier((far, x, passed))
        middle = swap(x, "patch", 4, 3, (1, 2))
        ends = lax.ppermute(far, "patch", [(1, 0), (2, 3)])
        slots.append([x, next_to, far, middle, ends])
    first = [*slots[0][:4], *slots[1][:3]]
    acc = first_product(where, first, slots[0][4], [out_weight, fetched, passed])
    terms = [second_product(where, at, *slots[1][3:], [fetched, passed], acc) for at in range(2)]
    blocks = []
    for keep, send in terms:
        total = add(where, keep, swap(send, "sub", 2, 1))
        blocks.append([total[0]] + [swap(total[rel], "patch", 4, rel) for rel in range(3, 0, -1)])
    return mix_columns(where, hidden_in, attn_gate, blocks)


def mix_columns_kernel(where_ref, hidden_ref, gate_ref, *refs):
    blocks, out_ref = refs[:-1], refs[-1]
    cols = blocks[0].shape[1]
    for chunk in range(2):
        for at, rel in enumerate((0, 3, 2, 1)):
            start = (2 * (where_ref[PATCH] ^ rel) + chunk) * cols
            lanes = pl.ds(pl.multiple_of(start, HEAD_DIM), cols)
            mixed = hidden_ref[:, lanes].astype(jnp.float32) + gate_ref[:, lanes] * blocks[
                4 * chunk + at
            ][...].astype(jnp.float32)
            out_ref[:, lanes] = mixed.astype(jnp.bfloat16)


def mix_columns(where, hidden_in, attn_gate, blocks):
    rows, width = hidden_in.shape
    flat = [x for chunk in blocks for x in chunk]
    return call(
        mix_columns_kernel,
        "mix",
        jax.ShapeDtypeStruct((rows, width), jnp.bfloat16),
        1,
        [spec((rows, width)), spec((1, width))] + [spec(flat[0].shape)] * len(flat),
        spec((rows, width)),
    )(where, hidden_in, attn_gate[None], *flat)


def body(sizes, queries, fresh_kv, cached_kv, exponents, out_weight, hidden_in, attn_gate):
    n_patch, n_head, n_sub = sizes["patch"], sizes["head"], sizes["sub"]
    tok, channels = queries.shape
    heads = channels // HEAD_DIM
    split = math.gcd(heads, n_patch)
    patch_at = lax.axis_index("patch")
    inner = (patch_at > 0) & (patch_at < n_patch - 1)
    where = jnp.stack(
        [
            patch_at,
            patch_at % split,
            lax.axis_index("head"),
            lax.axis_index("sub"),
            inner,
            lax.axis_index("grp"),
        ]
    ).astype(jnp.int32)

    arrays = (exponents, queries, fresh_kv, cached_kv)
    sent = pack(split, *arrays)
    far_first = [swap(sent[rel - 1], "patch", n_patch, rel) for rel in range(split - 1, 0, -1)]
    where, sent = lax.optimization_barrier((where, sent))
    pieces = [pack_own(split, where, *arrays), *far_first]
    kv_pieces = list(pieces)
    for rel in range(split, n_patch, split):
        kv_pieces += [swap(x, "patch", n_patch, rel) for x in pieces]

    tail = (sizes, where, pieces, kv_pieces, out_weight, hidden_in, attn_gate)
    if (sizes["grp"], n_head, split, n_patch) == (2, 2, 4, 4):
        return share_tail(*tail)
    return sum_tail(*tail)


def solution(mesh):
    in_specs = (
        P(("grp", "patch"), ("head", "sub")),
        P(None, ("grp", "patch"), ("head", "sub")),
        P(None, "grp", ("head", "sub")),
        P(None, ("grp", "patch"), ("head", "sub")),
        P(("head", "sub"), "patch"),
        P(("grp", "patch", "head", "sub"), None),
        P(),
    )
    out_specs = P(("grp", "patch", "head", "sub"), None)
    return jax.shard_map(
        functools.partial(body, dict(mesh.shape)),
        mesh=mesh,
        in_specs=in_specs,
        out_specs=out_specs,
        check_vma=False,
    )
```

```python
import functools
import math

import jax
import jax.numpy as jnp
from jax import lax
from jax.experimental import pallas as pl
from jax.experimental.pallas import tpu as pltpu
from jax.sharding import PartitionSpec as P

HEAD_DIM = 128
SCALE_ROWS = 128
SATURATION = 448.0
PACK_ROWS = 64
VMEM_BYTES = 32 * 1024 * 1024
PACK_VMEM_BYTES = 60 * 1024 * 1024
ATTEND_FLOPS = 1
PROJECT_FLOPS = 1

PATCH, NEAR, HEAD, SUB, INNER, GRP = range(6)


def spec(shape):
    return pl.BlockSpec(shape, lambda i, w: (0,) * len(shape))


def call(kernel, name, out_shape, grid, in_specs, out_specs, scratch=(), flops=1, vmem=VMEM_BYTES):
    return pl.pallas_call(
        kernel,
        out_shape=out_shape,
        grid_spec=pltpu.PrefetchScalarGridSpec(
            num_scalar_prefetch=1,
            grid=(grid,),
            in_specs=in_specs,
            out_specs=out_specs,
            scratch_shapes=list(scratch),
        ),
        compiler_params=pltpu.CompilerParams(vmem_limit_bytes=vmem),
        cost_estimate=pl.CostEstimate(flops=flops, bytes_accessed=0, transcendentals=0),
        name=name,
    )


def swap(x, axes, count, mask, only=None):
    pairs = [(at, at ^ mask) for at in range(count) if only is None or at in only]
    return lax.ppermute(x, axes, pairs)


def decode(fresh, cached, exponent):
    power = jnp.full((1, HEAD_DIM), exponent.astype(jnp.float32))
    cached = cached.astype(jnp.float32)
    residual = fresh.astype(jnp.float32) - cached
    codes = jnp.clip(residual * jnp.exp2(-power), -SATURATION, SATURATION).astype(jnp.bfloat16)
    return (cached + codes.astype(jnp.float32) * jnp.exp2(power)).astype(jnp.bfloat16)


def pack_kernel(split, per, exps_ref, q_ref, fresh_ref, cached_ref, *refs):
    outs, bufs = refs[: split - 1], refs[split - 1 : 2 * split - 2]
    q_buf, fresh_buf, cached_buf, sems, out_sems = refs[2 * split - 2 :]
    patch = lax.axis_index("patch")
    near = lax.rem(patch, split)
    tok = q_buf.shape[0]
    copies, sent = [], []
    for block in range(tok // PACK_ROWS):
        rows = pl.ds(block * PACK_ROWS, PACK_ROWS)
        there = pl.ds(pl.multiple_of(patch * tok + block * PACK_ROWS, PACK_ROWS), PACK_ROWS)
        copies.append(
            [
                pltpu.make_async_copy(q_ref.at[rows], q_buf.at[rows], sems.at[block, 0]),
                pltpu.make_async_copy(fresh_ref.at[:, rows], fresh_buf.at[:, rows], sems.at[block, 1]),
                pltpu.make_async_copy(cached_ref.at[:, there], cached_buf.at[:, rows], sems.at[block, 2]),
            ]
        )
        for copy in copies[-1]:
            copy.start()
    for block in range(tok // PACK_ROWS):
        rows = pl.ds(block * PACK_ROWS, PACK_ROWS)
        for copy in copies[block]:
            copy.wait()
        for rel in range(split - 1, 0, -1):
            buf = bufs[rel - 1]
            for chunk in range(per):
                head = (near ^ rel) * per + chunk
                lanes = pl.ds(pl.multiple_of(head * HEAD_DIM, HEAD_DIM), HEAD_DIM)
                here = pl.ds(chunk * HEAD_DIM, HEAD_DIM)
                buf[0, rows, here] = q_buf[rows, lanes]
                for stacked in range(2):
                    buf[1 + stacked, rows, here] = decode(
                        fresh_buf[stacked, rows, lanes],
                        cached_buf[stacked, rows, lanes],
                        exps_ref[stacked, block * PACK_ROWS // SCALE_ROWS, head],
                    )
            sent.append(
                pltpu.make_async_copy(
                    buf.at[:, rows], outs[rel - 1].at[:, rows], out_sems.at[block, rel - 1]
                )
            )
            sent[-1].start()
    for copy in sent:
        copy.wait()


def pack(split, exponents, queries, fresh_kv, cached_kv):
    tok, channels = queries.shape
    feat = channels // split
    blocks = tok // PACK_ROWS
    hbm = pl.BlockSpec(memory_space=pltpu.HBM)
    return pl.pallas_call(
        functools.partial(pack_kernel, split, feat // HEAD_DIM),
        out_shape=[jax.ShapeDtypeStruct((3, tok, feat), jnp.bfloat16)] * (split - 1),
        in_specs=[pl.BlockSpec(memory_space=pltpu.SMEM), hbm, hbm, hbm],
        out_specs=[hbm] * (split - 1),
        scratch_shapes=[pltpu.VMEM((3, tok, feat), jnp.bfloat16)] * (split - 1)
        + [
            pltpu.VMEM((tok, channels), jnp.bfloat16),
            pltpu.VMEM((2, tok, channels), jnp.bfloat16),
            pltpu.VMEM((2, tok, channels), jnp.bfloat16),
            pltpu.SemaphoreType.DMA((blocks, 3)),
            pltpu.SemaphoreType.DMA((blocks, split - 1)),
        ],
        compiler_params=pltpu.CompilerParams(vmem_limit_bytes=PACK_VMEM_BYTES),
        name="pack",
    )(exponents, queries, fresh_kv, cached_kv)


def own_kernel(per, where_ref, exps_ref, q_ref, fresh_ref, cached_ref, out_ref):
    out_ref[0] = q_ref[...]
    for chunk in range(per):
        lanes = pl.ds(chunk * HEAD_DIM, HEAD_DIM)
        for block in range(q_ref.shape[0] // SCALE_ROWS):
            rows = pl.ds(block * SCALE_ROWS, SCALE_ROWS)
            for stacked in range(2):
                out_ref[1 + stacked, rows, lanes] = decode(
                    fresh_ref[stacked, rows, lanes],
                    cached_ref[stacked, rows, lanes],
                    exps_ref[stacked, block, where_ref[NEAR] * per + chunk],
                )


def pack_own(split, where, exponents, queries, fresh_kv, cached_kv):
    tok, channels = queries.shape
    feat = channels // split
    out = jax.ShapeDtypeStruct((3, tok, feat), jnp.bfloat16)
    return call(
        functools.partial(own_kernel, feat // HEAD_DIM),
        "own",
        out,
        1,
        [
            pl.BlockSpec(memory_space=pltpu.SMEM),
            pl.BlockSpec((tok, feat), lambda i, w: (0, w[NEAR])),
            pl.BlockSpec((2, tok, feat), lambda i, w: (0, 0, w[NEAR])),
            pl.BlockSpec((2, tok, feat), lambda i, w: (0, w[PATCH], w[NEAR])),
        ],
        spec(out.shape),
    )(where, exponents, queries, fresh_kv, cached_kv)


def attend_kernel(split, part, where_ref, *refs):
    q_refs, kv_refs, out_ref = (refs[0], *refs[split - 1 : 0 : -1]), refs[:-1], refs[-1]
    factor = HEAD_DIM**-0.5 * math.log2(math.e)
    tok, feat = q_refs[0].shape[1:]
    count = out_ref.shape[1] // part[1]
    starts = [at * (tok // count) + part[0] for at in range(count)]
    for head in range(feat // HEAD_DIM):
        lanes = pl.ds(head * HEAD_DIM, HEAD_DIM)
        keys = jnp.concatenate([ref[1, :, lanes] for ref in kv_refs], axis=0)
        values = jnp.concatenate([ref[2, :, lanes] for ref in kv_refs], axis=0)
        values = jnp.concatenate([values, jnp.ones_like(values)], axis=1)
        for rel in range(split):
            rows = [q_refs[rel][0, start : start + part[1], lanes] for start in starts]
            query = jnp.concatenate(rows, axis=0) if len(rows) > 1 else rows[0]
            scores = lax.dot_general(
                query, keys, (((1,), (1,)), ((), ())), preferred_element_type=jnp.float32
            )
            peak = jnp.max(scores, axis=1, keepdims=True)
            expo = jnp.exp2((scores - peak) * factor).astype(jnp.bfloat16)
            mix = jnp.dot(expo, values, preferred_element_type=jnp.float32)
            mix = mix[:, :HEAD_DIM] / mix[:, HEAD_DIM:]
            out_ref[where_ref[NEAR] ^ rel, :, lanes] = mix.astype(jnp.bfloat16)


def attend(where, part, count, pieces, kv_pieces):
    split = len(pieces)
    _, tok, feat = pieces[0].shape
    out = jax.ShapeDtypeStruct((split, count * part[1], feat), jnp.bfloat16)
    return call(
        functools.partial(attend_kernel, split, part),
        "attend",
        out,
        1,
        [spec((3, tok, feat))] * len(kv_pieces),
        spec(out.shape),
        flops=ATTEND_FLOPS,
    )(where, *kv_pieces)


def project_kernel(split, n_slots, n_more, where_ref, *refs):
    slots, refs = refs[:n_slots], refs[n_slots:]
    more, weight_ref, refs = refs[:n_more], refs[n_more], refs[n_more + 1 :]
    outs, held_ref, acc_ref = refs[:-2], refs[-2], refs[-1]
    rows, feat = slots[0].shape
    n_sub, n_head = acc_ref.shape[3], acc_ref.shape[2]

    @pl.when(pl.program_id(0) == 0)
    def arrange():
        for at, slot in enumerate(slots):
            group, near = divmod(at, split)
            lane = (where_ref[NEAR] ^ near) * feat
            block = slot[...]
            if more and at == n_slots - 1:
                block = jnp.where(where_ref[INNER] == 1, block, more[0][...])
            held_ref[
                group * rows : (group + 1) * rows, pl.ds(pl.multiple_of(lane, HEAD_DIM), feat)
            ] = block

    acc = jnp.dot(held_ref[...], weight_ref[...], preferred_element_type=jnp.float32)
    acc_ref[...] = acc.reshape(acc_ref.shape)
    for sub in range(n_sub):
        for head in range(n_head):
            for at in range(n_slots):
                group, near = divmod(at, split)
                outs[sub][head, at] = acc_ref[
                    group, where_ref[NEAR] ^ near, where_ref[HEAD] ^ head, where_ref[SUB] ^ sub
                ].astype(jnp.bfloat16)


def project(split, where, slots, more, weight, n_head, n_sub):
    rows, feat = slots[0].shape
    n_patch = len(slots)
    total = rows * n_patch // split
    depth, cols = weight.shape
    wide = 640 if cols % 640 == 0 else cols
    piece = rows // (split * n_head * n_sub)
    return call(
        functools.partial(project_kernel, split, n_patch, len(more)),
        "project",
        [jax.ShapeDtypeStruct((n_head, n_patch, piece, cols), jnp.bfloat16)] * n_sub,
        cols // wide,
        [spec((rows, feat))] * (n_patch + len(more))
        + [pl.BlockSpec((depth, wide), lambda i, w: (0, i))],
        [pl.BlockSpec((n_head, n_patch, piece, wide), lambda i, w: (0, 0, 0, i))] * n_sub,
        [
            pltpu.VMEM((total, depth), jnp.bfloat16),
            pltpu.VMEM((n_patch // split, split, n_head, n_sub, piece, wide), jnp.float32),
        ],
        flops=PROJECT_FLOPS,
    )(where, *slots, *more, weight)


def mix_kernel(rels, where_ref, hidden_ref, gate_ref, *refs):
    blocks, out_ref = refs[:-1], refs[-1]
    piece, cols = blocks[0].shape
    for part in range(len(blocks) // len(rels)):
        rows = pl.ds(part * piece, piece)
        for at, rel in enumerate(rels):
            lanes = pl.ds(pl.multiple_of((where_ref[PATCH] ^ rel) * cols, HEAD_DIM), cols)
            mixed = hidden_ref[rows, lanes].astype(jnp.float32) + gate_ref[:, lanes] * blocks[
                part * len(rels) + at
            ][...].astype(jnp.float32)
            out_ref[rows, lanes] = mixed.astype(jnp.bfloat16)


def mix(where, hidden_in, attn_gate, blocks):
    rows, width = hidden_in.shape
    n_patch = len(blocks[0])
    piece, cols = blocks[0][0].shape
    if cols % HEAD_DIM:
        order = jnp.concatenate([jnp.stack(x) for x in blocks], axis=1)
        order = order[where[PATCH] ^ jnp.arange(n_patch)]
        projected = order.transpose(1, 0, 2).reshape(rows, width).astype(jnp.float32)
        return (hidden_in.astype(jnp.float32) + attn_gate * projected).astype(jnp.bfloat16)
    rels = [0, *range(n_patch - 1, 0, -1)]
    flat = [part[rel] for part in blocks for rel in rels]
    return call(
        functools.partial(mix_kernel, rels),
        "mix",
        jax.ShapeDtypeStruct((rows, width), jnp.bfloat16),
        1,
        [spec((rows, width)), spec((1, width))] + [spec((piece, cols))] * len(flat),
        spec((rows, width)),
    )(where, hidden_in, attn_gate[None], *flat)


def gather(parts, n_patch):
    if n_patch != 4:
        return [
            ([x] + [swap(x, "patch", n_patch, rel) for rel in range(1, n_patch)], [])
            for x in parts
        ]
    far = [swap(x, "patch", 4, 2) for x in parts]
    next_to = [swap(x, "patch", 4, 1) for x in parts]
    out = []
    for at, x in enumerate(parts):
        far[at], next_to[at], parts = lax.optimization_barrier((far[at], next_to[at], parts))
        middle = swap(parts[at], "patch", 4, 3, (1, 2))
        ends = lax.ppermute(far[at], "patch", [(1, 0), (2, 3)])
        if at + 1 < len(parts):
            ends, far[at + 1], next_to[at + 1] = lax.optimization_barrier(
                (ends, far[at + 1], next_to[at + 1])
            )
        out.append(([x, next_to[at], far[at], middle], [ends]))
    return out


def add_sub_kernel(n_sub, where_ref, *refs):
    terms, kept_ref, outs = refs[:n_sub], refs[n_sub], refs[n_sub + 1 :]
    for head in range(len(outs) + 1):
        total = terms[0][head].astype(jnp.float32)
        for term in terms[1:]:
            total += term[head].astype(jnp.float32)
        if head == 0:
            kept_ref[...] = total
        else:
            outs[head - 1][...] = total.astype(jnp.bfloat16)


def add_head_kernel(n_more, where_ref, kept_ref, *refs):
    for at, out in enumerate(refs[n_more:]):
        total = kept_ref[at]
        for term in refs[:n_more]:
            total += term[at].astype(jnp.float32)
        out[...] = total.astype(jnp.bfloat16)


def reduce_sub(sizes, where, terms):
    n_sub, n_head = sizes["sub"], sizes["head"]
    terms = [terms[0]] + [swap(terms[rel], "sub", n_sub, rel) for rel in range(1, n_sub)]
    shape = terms[0].shape[1:]
    return call(
        functools.partial(add_sub_kernel, n_sub),
        "add_sub",
        [jax.ShapeDtypeStruct(shape, jnp.float32)]
        + [jax.ShapeDtypeStruct(shape, jnp.bfloat16)] * (n_head - 1),
        1,
        [spec(terms[0].shape)] * n_sub,
        [spec(shape)] * n_head,
    )(where, *terms)


def reduce_head(sizes, where, sums):
    n_head = sizes["head"]
    shape = sums[0].shape
    sums = [sums[0]] + [swap(sums[rel], "head", n_head, rel) for rel in range(1, n_head)]
    return call(
        functools.partial(add_head_kernel, n_head - 1),
        "add_head",
        [jax.ShapeDtypeStruct(shape[1:], jnp.bfloat16)] * shape[0],
        1,
        [spec(shape)] * n_head,
        [spec(shape[1:])] * shape[0],
    )(where, *sums)


def sum_tail(sizes, where, pieces, kv_pieces, out_weight, hidden_in, attn_gate):
    n_patch, n_head, n_sub = sizes["patch"], sizes["head"], sizes["sub"]
    split, tok = len(pieces), pieces[0].shape[1]
    count = n_head * n_sub
    piece = tok // count
    parts = 2 if piece % 32 == 0 else 1
    attended = []
    for part in range(parts):
        rows = (part * (piece // parts), piece // parts)
        x = attend(where, rows, count, pieces, kv_pieces)
        attended.append(x.reshape(-1, x.shape[2]))
    slots = gather(attended, n_patch)
    blocks = []
    for part in range(parts):
        terms = project(split, where, *slots[part], out_weight, n_head, n_sub)
        total = reduce_head(sizes, where, reduce_sub(sizes, where, terms))
        blocks.append(
            [total[0]] + [swap(total[rel], "patch", n_patch, rel) for rel in range(1, n_patch)]
        )
    return mix(where, hidden_in, attn_gate, blocks)


def attend_halves_kernel(where_ref, *refs):
    pieces, outs = refs[:-2], refs[-2:]
    split = len(pieces)
    rels = [0, *range(split - 1, 0, -1)]
    factor = HEAD_DIM**-0.5 * math.log2(math.e)
    rows, feat = outs[0].shape[1:]
    for head in range(feat // HEAD_DIM):
        lanes = pl.ds(head * HEAD_DIM, HEAD_DIM)
        keys = jnp.concatenate([ref[1, :, lanes] for ref in pieces], axis=0)
        values = jnp.concatenate([ref[2, :, lanes] for ref in pieces], axis=0)
        values = jnp.concatenate([values, jnp.ones_like(values)], axis=1)
        for half, out in enumerate(outs):
            start = pl.multiple_of((where_ref[HEAD] ^ half) * rows, rows)
            query = jnp.concatenate([ref[0, pl.ds(start, rows), lanes] for ref in pieces], axis=0)
            scores = lax.dot_general(
                query, keys, (((1,), (1,)), ((), ())), preferred_element_type=jnp.float32
            )
            peak = jnp.max(scores, axis=1, keepdims=True)
            expo = jnp.exp2((scores - peak) * factor).astype(jnp.bfloat16)
            mix = jnp.dot(expo, values, preferred_element_type=jnp.float32)
            mix = (mix[:, :HEAD_DIM] / mix[:, HEAD_DIM:]).astype(jnp.bfloat16)
            for at, rel in enumerate(rels):
                out[where_ref[NEAR] ^ rel, :, lanes] = mix[at * rows : (at + 1) * rows]


def attend_halves(where, pieces):
    split = len(pieces)
    _, tok, feat = pieces[0].shape
    out = jax.ShapeDtypeStruct((split, tok // 2, feat), jnp.bfloat16)
    outs = call(
        attend_halves_kernel,
        "attend",
        [out] * 2,
        1,
        [spec((3, tok, feat))] * split,
        [spec(out.shape)] * 2,
    )(where, *pieces)
    return [x.reshape(-1, feat) for x in outs]


def first_kernel(where_ref, *refs):
    slots, (more, own_ref, partner_ref, out_ref, held_ref) = refs[:7], refs[7:]
    rows, feat = slots[0].shape
    depth = own_ref.shape[0]

    @pl.when(pl.program_id(0) == 0)
    def arrange():
        for index in range(8):
            half, at = divmod(index, 4)
            if index == 7:
                block = jnp.zeros((rows, feat), jnp.bfloat16)
            else:
                block = slots[index][...]
            if index == 3:
                block = jnp.where(where_ref[INNER] == 1, block, more[...])
            lane = half * depth + (where_ref[NEAR] ^ at) * feat
            held_ref[:, pl.ds(pl.multiple_of(lane, HEAD_DIM), feat)] = block

    acc = jnp.dot(held_ref[:, :depth], own_ref[...], preferred_element_type=jnp.float32)
    acc += jnp.dot(held_ref[:, depth:], partner_ref[...], preferred_element_type=jnp.float32)
    out_ref[...] = acc


def first_product(where, slots, more, weights):
    rows, feat = slots[0].shape
    depth, cols = weights[0].shape
    wide = cols // 2
    return call(
        first_kernel,
        "first",
        jax.ShapeDtypeStruct((rows, cols), jnp.float32),
        2,
        [spec((rows, feat))] * 8 + [pl.BlockSpec((depth, wide), lambda i, w: (0, i))] * 2,
        pl.BlockSpec((rows, wide), lambda i, w: (0, i)),
        [pltpu.VMEM((rows, 2 * depth), jnp.bfloat16)],
    )(where, *slots, more, *weights)


def second_kernel(where_ref, slot, more, weight_ref, acc_in, keep_ref, send_ref, acc_ref):
    block = jnp.where(where_ref[INNER] == 1, slot[...], more[...])
    acc = acc_in[...] + jnp.dot(block, weight_ref[...], preferred_element_type=jnp.float32)
    acc_ref[...] = acc.reshape(acc_ref.shape)
    for sub, out in enumerate((keep_ref, send_ref)):
        for at in range(4):
            out[at] = acc_ref[where_ref[NEAR] ^ at, where_ref[SUB] ^ sub].astype(jnp.bfloat16)


def second_product(where, chunk, slot, more, weight, acc):
    rows, feat = slot.shape
    wide = weight.shape[1] // 2
    out = jax.ShapeDtypeStruct((4, rows // 8, wide), jnp.bfloat16)
    return call(
        second_kernel,
        "second",
        [out] * 2,
        1,
        [spec((rows, feat))] * 2
        + [pl.BlockSpec((feat, wide), lambda i, w: (w[NEAR] ^ 3, chunk))]
        + [pl.BlockSpec((rows, wide), lambda i, w: (0, chunk))],
        [spec(out.shape)] * 2,
        [pltpu.VMEM((4, 2, rows // 8, wide), jnp.float32)],
    )(where, slot, more, weight, acc)


def add_kernel(where_ref, keep_ref, term_ref, *outs):
    for at, out in enumerate(outs):
        total = keep_ref[at].astype(jnp.float32) + term_ref[at].astype(jnp.float32)
        out[...] = total.astype(jnp.bfloat16)


def add(where, keep, term):
    return call(
        add_kernel,
        "add",
        [jax.ShapeDtypeStruct(keep.shape[1:], jnp.bfloat16)] * keep.shape[0],
        1,
        [spec(keep.shape)] * 2,
        [spec(keep.shape[1:])] * keep.shape[0],
    )(where, keep, term)


def share_tail(sizes, where, pieces, kv_pieces, out_weight, hidden_in, attn_gate):
    fetched = swap(out_weight, "head", 2, 1)

    mine, other = attend_halves(where, pieces)
    other = swap(other, "head", 2, 1)
    slots = []
    for at, x in enumerate((mine, other)):
        far, next_to = swap(x, "patch", 4, 2), swap(x, "patch", 4, 1)
        far, next_to, other, x = lax.optimization_barrier((far, next_to, other, x))
        if at == 1:
            far, x, fetched = lax.optimization_barrier((far, x, fetched))
        middle = swap(x, "patch", 4, 3, (1, 2))
        ends = lax.ppermute(far, "patch", [(1, 0), (2, 3)])
        slots.append([x, next_to, far, middle, ends])
    first = [*slots[0][:4], *slots[1][:3]]
    acc = first_product(where, first, slots[0][4], [out_weight, fetched])
    terms = [second_product(where, at, *slots[1][3:], fetched, acc) for at in range(2)]
    blocks = []
    for keep, send in terms:
        total = add(where, keep, swap(send, "sub", 2, 1))
        blocks.append([total[0]] + [swap(total[rel], "patch", 4, rel) for rel in range(3, 0, -1)])
    return mix_columns(where, hidden_in, attn_gate, blocks)


def mix_columns_kernel(where_ref, hidden_ref, gate_ref, *refs):
    blocks, out_ref = refs[:-1], refs[-1]
    cols = blocks[0].shape[1]
    for chunk in range(2):
        for at, rel in enumerate((0, 3, 2, 1)):
            start = (2 * (where_ref[PATCH] ^ rel) + chunk) * cols
            lanes = pl.ds(pl.multiple_of(start, HEAD_DIM), cols)
            mixed = hidden_ref[:, lanes].astype(jnp.float32) + gate_ref[:, lanes] * blocks[
                4 * chunk + at
            ][...].astype(jnp.float32)
            out_ref[:, lanes] = mixed.astype(jnp.bfloat16)


def mix_columns(where, hidden_in, attn_gate, blocks):
    rows, width = hidden_in.shape
    flat = [x for chunk in blocks for x in chunk]
    return call(
        mix_columns_kernel,
        "mix",
        jax.ShapeDtypeStruct((rows, width), jnp.bfloat16),
        1,
        [spec((rows, width)), spec((1, width))] + [spec(flat[0].shape)] * len(flat),
        spec((rows, width)),
    )(where, hidden_in, attn_gate[None], *flat)


def body(sizes, queries, fresh_kv, cached_kv, exponents, out_weight, hidden_in, attn_gate):
    n_patch, n_head, n_sub = sizes["patch"], sizes["head"], sizes["sub"]
    tok, channels = queries.shape
    heads = channels // HEAD_DIM
    split = math.gcd(heads, n_patch)
    patch_at = lax.axis_index("patch")
    inner = (patch_at > 0) & (patch_at < n_patch - 1)
    where = jnp.stack(
        [
            patch_at,
            patch_at % split,
            lax.axis_index("head"),
            lax.axis_index("sub"),
            inner,
            lax.axis_index("grp"),
        ]
    ).astype(jnp.int32)

    arrays = (exponents, queries, fresh_kv, cached_kv)
    sent = pack(split, *arrays)
    far_first = [swap(sent[rel - 1], "patch", n_patch, rel) for rel in range(split - 1, 0, -1)]
    where, sent = lax.optimization_barrier((where, sent))
    pieces = [pack_own(split, where, *arrays), *far_first]
    kv_pieces = list(pieces)
    for rel in range(split, n_patch, split):
        kv_pieces += [swap(x, "patch", n_patch, rel) for x in pieces]

    tail = (sizes, where, pieces, kv_pieces, out_weight, hidden_in, attn_gate)
    if (sizes["grp"], n_head, split, n_patch) == (2, 2, 4, 4):
        return share_tail(*tail)
    return sum_tail(*tail)


def solution(mesh):
    in_specs = (
        P(("grp", "patch"), ("head", "sub")),
        P(None, ("grp", "patch"), ("head", "sub")),
        P(None, "grp", ("head", "sub")),
        P(None, ("grp", "patch"), ("head", "sub")),
        P(("head", "sub"), "patch"),
        P(("grp", "patch", "head", "sub"), None),
        P(),
    )
    out_specs = P(("grp", "patch", "head", "sub"), None)
    return jax.shard_map(
        functools.partial(body, dict(mesh.shape)),
        mesh=mesh,
        in_specs=in_specs,
        out_specs=out_specs,
        check_vma=False,
    )
```

```python
import functools
import math

import jax
import jax.numpy as jnp
from jax import lax
from jax.experimental import pallas as pl
from jax.experimental.pallas import tpu as pltpu
from jax.sharding import PartitionSpec as P

HEAD_DIM = 128
SCALE_ROWS = 128
SATURATION = 448.0
PACK_ROWS = 64
VMEM_BYTES = 32 * 1024 * 1024
PACK_VMEM_BYTES = 60 * 1024 * 1024
ATTEND_FLOPS = 1
PROJECT_FLOPS = 1

PATCH, NEAR, HEAD, SUB, INNER, GRP = range(6)


def spec(shape):
    return pl.BlockSpec(shape, lambda i, w: (0,) * len(shape))


def call(kernel, name, out_shape, grid, in_specs, out_specs, scratch=(), flops=1, vmem=VMEM_BYTES):
    return pl.pallas_call(
        kernel,
        out_shape=out_shape,
        grid_spec=pltpu.PrefetchScalarGridSpec(
            num_scalar_prefetch=1,
            grid=(grid,),
            in_specs=in_specs,
            out_specs=out_specs,
            scratch_shapes=list(scratch),
        ),
        compiler_params=pltpu.CompilerParams(vmem_limit_bytes=vmem),
        cost_estimate=pl.CostEstimate(flops=flops, bytes_accessed=0, transcendentals=0),
        name=name,
    )


def swap(x, axes, count, mask, only=None):
    pairs = [(at, at ^ mask) for at in range(count) if only is None or at in only]
    return lax.ppermute(x, axes, pairs)


def decode(fresh, cached, exponent):
    power = jnp.full((1, HEAD_DIM), exponent.astype(jnp.float32))
    cached = cached.astype(jnp.float32)
    residual = fresh.astype(jnp.float32) - cached
    codes = jnp.clip(residual * jnp.exp2(-power), -SATURATION, SATURATION).astype(jnp.bfloat16)
    return (cached + codes.astype(jnp.float32) * jnp.exp2(power)).astype(jnp.bfloat16)


def piece_place(split, per, rel, chunk):
    if rel < split - 1 or rel == 0:
        return rel, chunk
    return rel + chunk, 0


def pack_kernel(split, per, exps_ref, q_ref, fresh_ref, cached_ref, *refs):
    count = split - 2 + per
    outs, bufs = refs[:count], refs[count : 2 * count]
    q_buf, fresh_buf, cached_buf, sems, out_sems = refs[2 * count :]
    patch = lax.axis_index("patch")
    near = lax.rem(patch, split)
    tok = q_buf.shape[0]
    copies, sent = [], []
    for block in range(tok // PACK_ROWS):
        rows = pl.ds(block * PACK_ROWS, PACK_ROWS)
        there = pl.ds(pl.multiple_of(patch * tok + block * PACK_ROWS, PACK_ROWS), PACK_ROWS)
        copies.append(
            [
                pltpu.make_async_copy(q_ref.at[rows], q_buf.at[rows], sems.at[block, 0]),
                pltpu.make_async_copy(fresh_ref.at[:, rows], fresh_buf.at[:, rows], sems.at[block, 1]),
                pltpu.make_async_copy(cached_ref.at[:, there], cached_buf.at[:, rows], sems.at[block, 2]),
            ]
        )
        for copy in copies[-1]:
            copy.start()
    for block in range(tok // PACK_ROWS):
        rows = pl.ds(block * PACK_ROWS, PACK_ROWS)
        for copy in copies[block]:
            copy.wait()
        for rel in range(split - 1, 0, -1):
            for chunk in range(per):
                head = (near ^ rel) * per + chunk
                lanes = pl.ds(pl.multiple_of(head * HEAD_DIM, HEAD_DIM), HEAD_DIM)
                number, place = piece_place(split, per, rel, chunk)
                buf, here = bufs[number - 1], pl.ds(place * HEAD_DIM, HEAD_DIM)
                buf[0, rows, here] = q_buf[rows, lanes]
                for stacked in range(2):
                    buf[1 + stacked, rows, here] = decode(
                        fresh_buf[stacked, rows, lanes],
                        cached_buf[stacked, rows, lanes],
                        exps_ref[stacked, block * PACK_ROWS // SCALE_ROWS, head],
                    )
        for at, (buf, out) in enumerate(zip(bufs, outs)):
            sent.append(
                pltpu.make_async_copy(buf.at[:, rows], out.at[:, rows], out_sems.at[block, at])
            )
            sent[-1].start()
    for copy in sent:
        copy.wait()


def pack(split, exponents, queries, fresh_kv, cached_kv):
    tok, channels = queries.shape
    per = channels // split // HEAD_DIM
    wide = [per] * (split - 2) + [1] * per
    shapes = [(3, tok, x * HEAD_DIM) for x in wide]
    blocks = tok // PACK_ROWS
    hbm = pl.BlockSpec(memory_space=pltpu.HBM)
    return pl.pallas_call(
        functools.partial(pack_kernel, split, per),
        out_shape=[jax.ShapeDtypeStruct(shape, jnp.bfloat16) for shape in shapes],
        in_specs=[pl.BlockSpec(memory_space=pltpu.SMEM), hbm, hbm, hbm],
        out_specs=[hbm] * len(shapes),
        scratch_shapes=[pltpu.VMEM(shape, jnp.bfloat16) for shape in shapes]
        + [
            pltpu.VMEM((tok, channels), jnp.bfloat16),
            pltpu.VMEM((2, tok, channels), jnp.bfloat16),
            pltpu.VMEM((2, tok, channels), jnp.bfloat16),
            pltpu.SemaphoreType.DMA((blocks, 3)),
            pltpu.SemaphoreType.DMA((blocks, len(shapes))),
        ],
        compiler_params=pltpu.CompilerParams(vmem_limit_bytes=PACK_VMEM_BYTES),
        name="pack",
    )(exponents, queries, fresh_kv, cached_kv)


def own_kernel(per, where_ref, exps_ref, q_ref, fresh_ref, cached_ref, out_ref):
    out_ref[0] = q_ref[...]
    for chunk in range(per):
        lanes = pl.ds(chunk * HEAD_DIM, HEAD_DIM)
        for block in range(q_ref.shape[0] // SCALE_ROWS):
            rows = pl.ds(block * SCALE_ROWS, SCALE_ROWS)
            for stacked in range(2):
                out_ref[1 + stacked, rows, lanes] = decode(
                    fresh_ref[stacked, rows, lanes],
                    cached_ref[stacked, rows, lanes],
                    exps_ref[stacked, block, where_ref[NEAR] * per + chunk],
                )


def pack_own(split, where, exponents, queries, fresh_kv, cached_kv):
    tok, channels = queries.shape
    feat = channels // split
    out = jax.ShapeDtypeStruct((3, tok, feat), jnp.bfloat16)
    return call(
        functools.partial(own_kernel, feat // HEAD_DIM),
        "own",
        out,
        1,
        [
            pl.BlockSpec(memory_space=pltpu.SMEM),
            pl.BlockSpec((tok, feat), lambda i, w: (0, w[NEAR])),
            pl.BlockSpec((2, tok, feat), lambda i, w: (0, 0, w[NEAR])),
            pl.BlockSpec((2, tok, feat), lambda i, w: (0, w[PATCH], w[NEAR])),
        ],
        spec(out.shape),
    )(where, exponents, queries, fresh_kv, cached_kv)


def attend_kernel(split, part, where_ref, *refs):
    q_refs, kv_refs, out_ref = (refs[0], *refs[split - 1 : 0 : -1]), refs[:-1], refs[-1]
    factor = HEAD_DIM**-0.5 * math.log2(math.e)
    tok, feat = q_refs[0].shape[1:]
    count = out_ref.shape[1] // part[1]
    starts = [at * (tok // count) + part[0] for at in range(count)]
    for head in range(feat // HEAD_DIM):
        lanes = pl.ds(head * HEAD_DIM, HEAD_DIM)
        keys = jnp.concatenate([ref[1, :, lanes] for ref in kv_refs], axis=0)
        values = jnp.concatenate([ref[2, :, lanes] for ref in kv_refs], axis=0)
        values = jnp.concatenate([values, jnp.ones_like(values)], axis=1)
        for rel in range(split):
            rows = [q_refs[rel][0, start : start + part[1], lanes] for start in starts]
            query = jnp.concatenate(rows, axis=0) if len(rows) > 1 else rows[0]
            scores = lax.dot_general(
                query, keys, (((1,), (1,)), ((), ())), preferred_element_type=jnp.float32
            )
            peak = jnp.max(scores, axis=1, keepdims=True)
            expo = jnp.exp2((scores - peak) * factor).astype(jnp.bfloat16)
            mix = jnp.dot(expo, values, preferred_element_type=jnp.float32)
            mix = mix[:, :HEAD_DIM] / mix[:, HEAD_DIM:]
            out_ref[where_ref[NEAR] ^ rel, :, lanes] = mix.astype(jnp.bfloat16)


def attend(where, part, count, pieces, kv_pieces):
    split = len(pieces)
    _, tok, feat = pieces[0].shape
    out = jax.ShapeDtypeStruct((split, count * part[1], feat), jnp.bfloat16)
    return call(
        functools.partial(attend_kernel, split, part),
        "attend",
        out,
        1,
        [spec((3, tok, feat))] * len(kv_pieces),
        spec(out.shape),
        flops=ATTEND_FLOPS,
    )(where, *kv_pieces)


def project_kernel(split, n_slots, n_more, where_ref, *refs):
    slots, refs = refs[:n_slots], refs[n_slots:]
    more, weight_ref, refs = refs[:n_more], refs[n_more], refs[n_more + 1 :]
    outs, held_ref, acc_ref = refs[:-2], refs[-2], refs[-1]
    rows, feat = slots[0].shape
    n_sub, n_head = acc_ref.shape[3], acc_ref.shape[2]

    @pl.when(pl.program_id(0) == 0)
    def arrange():
        for at, slot in enumerate(slots):
            group, near = divmod(at, split)
            lane = (where_ref[NEAR] ^ near) * feat
            block = slot[...]
            if more and at == n_slots - 1:
                block = jnp.where(where_ref[INNER] == 1, block, more[0][...])
            held_ref[
                group * rows : (group + 1) * rows, pl.ds(pl.multiple_of(lane, HEAD_DIM), feat)
            ] = block

    acc = jnp.dot(held_ref[...], weight_ref[...], preferred_element_type=jnp.float32)
    acc_ref[...] = acc.reshape(acc_ref.shape)
    for sub in range(n_sub):
        for head in range(n_head):
            for at in range(n_slots):
                group, near = divmod(at, split)
                outs[sub][head, at] = acc_ref[
                    group, where_ref[NEAR] ^ near, where_ref[HEAD] ^ head, where_ref[SUB] ^ sub
                ].astype(jnp.bfloat16)


def project(split, where, slots, more, weight, n_head, n_sub):
    rows, feat = slots[0].shape
    n_patch = len(slots)
    total = rows * n_patch // split
    depth, cols = weight.shape
    wide = 640 if cols % 640 == 0 else cols
    piece = rows // (split * n_head * n_sub)
    return call(
        functools.partial(project_kernel, split, n_patch, len(more)),
        "project",
        [jax.ShapeDtypeStruct((n_head, n_patch, piece, cols), jnp.bfloat16)] * n_sub,
        cols // wide,
        [spec((rows, feat))] * (n_patch + len(more))
        + [pl.BlockSpec((depth, wide), lambda i, w: (0, i))],
        [pl.BlockSpec((n_head, n_patch, piece, wide), lambda i, w: (0, 0, 0, i))] * n_sub,
        [
            pltpu.VMEM((total, depth), jnp.bfloat16),
            pltpu.VMEM((n_patch // split, split, n_head, n_sub, piece, wide), jnp.float32),
        ],
        flops=PROJECT_FLOPS,
    )(where, *slots, *more, weight)


def mix_kernel(rels, where_ref, hidden_ref, gate_ref, *refs):
    blocks, out_ref = refs[:-1], refs[-1]
    piece, cols = blocks[0].shape
    for part in range(len(blocks) // len(rels)):
        rows = pl.ds(part * piece, piece)
        for at, rel in enumerate(rels):
            lanes = pl.ds(pl.multiple_of((where_ref[PATCH] ^ rel) * cols, HEAD_DIM), cols)
            mixed = hidden_ref[rows, lanes].astype(jnp.float32) + gate_ref[:, lanes] * blocks[
                part * len(rels) + at
            ][...].astype(jnp.float32)
            out_ref[rows, lanes] = mixed.astype(jnp.bfloat16)


def mix(where, hidden_in, attn_gate, blocks):
    rows, width = hidden_in.shape
    n_patch = len(blocks[0])
    piece, cols = blocks[0][0].shape
    if cols % HEAD_DIM:
        order = jnp.concatenate([jnp.stack(x) for x in blocks], axis=1)
        order = order[where[PATCH] ^ jnp.arange(n_patch)]
        projected = order.transpose(1, 0, 2).reshape(rows, width).astype(jnp.float32)
        return (hidden_in.astype(jnp.float32) + attn_gate * projected).astype(jnp.bfloat16)
    rels = [0, *range(n_patch - 1, 0, -1)]
    flat = [part[rel] for part in blocks for rel in rels]
    return call(
        functools.partial(mix_kernel, rels),
        "mix",
        jax.ShapeDtypeStruct((rows, width), jnp.bfloat16),
        1,
        [spec((rows, width)), spec((1, width))] + [spec((piece, cols))] * len(flat),
        spec((rows, width)),
    )(where, hidden_in, attn_gate[None], *flat)


def gather(parts, n_patch):
    if n_patch != 4:
        return [
            ([x] + [swap(x, "patch", n_patch, rel) for rel in range(1, n_patch)], [])
            for x in parts
        ]
    far = [swap(x, "patch", 4, 2) for x in parts]
    next_to = [swap(x, "patch", 4, 1) for x in parts]
    out = []
    for at, x in enumerate(parts):
        far[at], next_to[at], parts = lax.optimization_barrier((far[at], next_to[at], parts))
        middle = swap(parts[at], "patch", 4, 3, (1, 2))
        ends = lax.ppermute(far[at], "patch", [(1, 0), (2, 3)])
        if at + 1 < len(parts):
            ends, far[at + 1], next_to[at + 1] = lax.optimization_barrier(
                (ends, far[at + 1], next_to[at + 1])
            )
        out.append(([x, next_to[at], far[at], middle], [ends]))
    return out


def add_sub_kernel(n_sub, where_ref, *refs):
    terms, kept_ref, outs = refs[:n_sub], refs[n_sub], refs[n_sub + 1 :]
    for head in range(len(outs) + 1):
        total = terms[0][head].astype(jnp.float32)
        for term in terms[1:]:
            total += term[head].astype(jnp.float32)
        if head == 0:
            kept_ref[...] = total
        else:
            outs[head - 1][...] = total.astype(jnp.bfloat16)


def add_head_kernel(n_more, where_ref, kept_ref, *refs):
    for at, out in enumerate(refs[n_more:]):
        total = kept_ref[at]
        for term in refs[:n_more]:
            total += term[at].astype(jnp.float32)
        out[...] = total.astype(jnp.bfloat16)


def reduce_sub(sizes, where, terms):
    n_sub, n_head = sizes["sub"], sizes["head"]
    terms = [terms[0]] + [swap(terms[rel], "sub", n_sub, rel) for rel in range(1, n_sub)]
    shape = terms[0].shape[1:]
    return call(
        functools.partial(add_sub_kernel, n_sub),
        "add_sub",
        [jax.ShapeDtypeStruct(shape, jnp.float32)]
        + [jax.ShapeDtypeStruct(shape, jnp.bfloat16)] * (n_head - 1),
        1,
        [spec(terms[0].shape)] * n_sub,
        [spec(shape)] * n_head,
    )(where, *terms)


def reduce_head(sizes, where, sums):
    n_head = sizes["head"]
    shape = sums[0].shape
    sums = [sums[0]] + [swap(sums[rel], "head", n_head, rel) for rel in range(1, n_head)]
    return call(
        functools.partial(add_head_kernel, n_head - 1),
        "add_head",
        [jax.ShapeDtypeStruct(shape[1:], jnp.bfloat16)] * shape[0],
        1,
        [spec(shape)] * n_head,
        [spec(shape[1:])] * shape[0],
    )(where, *sums)


def sum_tail(sizes, where, chunks, out_weight, hidden_in, attn_gate):
    n_patch, n_head, n_sub = sizes["patch"], sizes["head"], sizes["sub"]
    pieces = []
    for same in zip(*chunks):
        cut = [x[:, :, at * HEAD_DIM : (at + 1) * HEAD_DIM] for x, at in same]
        pieces.append(jnp.concatenate(cut, axis=2))
    pieces = [pieces[0], *pieces[:0:-1]]
    kv_pieces = list(pieces)
    for rel in range(len(pieces), n_patch, len(pieces)):
        kv_pieces += [swap(x, "patch", n_patch, rel) for x in pieces]
    split, tok = len(pieces), pieces[0].shape[1]
    count = n_head * n_sub
    piece = tok // count
    parts = 2 if piece % 32 == 0 else 1
    attended = []
    for part in range(parts):
        rows = (part * (piece // parts), piece // parts)
        x = attend(where, rows, count, pieces, kv_pieces)
        attended.append(x.reshape(-1, x.shape[2]))
    slots = gather(attended, n_patch)
    blocks = []
    for part in range(parts):
        terms = project(split, where, *slots[part], out_weight, n_head, n_sub)
        total = reduce_head(sizes, where, reduce_sub(sizes, where, terms))
        blocks.append(
            [total[0]] + [swap(total[rel], "patch", n_patch, rel) for rel in range(1, n_patch)]
        )
    return mix(where, hidden_in, attn_gate, blocks)


def attend_halves_kernel(rels, where_ref, *refs):
    pieces, outs = refs[:-2], refs[-2:]
    factor = HEAD_DIM**-0.5 * math.log2(math.e)
    rows = outs[0].shape[1]
    keys = jnp.concatenate([ref[1] for ref in pieces], axis=0)
    values = jnp.concatenate([ref[2] for ref in pieces], axis=0)
    values = jnp.concatenate([values, jnp.ones_like(values)], axis=1)
    for half, out in enumerate(outs):
        start = pl.multiple_of((where_ref[HEAD] ^ half) * rows, rows)
        query = jnp.concatenate([ref[0, pl.ds(start, rows)] for ref in pieces], axis=0)
        scores = lax.dot_general(
            query, keys, (((1,), (1,)), ((), ())), preferred_element_type=jnp.float32
        )
        peak = jnp.max(scores, axis=1, keepdims=True)
        expo = jnp.exp2((scores - peak) * factor).astype(jnp.bfloat16)
        mix = jnp.dot(expo, values, preferred_element_type=jnp.float32)
        mix = (mix[:, :HEAD_DIM] / mix[:, HEAD_DIM:]).astype(jnp.bfloat16)
        for at, rel in enumerate(rels):
            out[where_ref[NEAR] ^ rel] = mix[at * rows : (at + 1) * rows]


def attend_halves(where, chunk):
    tok = chunk[0][0].shape[1]
    rels = [0, *range(len(chunk) - 1, 0, -1)]
    chunk = [chunk[rel] for rel in rels]
    out = jax.ShapeDtypeStruct((len(chunk), tok // 2, HEAD_DIM), jnp.bfloat16)
    outs = call(
        functools.partial(attend_halves_kernel, rels),
        "attend",
        [out] * 2,
        1,
        [pl.BlockSpec((3, tok, HEAD_DIM), lambda i, w, at=at: (0, 0, at)) for _, at in chunk],
        [spec(out.shape)] * 2,
    )(where, *[x for x, _ in chunk])
    return [x.reshape(-1, HEAD_DIM) for x in outs]


def first_kernel(where_ref, *refs):
    slots, (more, own_ref, fetched_ref, passed_ref, out_ref, held_ref) = refs[:7], refs[7:]
    depth = own_ref.shape[0]

    def put(at, chunk, value):
        place = where_ref[NEAR] ^ at
        there = 4 + (2 * ((place // 2) ^ where_ref[GRP]) + place % 2)
        for half, spot in enumerate((place, there)):
            lane = (2 * spot + chunk) * HEAD_DIM
            held_ref[:, pl.ds(pl.multiple_of(lane, HEAD_DIM), HEAD_DIM)] = value[
                :, half * HEAD_DIM : (half + 1) * HEAD_DIM
            ]

    @pl.when(pl.program_id(0) == 0)
    def arrange():
        for index, slot in enumerate(slots):
            chunk, at = divmod(index, 4)
            block = slot[...]
            if at == 3:
                block = jnp.where(where_ref[INNER] == 1, block, more[...])
            put(at, chunk, block)
        put(3, 1, jnp.zeros(more.shape, jnp.bfloat16))

    acc = jnp.dot(held_ref[:, :depth], own_ref[...], preferred_element_type=jnp.float32)
    half = depth // 2
    for at, weight in enumerate((fetched_ref, passed_ref)):
        acc += jnp.dot(
            held_ref[:, depth + at * half : depth + (at + 1) * half],
            weight[...],
            preferred_element_type=jnp.float32,
        )
    out_ref[...] = acc


def first_product(where, slots, more, weights):
    rows, feat = slots[0].shape
    depth, cols = weights[0].shape
    wide = cols // 2
    return call(
        first_kernel,
        "first",
        jax.ShapeDtypeStruct((rows, cols), jnp.float32),
        2,
        [spec((rows, feat))] * 8
        + [pl.BlockSpec((x.shape[0], wide), lambda i, w: (0, i)) for x in weights],
        pl.BlockSpec((rows, wide), lambda i, w: (0, i)),
        [pltpu.VMEM((rows, 2 * depth), jnp.bfloat16)],
    )(where, *slots, more, *weights)


def second_kernel(
    where_ref, slot, more, own_ref, fetched_ref, passed_ref, acc_in, keep_ref, send_ref, acc_ref
):
    place = where_ref[NEAR] ^ 3
    here = pl.ds(pl.multiple_of((2 * (place % 2) + 1) * HEAD_DIM, HEAD_DIM), HEAD_DIM)
    partner = jnp.where((place // 2) == where_ref[GRP], fetched_ref[here, :], passed_ref[here, :])
    weight = jnp.concatenate([own_ref[...], partner], axis=0)
    block = jnp.where(where_ref[INNER] == 1, slot[...], more[...])
    acc = acc_in[...] + jnp.dot(block, weight, preferred_element_type=jnp.float32)
    acc_ref[...] = acc.reshape(acc_ref.shape)
    for sub, out in enumerate((keep_ref, send_ref)):
        for at in range(4):
            out[at] = acc_ref[where_ref[NEAR] ^ at, where_ref[SUB] ^ sub].astype(jnp.bfloat16)


def second_product(where, chunk, slot, more, weights, acc):
    rows, feat = slot.shape
    depth, cols = weights[1].shape
    wide = cols // 2
    out = jax.ShapeDtypeStruct((4, rows // 8, wide), jnp.bfloat16)
    return call(
        second_kernel,
        "second",
        [out] * 2,
        1,
        [spec((rows, feat))] * 2
        + [pl.BlockSpec((HEAD_DIM, wide), lambda i, w: (2 * (w[NEAR] ^ 3) + 1, chunk))]
        + [pl.BlockSpec((depth, wide), lambda i, w: (0, chunk))] * 2
        + [pl.BlockSpec((rows, wide), lambda i, w: (0, chunk))],
        [spec(out.shape)] * 2,
        [pltpu.VMEM((4, 2, rows // 8, wide), jnp.float32)],
    )(where, slot, more, *weights, acc)


def add_kernel(where_ref, keep_ref, term_ref, *outs):
    for at, out in enumerate(outs):
        total = keep_ref[at].astype(jnp.float32) + term_ref[at].astype(jnp.float32)
        out[...] = total.astype(jnp.bfloat16)


def add(where, keep, term):
    return call(
        add_kernel,
        "add",
        [jax.ShapeDtypeStruct(keep.shape[1:], jnp.bfloat16)] * keep.shape[0],
        1,
        [spec(keep.shape)] * 2,
        [spec(keep.shape[1:])] * keep.shape[0],
    )(where, keep, term)


def share_tail(sizes, where, chunks, out_weight, hidden_in, attn_gate):
    half = out_weight.shape[0] // 2
    out_weight, where = lax.optimization_barrier((out_weight, where))
    start = lax.axis_index("grp") * half
    fetched = swap(lax.dynamic_slice_in_dim(out_weight, start, half, 0), "head", 2, 1)
    early, fetched = lax.optimization_barrier(([x for x, _ in chunks[0]], fetched))
    chunks[0] = [(x, place) for x, (_, place) in zip(early, chunks[0])]
    passed = swap(fetched, "grp", 2, 1)

    mine, other = attend_halves(where, chunks[0])
    other = swap(other, "head", 2, 1)
    late, other = lax.optimization_barrier(([x for x, _ in chunks[1]], other))
    joined = jnp.concatenate([mine, other], axis=1)
    chunks[1] = [(x, place) for x, (_, place) in zip(late, chunks[1])]
    mine, other = attend_halves(where, chunks[1])
    slots = [[joined], [jnp.concatenate([mine, swap(other, "head", 2, 1)], axis=1)]]
    for at, slot in enumerate(slots):
        far, next_to = swap(slot[0], "patch", 4, 2), swap(slot[0], "patch", 4, 1)
        far, next_to, slots[1][0], slot[0] = lax.optimization_barrier(
            (far, next_to, slots[1][0], slot[0])
        )
        if at == 1:
            far, slot[0], passed = lax.optimization_barrier((far, slot[0], passed))
        middle = swap(slot[0], "patch", 4, 3, (1, 2))
        ends = lax.ppermute(far, "patch", [(1, 0), (2, 3)])
        slot += [next_to, far, middle, ends]
    weights = [out_weight, fetched, passed]
    acc = first_product(where, [*slots[0][:4], *slots[1][:3]], slots[0][4], weights)
    terms = [second_product(where, at, *slots[1][3:], weights, acc) for at in range(2)]
    blocks = []
    for keep, send in terms:
        total = add(where, keep, swap(send, "sub", 2, 1))
        blocks.append([total[0]] + [swap(total[rel], "patch", 4, rel) for rel in range(3, 0, -1)])
    return mix_columns(where, hidden_in, attn_gate, blocks)


def mix_columns_kernel(where_ref, hidden_ref, gate_ref, *refs):
    blocks, out_ref = refs[:-1], refs[-1]
    cols = blocks[0].shape[1]
    for chunk in range(2):
        for at, rel in enumerate((0, 3, 2, 1)):
            start = (2 * (where_ref[PATCH] ^ rel) + chunk) * cols
            lanes = pl.ds(pl.multiple_of(start, HEAD_DIM), cols)
            mixed = hidden_ref[:, lanes].astype(jnp.float32) + gate_ref[:, lanes] * blocks[
                4 * chunk + at
            ][...].astype(jnp.float32)
            out_ref[:, lanes] = mixed.astype(jnp.bfloat16)


def mix_columns(where, hidden_in, attn_gate, blocks):
    rows, width = hidden_in.shape
    flat = [x for chunk in blocks for x in chunk]
    return call(
        mix_columns_kernel,
        "mix",
        jax.ShapeDtypeStruct((rows, width), jnp.bfloat16),
        1,
        [spec((rows, width)), spec((1, width))] + [spec(flat[0].shape)] * len(flat),
        spec((rows, width)),
    )(where, hidden_in, attn_gate[None], *flat)


def body(sizes, queries, fresh_kv, cached_kv, exponents, out_weight, hidden_in, attn_gate):
    n_patch, n_head, n_sub = sizes["patch"], sizes["head"], sizes["sub"]
    tok, channels = queries.shape
    heads = channels // HEAD_DIM
    split = math.gcd(heads, n_patch)
    patch_at = lax.axis_index("patch")
    inner = (patch_at > 0) & (patch_at < n_patch - 1)
    where = jnp.stack(
        [
            patch_at,
            patch_at % split,
            lax.axis_index("head"),
            lax.axis_index("sub"),
            inner,
            lax.axis_index("grp"),
        ]
    ).astype(jnp.int32)

    arrays = (exponents, queries, fresh_kv, cached_kv)
    sent = pack(split, *arrays)
    arrived = {
        at + 1: swap(x, "patch", n_patch, min(at + 1, split - 1)) for at, x in enumerate(sent)
    }
    where, sent = lax.optimization_barrier((where, sent))
    arrived[0] = pack_own(split, where, *arrays)
    chunks = []
    for chunk in range(heads // split):
        places = [piece_place(split, heads // split, rel, chunk) for rel in range(split)]
        chunks.append([(arrived[number], place) for number, place in places])
    tail = (sizes, where, chunks, out_weight, hidden_in, attn_gate)
    if (sizes["grp"], n_head, split, n_patch, heads) == (2, 2, 4, 4, 8):
        return share_tail(*tail)
    return sum_tail(*tail)


def solution(mesh):
    in_specs = (
        P(("grp", "patch"), ("head", "sub")),
        P(None, ("grp", "patch"), ("head", "sub")),
        P(None, "grp", ("head", "sub")),
        P(None, ("grp", "patch"), ("head", "sub")),
        P(("head", "sub"), "patch"),
        P(("grp", "patch", "head", "sub"), None),
        P(),
    )
    out_specs = P(("grp", "patch", "head", "sub"), None)
    return jax.shard_map(
        functools.partial(body, dict(mesh.shape)),
        mesh=mesh,
        in_specs=in_specs,
        out_specs=out_specs,
        check_vma=False,
    )
```

```python
import functools
import math

import jax
import jax.numpy as jnp
from jax import lax
from jax.experimental import pallas as pl
from jax.experimental.pallas import tpu as pltpu
from jax.sharding import PartitionSpec as P

HEAD_DIM = 128
SCALE_ROWS = 128
SATURATION = 448.0
PACK_ROWS = 64
VMEM_BYTES = 32 * 1024 * 1024
PACK_VMEM_BYTES = 60 * 1024 * 1024
ATTEND_FLOPS = 1
PROJECT_FLOPS = 1
OWN_FLOPS = 50_000_000_000
FETCHED = 5
ZERO_FLOPS = 20_000_000_000
HALF_FLOPS = 1

PATCH, NEAR, HEAD, SUB, INNER, GRP = range(6)


def spec(shape):
    return pl.BlockSpec(shape, lambda i, w: (0,) * len(shape))


def call(kernel, name, out_shape, grid, in_specs, out_specs, scratch=(), flops=1, vmem=VMEM_BYTES):
    return pl.pallas_call(
        kernel,
        out_shape=out_shape,
        grid_spec=pltpu.PrefetchScalarGridSpec(
            num_scalar_prefetch=1,
            grid=(grid,),
            in_specs=in_specs,
            out_specs=out_specs,
            scratch_shapes=list(scratch),
        ),
        compiler_params=pltpu.CompilerParams(vmem_limit_bytes=vmem),
        cost_estimate=pl.CostEstimate(flops=flops, bytes_accessed=0, transcendentals=0),
        name=name,
    )


def swap(x, axes, count, mask, only=None):
    pairs = [(at, at ^ mask) for at in range(count) if only is None or at in only]
    return lax.ppermute(x, axes, pairs)


def decode(fresh, cached, exponent):
    power = jnp.full((1, HEAD_DIM), exponent.astype(jnp.float32))
    cached = cached.astype(jnp.float32)
    residual = fresh.astype(jnp.float32) - cached
    codes = jnp.clip(residual * jnp.exp2(-power), -SATURATION, SATURATION).astype(jnp.bfloat16)
    return (cached + codes.astype(jnp.float32) * jnp.exp2(power)).astype(jnp.bfloat16)


def pack_kernel(split, per, exps_ref, q_ref, fresh_ref, cached_ref, *refs):
    outs, bufs = refs[: split - 1], refs[split - 1 : 2 * split - 2]
    q_buf, fresh_buf, cached_buf, sems, out_sems = refs[2 * split - 2 :]
    patch = lax.axis_index("patch")
    near = lax.rem(patch, split)
    tok = q_buf.shape[0]
    copies, sent = [], []
    for block in range(tok // PACK_ROWS):
        rows = pl.ds(block * PACK_ROWS, PACK_ROWS)
        there = pl.ds(pl.multiple_of(patch * tok + block * PACK_ROWS, PACK_ROWS), PACK_ROWS)
        copies.append(
            [
                pltpu.make_async_copy(q_ref.at[rows], q_buf.at[rows], sems.at[block, 0]),
                pltpu.make_async_copy(fresh_ref.at[:, rows], fresh_buf.at[:, rows], sems.at[block, 1]),
                pltpu.make_async_copy(cached_ref.at[:, there], cached_buf.at[:, rows], sems.at[block, 2]),
            ]
        )
        for copy in copies[-1]:
            copy.start()
    for block in range(tok // PACK_ROWS):
        rows = pl.ds(block * PACK_ROWS, PACK_ROWS)
        for copy in copies[block]:
            copy.wait()
        for rel in range(split - 1, 0, -1):
            buf = bufs[split - 1 - rel]
            for chunk in range(per):
                head = (near ^ rel) * per + chunk
                lanes = pl.ds(pl.multiple_of(head * HEAD_DIM, HEAD_DIM), HEAD_DIM)
                here = pl.ds(chunk * HEAD_DIM, HEAD_DIM)
                buf[0, rows, here] = q_buf[rows, lanes]
                for stacked in range(2):
                    buf[1 + stacked, rows, here] = decode(
                        fresh_buf[stacked, rows, lanes],
                        cached_buf[stacked, rows, lanes],
                        exps_ref[stacked, block * PACK_ROWS // SCALE_ROWS, head],
                    )
            sent.append(
                pltpu.make_async_copy(
                    buf.at[:, rows],
                    outs[split - 1 - rel].at[:, rows],
                    out_sems.at[block, rel - 1],
                )
            )
            sent[-1].start()
    for copy in sent:
        copy.wait()


def pack(split, exponents, queries, fresh_kv, cached_kv):
    tok, channels = queries.shape
    feat = channels // split
    blocks = tok // PACK_ROWS
    hbm = pl.BlockSpec(memory_space=pltpu.HBM)
    return pl.pallas_call(
        functools.partial(pack_kernel, split, feat // HEAD_DIM),
        out_shape=[jax.ShapeDtypeStruct((3, tok, feat), jnp.bfloat16)] * (split - 1),
        in_specs=[pl.BlockSpec(memory_space=pltpu.SMEM), hbm, hbm, hbm],
        out_specs=[hbm] * (split - 1),
        scratch_shapes=[pltpu.VMEM((3, tok, feat), jnp.bfloat16)] * (split - 1)
        + [
            pltpu.VMEM((tok, channels), jnp.bfloat16),
            pltpu.VMEM((2, tok, channels), jnp.bfloat16),
            pltpu.VMEM((2, tok, channels), jnp.bfloat16),
            pltpu.SemaphoreType.DMA((blocks, 3)),
            pltpu.SemaphoreType.DMA((blocks, split - 1)),
        ],
        compiler_params=pltpu.CompilerParams(vmem_limit_bytes=PACK_VMEM_BYTES),
        name="pack",
    )(exponents, queries, fresh_kv, cached_kv)


def own_kernel(per, where_ref, exps_ref, q_ref, fresh_ref, cached_ref, out_ref):
    out_ref[0] = q_ref[...]
    for chunk in range(per):
        lanes = pl.ds(chunk * HEAD_DIM, HEAD_DIM)
        for block in range(q_ref.shape[0] // SCALE_ROWS):
            rows = pl.ds(block * SCALE_ROWS, SCALE_ROWS)
            for stacked in range(2):
                out_ref[1 + stacked, rows, lanes] = decode(
                    fresh_ref[stacked, rows, lanes],
                    cached_ref[stacked, rows, lanes],
                    exps_ref[stacked, block, where_ref[NEAR] * per + chunk],
                )


def pack_own(split, where, exponents, queries, fresh_kv, cached_kv):
    tok, channels = queries.shape
    feat = channels // split
    out = jax.ShapeDtypeStruct((3, tok, feat), jnp.bfloat16)
    return call(
        functools.partial(own_kernel, feat // HEAD_DIM),
        "own",
        out,
        1,
        [
            pl.BlockSpec(memory_space=pltpu.SMEM),
            pl.BlockSpec((tok, feat), lambda i, w: (0, w[NEAR])),
            pl.BlockSpec((2, tok, feat), lambda i, w: (0, 0, w[NEAR])),
            pl.BlockSpec((2, tok, feat), lambda i, w: (0, w[PATCH], w[NEAR])),
        ],
        spec(out.shape),
        flops=OWN_FLOPS,
    )(where, exponents, queries, fresh_kv, cached_kv)


def attend_kernel(split, part, where_ref, *refs):
    q_refs, kv_refs, out_ref = (refs[0], *refs[split - 1 : 0 : -1]), refs[:-1], refs[-1]
    factor = HEAD_DIM**-0.5 * math.log2(math.e)
    tok, feat = q_refs[0].shape[1:]
    count = out_ref.shape[1] // part[1]
    starts = [at * (tok // count) + part[0] for at in range(count)]
    for head in range(feat // HEAD_DIM):
        lanes = pl.ds(head * HEAD_DIM, HEAD_DIM)
        keys = jnp.concatenate([ref[1, :, lanes] for ref in kv_refs], axis=0)
        values = jnp.concatenate([ref[2, :, lanes] for ref in kv_refs], axis=0)
        values = jnp.concatenate([values, jnp.ones_like(values)], axis=1)
        for rel in range(split):
            rows = [q_refs[rel][0, start : start + part[1], lanes] for start in starts]
            query = jnp.concatenate(rows, axis=0) if len(rows) > 1 else rows[0]
            scores = lax.dot_general(
                query, keys, (((1,), (1,)), ((), ())), preferred_element_type=jnp.float32
            )
            peak = jnp.max(scores, axis=1, keepdims=True)
            expo = jnp.exp2((scores - peak) * factor).astype(jnp.bfloat16)
            mix = jnp.dot(expo, values, preferred_element_type=jnp.float32)
            mix = mix[:, :HEAD_DIM] / mix[:, HEAD_DIM:]
            out_ref[where_ref[NEAR] ^ rel, :, lanes] = mix.astype(jnp.bfloat16)


def attend(where, part, count, pieces, kv_pieces):
    split = len(pieces)
    _, tok, feat = pieces[0].shape
    out = jax.ShapeDtypeStruct((split, count * part[1], feat), jnp.bfloat16)
    return call(
        functools.partial(attend_kernel, split, part),
        "attend",
        out,
        1,
        [spec((3, tok, feat))] * len(kv_pieces),
        spec(out.shape),
        flops=ATTEND_FLOPS,
    )(where, *kv_pieces)


def project_kernel(split, n_slots, n_more, where_ref, *refs):
    slots, refs = refs[:n_slots], refs[n_slots:]
    more, weight_ref, refs = refs[:n_more], refs[n_more], refs[n_more + 1 :]
    outs, held_ref, acc_ref = refs[:-2], refs[-2], refs[-1]
    rows, feat = slots[0].shape
    n_sub, n_head = acc_ref.shape[3], acc_ref.shape[2]

    @pl.when(pl.program_id(0) == 0)
    def arrange():
        for at, slot in enumerate(slots):
            group, near = divmod(at, split)
            lane = (where_ref[NEAR] ^ near) * feat
            block = slot[...]
            if more and at == n_slots - 1:
                block = jnp.where(where_ref[INNER] == 1, block, more[0][...])
            held_ref[
                group * rows : (group + 1) * rows, pl.ds(pl.multiple_of(lane, HEAD_DIM), feat)
            ] = block

    acc = jnp.dot(held_ref[...], weight_ref[...], preferred_element_type=jnp.float32)
    acc_ref[...] = acc.reshape(acc_ref.shape)
    for sub in range(n_sub):
        for head in range(n_head):
            for at in range(n_slots):
                group, near = divmod(at, split)
                outs[sub][head, at] = acc_ref[
                    group, where_ref[NEAR] ^ near, where_ref[HEAD] ^ head, where_ref[SUB] ^ sub
                ].astype(jnp.bfloat16)


def project(split, where, slots, more, weight, n_head, n_sub):
    rows, feat = slots[0].shape
    n_patch = len(slots)
    total = rows * n_patch // split
    depth, cols = weight.shape
    wide = 640 if cols % 640 == 0 else cols
    piece = rows // (split * n_head * n_sub)
    return call(
        functools.partial(project_kernel, split, n_patch, len(more)),
        "project",
        [jax.ShapeDtypeStruct((n_head, n_patch, piece, cols), jnp.bfloat16)] * n_sub,
        cols // wide,
        [spec((rows, feat))] * (n_patch + len(more))
        + [pl.BlockSpec((depth, wide), lambda i, w: (0, i))],
        [pl.BlockSpec((n_head, n_patch, piece, wide), lambda i, w: (0, 0, 0, i))] * n_sub,
        [
            pltpu.VMEM((total, depth), jnp.bfloat16),
            pltpu.VMEM((n_patch // split, split, n_head, n_sub, piece, wide), jnp.float32),
        ],
        flops=PROJECT_FLOPS,
    )(where, *slots, *more, weight)


def mix_kernel(rels, where_ref, hidden_ref, gate_ref, *refs):
    blocks, out_ref = refs[:-1], refs[-1]
    piece, cols = blocks[0].shape
    for part in range(len(blocks) // len(rels)):
        rows = pl.ds(part * piece, piece)
        for at, rel in enumerate(rels):
            lanes = pl.ds(pl.multiple_of((where_ref[PATCH] ^ rel) * cols, HEAD_DIM), cols)
            mixed = hidden_ref[rows, lanes].astype(jnp.float32) + gate_ref[:, lanes] * blocks[
                part * len(rels) + at
            ][...].astype(jnp.float32)
            out_ref[rows, lanes] = mixed.astype(jnp.bfloat16)


def mix(where, hidden_in, attn_gate, blocks):
    rows, width = hidden_in.shape
    n_patch = len(blocks[0])
    piece, cols = blocks[0][0].shape
    if cols % HEAD_DIM:
        order = jnp.concatenate([jnp.stack(x) for x in blocks], axis=1)
        order = order[where[PATCH] ^ jnp.arange(n_patch)]
        projected = order.transpose(1, 0, 2).reshape(rows, width).astype(jnp.float32)
        return (hidden_in.astype(jnp.float32) + attn_gate * projected).astype(jnp.bfloat16)
    rels = [0, *range(n_patch - 1, 0, -1)]
    flat = [part[rel] for part in blocks for rel in rels]
    return call(
        functools.partial(mix_kernel, rels),
        "mix",
        jax.ShapeDtypeStruct((rows, width), jnp.bfloat16),
        1,
        [spec((rows, width)), spec((1, width))] + [spec((piece, cols))] * len(flat),
        spec((rows, width)),
    )(where, hidden_in, attn_gate[None], *flat)


def gather(parts, n_patch):
    if n_patch != 4:
        return [
            ([x] + [swap(x, "patch", n_patch, rel) for rel in range(1, n_patch)], [])
            for x in parts
        ]
    far = [swap(x, "patch", 4, 2) for x in parts]
    next_to = [swap(x, "patch", 4, 1) for x in parts]
    out = []
    for at, x in enumerate(parts):
        far[at], next_to[at], parts = lax.optimization_barrier((far[at], next_to[at], parts))
        middle = swap(parts[at], "patch", 4, 3, (1, 2))
        ends = lax.ppermute(far[at], "patch", [(1, 0), (2, 3)])
        if at + 1 < len(parts):
            ends, far[at + 1], next_to[at + 1] = lax.optimization_barrier(
                (ends, far[at + 1], next_to[at + 1])
            )
        out.append(([x, next_to[at], far[at], middle], [ends]))
    return out


def add_sub_kernel(n_sub, where_ref, *refs):
    terms, kept_ref, outs = refs[:n_sub], refs[n_sub], refs[n_sub + 1 :]
    for head in range(len(outs) + 1):
        total = terms[0][head].astype(jnp.float32)
        for term in terms[1:]:
            total += term[head].astype(jnp.float32)
        if head == 0:
            kept_ref[...] = total
        else:
            outs[head - 1][...] = total.astype(jnp.bfloat16)


def add_head_kernel(n_more, where_ref, kept_ref, *refs):
    for at, out in enumerate(refs[n_more:]):
        total = kept_ref[at]
        for term in refs[:n_more]:
            total += term[at].astype(jnp.float32)
        out[...] = total.astype(jnp.bfloat16)


def reduce_sub(sizes, where, terms):
    n_sub, n_head = sizes["sub"], sizes["head"]
    terms = [terms[0]] + [swap(terms[rel], "sub", n_sub, rel) for rel in range(1, n_sub)]
    shape = terms[0].shape[1:]
    return call(
        functools.partial(add_sub_kernel, n_sub),
        "add_sub",
        [jax.ShapeDtypeStruct(shape, jnp.float32)]
        + [jax.ShapeDtypeStruct(shape, jnp.bfloat16)] * (n_head - 1),
        1,
        [spec(terms[0].shape)] * n_sub,
        [spec(shape)] * n_head,
    )(where, *terms)


def reduce_head(sizes, where, sums):
    n_head = sizes["head"]
    shape = sums[0].shape
    sums = [sums[0]] + [swap(sums[rel], "head", n_head, rel) for rel in range(1, n_head)]
    return call(
        functools.partial(add_head_kernel, n_head - 1),
        "add_head",
        [jax.ShapeDtypeStruct(shape[1:], jnp.bfloat16)] * shape[0],
        1,
        [spec(shape)] * n_head,
        [spec(shape[1:])] * shape[0],
    )(where, *sums)


def sum_tail(sizes, where, pieces, kv_pieces, out_weight, hidden_in, attn_gate):
    n_patch, n_head, n_sub = sizes["patch"], sizes["head"], sizes["sub"]
    split, tok = len(pieces), pieces[0].shape[1]
    count = n_head * n_sub
    piece = tok // count
    parts = 2 if piece % 32 == 0 else 1
    attended = []
    for part in range(parts):
        rows = (part * (piece // parts), piece // parts)
        x = attend(where, rows, count, pieces, kv_pieces)
        attended.append(x.reshape(-1, x.shape[2]))
    slots = gather(attended, n_patch)
    blocks = []
    for part in range(parts):
        terms = project(split, where, *slots[part], out_weight, n_head, n_sub)
        total = reduce_head(sizes, where, reduce_sub(sizes, where, terms))
        blocks.append(
            [total[0]] + [swap(total[rel], "patch", n_patch, rel) for rel in range(1, n_patch)]
        )
    return mix(where, hidden_in, attn_gate, blocks)


def attend_half_kernel(half, where_ref, *refs):
    pieces, out = refs[:-1], refs[-1]
    factor = HEAD_DIM**-0.5 * math.log2(math.e)
    rows, feat = out.shape[1:]
    start = pl.multiple_of((where_ref[HEAD] ^ half) * rows, rows)
    for head in range(feat // HEAD_DIM):
        lanes = pl.ds(head * HEAD_DIM, HEAD_DIM)
        keys = jnp.concatenate([ref[1, :, lanes] for ref in pieces], axis=0)
        values = jnp.concatenate([ref[2, :, lanes] for ref in pieces], axis=0)
        values = jnp.concatenate([values, jnp.ones_like(values)], axis=1)
        query = jnp.concatenate([ref[0, pl.ds(start, rows), lanes] for ref in pieces], axis=0)
        scores = lax.dot_general(
            query, keys, (((1,), (1,)), ((), ())), preferred_element_type=jnp.float32
        )
        peak = jnp.max(scores, axis=1, keepdims=True)
        expo = jnp.exp2((scores - peak) * factor).astype(jnp.bfloat16)
        mix = jnp.dot(expo, values, preferred_element_type=jnp.float32)
        mix = (mix[:, :HEAD_DIM] / mix[:, HEAD_DIM:]).astype(jnp.bfloat16)
        for rel in range(len(pieces)):
            out[where_ref[NEAR] ^ rel, :, lanes] = mix[rel * rows : (rel + 1) * rows]


def attend_half(where, half, pieces):
    _, tok, feat = pieces[0].shape
    out = jax.ShapeDtypeStruct((len(pieces), tok // 2, feat), jnp.bfloat16)
    return call(
        functools.partial(attend_half_kernel, half),
        "attend",
        out,
        1,
        [spec((3, tok, feat))] * len(pieces),
        spec(out.shape),
        flops=HALF_FLOPS,
    )(where, *pieces).reshape(-1, feat)


def zeroth_kernel(where_ref, slot, weight_ref, out_ref):
    out_ref[...] = jnp.dot(slot[...], weight_ref[...], preferred_element_type=jnp.float32)


def zeroth_product(where, slot, weight):
    rows, feat = slot.shape
    cols = weight.shape[1]
    wide = cols // 2
    return call(
        zeroth_kernel,
        "zeroth",
        jax.ShapeDtypeStruct((rows, cols), jnp.float32),
        2,
        [spec((rows, feat)), pl.BlockSpec((feat, wide), lambda i, w: (w[NEAR], i))],
        pl.BlockSpec((rows, wide), lambda i, w: (0, i)),
        flops=ZERO_FLOPS,
    )(where, slot, weight)


def partner_place(where_ref, head):
    return (head + FETCHED * where_ref[GRP]) % 8


def first_kernel(where_ref, *refs):
    slots, refs = refs[:6], refs[6:]
    more, acc_ref, own_ref, fetched_ref, passed_ref, out_ref, held_ref = refs
    rows, feat = slots[0].shape
    depth, cut = own_ref.shape[0], own_ref.shape[0] + fetched_ref.shape[0]

    def put(place, block):
        lanes = pl.ds(pl.multiple_of(place * HEAD_DIM, HEAD_DIM), block.shape[1])
        held_ref[:, lanes] = block

    @pl.when(pl.program_id(0) == 0)
    def arrange():
        nothing = jnp.zeros((rows, feat), jnp.bfloat16)
        mine, partner = dict(zip((2, 1, 3), slots[:3])), dict(zip((0, 2, 1), slots[3:]))
        for at in range(4):
            place = where_ref[NEAR] ^ at
            block = mine[at][...] if at else nothing
            if at == 3:
                block = jnp.where(where_ref[INNER] == 1, block, more[...])
            put(2 * place, block)
            block = nothing if at == 3 else partner[at][...]
            for head in range(2):
                there = partner_place(where_ref, 2 * place + head)
                put(8 + there, block[:, head * HEAD_DIM : (head + 1) * HEAD_DIM])

    acc = acc_ref[...]
    acc += jnp.dot(held_ref[:, :depth], own_ref[...], preferred_element_type=jnp.float32)
    acc += jnp.dot(held_ref[:, depth:cut], fetched_ref[...], preferred_element_type=jnp.float32)
    acc += jnp.dot(held_ref[:, cut:], passed_ref[...], preferred_element_type=jnp.float32)
    out_ref[...] = acc


def first_product(where, slots, more, acc, weights):
    rows, feat = slots[0].shape
    cols = weights[0].shape[1]
    wide = cols // 2
    whole = pl.BlockSpec((rows, wide), lambda i, w: (0, i))
    return call(
        first_kernel,
        "first",
        jax.ShapeDtypeStruct((rows, cols), jnp.float32),
        2,
        [spec((rows, feat))] * 7
        + [whole]
        + [pl.BlockSpec((x.shape[0], wide), lambda i, w: (0, i)) for x in weights],
        whole,
        [pltpu.VMEM((rows, 8 * feat), jnp.bfloat16)],
    )(where, *slots, more, acc, *weights)


def second_kernel(where_ref, slot, more, fetched_ref, passed_ref, acc_in, keep_ref, send_ref, acc_ref):
    weight = []
    for head in range(2):
        place = partner_place(where_ref, 2 * (where_ref[NEAR] ^ 3) + head)
        here = jnp.minimum(place, FETCHED - 1) * HEAD_DIM
        there = jnp.maximum(place - FETCHED, 0) * HEAD_DIM
        weight.append(
            jnp.where(
                place < FETCHED,
                fetched_ref[pl.ds(pl.multiple_of(here, HEAD_DIM), HEAD_DIM), :],
                passed_ref[pl.ds(pl.multiple_of(there, HEAD_DIM), HEAD_DIM), :],
            )
        )
    block = jnp.where(where_ref[INNER] == 1, slot[...], more[...])
    acc = acc_in[...] + jnp.dot(
        block, jnp.concatenate(weight, axis=0), preferred_element_type=jnp.float32
    )
    acc_ref[...] = acc.reshape(acc_ref.shape)
    for sub, out in enumerate((keep_ref, send_ref)):
        for at in range(4):
            out[at] = acc_ref[where_ref[NEAR] ^ at, where_ref[SUB] ^ sub].astype(jnp.bfloat16)


def second_product(where, chunk, slot, more, weights, acc):
    rows, feat = slot.shape
    cols = weights[0].shape[1]
    wide = cols // 2
    out = jax.ShapeDtypeStruct((4, rows // 8, wide), jnp.bfloat16)
    return call(
        second_kernel,
        "second",
        [out] * 2,
        1,
        [spec((rows, feat))] * 2
        + [pl.BlockSpec((x.shape[0], wide), lambda i, w: (0, chunk)) for x in weights]
        + [pl.BlockSpec((rows, wide), lambda i, w: (0, chunk))],
        [spec(out.shape)] * 2,
        [pltpu.VMEM((4, 2, rows // 8, wide), jnp.float32)],
    )(where, slot, more, *weights, acc)


def add_kernel(where_ref, keep_ref, term_ref, *outs):
    for at, out in enumerate(outs):
        total = keep_ref[at].astype(jnp.float32) + term_ref[at].astype(jnp.float32)
        out[...] = total.astype(jnp.bfloat16)


def add(where, keep, term):
    return call(
        add_kernel,
        "add",
        [jax.ShapeDtypeStruct(keep.shape[1:], jnp.bfloat16)] * keep.shape[0],
        1,
        [spec(keep.shape)] * 2,
        [spec(keep.shape[1:])] * keep.shape[0],
    )(where, keep, term)


def share_tail(sizes, where, pieces, kv_pieces, out_weight, hidden_in, attn_gate):
    fetch, pass_on = FETCHED * HEAD_DIM, (8 - FETCHED) * HEAD_DIM
    out_weight, where = lax.optimization_barrier((out_weight, where))
    start = lax.axis_index("grp") * pass_on
    fetched = swap(lax.dynamic_slice_in_dim(out_weight, start, fetch, 0), "head", 2, 1)
    start = lax.axis_index("grp") * (fetch - pass_on)
    passed = swap(lax.dynamic_slice_in_dim(fetched, start, pass_on, 0), "grp", 2, 1)

    pieces = [pieces[0], *pieces[:0:-1]]
    mine = attend_half(where, 0, pieces)
    where, mine = lax.optimization_barrier((where, mine))
    other = swap(attend_half(where, 1, pieces), "head", 2, 1)
    acc = zeroth_product(where, mine, out_weight)
    other, acc = lax.optimization_barrier((other, acc))
    slots = []
    for at, x in enumerate((mine, other)):
        next_to, far = swap(x, "patch", 4, 1), swap(x, "patch", 4, 2)
        next_to, far, other, x = lax.optimization_barrier((next_to, far, other, x))
        middle = swap(x, "patch", 4, 3, (1, 2))
        ends = lax.ppermute(far, "patch", [(1, 0), (2, 3)])
        slots.append([x, next_to, far, middle, ends])
    first = [slots[0][at] for at in (2, 1, 3)] + [slots[1][at] for at in (0, 2, 1)]
    acc = first_product(where, first, slots[0][4], acc, [out_weight, fetched, passed])
    terms = [second_product(where, at, *slots[1][3:], [fetched, passed], acc) for at in range(2)]
    blocks = []
    for keep, send in terms:
        total = add(where, keep, swap(send, "sub", 2, 1))
        blocks.append([total[0]] + [swap(total[rel], "patch", 4, rel) for rel in range(3, 0, -1)])
    return mix_columns(where, hidden_in, attn_gate, blocks)


def mix_columns_kernel(where_ref, hidden_ref, gate_ref, *refs):
    blocks, out_ref = refs[:-1], refs[-1]
    cols = blocks[0].shape[1]
    for chunk in range(2):
        for at, rel in enumerate((0, 3, 2, 1)):
            start = (2 * (where_ref[PATCH] ^ rel) + chunk) * cols
            lanes = pl.ds(pl.multiple_of(start, HEAD_DIM), cols)
            mixed = hidden_ref[:, lanes].astype(jnp.float32) + gate_ref[:, lanes] * blocks[
                4 * chunk + at
            ][...].astype(jnp.float32)
            out_ref[:, lanes] = mixed.astype(jnp.bfloat16)


def mix_columns(where, hidden_in, attn_gate, blocks):
    rows, width = hidden_in.shape
    flat = [x for chunk in blocks for x in chunk]
    return call(
        mix_columns_kernel,
        "mix",
        jax.ShapeDtypeStruct((rows, width), jnp.bfloat16),
        1,
        [spec((rows, width)), spec((1, width))] + [spec(flat[0].shape)] * len(flat),
        spec((rows, width)),
    )(where, hidden_in, attn_gate[None], *flat)


def body(sizes, queries, fresh_kv, cached_kv, exponents, out_weight, hidden_in, attn_gate):
    n_patch, n_head, n_sub = sizes["patch"], sizes["head"], sizes["sub"]
    tok, channels = queries.shape
    heads = channels // HEAD_DIM
    split = math.gcd(heads, n_patch)
    patch_at = lax.axis_index("patch")
    inner = (patch_at > 0) & (patch_at < n_patch - 1)
    where = jnp.stack(
        [
            patch_at,
            patch_at % split,
            lax.axis_index("head"),
            lax.axis_index("sub"),
            inner,
            lax.axis_index("grp"),
        ]
    ).astype(jnp.int32)

    arrays = (exponents, queries, fresh_kv, cached_kv)
    sent = pack(split, *arrays)
    far_first = [
        swap(x, "patch", n_patch, split - 1 - at) for at, x in enumerate(sent)
    ]
    where, sent = lax.optimization_barrier((where, sent))
    pieces = [pack_own(split, where, *arrays), *far_first]
    kv_pieces = list(pieces)
    for rel in range(split, n_patch, split):
        kv_pieces += [swap(x, "patch", n_patch, rel) for x in pieces]

    tail = (sizes, where, pieces, kv_pieces, out_weight, hidden_in, attn_gate)
    if (sizes["grp"], n_head, split, n_patch) == (2, 2, 4, 4):
        return share_tail(*tail)
    return sum_tail(*tail)


def solution(mesh):
    in_specs = (
        P(("grp", "patch"), ("head", "sub")),
        P(None, ("grp", "patch"), ("head", "sub")),
        P(None, "grp", ("head", "sub")),
        P(None, ("grp", "patch"), ("head", "sub")),
        P(("head", "sub"), "patch"),
        P(("grp", "patch", "head", "sub"), None),
        P(),
    )
    out_specs = P(("grp", "patch", "head", "sub"), None)
    return jax.shard_map(
        functools.partial(body, dict(mesh.shape)),
        mesh=mesh,
        in_specs=in_specs,
        out_specs=out_specs,
        check_vma=False,
    )
```

```python
import functools
import math

import jax
import jax.numpy as jnp
from jax import lax
from jax.experimental import pallas as pl
from jax.experimental.pallas import tpu as pltpu
from jax.sharding import PartitionSpec as P

HEAD_DIM = 128
SCALE_ROWS = 128
SATURATION = 448.0
PACK_ROWS = 64
VMEM_BYTES = 16 * 1024 * 1024
PACK_VMEM_BYTES = 60 * 1024 * 1024
ATTEND_FLOPS = 1
PROJECT_FLOPS = 1
OWN_FLOPS = 50_000_000_000
FETCHED = 5
ZERO_FLOPS = 20_000_000_000
HALF_FLOPS = 1

PATCH, NEAR, HEAD, SUB, INNER, GRP = range(6)


def spec(shape):
    return pl.BlockSpec(shape, lambda i, w: (0,) * len(shape))


def call(kernel, name, out_shape, grid, in_specs, out_specs, scratch=(), flops=1, vmem=VMEM_BYTES):
    return pl.pallas_call(
        kernel,
        out_shape=out_shape,
        grid_spec=pltpu.PrefetchScalarGridSpec(
            num_scalar_prefetch=1,
            grid=(grid,),
            in_specs=in_specs,
            out_specs=out_specs,
            scratch_shapes=list(scratch),
        ),
        compiler_params=pltpu.CompilerParams(vmem_limit_bytes=vmem),
        cost_estimate=pl.CostEstimate(flops=flops, bytes_accessed=0, transcendentals=0),
        name=name,
    )


def swap(x, axes, count, mask, only=None):
    pairs = [(at, at ^ mask) for at in range(count) if only is None or at in only]
    return lax.ppermute(x, axes, pairs)


def decode(fresh, cached, exponent):
    power = jnp.full((1, HEAD_DIM), exponent.astype(jnp.float32))
    cached = cached.astype(jnp.float32)
    residual = fresh.astype(jnp.float32) - cached
    codes = jnp.clip(residual * jnp.exp2(-power), -SATURATION, SATURATION).astype(jnp.bfloat16)
    return (cached + codes.astype(jnp.float32) * jnp.exp2(power)).astype(jnp.bfloat16)


def pack_kernel(split, per, exps_ref, q_ref, fresh_ref, cached_ref, *refs):
    outs, bufs = refs[: split - 1], refs[split - 1 : 2 * split - 2]
    q_buf, fresh_buf, cached_buf, sems, out_sems = refs[2 * split - 2 :]
    patch = lax.axis_index("patch")
    near = lax.rem(patch, split)
    tok = q_buf.shape[0]
    copies, sent = [], []
    for block in range(tok // PACK_ROWS):
        rows = pl.ds(block * PACK_ROWS, PACK_ROWS)
        there = pl.ds(pl.multiple_of(patch * tok + block * PACK_ROWS, PACK_ROWS), PACK_ROWS)
        copies.append(
            [
                pltpu.make_async_copy(q_ref.at[rows], q_buf.at[rows], sems.at[block, 0]),
                pltpu.make_async_copy(fresh_ref.at[:, rows], fresh_buf.at[:, rows], sems.at[block, 1]),
                pltpu.make_async_copy(cached_ref.at[:, there], cached_buf.at[:, rows], sems.at[block, 2]),
            ]
        )
        for copy in copies[-1]:
            copy.start()
    for block in range(tok // PACK_ROWS):
        rows = pl.ds(block * PACK_ROWS, PACK_ROWS)
        for copy in copies[block]:
            copy.wait()
        for rel in range(split - 1, 0, -1):
            buf = bufs[split - 1 - rel]
            for chunk in range(per):
                head = (near ^ rel) * per + chunk
                lanes = pl.ds(pl.multiple_of(head * HEAD_DIM, HEAD_DIM), HEAD_DIM)
                here = pl.ds(chunk * HEAD_DIM, HEAD_DIM)
                buf[0, rows, here] = q_buf[rows, lanes]
                for stacked in range(2):
                    buf[1 + stacked, rows, here] = decode(
                        fresh_buf[stacked, rows, lanes],
                        cached_buf[stacked, rows, lanes],
                        exps_ref[stacked, block * PACK_ROWS // SCALE_ROWS, head],
                    )
            sent.append(
                pltpu.make_async_copy(
                    buf.at[:, rows],
                    outs[split - 1 - rel].at[:, rows],
                    out_sems.at[block, rel - 1],
                )
            )
            sent[-1].start()
    for copy in sent:
        copy.wait()


def pack(split, exponents, queries, fresh_kv, cached_kv):
    tok, channels = queries.shape
    feat = channels // split
    blocks = tok // PACK_ROWS
    hbm = pl.BlockSpec(memory_space=pltpu.HBM)
    return pl.pallas_call(
        functools.partial(pack_kernel, split, feat // HEAD_DIM),
        out_shape=[jax.ShapeDtypeStruct((3, tok, feat), jnp.bfloat16)] * (split - 1),
        in_specs=[pl.BlockSpec(memory_space=pltpu.SMEM), hbm, hbm, hbm],
        out_specs=[hbm] * (split - 1),
        scratch_shapes=[pltpu.VMEM((3, tok, feat), jnp.bfloat16)] * (split - 1)
        + [
            pltpu.VMEM((tok, channels), jnp.bfloat16),
            pltpu.VMEM((2, tok, channels), jnp.bfloat16),
            pltpu.VMEM((2, tok, channels), jnp.bfloat16),
            pltpu.SemaphoreType.DMA((blocks, 3)),
            pltpu.SemaphoreType.DMA((blocks, split - 1)),
        ],
        compiler_params=pltpu.CompilerParams(vmem_limit_bytes=PACK_VMEM_BYTES),
        name="pack",
    )(exponents, queries, fresh_kv, cached_kv)


def own_kernel(per, where_ref, exps_ref, q_ref, fresh_ref, cached_ref, out_ref):
    out_ref[0] = q_ref[...]
    for chunk in range(per):
        lanes = pl.ds(chunk * HEAD_DIM, HEAD_DIM)
        for block in range(q_ref.shape[0] // SCALE_ROWS):
            rows = pl.ds(block * SCALE_ROWS, SCALE_ROWS)
            for stacked in range(2):
                out_ref[1 + stacked, rows, lanes] = decode(
                    fresh_ref[stacked, rows, lanes],
                    cached_ref[stacked, rows, lanes],
                    exps_ref[stacked, block, where_ref[NEAR] * per + chunk],
                )


def pack_own(split, where, exponents, queries, fresh_kv, cached_kv):
    tok, channels = queries.shape
    feat = channels // split
    out = jax.ShapeDtypeStruct((3, tok, feat), jnp.bfloat16)
    return call(
        functools.partial(own_kernel, feat // HEAD_DIM),
        "own",
        out,
        1,
        [
            pl.BlockSpec(memory_space=pltpu.SMEM),
            pl.BlockSpec((tok, feat), lambda i, w: (0, w[NEAR])),
            pl.BlockSpec((2, tok, feat), lambda i, w: (0, 0, w[NEAR])),
            pl.BlockSpec((2, tok, feat), lambda i, w: (0, w[PATCH], w[NEAR])),
        ],
        spec(out.shape),
        flops=OWN_FLOPS,
    )(where, exponents, queries, fresh_kv, cached_kv)


def attend_kernel(split, part, where_ref, *refs):
    q_refs, kv_refs, out_ref = (refs[0], *refs[split - 1 : 0 : -1]), refs[:-1], refs[-1]
    factor = HEAD_DIM**-0.5 * math.log2(math.e)
    tok, feat = q_refs[0].shape[1:]
    count = out_ref.shape[1] // part[1]
    starts = [at * (tok // count) + part[0] for at in range(count)]
    for head in range(feat // HEAD_DIM):
        lanes = pl.ds(head * HEAD_DIM, HEAD_DIM)
        keys = jnp.concatenate([ref[1, :, lanes] for ref in kv_refs], axis=0)
        values = jnp.concatenate([ref[2, :, lanes] for ref in kv_refs], axis=0)
        values = jnp.concatenate([values, jnp.ones_like(values)], axis=1)
        for rel in range(split):
            rows = [q_refs[rel][0, start : start + part[1], lanes] for start in starts]
            query = jnp.concatenate(rows, axis=0) if len(rows) > 1 else rows[0]
            scores = lax.dot_general(
                query, keys, (((1,), (1,)), ((), ())), preferred_element_type=jnp.float32
            )
            peak = jnp.max(scores, axis=1, keepdims=True)
            expo = jnp.exp2((scores - peak) * factor).astype(jnp.bfloat16)
            mix = jnp.dot(expo, values, preferred_element_type=jnp.float32)
            mix = mix[:, :HEAD_DIM] / mix[:, HEAD_DIM:]
            out_ref[where_ref[NEAR] ^ rel, :, lanes] = mix.astype(jnp.bfloat16)


def attend(where, part, count, pieces, kv_pieces):
    split = len(pieces)
    _, tok, feat = pieces[0].shape
    out = jax.ShapeDtypeStruct((split, count * part[1], feat), jnp.bfloat16)
    return call(
        functools.partial(attend_kernel, split, part),
        "attend",
        out,
        1,
        [spec((3, tok, feat))] * len(kv_pieces),
        spec(out.shape),
        flops=ATTEND_FLOPS,
    )(where, *kv_pieces)


def project_kernel(split, n_slots, n_more, where_ref, *refs):
    slots, refs = refs[:n_slots], refs[n_slots:]
    more, weight_ref, refs = refs[:n_more], refs[n_more], refs[n_more + 1 :]
    outs, held_ref, acc_ref = refs[:-2], refs[-2], refs[-1]
    rows, feat = slots[0].shape
    n_sub, n_head = acc_ref.shape[3], acc_ref.shape[2]

    @pl.when(pl.program_id(0) == 0)
    def arrange():
        for at, slot in enumerate(slots):
            group, near = divmod(at, split)
            lane = (where_ref[NEAR] ^ near) * feat
            block = slot[...]
            if more and at == n_slots - 1:
                block = jnp.where(where_ref[INNER] == 1, block, more[0][...])
            held_ref[
                group * rows : (group + 1) * rows, pl.ds(pl.multiple_of(lane, HEAD_DIM), feat)
            ] = block

    acc = jnp.dot(held_ref[...], weight_ref[...], preferred_element_type=jnp.float32)
    acc_ref[...] = acc.reshape(acc_ref.shape)
    for sub in range(n_sub):
        for head in range(n_head):
            for at in range(n_slots):
                group, near = divmod(at, split)
                outs[sub][head, at] = acc_ref[
                    group, where_ref[NEAR] ^ near, where_ref[HEAD] ^ head, where_ref[SUB] ^ sub
                ].astype(jnp.bfloat16)


def project(split, where, slots, more, weight, n_head, n_sub):
    rows, feat = slots[0].shape
    n_patch = len(slots)
    total = rows * n_patch // split
    depth, cols = weight.shape
    wide = 640 if cols % 640 == 0 else cols
    piece = rows // (split * n_head * n_sub)
    return call(
        functools.partial(project_kernel, split, n_patch, len(more)),
        "project",
        [jax.ShapeDtypeStruct((n_head, n_patch, piece, cols), jnp.bfloat16)] * n_sub,
        cols // wide,
        [spec((rows, feat))] * (n_patch + len(more))
        + [pl.BlockSpec((depth, wide), lambda i, w: (0, i))],
        [pl.BlockSpec((n_head, n_patch, piece, wide), lambda i, w: (0, 0, 0, i))] * n_sub,
        [
            pltpu.VMEM((total, depth), jnp.bfloat16),
            pltpu.VMEM((n_patch // split, split, n_head, n_sub, piece, wide), jnp.float32),
        ],
        flops=PROJECT_FLOPS,
    )(where, *slots, *more, weight)


def mix_kernel(rels, where_ref, hidden_ref, gate_ref, *refs):
    blocks, out_ref = refs[:-1], refs[-1]
    piece, cols = blocks[0].shape
    for part in range(len(blocks) // len(rels)):
        rows = pl.ds(part * piece, piece)
        for at, rel in enumerate(rels):
            lanes = pl.ds(pl.multiple_of((where_ref[PATCH] ^ rel) * cols, HEAD_DIM), cols)
            mixed = hidden_ref[rows, lanes].astype(jnp.float32) + gate_ref[:, lanes] * blocks[
                part * len(rels) + at
            ][...].astype(jnp.float32)
            out_ref[rows, lanes] = mixed.astype(jnp.bfloat16)


def mix(where, hidden_in, attn_gate, blocks):
    rows, width = hidden_in.shape
    n_patch = len(blocks[0])
    piece, cols = blocks[0][0].shape
    if cols % HEAD_DIM:
        order = jnp.concatenate([jnp.stack(x) for x in blocks], axis=1)
        order = order[where[PATCH] ^ jnp.arange(n_patch)]
        projected = order.transpose(1, 0, 2).reshape(rows, width).astype(jnp.float32)
        return (hidden_in.astype(jnp.float32) + attn_gate * projected).astype(jnp.bfloat16)
    rels = [0, *range(n_patch - 1, 0, -1)]
    flat = [part[rel] for part in blocks for rel in rels]
    return call(
        functools.partial(mix_kernel, rels),
        "mix",
        jax.ShapeDtypeStruct((rows, width), jnp.bfloat16),
        1,
        [spec((rows, width)), spec((1, width))] + [spec((piece, cols))] * len(flat),
        spec((rows, width)),
    )(where, hidden_in, attn_gate[None], *flat)


def gather(parts, n_patch):
    if n_patch != 4:
        return [
            ([x] + [swap(x, "patch", n_patch, rel) for rel in range(1, n_patch)], [])
            for x in parts
        ]
    far = [swap(x, "patch", 4, 2) for x in parts]
    next_to = [swap(x, "patch", 4, 1) for x in parts]
    out = []
    for at, x in enumerate(parts):
        far[at], next_to[at], parts = lax.optimization_barrier((far[at], next_to[at], parts))
        middle = swap(parts[at], "patch", 4, 3, (1, 2))
        ends = lax.ppermute(far[at], "patch", [(1, 0), (2, 3)])
        if at + 1 < len(parts):
            ends, far[at + 1], next_to[at + 1] = lax.optimization_barrier(
                (ends, far[at + 1], next_to[at + 1])
            )
        out.append(([x, next_to[at], far[at], middle], [ends]))
    return out


def add_sub_kernel(n_sub, where_ref, *refs):
    terms, kept_ref, outs = refs[:n_sub], refs[n_sub], refs[n_sub + 1 :]
    for head in range(len(outs) + 1):
        total = terms[0][head].astype(jnp.float32)
        for term in terms[1:]:
            total += term[head].astype(jnp.float32)
        if head == 0:
            kept_ref[...] = total
        else:
            outs[head - 1][...] = total.astype(jnp.bfloat16)


def add_head_kernel(n_more, where_ref, kept_ref, *refs):
    for at, out in enumerate(refs[n_more:]):
        total = kept_ref[at]
        for term in refs[:n_more]:
            total += term[at].astype(jnp.float32)
        out[...] = total.astype(jnp.bfloat16)


def reduce_sub(sizes, where, terms):
    n_sub, n_head = sizes["sub"], sizes["head"]
    terms = [terms[0]] + [swap(terms[rel], "sub", n_sub, rel) for rel in range(1, n_sub)]
    shape = terms[0].shape[1:]
    return call(
        functools.partial(add_sub_kernel, n_sub),
        "add_sub",
        [jax.ShapeDtypeStruct(shape, jnp.float32)]
        + [jax.ShapeDtypeStruct(shape, jnp.bfloat16)] * (n_head - 1),
        1,
        [spec(terms[0].shape)] * n_sub,
        [spec(shape)] * n_head,
    )(where, *terms)


def reduce_head(sizes, where, sums):
    n_head = sizes["head"]
    shape = sums[0].shape
    sums = [sums[0]] + [swap(sums[rel], "head", n_head, rel) for rel in range(1, n_head)]
    return call(
        functools.partial(add_head_kernel, n_head - 1),
        "add_head",
        [jax.ShapeDtypeStruct(shape[1:], jnp.bfloat16)] * shape[0],
        1,
        [spec(shape)] * n_head,
        [spec(shape[1:])] * shape[0],
    )(where, *sums)


def sum_tail(sizes, where, pieces, kv_pieces, out_weight, hidden_in, attn_gate):
    n_patch, n_head, n_sub = sizes["patch"], sizes["head"], sizes["sub"]
    split, tok = len(pieces), pieces[0].shape[1]
    count = n_head * n_sub
    piece = tok // count
    parts = 2 if piece % 32 == 0 else 1
    attended = []
    for part in range(parts):
        rows = (part * (piece // parts), piece // parts)
        x = attend(where, rows, count, pieces, kv_pieces)
        attended.append(x.reshape(-1, x.shape[2]))
    slots = gather(attended, n_patch)
    blocks = []
    for part in range(parts):
        terms = project(split, where, *slots[part], out_weight, n_head, n_sub)
        total = reduce_head(sizes, where, reduce_sub(sizes, where, terms))
        blocks.append(
            [total[0]] + [swap(total[rel], "patch", n_patch, rel) for rel in range(1, n_patch)]
        )
    return mix(where, hidden_in, attn_gate, blocks)


def attend_half_kernel(half, where_ref, *refs):
    pieces, out = refs[:-1], refs[-1]
    factor = HEAD_DIM**-0.5 * math.log2(math.e)
    rows, feat = out.shape[1:]
    start = pl.multiple_of((where_ref[HEAD] ^ half) * rows, rows)
    for head in range(feat // HEAD_DIM):
        lanes = pl.ds(head * HEAD_DIM, HEAD_DIM)
        keys = jnp.concatenate([ref[1, :, lanes] for ref in pieces], axis=0)
        values = jnp.concatenate([ref[2, :, lanes] for ref in pieces], axis=0)
        values = jnp.concatenate([values, jnp.ones_like(values)], axis=1)
        query = jnp.concatenate([ref[0, pl.ds(start, rows), lanes] for ref in pieces], axis=0)
        scores = lax.dot_general(
            query, keys, (((1,), (1,)), ((), ())), preferred_element_type=jnp.float32
        )
        peak = jnp.max(scores, axis=1, keepdims=True)
        expo = jnp.exp2((scores - peak) * factor).astype(jnp.bfloat16)
        mix = jnp.dot(expo, values, preferred_element_type=jnp.float32)
        mix = (mix[:, :HEAD_DIM] / mix[:, HEAD_DIM:]).astype(jnp.bfloat16)
        for rel in range(len(pieces)):
            out[where_ref[NEAR] ^ rel, :, lanes] = mix[rel * rows : (rel + 1) * rows]


def attend_half(where, half, pieces):
    _, tok, feat = pieces[0].shape
    out = jax.ShapeDtypeStruct((len(pieces), tok // 2, feat), jnp.bfloat16)
    return call(
        functools.partial(attend_half_kernel, half),
        "attend",
        out,
        1,
        [spec((3, tok, feat))] * len(pieces),
        spec(out.shape),
        flops=HALF_FLOPS,
    )(where, *pieces).reshape(-1, feat)


def add_product_kernel(count, where_ref, *refs):
    total = refs[2 * count][...] if len(refs) > 2 * count + 1 else None
    for slot, weight in zip(refs[:count], refs[count : 2 * count]):
        term = jnp.dot(slot[...], weight[...], preferred_element_type=jnp.float32)
        total = term if total is None else total + term
    refs[-1][...] = total


def add_product(where, slots, weight, acc=None):
    rows, feat = next(iter(slots.values())).shape
    cols = weight.shape[1]
    wide = cols // 2
    whole = pl.BlockSpec((rows, wide), lambda i, w: (0, i))
    rels = list(slots)
    return call(
        functools.partial(add_product_kernel, len(rels)),
        "products",
        jax.ShapeDtypeStruct((rows, cols), jnp.float32),
        2,
        [spec((rows, feat))] * len(rels)
        + [pl.BlockSpec((feat, wide), lambda i, w, rel=rel: (w[NEAR] ^ rel, i)) for rel in rels]
        + ([] if acc is None else [whole]),
        whole,
        flops=ZERO_FLOPS if acc is None else 1,
    )(where, *slots.values(), *[weight] * len(rels), *([] if acc is None else [acc]))


def partner_place(where_ref, head):
    return (head + FETCHED * where_ref[GRP]) % 8


def first_kernel(where_ref, *refs):
    last, more, slots = refs[0], refs[1], refs[2:5]
    acc_ref, own_ref, fetched_ref, passed_ref, out_ref, held_ref = refs[5:]
    rows, feat = last.shape
    cut = fetched_ref.shape[0]

    def put(at, block):
        for head in range(2):
            there = partner_place(where_ref, 2 * (where_ref[NEAR] ^ at) + head)
            lanes = pl.ds(pl.multiple_of(there * HEAD_DIM, HEAD_DIM), HEAD_DIM)
            held_ref[:, lanes] = block[:, head * HEAD_DIM : (head + 1) * HEAD_DIM]

    @pl.when(pl.program_id(0) == 0)
    def arrange():
        for at, slot in zip((0, 2, 1), slots):
            put(at, slot[...])
        put(3, jnp.zeros((rows, feat), jnp.bfloat16))

    block = jnp.where(where_ref[INNER] == 1, last[...], more[...])
    acc = acc_ref[...]
    acc += jnp.dot(block, own_ref[...], preferred_element_type=jnp.float32)
    acc += jnp.dot(held_ref[:, :cut], fetched_ref[...], preferred_element_type=jnp.float32)
    acc += jnp.dot(held_ref[:, cut:], passed_ref[...], preferred_element_type=jnp.float32)
    out_ref[...] = acc


def first_product(where, last, more, slots, acc, weights):
    rows, feat = last.shape
    own, fetched, passed = weights
    wide = own.shape[1] // 2
    whole = pl.BlockSpec((rows, wide), lambda i, w: (0, i))
    return call(
        first_kernel,
        "first",
        jax.ShapeDtypeStruct(acc.shape, jnp.float32),
        2,
        [spec((rows, feat))] * 5
        + [whole, pl.BlockSpec((feat, wide), lambda i, w: (w[NEAR] ^ 3, i))]
        + [pl.BlockSpec((x.shape[0], wide), lambda i, w: (0, i)) for x in (fetched, passed)],
        whole,
        [pltpu.VMEM((rows, 4 * feat), jnp.bfloat16)],
    )(where, last, more, *slots, acc, own, fetched, passed)


def second_kernel(where_ref, slot, more, fetched_ref, passed_ref, acc_in, keep_ref, send_ref, acc_ref):
    weight = []
    for head in range(2):
        place = partner_place(where_ref, 2 * (where_ref[NEAR] ^ 3) + head)
        here = jnp.minimum(place, FETCHED - 1) * HEAD_DIM
        there = jnp.maximum(place - FETCHED, 0) * HEAD_DIM
        weight.append(
            jnp.where(
                place < FETCHED,
                fetched_ref[pl.ds(pl.multiple_of(here, HEAD_DIM), HEAD_DIM), :],
                passed_ref[pl.ds(pl.multiple_of(there, HEAD_DIM), HEAD_DIM), :],
            )
        )
    block = jnp.where(where_ref[INNER] == 1, slot[...], more[...])
    acc = acc_in[...] + jnp.dot(
        block, jnp.concatenate(weight, axis=0), preferred_element_type=jnp.float32
    )
    acc_ref[...] = acc.reshape(acc_ref.shape)
    for sub, out in enumerate((keep_ref, send_ref)):
        for at in range(4):
            out[at] = acc_ref[where_ref[NEAR] ^ at, where_ref[SUB] ^ sub].astype(jnp.bfloat16)


def second_product(where, chunk, slot, more, weights, acc):
    rows, feat = slot.shape
    cols = weights[0].shape[1]
    wide = cols // 2
    out = jax.ShapeDtypeStruct((4, rows // 8, wide), jnp.bfloat16)
    return call(
        second_kernel,
        "second",
        [out] * 2,
        1,
        [spec((rows, feat))] * 2
        + [pl.BlockSpec((x.shape[0], wide), lambda i, w: (0, chunk)) for x in weights]
        + [pl.BlockSpec((rows, wide), lambda i, w: (0, chunk))],
        [spec(out.shape)] * 2,
        [pltpu.VMEM((4, 2, rows // 8, wide), jnp.float32)],
    )(where, slot, more, *weights, acc)


def add_kernel(where_ref, keep_ref, term_ref, *outs):
    for at, out in enumerate(outs):
        total = keep_ref[at].astype(jnp.float32) + term_ref[at].astype(jnp.float32)
        out[...] = total.astype(jnp.bfloat16)


def add(where, keep, term):
    return call(
        add_kernel,
        "add",
        [jax.ShapeDtypeStruct(keep.shape[1:], jnp.bfloat16)] * keep.shape[0],
        1,
        [spec(keep.shape)] * 2,
        [spec(keep.shape[1:])] * keep.shape[0],
    )(where, keep, term)


def share_tail(sizes, where, pieces, kv_pieces, out_weight, hidden_in, attn_gate):
    fetch, pass_on = FETCHED * HEAD_DIM, (8 - FETCHED) * HEAD_DIM
    out_weight, where = lax.optimization_barrier((out_weight, where))
    start = lax.axis_index("grp") * pass_on
    fetched = swap(lax.dynamic_slice_in_dim(out_weight, start, fetch, 0), "head", 2, 1)
    start = lax.axis_index("grp") * (fetch - pass_on)
    passed = swap(lax.dynamic_slice_in_dim(fetched, start, pass_on, 0), "grp", 2, 1)

    pieces = [pieces[0], *pieces[:0:-1]]
    mine = attend_half(where, 0, pieces)
    where, mine = lax.optimization_barrier((where, mine))
    other = swap(attend_half(where, 1, pieces), "head", 2, 1)
    acc = add_product(where, {0: mine}, out_weight)
    other, acc = lax.optimization_barrier((other, acc))
    slots = []
    for at, x in enumerate((mine, other)):
        next_to, far = swap(x, "patch", 4, 1), swap(x, "patch", 4, 2)
        next_to, far, other, x = lax.optimization_barrier((next_to, far, other, x))
        if at == 1:
            acc = add_product(where, {2: slots[0][2], 1: slots[0][1]}, out_weight, acc)
            far, x, acc = lax.optimization_barrier((far, x, acc))
        middle = swap(x, "patch", 4, 3, (1, 2))
        ends = lax.ppermute(far, "patch", [(1, 0), (2, 3)])
        slots.append([x, next_to, far, middle, ends])
    weights = [out_weight, fetched, passed]
    partner = [slots[1][at] for at in (0, 2, 1)]
    acc = first_product(where, *slots[0][3:], partner, acc, weights)
    terms = [second_product(where, at, *slots[1][3:], [fetched, passed], acc) for at in range(2)]
    blocks = []
    for keep, send in terms:
        total = add(where, keep, swap(send, "sub", 2, 1))
        blocks.append([total[0]] + [swap(total[rel], "patch", 4, rel) for rel in range(3, 0, -1)])
    return mix_columns(where, hidden_in, attn_gate, blocks)


def mix_columns_kernel(where_ref, hidden_ref, gate_ref, *refs):
    blocks, out_ref = refs[:-1], refs[-1]
    cols = blocks[0].shape[1]
    for chunk in range(2):
        for at, rel in enumerate((0, 3, 2, 1)):
            start = (2 * (where_ref[PATCH] ^ rel) + chunk) * cols
            lanes = pl.ds(pl.multiple_of(start, HEAD_DIM), cols)
            mixed = hidden_ref[:, lanes].astype(jnp.float32) + gate_ref[:, lanes] * blocks[
                4 * chunk + at
            ][...].astype(jnp.float32)
            out_ref[:, lanes] = mixed.astype(jnp.bfloat16)


def mix_columns(where, hidden_in, attn_gate, blocks):
    rows, width = hidden_in.shape
    flat = [x for chunk in blocks for x in chunk]
    return call(
        mix_columns_kernel,
        "mix",
        jax.ShapeDtypeStruct((rows, width), jnp.bfloat16),
        2,
        [pl.BlockSpec((rows // 2, width), lambda i, w: (i, 0)), spec((1, width))]
        + [pl.BlockSpec((rows // 2, flat[0].shape[1]), lambda i, w: (i, 0))] * len(flat),
        pl.BlockSpec((rows // 2, width), lambda i, w: (i, 0)),
    )(where, hidden_in, attn_gate[None], *flat)


def body(sizes, queries, fresh_kv, cached_kv, exponents, out_weight, hidden_in, attn_gate):
    n_patch, n_head, n_sub = sizes["patch"], sizes["head"], sizes["sub"]
    tok, channels = queries.shape
    heads = channels // HEAD_DIM
    split = math.gcd(heads, n_patch)
    patch_at = lax.axis_index("patch")
    inner = (patch_at > 0) & (patch_at < n_patch - 1)
    where = jnp.stack(
        [
            patch_at,
            patch_at % split,
            lax.axis_index("head"),
            lax.axis_index("sub"),
            inner,
            lax.axis_index("grp"),
        ]
    ).astype(jnp.int32)

    arrays = (exponents, queries, fresh_kv, cached_kv)
    sent = pack(split, *arrays)
    far_first = [
        swap(x, "patch", n_patch, split - 1 - at) for at, x in enumerate(sent)
    ]
    where, sent = lax.optimization_barrier((where, sent))
    pieces = [pack_own(split, where, *arrays), *far_first]
    kv_pieces = list(pieces)
    for rel in range(split, n_patch, split):
        kv_pieces += [swap(x, "patch", n_patch, rel) for x in pieces]

    tail = (sizes, where, pieces, kv_pieces, out_weight, hidden_in, attn_gate)
    if (sizes["grp"], n_head, split, n_patch) == (2, 2, 4, 4):
        return share_tail(*tail)
    return sum_tail(*tail)


def solution(mesh):
    in_specs = (
        P(("grp", "patch"), ("head", "sub")),
        P(None, ("grp", "patch"), ("head", "sub")),
        P(None, "grp", ("head", "sub")),
        P(None, ("grp", "patch"), ("head", "sub")),
        P(("head", "sub"), "patch"),
        P(("grp", "patch", "head", "sub"), None),
        P(),
    )
    out_specs = P(("grp", "patch", "head", "sub"), None)
    return jax.shard_map(
        functools.partial(body, dict(mesh.shape)),
        mesh=mesh,
        in_specs=in_specs,
        out_specs=out_specs,
        check_vma=False,
    )
```

```python
import functools
import math

import jax
import jax.numpy as jnp
from jax import lax
from jax.experimental import pallas as pl
from jax.experimental.pallas import tpu as pltpu
from jax.sharding import PartitionSpec as P

HEAD_DIM = 128
SCALE_ROWS = 128
SATURATION = 448.0
PACK_ROWS = 64
VMEM_BYTES = 32 * 1024 * 1024
PACK_VMEM_BYTES = 60 * 1024 * 1024
ATTEND_FLOPS = 1
PROJECT_FLOPS = 1
OWN_FLOPS = 50_000_000_000
FETCHED = 5
ZERO_FLOPS = 20_000_000_000
HALF_FLOPS = 1

PATCH, NEAR, HEAD, SUB, INNER, GRP = range(6)


def spec(shape):
    return pl.BlockSpec(shape, lambda i, w: (0,) * len(shape))


def call(kernel, name, out_shape, grid, in_specs, out_specs, scratch=(), flops=1, vmem=VMEM_BYTES):
    return pl.pallas_call(
        kernel,
        out_shape=out_shape,
        grid_spec=pltpu.PrefetchScalarGridSpec(
            num_scalar_prefetch=1,
            grid=(grid,),
            in_specs=in_specs,
            out_specs=out_specs,
            scratch_shapes=list(scratch),
        ),
        compiler_params=pltpu.CompilerParams(vmem_limit_bytes=vmem),
        cost_estimate=pl.CostEstimate(flops=flops, bytes_accessed=0, transcendentals=0),
        name=name,
    )


def swap(x, axes, count, mask, only=None):
    pairs = [(at, at ^ mask) for at in range(count) if only is None or at in only]
    return lax.ppermute(x, axes, pairs)


def decode(fresh, cached, exponent):
    power = jnp.full((1, HEAD_DIM), exponent.astype(jnp.float32))
    cached = cached.astype(jnp.float32)
    residual = fresh.astype(jnp.float32) - cached
    codes = jnp.clip(residual * jnp.exp2(-power), -SATURATION, SATURATION).astype(jnp.bfloat16)
    return (cached + codes.astype(jnp.float32) * jnp.exp2(power)).astype(jnp.bfloat16)


def pack_kernel(split, per, exps_ref, q_ref, fresh_ref, cached_ref, *refs):
    outs, bufs = refs[: split - 1], refs[split - 1 : 2 * split - 2]
    q_buf, fresh_buf, cached_buf, sems, out_sems = refs[2 * split - 2 :]
    patch = lax.axis_index("patch")
    near = lax.rem(patch, split)
    tok = q_buf.shape[0]
    copies, sent = [], []
    for block in range(tok // PACK_ROWS):
        rows = pl.ds(block * PACK_ROWS, PACK_ROWS)
        there = pl.ds(pl.multiple_of(patch * tok + block * PACK_ROWS, PACK_ROWS), PACK_ROWS)
        copies.append(
            [
                pltpu.make_async_copy(q_ref.at[rows], q_buf.at[rows], sems.at[block, 0]),
                pltpu.make_async_copy(fresh_ref.at[:, rows], fresh_buf.at[:, rows], sems.at[block, 1]),
                pltpu.make_async_copy(cached_ref.at[:, there], cached_buf.at[:, rows], sems.at[block, 2]),
            ]
        )
        for copy in copies[-1]:
            copy.start()
    for block in range(tok // PACK_ROWS):
        rows = pl.ds(block * PACK_ROWS, PACK_ROWS)
        for copy in copies[block]:
            copy.wait()
        for rel in range(split - 1, 0, -1):
            buf = bufs[split - 1 - rel]
            for chunk in range(per):
                head = (near ^ rel) * per + chunk
                lanes = pl.ds(pl.multiple_of(head * HEAD_DIM, HEAD_DIM), HEAD_DIM)
                here = pl.ds(chunk * HEAD_DIM, HEAD_DIM)
                buf[0, rows, here] = q_buf[rows, lanes]
                for stacked in range(2):
                    buf[1 + stacked, rows, here] = decode(
                        fresh_buf[stacked, rows, lanes],
                        cached_buf[stacked, rows, lanes],
                        exps_ref[stacked, block * PACK_ROWS // SCALE_ROWS, head],
                    )
            sent.append(
                pltpu.make_async_copy(
                    buf.at[:, rows],
                    outs[split - 1 - rel].at[:, rows],
                    out_sems.at[block, rel - 1],
                )
            )
            sent[-1].start()
    for copy in sent:
        copy.wait()


def pack(split, exponents, queries, fresh_kv, cached_kv):
    tok, channels = queries.shape
    feat = channels // split
    blocks = tok // PACK_ROWS
    hbm = pl.BlockSpec(memory_space=pltpu.HBM)
    return pl.pallas_call(
        functools.partial(pack_kernel, split, feat // HEAD_DIM),
        out_shape=[jax.ShapeDtypeStruct((3, tok, feat), jnp.bfloat16)] * (split - 1),
        in_specs=[pl.BlockSpec(memory_space=pltpu.SMEM), hbm, hbm, hbm],
        out_specs=[hbm] * (split - 1),
        scratch_shapes=[pltpu.VMEM((3, tok, feat), jnp.bfloat16)] * (split - 1)
        + [
            pltpu.VMEM((tok, channels), jnp.bfloat16),
            pltpu.VMEM((2, tok, channels), jnp.bfloat16),
            pltpu.VMEM((2, tok, channels), jnp.bfloat16),
            pltpu.SemaphoreType.DMA((blocks, 3)),
            pltpu.SemaphoreType.DMA((blocks, split - 1)),
        ],
        compiler_params=pltpu.CompilerParams(vmem_limit_bytes=PACK_VMEM_BYTES),
        name="pack",
    )(exponents, queries, fresh_kv, cached_kv)


def own_kernel(per, where_ref, exps_ref, q_ref, fresh_ref, cached_ref, out_ref):
    out_ref[0] = q_ref[...]
    for chunk in range(per):
        lanes = pl.ds(chunk * HEAD_DIM, HEAD_DIM)
        for block in range(q_ref.shape[0] // SCALE_ROWS):
            rows = pl.ds(block * SCALE_ROWS, SCALE_ROWS)
            for stacked in range(2):
                out_ref[1 + stacked, rows, lanes] = decode(
                    fresh_ref[stacked, rows, lanes],
                    cached_ref[stacked, rows, lanes],
                    exps_ref[stacked, block, where_ref[NEAR] * per + chunk],
                )


def pack_own(split, where, exponents, queries, fresh_kv, cached_kv):
    tok, channels = queries.shape
    feat = channels // split
    patch_at, near = where[PATCH], where[NEAR]
    queries = lax.dynamic_slice_in_dim(queries, near * feat, feat, 1)
    fresh_kv = lax.dynamic_slice_in_dim(fresh_kv, near * feat, feat, 2)
    cached_kv = lax.dynamic_slice(cached_kv, (0, patch_at * tok, near * feat), (2, tok, feat))
    out = jax.ShapeDtypeStruct((3, tok, feat), jnp.bfloat16)
    return call(
        functools.partial(own_kernel, feat // HEAD_DIM),
        "own",
        out,
        1,
        [pl.BlockSpec(memory_space=pltpu.SMEM)]
        + [spec(x.shape) for x in (queries, fresh_kv, cached_kv)],
        spec(out.shape),
        flops=OWN_FLOPS,
    )(where, exponents, queries, fresh_kv, cached_kv)


def attend_kernel(split, part, where_ref, *refs):
    q_refs, kv_refs, out_ref = (refs[0], *refs[split - 1 : 0 : -1]), refs[:-1], refs[-1]
    factor = HEAD_DIM**-0.5 * math.log2(math.e)
    tok, feat = q_refs[0].shape[1:]
    count = out_ref.shape[1] // part[1]
    starts = [at * (tok // count) + part[0] for at in range(count)]
    for head in range(feat // HEAD_DIM):
        lanes = pl.ds(head * HEAD_DIM, HEAD_DIM)
        keys = jnp.concatenate([ref[1, :, lanes] for ref in kv_refs], axis=0)
        values = jnp.concatenate([ref[2, :, lanes] for ref in kv_refs], axis=0)
        values = jnp.concatenate([values, jnp.ones_like(values)], axis=1)
        for rel in range(split):
            rows = [q_refs[rel][0, start : start + part[1], lanes] for start in starts]
            query = jnp.concatenate(rows, axis=0) if len(rows) > 1 else rows[0]
            scores = lax.dot_general(
                query, keys, (((1,), (1,)), ((), ())), preferred_element_type=jnp.float32
            )
            peak = jnp.max(scores, axis=1, keepdims=True)
            expo = jnp.exp2((scores - peak) * factor).astype(jnp.bfloat16)
            mix = jnp.dot(expo, values, preferred_element_type=jnp.float32)
            mix = mix[:, :HEAD_DIM] / mix[:, HEAD_DIM:]
            out_ref[where_ref[NEAR] ^ rel, :, lanes] = mix.astype(jnp.bfloat16)


def attend(where, part, count, pieces, kv_pieces):
    split = len(pieces)
    _, tok, feat = pieces[0].shape
    out = jax.ShapeDtypeStruct((split, count * part[1], feat), jnp.bfloat16)
    return call(
        functools.partial(attend_kernel, split, part),
        "attend",
        out,
        1,
        [spec((3, tok, feat))] * len(kv_pieces),
        spec(out.shape),
        flops=ATTEND_FLOPS,
    )(where, *kv_pieces)


def project_kernel(split, n_slots, n_more, where_ref, *refs):
    slots, refs = refs[:n_slots], refs[n_slots:]
    more, weight_ref, refs = refs[:n_more], refs[n_more], refs[n_more + 1 :]
    outs, held_ref, acc_ref = refs[:-2], refs[-2], refs[-1]
    rows, feat = slots[0].shape
    n_sub, n_head = acc_ref.shape[3], acc_ref.shape[2]

    @pl.when(pl.program_id(0) == 0)
    def arrange():
        for at, slot in enumerate(slots):
            group, near = divmod(at, split)
            lane = (where_ref[NEAR] ^ near) * feat
            block = slot[...]
            if more and at == n_slots - 1:
                block = jnp.where(where_ref[INNER] == 1, block, more[0][...])
            held_ref[
                group * rows : (group + 1) * rows, pl.ds(pl.multiple_of(lane, HEAD_DIM), feat)
            ] = block

    acc = jnp.dot(held_ref[...], weight_ref[...], preferred_element_type=jnp.float32)
    acc_ref[...] = acc.reshape(acc_ref.shape)
    for sub in range(n_sub):
        for head in range(n_head):
            for at in range(n_slots):
                group, near = divmod(at, split)
                outs[sub][head, at] = acc_ref[
                    group, where_ref[NEAR] ^ near, where_ref[HEAD] ^ head, where_ref[SUB] ^ sub
                ].astype(jnp.bfloat16)


def project(split, where, slots, more, weight, n_head, n_sub):
    rows, feat = slots[0].shape
    n_patch = len(slots)
    total = rows * n_patch // split
    depth, cols = weight.shape
    wide = 640 if cols % 640 == 0 else cols
    piece = rows // (split * n_head * n_sub)
    return call(
        functools.partial(project_kernel, split, n_patch, len(more)),
        "project",
        [jax.ShapeDtypeStruct((n_head, n_patch, piece, cols), jnp.bfloat16)] * n_sub,
        cols // wide,
        [spec((rows, feat))] * (n_patch + len(more))
        + [pl.BlockSpec((depth, wide), lambda i, w: (0, i))],
        [pl.BlockSpec((n_head, n_patch, piece, wide), lambda i, w: (0, 0, 0, i))] * n_sub,
        [
            pltpu.VMEM((total, depth), jnp.bfloat16),
            pltpu.VMEM((n_patch // split, split, n_head, n_sub, piece, wide), jnp.float32),
        ],
        flops=PROJECT_FLOPS,
    )(where, *slots, *more, weight)


def mix_kernel(rels, where_ref, hidden_ref, gate_ref, *refs):
    blocks, out_ref = refs[:-1], refs[-1]
    piece, cols = blocks[0].shape
    for part in range(len(blocks) // len(rels)):
        rows = pl.ds(part * piece, piece)
        for at, rel in enumerate(rels):
            lanes = pl.ds(pl.multiple_of((where_ref[PATCH] ^ rel) * cols, HEAD_DIM), cols)
            mixed = hidden_ref[rows, lanes].astype(jnp.float32) + gate_ref[:, lanes] * blocks[
                part * len(rels) + at
            ][...].astype(jnp.float32)
            out_ref[rows, lanes] = mixed.astype(jnp.bfloat16)


def mix(where, hidden_in, attn_gate, blocks):
    rows, width = hidden_in.shape
    n_patch = len(blocks[0])
    piece, cols = blocks[0][0].shape
    if cols % HEAD_DIM:
        order = jnp.concatenate([jnp.stack(x) for x in blocks], axis=1)
        order = order[where[PATCH] ^ jnp.arange(n_patch)]
        projected = order.transpose(1, 0, 2).reshape(rows, width).astype(jnp.float32)
        return (hidden_in.astype(jnp.float32) + attn_gate * projected).astype(jnp.bfloat16)
    rels = [0, *range(n_patch - 1, 0, -1)]
    flat = [part[rel] for part in blocks for rel in rels]
    return call(
        functools.partial(mix_kernel, rels),
        "mix",
        jax.ShapeDtypeStruct((rows, width), jnp.bfloat16),
        1,
        [spec((rows, width)), spec((1, width))] + [spec((piece, cols))] * len(flat),
        spec((rows, width)),
    )(where, hidden_in, attn_gate[None], *flat)


def gather(parts, n_patch):
    if n_patch != 4:
        return [
            ([x] + [swap(x, "patch", n_patch, rel) for rel in range(1, n_patch)], [])
            for x in parts
        ]
    far = [swap(x, "patch", 4, 2) for x in parts]
    next_to = [swap(x, "patch", 4, 1) for x in parts]
    out = []
    for at, x in enumerate(parts):
        far[at], next_to[at], parts = lax.optimization_barrier((far[at], next_to[at], parts))
        middle = swap(parts[at], "patch", 4, 3, (1, 2))
        ends = lax.ppermute(far[at], "patch", [(1, 0), (2, 3)])
        if at + 1 < len(parts):
            ends, far[at + 1], next_to[at + 1] = lax.optimization_barrier(
                (ends, far[at + 1], next_to[at + 1])
            )
        out.append(([x, next_to[at], far[at], middle], [ends]))
    return out


def add_sub_kernel(n_sub, where_ref, *refs):
    terms, kept_ref, outs = refs[:n_sub], refs[n_sub], refs[n_sub + 1 :]
    for head in range(len(outs) + 1):
        total = terms[0][head].astype(jnp.float32)
        for term in terms[1:]:
            total += term[head].astype(jnp.float32)
        if head == 0:
            kept_ref[...] = total
        else:
            outs[head - 1][...] = total.astype(jnp.bfloat16)


def add_head_kernel(n_more, where_ref, kept_ref, *refs):
    for at, out in enumerate(refs[n_more:]):
        total = kept_ref[at]
        for term in refs[:n_more]:
            total += term[at].astype(jnp.float32)
        out[...] = total.astype(jnp.bfloat16)


def reduce_sub(sizes, where, terms):
    n_sub, n_head = sizes["sub"], sizes["head"]
    terms = [terms[0]] + [swap(terms[rel], "sub", n_sub, rel) for rel in range(1, n_sub)]
    shape = terms[0].shape[1:]
    return call(
        functools.partial(add_sub_kernel, n_sub),
        "add_sub",
        [jax.ShapeDtypeStruct(shape, jnp.float32)]
        + [jax.ShapeDtypeStruct(shape, jnp.bfloat16)] * (n_head - 1),
        1,
        [spec(terms[0].shape)] * n_sub,
        [spec(shape)] * n_head,
    )(where, *terms)


def reduce_head(sizes, where, sums):
    n_head = sizes["head"]
    shape = sums[0].shape
    sums = [sums[0]] + [swap(sums[rel], "head", n_head, rel) for rel in range(1, n_head)]
    return call(
        functools.partial(add_head_kernel, n_head - 1),
        "add_head",
        [jax.ShapeDtypeStruct(shape[1:], jnp.bfloat16)] * shape[0],
        1,
        [spec(shape)] * n_head,
        [spec(shape[1:])] * shape[0],
    )(where, *sums)


def sum_tail(sizes, where, pieces, kv_pieces, out_weight, hidden_in, attn_gate):
    n_patch, n_head, n_sub = sizes["patch"], sizes["head"], sizes["sub"]
    split, tok = len(pieces), pieces[0].shape[1]
    count = n_head * n_sub
    piece = tok // count
    parts = 2 if piece % 32 == 0 else 1
    attended = []
    for part in range(parts):
        rows = (part * (piece // parts), piece // parts)
        x = attend(where, rows, count, pieces, kv_pieces)
        attended.append(x.reshape(-1, x.shape[2]))
    slots = gather(attended, n_patch)
    blocks = []
    for part in range(parts):
        terms = project(split, where, *slots[part], out_weight, n_head, n_sub)
        total = reduce_head(sizes, where, reduce_sub(sizes, where, terms))
        blocks.append(
            [total[0]] + [swap(total[rel], "patch", n_patch, rel) for rel in range(1, n_patch)]
        )
    return mix(where, hidden_in, attn_gate, blocks)


def attend_half_kernel(half, where_ref, *refs):
    pieces, out = refs[:-1], refs[-1]
    factor = HEAD_DIM**-0.5 * math.log2(math.e)
    rows, feat = out.shape[1:]
    start = pl.multiple_of((where_ref[HEAD] ^ half) * rows, rows)
    for head in range(feat // HEAD_DIM):
        lanes = pl.ds(head * HEAD_DIM, HEAD_DIM)
        keys = jnp.concatenate([ref[1, :, lanes] for ref in pieces], axis=0)
        values = jnp.concatenate([ref[2, :, lanes] for ref in pieces], axis=0)
        values = jnp.concatenate([values, jnp.ones_like(values)], axis=1)
        query = jnp.concatenate([ref[0, pl.ds(start, rows), lanes] for ref in pieces], axis=0)
        scores = lax.dot_general(
            query, keys, (((1,), (1,)), ((), ())), preferred_element_type=jnp.float32
        )
        peak = jnp.max(scores, axis=1, keepdims=True)
        expo = jnp.exp2((scores - peak) * factor).astype(jnp.bfloat16)
        mix = jnp.dot(expo, values, preferred_element_type=jnp.float32)
        mix = (mix[:, :HEAD_DIM] / mix[:, HEAD_DIM:]).astype(jnp.bfloat16)
        for rel in range(len(pieces)):
            out[where_ref[NEAR] ^ rel, :, lanes] = mix[rel * rows : (rel + 1) * rows]


def attend_half(where, half, pieces):
    _, tok, feat = pieces[0].shape
    out = jax.ShapeDtypeStruct((len(pieces), tok // 2, feat), jnp.bfloat16)
    return call(
        functools.partial(attend_half_kernel, half),
        "attend",
        out,
        1,
        [spec((3, tok, feat))] * len(pieces),
        spec(out.shape),
        flops=HALF_FLOPS,
    )(where, *pieces).reshape(-1, feat)


def add_product_kernel(count, where_ref, *refs):
    total = refs[2 * count][...] if len(refs) > 2 * count + 1 else None
    for slot, weight in zip(refs[:count], refs[count : 2 * count]):
        term = jnp.dot(slot[...], weight[...], preferred_element_type=jnp.float32)
        total = term if total is None else total + term
    refs[-1][...] = total


def add_product(where, slots, weight, acc=None):
    rows, feat = next(iter(slots.values())).shape
    cols = weight.shape[1]
    wide = cols // 2
    whole = pl.BlockSpec((rows, wide), lambda i, w: (0, i))
    rels = list(slots)
    return call(
        functools.partial(add_product_kernel, len(rels)),
        "products",
        jax.ShapeDtypeStruct((rows, cols), jnp.float32),
        2,
        [spec((rows, feat))] * len(rels)
        + [pl.BlockSpec((feat, wide), lambda i, w, rel=rel: (w[NEAR] ^ rel, i)) for rel in rels]
        + ([] if acc is None else [whole]),
        whole,
        flops=ZERO_FLOPS if acc is None else 1,
    )(where, *slots.values(), *[weight] * len(rels), *([] if acc is None else [acc]))


def partner_place(where_ref, head):
    return (head + FETCHED * where_ref[GRP]) % 8


def first_kernel(where_ref, *refs):
    last, more, slots = refs[0], refs[1], refs[2:5]
    acc_ref, own_ref, fetched_ref, passed_ref, out_ref, held_ref = refs[5:]
    rows, feat = last.shape
    cut = fetched_ref.shape[0]

    def put(at, block):
        for head in range(2):
            there = partner_place(where_ref, 2 * (where_ref[NEAR] ^ at) + head)
            lanes = pl.ds(pl.multiple_of(there * HEAD_DIM, HEAD_DIM), HEAD_DIM)
            held_ref[:, lanes] = block[:, head * HEAD_DIM : (head + 1) * HEAD_DIM]

    @pl.when(pl.program_id(0) == 0)
    def arrange():
        for at, slot in zip((0, 2, 1), slots):
            put(at, slot[...])
        put(3, jnp.zeros((rows, feat), jnp.bfloat16))

    block = jnp.where(where_ref[INNER] == 1, last[...], more[...])
    acc = acc_ref[...]
    acc += jnp.dot(block, own_ref[...], preferred_element_type=jnp.float32)
    acc += jnp.dot(held_ref[:, :cut], fetched_ref[...], preferred_element_type=jnp.float32)
    acc += jnp.dot(held_ref[:, cut:], passed_ref[...], preferred_element_type=jnp.float32)
    out_ref[...] = acc


def first_product(where, last, more, slots, acc, weights):
    rows, feat = last.shape
    own, fetched, passed = weights
    wide = own.shape[1] // 2
    whole = pl.BlockSpec((rows, wide), lambda i, w: (0, i))
    return call(
        first_kernel,
        "first",
        jax.ShapeDtypeStruct(acc.shape, jnp.float32),
        2,
        [spec((rows, feat))] * 5
        + [whole, pl.BlockSpec((feat, wide), lambda i, w: (w[NEAR] ^ 3, i))]
        + [pl.BlockSpec((x.shape[0], wide), lambda i, w: (0, i)) for x in (fetched, passed)],
        whole,
        [pltpu.VMEM((rows, 4 * feat), jnp.bfloat16)],
    )(where, last, more, *slots, acc, own, fetched, passed)


def second_kernel(where_ref, slot, more, fetched_ref, passed_ref, acc_in, keep_ref, send_ref, acc_ref):
    weight = []
    for head in range(2):
        place = partner_place(where_ref, 2 * (where_ref[NEAR] ^ 3) + head)
        here = jnp.minimum(place, FETCHED - 1) * HEAD_DIM
        there = jnp.maximum(place - FETCHED, 0) * HEAD_DIM
        weight.append(
            jnp.where(
                place < FETCHED,
                fetched_ref[pl.ds(pl.multiple_of(here, HEAD_DIM), HEAD_DIM), :],
                passed_ref[pl.ds(pl.multiple_of(there, HEAD_DIM), HEAD_DIM), :],
            )
        )
    block = jnp.where(where_ref[INNER] == 1, slot[...], more[...])
    acc = acc_in[...] + jnp.dot(
        block, jnp.concatenate(weight, axis=0), preferred_element_type=jnp.float32
    )
    acc_ref[...] = acc.reshape(acc_ref.shape)
    for sub, out in enumerate((keep_ref, send_ref)):
        for at in range(4):
            out[at] = acc_ref[where_ref[NEAR] ^ at, where_ref[SUB] ^ sub].astype(jnp.bfloat16)


def second_product(where, chunk, slot, more, weights, acc):
    rows, feat = slot.shape
    cols = weights[0].shape[1]
    wide = cols // 2
    out = jax.ShapeDtypeStruct((4, rows // 8, wide), jnp.bfloat16)
    return call(
        second_kernel,
        "second",
        [out] * 2,
        1,
        [spec((rows, feat))] * 2
        + [pl.BlockSpec((x.shape[0], wide), lambda i, w: (0, chunk)) for x in weights]
        + [pl.BlockSpec((rows, wide), lambda i, w: (0, chunk))],
        [spec(out.shape)] * 2,
        [pltpu.VMEM((4, 2, rows // 8, wide), jnp.float32)],
    )(where, slot, more, *weights, acc)


def add_kernel(where_ref, keep_ref, term_ref, *outs):
    for at, out in enumerate(outs):
        total = keep_ref[at].astype(jnp.float32) + term_ref[at].astype(jnp.float32)
        out[...] = total.astype(jnp.bfloat16)


def add(where, keep, term):
    return call(
        add_kernel,
        "add",
        [jax.ShapeDtypeStruct(keep.shape[1:], jnp.bfloat16)] * keep.shape[0],
        1,
        [spec(keep.shape)] * 2,
        [spec(keep.shape[1:])] * keep.shape[0],
    )(where, keep, term)


def share_tail(sizes, where, pieces, kv_pieces, out_weight, hidden_in, attn_gate):
    fetch, pass_on = FETCHED * HEAD_DIM, (8 - FETCHED) * HEAD_DIM
    out_weight, where = lax.optimization_barrier((out_weight, where))
    start = lax.axis_index("grp") * pass_on
    fetched = swap(lax.dynamic_slice_in_dim(out_weight, start, fetch, 0), "head", 2, 1)
    start = lax.axis_index("grp") * (fetch - pass_on)
    passed = swap(lax.dynamic_slice_in_dim(fetched, start, pass_on, 0), "grp", 2, 1)

    pieces = [pieces[0], *pieces[:0:-1]]
    mine = attend_half(where, 0, pieces)
    where, mine = lax.optimization_barrier((where, mine))
    other = swap(attend_half(where, 1, pieces), "head", 2, 1)
    acc = add_product(where, {0: mine}, out_weight)
    other, acc = lax.optimization_barrier((other, acc))
    slots = []
    for at, x in enumerate((mine, other)):
        next_to, far = swap(x, "patch", 4, 1), swap(x, "patch", 4, 2)
        next_to, far, other, x = lax.optimization_barrier((next_to, far, other, x))
        if at == 1:
            acc = add_product(where, {2: slots[0][2], 1: slots[0][1]}, out_weight, acc)
            far, x, acc = lax.optimization_barrier((far, x, acc))
        middle = swap(x, "patch", 4, 3, (1, 2))
        ends = lax.ppermute(far, "patch", [(1, 0), (2, 3)])
        slots.append([x, next_to, far, middle, ends])
    weights = [out_weight, fetched, passed]
    partner = [slots[1][at] for at in (0, 2, 1)]
    acc = first_product(where, *slots[0][3:], partner, acc, weights)
    terms = [second_product(where, at, *slots[1][3:], [fetched, passed], acc) for at in range(2)]
    blocks = []
    for keep, send in terms:
        total = add(where, keep, swap(send, "sub", 2, 1))
        blocks.append([total[0]] + [swap(total[rel], "patch", 4, rel) for rel in range(3, 0, -1)])
    return mix_columns(where, hidden_in, attn_gate, blocks)


def mix_columns_kernel(where_ref, hidden_ref, gate_ref, *refs):
    blocks, out_ref = refs[:-1], refs[-1]
    cols = blocks[0].shape[1]
    for chunk in range(2):
        for at, rel in enumerate((0, 3, 2, 1)):
            start = (2 * (where_ref[PATCH] ^ rel) + chunk) * cols
            lanes = pl.ds(pl.multiple_of(start, HEAD_DIM), cols)
            mixed = hidden_ref[:, lanes].astype(jnp.float32) + gate_ref[:, lanes] * blocks[
                4 * chunk + at
            ][...].astype(jnp.float32)
            out_ref[:, lanes] = mixed.astype(jnp.bfloat16)


def mix_columns(where, hidden_in, attn_gate, blocks):
    rows, width = hidden_in.shape
    flat = [x for chunk in blocks for x in chunk]
    return call(
        mix_columns_kernel,
        "mix",
        jax.ShapeDtypeStruct((rows, width), jnp.bfloat16),
        2,
        [pl.BlockSpec((rows // 2, width), lambda i, w: (i, 0)), spec((1, width))]
        + [pl.BlockSpec((rows // 2, flat[0].shape[1]), lambda i, w: (i, 0))] * len(flat),
        pl.BlockSpec((rows // 2, width), lambda i, w: (i, 0)),
    )(where, hidden_in, attn_gate[None], *flat)


def body(sizes, queries, fresh_kv, cached_kv, exponents, out_weight, hidden_in, attn_gate):
    n_patch, n_head, n_sub = sizes["patch"], sizes["head"], sizes["sub"]
    tok, channels = queries.shape
    heads = channels // HEAD_DIM
    split = math.gcd(heads, n_patch)
    patch_at = lax.axis_index("patch")
    inner = (patch_at > 0) & (patch_at < n_patch - 1)
    where = jnp.stack(
        [
            patch_at,
            patch_at % split,
            lax.axis_index("head"),
            lax.axis_index("sub"),
            inner,
            lax.axis_index("grp"),
        ]
    ).astype(jnp.int32)

    arrays = (exponents, queries, fresh_kv, cached_kv)
    sent = pack(split, *arrays)
    far_first = [
        swap(x, "patch", n_patch, split - 1 - at) for at, x in enumerate(sent)
    ]
    where, sent = lax.optimization_barrier((where, sent))
    pieces = [pack_own(split, where, *arrays), *far_first]
    kv_pieces = list(pieces)
    for rel in range(split, n_patch, split):
        kv_pieces += [swap(x, "patch", n_patch, rel) for x in pieces]

    tail = (sizes, where, pieces, kv_pieces, out_weight, hidden_in, attn_gate)
    if (sizes["grp"], n_head, split, n_patch) == (2, 2, 4, 4):
        return share_tail(*tail)
    return sum_tail(*tail)


def solution(mesh):
    in_specs = (
        P(("grp", "patch"), ("head", "sub")),
        P(None, ("grp", "patch"), ("head", "sub")),
        P(None, "grp", ("head", "sub")),
        P(None, ("grp", "patch"), ("head", "sub")),
        P(("head", "sub"), "patch"),
        P(("grp", "patch", "head", "sub"), None),
        P(),
    )
    out_specs = P(("grp", "patch", "head", "sub"), None)
    return jax.shard_map(
        functools.partial(body, dict(mesh.shape)),
        mesh=mesh,
        in_specs=in_specs,
        out_specs=out_specs,
        check_vma=False,
    )
```

```python
import functools
import math

import jax
import jax.numpy as jnp
from jax import lax
from jax.experimental import pallas as pl
from jax.experimental.pallas import tpu as pltpu
from jax.sharding import PartitionSpec as P

HEAD_DIM = 128
SCALE_ROWS = 128
SATURATION = 448.0
PACK_ROWS = 64
VMEM_BYTES = 32 * 1024 * 1024
PACK_VMEM_BYTES = 60 * 1024 * 1024
ATTEND_FLOPS = 1
PROJECT_FLOPS = 1
OWN_FLOPS = 1
FETCHED = 4
ZERO_FLOPS = 6_000_000_000
HALF_FLOPS = 1

PATCH, NEAR, HEAD, SUB, INNER, GRP = range(6)


def spec(shape):
    return pl.BlockSpec(shape, lambda i, w: (0,) * len(shape))


def call(kernel, name, out_shape, grid, in_specs, out_specs, scratch=(), flops=1, vmem=VMEM_BYTES):
    return pl.pallas_call(
        kernel,
        out_shape=out_shape,
        grid_spec=pltpu.PrefetchScalarGridSpec(
            num_scalar_prefetch=1,
            grid=(grid,),
            in_specs=in_specs,
            out_specs=out_specs,
            scratch_shapes=list(scratch),
        ),
        compiler_params=pltpu.CompilerParams(vmem_limit_bytes=vmem),
        cost_estimate=pl.CostEstimate(flops=flops, bytes_accessed=0, transcendentals=0),
        name=name,
    )


def swap(x, axes, count, mask, only=None):
    pairs = [(at, at ^ mask) for at in range(count) if only is None or at in only]
    return lax.ppermute(x, axes, pairs)


def decode(fresh, cached, exponent):
    power = jnp.full((1, HEAD_DIM), exponent.astype(jnp.float32))
    cached = cached.astype(jnp.float32)
    residual = fresh.astype(jnp.float32) - cached
    codes = jnp.clip(residual * jnp.exp2(-power), -SATURATION, SATURATION).astype(jnp.bfloat16)
    return (cached + codes.astype(jnp.float32) * jnp.exp2(power)).astype(jnp.bfloat16)


def pack_kernel(split, per, exps_ref, q_ref, fresh_ref, cached_ref, *refs):
    outs, bufs = refs[: split - 1], refs[split - 1 : 2 * split - 2]
    q_buf, fresh_buf, cached_buf, sems, out_sems = refs[2 * split - 2 :]
    patch = lax.axis_index("patch")
    near = lax.rem(patch, split)
    tok = q_buf.shape[0]
    copies, sent = [], []
    for block in range(tok // PACK_ROWS):
        rows = pl.ds(block * PACK_ROWS, PACK_ROWS)
        there = pl.ds(pl.multiple_of(patch * tok + block * PACK_ROWS, PACK_ROWS), PACK_ROWS)
        copies.append(
            [
                pltpu.make_async_copy(q_ref.at[rows], q_buf.at[rows], sems.at[block, 0]),
                pltpu.make_async_copy(fresh_ref.at[:, rows], fresh_buf.at[:, rows], sems.at[block, 1]),
                pltpu.make_async_copy(cached_ref.at[:, there], cached_buf.at[:, rows], sems.at[block, 2]),
            ]
        )
        for copy in copies[-1]:
            copy.start()
    for block in range(tok // PACK_ROWS):
        rows = pl.ds(block * PACK_ROWS, PACK_ROWS)
        for copy in copies[block]:
            copy.wait()
        for rel in range(split - 1, 0, -1):
            buf = bufs[split - 1 - rel]
            for chunk in range(per):
                head = (near ^ rel) * per + chunk
                lanes = pl.ds(pl.multiple_of(head * HEAD_DIM, HEAD_DIM), HEAD_DIM)
                here = pl.ds(chunk * HEAD_DIM, HEAD_DIM)
                buf[0, rows, here] = q_buf[rows, lanes]
                for stacked in range(2):
                    buf[1 + stacked, rows, here] = decode(
                        fresh_buf[stacked, rows, lanes],
                        cached_buf[stacked, rows, lanes],
                        exps_ref[stacked, block * PACK_ROWS // SCALE_ROWS, head],
                    )
            sent.append(
                pltpu.make_async_copy(
                    buf.at[:, rows],
                    outs[split - 1 - rel].at[:, rows],
                    out_sems.at[block, rel - 1],
                )
            )
            sent[-1].start()
    for copy in sent:
        copy.wait()


def pack(split, exponents, queries, fresh_kv, cached_kv):
    tok, channels = queries.shape
    feat = channels // split
    blocks = tok // PACK_ROWS
    hbm = pl.BlockSpec(memory_space=pltpu.HBM)
    return pl.pallas_call(
        functools.partial(pack_kernel, split, feat // HEAD_DIM),
        out_shape=[jax.ShapeDtypeStruct((3, tok, feat), jnp.bfloat16)] * (split - 1),
        in_specs=[pl.BlockSpec(memory_space=pltpu.SMEM), hbm, hbm, hbm],
        out_specs=[hbm] * (split - 1),
        scratch_shapes=[pltpu.VMEM((3, tok, feat), jnp.bfloat16)] * (split - 1)
        + [
            pltpu.VMEM((tok, channels), jnp.bfloat16),
            pltpu.VMEM((2, tok, channels), jnp.bfloat16),
            pltpu.VMEM((2, tok, channels), jnp.bfloat16),
            pltpu.SemaphoreType.DMA((blocks, 3)),
            pltpu.SemaphoreType.DMA((blocks, split - 1)),
        ],
        compiler_params=pltpu.CompilerParams(vmem_limit_bytes=PACK_VMEM_BYTES),
        name="pack",
    )(exponents, queries, fresh_kv, cached_kv)


def own_kernel(per, where_ref, exps_ref, q_ref, fresh_ref, cached_ref, out_ref):
    out_ref[0] = q_ref[...]
    for chunk in range(per):
        lanes = pl.ds(chunk * HEAD_DIM, HEAD_DIM)
        for block in range(q_ref.shape[0] // SCALE_ROWS):
            rows = pl.ds(block * SCALE_ROWS, SCALE_ROWS)
            for stacked in range(2):
                out_ref[1 + stacked, rows, lanes] = decode(
                    fresh_ref[stacked, rows, lanes],
                    cached_ref[stacked, rows, lanes],
                    exps_ref[stacked, block, where_ref[NEAR] * per + chunk],
                )


def pack_own(split, where, exponents, queries, fresh_kv, cached_kv):
    tok, channels = queries.shape
    feat = channels // split
    patch_at, near = where[PATCH], where[NEAR]
    queries = lax.dynamic_slice_in_dim(queries, near * feat, feat, 1)
    fresh_kv = lax.dynamic_slice_in_dim(fresh_kv, near * feat, feat, 2)
    cached_kv = lax.dynamic_slice(cached_kv, (0, patch_at * tok, near * feat), (2, tok, feat))
    out = jax.ShapeDtypeStruct((3, tok, feat), jnp.bfloat16)
    return call(
        functools.partial(own_kernel, feat // HEAD_DIM),
        "own",
        out,
        1,
        [pl.BlockSpec(memory_space=pltpu.SMEM)]
        + [spec(x.shape) for x in (queries, fresh_kv, cached_kv)],
        spec(out.shape),
        flops=OWN_FLOPS,
    )(where, exponents, queries, fresh_kv, cached_kv)


def attend_kernel(split, part, where_ref, *refs):
    q_refs, kv_refs, out_ref = (refs[0], *refs[split - 1 : 0 : -1]), refs[:-1], refs[-1]
    factor = HEAD_DIM**-0.5 * math.log2(math.e)
    tok, feat = q_refs[0].shape[1:]
    count = out_ref.shape[1] // part[1]
    starts = [at * (tok // count) + part[0] for at in range(count)]
    for head in range(feat // HEAD_DIM):
        lanes = pl.ds(head * HEAD_DIM, HEAD_DIM)
        keys = jnp.concatenate([ref[1, :, lanes] for ref in kv_refs], axis=0)
        values = jnp.concatenate([ref[2, :, lanes] for ref in kv_refs], axis=0)
        values = jnp.concatenate([values, jnp.ones_like(values)], axis=1)
        for rel in range(split):
            rows = [q_refs[rel][0, start : start + part[1], lanes] for start in starts]
            query = jnp.concatenate(rows, axis=0) if len(rows) > 1 else rows[0]
            scores = lax.dot_general(
                query, keys, (((1,), (1,)), ((), ())), preferred_element_type=jnp.float32
            )
            peak = jnp.max(scores, axis=1, keepdims=True)
            expo = jnp.exp2((scores - peak) * factor).astype(jnp.bfloat16)
            mix = jnp.dot(expo, values, preferred_element_type=jnp.float32)
            mix = mix[:, :HEAD_DIM] / mix[:, HEAD_DIM:]
            out_ref[where_ref[NEAR] ^ rel, :, lanes] = mix.astype(jnp.bfloat16)


def attend(where, part, count, pieces, kv_pieces):
    split = len(pieces)
    _, tok, feat = pieces[0].shape
    out = jax.ShapeDtypeStruct((split, count * part[1], feat), jnp.bfloat16)
    return call(
        functools.partial(attend_kernel, split, part),
        "attend",
        out,
        1,
        [spec((3, tok, feat))] * len(kv_pieces),
        spec(out.shape),
        flops=ATTEND_FLOPS,
    )(where, *kv_pieces)


def project_kernel(split, n_slots, n_more, where_ref, *refs):
    slots, refs = refs[:n_slots], refs[n_slots:]
    more, weight_ref, refs = refs[:n_more], refs[n_more], refs[n_more + 1 :]
    outs, held_ref, acc_ref = refs[:-2], refs[-2], refs[-1]
    rows, feat = slots[0].shape
    n_sub, n_head = acc_ref.shape[3], acc_ref.shape[2]

    @pl.when(pl.program_id(0) == 0)
    def arrange():
        for at, slot in enumerate(slots):
            group, near = divmod(at, split)
            lane = (where_ref[NEAR] ^ near) * feat
            block = slot[...]
            if more and at == n_slots - 1:
                block = jnp.where(where_ref[INNER] == 1, block, more[0][...])
            held_ref[
                group * rows : (group + 1) * rows, pl.ds(pl.multiple_of(lane, HEAD_DIM), feat)
            ] = block

    acc = jnp.dot(held_ref[...], weight_ref[...], preferred_element_type=jnp.float32)
    acc_ref[...] = acc.reshape(acc_ref.shape)
    for sub in range(n_sub):
        for head in range(n_head):
            for at in range(n_slots):
                group, near = divmod(at, split)
                outs[sub][head, at] = acc_ref[
                    group, where_ref[NEAR] ^ near, where_ref[HEAD] ^ head, where_ref[SUB] ^ sub
                ].astype(jnp.bfloat16)


def project(split, where, slots, more, weight, n_head, n_sub):
    rows, feat = slots[0].shape
    n_patch = len(slots)
    total = rows * n_patch // split
    depth, cols = weight.shape
    wide = 640 if cols % 640 == 0 else cols
    piece = rows // (split * n_head * n_sub)
    return call(
        functools.partial(project_kernel, split, n_patch, len(more)),
        "project",
        [jax.ShapeDtypeStruct((n_head, n_patch, piece, cols), jnp.bfloat16)] * n_sub,
        cols // wide,
        [spec((rows, feat))] * (n_patch + len(more))
        + [pl.BlockSpec((depth, wide), lambda i, w: (0, i))],
        [pl.BlockSpec((n_head, n_patch, piece, wide), lambda i, w: (0, 0, 0, i))] * n_sub,
        [
            pltpu.VMEM((total, depth), jnp.bfloat16),
            pltpu.VMEM((n_patch // split, split, n_head, n_sub, piece, wide), jnp.float32),
        ],
        flops=PROJECT_FLOPS,
    )(where, *slots, *more, weight)


def mix_kernel(rels, where_ref, hidden_ref, gate_ref, *refs):
    blocks, out_ref = refs[:-1], refs[-1]
    piece, cols = blocks[0].shape
    for part in range(len(blocks) // len(rels)):
        rows = pl.ds(part * piece, piece)
        for at, rel in enumerate(rels):
            lanes = pl.ds(pl.multiple_of((where_ref[PATCH] ^ rel) * cols, HEAD_DIM), cols)
            mixed = hidden_ref[rows, lanes].astype(jnp.float32) + gate_ref[:, lanes] * blocks[
                part * len(rels) + at
            ][...].astype(jnp.float32)
            out_ref[rows, lanes] = mixed.astype(jnp.bfloat16)


def mix(where, hidden_in, attn_gate, blocks):
    rows, width = hidden_in.shape
    n_patch = len(blocks[0])
    piece, cols = blocks[0][0].shape
    if cols % HEAD_DIM:
        order = jnp.concatenate([jnp.stack(x) for x in blocks], axis=1)
        order = order[where[PATCH] ^ jnp.arange(n_patch)]
        projected = order.transpose(1, 0, 2).reshape(rows, width).astype(jnp.float32)
        return (hidden_in.astype(jnp.float32) + attn_gate * projected).astype(jnp.bfloat16)
    rels = [0, *range(n_patch - 1, 0, -1)]
    flat = [part[rel] for part in blocks for rel in rels]
    return call(
        functools.partial(mix_kernel, rels),
        "mix",
        jax.ShapeDtypeStruct((rows, width), jnp.bfloat16),
        1,
        [spec((rows, width)), spec((1, width))] + [spec((piece, cols))] * len(flat),
        spec((rows, width)),
    )(where, hidden_in, attn_gate[None], *flat)


def gather(parts, n_patch):
    if n_patch != 4:
        return [
            ([x] + [swap(x, "patch", n_patch, rel) for rel in range(1, n_patch)], [])
            for x in parts
        ]
    far = [swap(x, "patch", 4, 2) for x in parts]
    next_to = [swap(x, "patch", 4, 1) for x in parts]
    out = []
    for at, x in enumerate(parts):
        far[at], next_to[at], parts = lax.optimization_barrier((far[at], next_to[at], parts))
        middle = swap(parts[at], "patch", 4, 3, (1, 2))
        ends = lax.ppermute(far[at], "patch", [(1, 0), (2, 3)])
        if at + 1 < len(parts):
            ends, far[at + 1], next_to[at + 1] = lax.optimization_barrier(
                (ends, far[at + 1], next_to[at + 1])
            )
        out.append(([x, next_to[at], far[at], middle], [ends]))
    return out


def add_sub_kernel(n_sub, where_ref, *refs):
    terms, kept_ref, outs = refs[:n_sub], refs[n_sub], refs[n_sub + 1 :]
    for head in range(len(outs) + 1):
        total = terms[0][head].astype(jnp.float32)
        for term in terms[1:]:
            total += term[head].astype(jnp.float32)
        if head == 0:
            kept_ref[...] = total
        else:
            outs[head - 1][...] = total.astype(jnp.bfloat16)


def add_head_kernel(n_more, where_ref, kept_ref, *refs):
    for at, out in enumerate(refs[n_more:]):
        total = kept_ref[at]
        for term in refs[:n_more]:
            total += term[at].astype(jnp.float32)
        out[...] = total.astype(jnp.bfloat16)


def reduce_sub(sizes, where, terms):
    n_sub, n_head = sizes["sub"], sizes["head"]
    terms = [terms[0]] + [swap(terms[rel], "sub", n_sub, rel) for rel in range(1, n_sub)]
    shape = terms[0].shape[1:]
    return call(
        functools.partial(add_sub_kernel, n_sub),
        "add_sub",
        [jax.ShapeDtypeStruct(shape, jnp.float32)]
        + [jax.ShapeDtypeStruct(shape, jnp.bfloat16)] * (n_head - 1),
        1,
        [spec(terms[0].shape)] * n_sub,
        [spec(shape)] * n_head,
    )(where, *terms)


def reduce_head(sizes, where, sums):
    n_head = sizes["head"]
    shape = sums[0].shape
    sums = [sums[0]] + [swap(sums[rel], "head", n_head, rel) for rel in range(1, n_head)]
    return call(
        functools.partial(add_head_kernel, n_head - 1),
        "add_head",
        [jax.ShapeDtypeStruct(shape[1:], jnp.bfloat16)] * shape[0],
        1,
        [spec(shape)] * n_head,
        [spec(shape[1:])] * shape[0],
    )(where, *sums)


def sum_tail(sizes, where, pieces, kv_pieces, out_weight, hidden_in, attn_gate):
    n_patch, n_head, n_sub = sizes["patch"], sizes["head"], sizes["sub"]
    split, tok = len(pieces), pieces[0].shape[1]
    count = n_head * n_sub
    piece = tok // count
    parts = 2 if piece % 32 == 0 else 1
    attended = []
    for part in range(parts):
        rows = (part * (piece // parts), piece // parts)
        x = attend(where, rows, count, pieces, kv_pieces)
        attended.append(x.reshape(-1, x.shape[2]))
    slots = gather(attended, n_patch)
    blocks = []
    for part in range(parts):
        terms = project(split, where, *slots[part], out_weight, n_head, n_sub)
        total = reduce_head(sizes, where, reduce_sub(sizes, where, terms))
        blocks.append(
            [total[0]] + [swap(total[rel], "patch", n_patch, rel) for rel in range(1, n_patch)]
        )
    return mix(where, hidden_in, attn_gate, blocks)


def attend_half_kernel(half, where_ref, *refs):
    pieces, out = refs[:-1], refs[-1]
    factor = HEAD_DIM**-0.5 * math.log2(math.e)
    rows, feat = out.shape[1:]
    start = pl.multiple_of((where_ref[HEAD] ^ half) * rows, rows)
    for head in range(feat // HEAD_DIM):
        lanes = pl.ds(head * HEAD_DIM, HEAD_DIM)
        keys = jnp.concatenate([ref[1, :, lanes] for ref in pieces], axis=0)
        values = jnp.concatenate([ref[2, :, lanes] for ref in pieces], axis=0)
        values = jnp.concatenate([values, jnp.ones_like(values)], axis=1)
        query = jnp.concatenate([ref[0, pl.ds(start, rows), lanes] for ref in pieces], axis=0)
        scores = lax.dot_general(
            query, keys, (((1,), (1,)), ((), ())), preferred_element_type=jnp.float32
        )
        peak = jnp.max(scores, axis=1, keepdims=True)
        expo = jnp.exp2((scores - peak) * factor).astype(jnp.bfloat16)
        mix = jnp.dot(expo, values, preferred_element_type=jnp.float32)
        mix = (mix[:, :HEAD_DIM] / mix[:, HEAD_DIM:]).astype(jnp.bfloat16)
        for rel in range(len(pieces)):
            out[where_ref[NEAR] ^ rel, :, lanes] = mix[rel * rows : (rel + 1) * rows]


def attend_half(where, half, pieces):
    _, tok, feat = pieces[0].shape
    out = jax.ShapeDtypeStruct((len(pieces), tok // 2, feat), jnp.bfloat16)
    return call(
        functools.partial(attend_half_kernel, half),
        "attend",
        out,
        1,
        [spec((3, tok, feat))] * len(pieces),
        spec(out.shape),
        flops=HALF_FLOPS,
    )(where, *pieces).reshape(-1, feat)


def add_product_kernel(count, where_ref, *refs):
    total = refs[2 * count][...] if len(refs) > 2 * count + 1 else None
    for slot, weight in zip(refs[:count], refs[count : 2 * count]):
        term = jnp.dot(slot[...], weight[...], preferred_element_type=jnp.float32)
        total = term if total is None else total + term
    refs[-1][...] = total


def add_product(where, slots, weight, acc=None):
    rows, feat = next(iter(slots.values())).shape
    cols = weight.shape[1]
    wide = cols // 2
    whole = pl.BlockSpec((rows, wide), lambda i, w: (0, i))
    rels = list(slots)
    return call(
        functools.partial(add_product_kernel, len(rels)),
        "products",
        jax.ShapeDtypeStruct((rows, cols), jnp.float32),
        2,
        [spec((rows, feat))] * len(rels)
        + [pl.BlockSpec((feat, wide), lambda i, w, rel=rel: (w[NEAR] ^ rel, i)) for rel in rels]
        + ([] if acc is None else [whole]),
        whole,
        flops=ZERO_FLOPS if acc is None else 1,
    )(where, *slots.values(), *[weight] * len(rels), *([] if acc is None else [acc]))


def partner_place(where_ref, head):
    return (head + FETCHED * where_ref[GRP]) % 8


def first_kernel(where_ref, *refs):
    last, more, slots = refs[0], refs[1], refs[2:5]
    acc_ref, own_ref, fetched_ref, passed_ref, out_ref, held_ref = refs[5:]
    rows, feat = last.shape
    cut = fetched_ref.shape[0]

    def put(at, block):
        for head in range(2):
            there = partner_place(where_ref, 2 * (where_ref[NEAR] ^ at) + head)
            lanes = pl.ds(pl.multiple_of(there * HEAD_DIM, HEAD_DIM), HEAD_DIM)
            held_ref[:, lanes] = block[:, head * HEAD_DIM : (head + 1) * HEAD_DIM]

    @pl.when(pl.program_id(0) == 0)
    def arrange():
        for at, slot in zip((0, 2, 1), slots):
            put(at, slot[...])
        put(3, jnp.zeros((rows, feat), jnp.bfloat16))

    block = jnp.where(where_ref[INNER] == 1, last[...], more[...])
    acc = acc_ref[...]
    acc += jnp.dot(block, own_ref[...], preferred_element_type=jnp.float32)
    acc += jnp.dot(held_ref[:, :cut], fetched_ref[...], preferred_element_type=jnp.float32)
    acc += jnp.dot(held_ref[:, cut:], passed_ref[...], preferred_element_type=jnp.float32)
    out_ref[...] = acc


def first_product(where, last, more, slots, acc, weights):
    rows, feat = last.shape
    own, fetched, passed = weights
    wide = own.shape[1] // 2
    whole = pl.BlockSpec((rows, wide), lambda i, w: (0, i))
    return call(
        first_kernel,
        "first",
        jax.ShapeDtypeStruct(acc.shape, jnp.float32),
        2,
        [spec((rows, feat))] * 5
        + [whole, pl.BlockSpec((feat, wide), lambda i, w: (w[NEAR] ^ 3, i))]
        + [pl.BlockSpec((x.shape[0], wide), lambda i, w: (0, i)) for x in (fetched, passed)],
        whole,
        [pltpu.VMEM((rows, 4 * feat), jnp.bfloat16)],
    )(where, last, more, *slots, acc, own, fetched, passed)


def second_kernel(where_ref, slot, more, fetched_ref, passed_ref, acc_in, keep_ref, send_ref, acc_ref):
    weight = []
    for head in range(2):
        place = partner_place(where_ref, 2 * (where_ref[NEAR] ^ 3) + head)
        here = jnp.minimum(place, FETCHED - 1) * HEAD_DIM
        there = jnp.maximum(place - FETCHED, 0) * HEAD_DIM
        weight.append(
            jnp.where(
                place < FETCHED,
                fetched_ref[pl.ds(pl.multiple_of(here, HEAD_DIM), HEAD_DIM), :],
                passed_ref[pl.ds(pl.multiple_of(there, HEAD_DIM), HEAD_DIM), :],
            )
        )
    block = jnp.where(where_ref[INNER] == 1, slot[...], more[...])
    acc = acc_in[...] + jnp.dot(
        block, jnp.concatenate(weight, axis=0), preferred_element_type=jnp.float32
    )
    acc_ref[...] = acc.reshape(acc_ref.shape)
    for sub, out in enumerate((keep_ref, send_ref)):
        for at in range(4):
            out[at] = acc_ref[where_ref[NEAR] ^ at, where_ref[SUB] ^ sub].astype(jnp.bfloat16)


def second_product(where, chunk, slot, more, weights, acc):
    rows, feat = slot.shape
    cols = weights[0].shape[1]
    wide = cols // 2
    out = jax.ShapeDtypeStruct((4, rows // 8, wide), jnp.bfloat16)
    return call(
        second_kernel,
        "second",
        [out] * 2,
        1,
        [spec((rows, feat))] * 2
        + [pl.BlockSpec((x.shape[0], wide), lambda i, w: (0, chunk)) for x in weights]
        + [pl.BlockSpec((rows, wide), lambda i, w: (0, chunk))],
        [spec(out.shape)] * 2,
        [pltpu.VMEM((4, 2, rows // 8, wide), jnp.float32)],
    )(where, slot, more, *weights, acc)


def add_kernel(where_ref, keep_ref, term_ref, *outs):
    for at, out in enumerate(outs):
        total = keep_ref[at].astype(jnp.float32) + term_ref[at].astype(jnp.float32)
        out[...] = total.astype(jnp.bfloat16)


def add(where, keep, term):
    return call(
        add_kernel,
        "add",
        [jax.ShapeDtypeStruct(keep.shape[1:], jnp.bfloat16)] * keep.shape[0],
        1,
        [spec(keep.shape)] * 2,
        [spec(keep.shape[1:])] * keep.shape[0],
    )(where, keep, term)


def share_tail(sizes, where, pieces, kv_pieces, out_weight, hidden_in, attn_gate):
    fetch, pass_on = FETCHED * HEAD_DIM, (8 - FETCHED) * HEAD_DIM
    out_weight, where = lax.optimization_barrier((out_weight, where))
    start = lax.axis_index("grp") * pass_on
    fetched = swap(lax.dynamic_slice_in_dim(out_weight, start, fetch, 0), "head", 2, 1)
    own, fetched = lax.optimization_barrier((pieces[0], fetched))
    pieces = [own, *pieces[1:]]
    start = lax.axis_index("grp") * (fetch - pass_on)
    passed = swap(lax.dynamic_slice_in_dim(fetched, start, pass_on, 0), "grp", 2, 1)

    pieces = [pieces[0], *pieces[:0:-1]]
    mine = attend_half(where, 0, pieces)
    where, mine = lax.optimization_barrier((where, mine))
    other = swap(attend_half(where, 1, pieces), "head", 2, 1)
    acc = add_product(where, {0: mine}, out_weight)
    other, acc = lax.optimization_barrier((other, acc))
    slots = []
    for at, x in enumerate((mine, other)):
        next_to, far = swap(x, "patch", 4, 1), swap(x, "patch", 4, 2)
        next_to, far, other, x = lax.optimization_barrier((next_to, far, other, x))
        if at == 1:
            acc = add_product(where, {2: slots[0][2], 1: slots[0][1]}, out_weight, acc)
            far, x, acc = lax.optimization_barrier((far, x, acc))
        middle = swap(x, "patch", 4, 3, (1, 2))
        ends = lax.ppermute(far, "patch", [(1, 0), (2, 3)])
        slots.append([x, next_to, far, middle, ends])
    weights = [out_weight, fetched, passed]
    partner = [slots[1][at] for at in (0, 2, 1)]
    acc = first_product(where, *slots[0][3:], partner, acc, weights)
    terms = [second_product(where, at, *slots[1][3:], [fetched, passed], acc) for at in range(2)]
    blocks = []
    for keep, send in terms:
        total = add(where, keep, swap(send, "sub", 2, 1))
        blocks.append([total[0]] + [swap(total[rel], "patch", 4, rel) for rel in range(3, 0, -1)])
    return mix_columns(where, hidden_in, attn_gate, blocks)


def mix_columns_kernel(where_ref, hidden_ref, gate_ref, *refs):
    blocks, out_ref = refs[:-1], refs[-1]
    cols = blocks[0].shape[1]
    for chunk in range(2):
        for at, rel in enumerate((0, 3, 2, 1)):
            start = (2 * (where_ref[PATCH] ^ rel) + chunk) * cols
            lanes = pl.ds(pl.multiple_of(start, HEAD_DIM), cols)
            mixed = hidden_ref[:, lanes].astype(jnp.float32) + gate_ref[:, lanes] * blocks[
                4 * chunk + at
            ][...].astype(jnp.float32)
            out_ref[:, lanes] = mixed.astype(jnp.bfloat16)


def mix_columns(where, hidden_in, attn_gate, blocks):
    rows, width = hidden_in.shape
    flat = [x for chunk in blocks for x in chunk]
    return call(
        mix_columns_kernel,
        "mix",
        jax.ShapeDtypeStruct((rows, width), jnp.bfloat16),
        2,
        [pl.BlockSpec((rows // 2, width), lambda i, w: (i, 0)), spec((1, width))]
        + [pl.BlockSpec((rows // 2, flat[0].shape[1]), lambda i, w: (i, 0))] * len(flat),
        pl.BlockSpec((rows // 2, width), lambda i, w: (i, 0)),
    )(where, hidden_in, attn_gate[None], *flat)


def body(sizes, queries, fresh_kv, cached_kv, exponents, out_weight, hidden_in, attn_gate):
    n_patch, n_head, n_sub = sizes["patch"], sizes["head"], sizes["sub"]
    tok, channels = queries.shape
    heads = channels // HEAD_DIM
    split = math.gcd(heads, n_patch)
    patch_at = lax.axis_index("patch")
    inner = (patch_at > 0) & (patch_at < n_patch - 1)
    where = jnp.stack(
        [
            patch_at,
            patch_at % split,
            lax.axis_index("head"),
            lax.axis_index("sub"),
            inner,
            lax.axis_index("grp"),
        ]
    ).astype(jnp.int32)

    arrays = (exponents, queries, fresh_kv, cached_kv)
    sent = pack(split, *arrays)
    far_first = [
        swap(x, "patch", n_patch, split - 1 - at) for at, x in enumerate(sent)
    ]
    where, sent = lax.optimization_barrier((where, sent))
    pieces = [pack_own(split, where, *arrays), *far_first]
    kv_pieces = list(pieces)
    for rel in range(split, n_patch, split):
        kv_pieces += [swap(x, "patch", n_patch, rel) for x in pieces]

    tail = (sizes, where, pieces, kv_pieces, out_weight, hidden_in, attn_gate)
    if (sizes["grp"], n_head, split, n_patch) == (2, 2, 4, 4):
        return share_tail(*tail)
    return sum_tail(*tail)


def solution(mesh):
    in_specs = (
        P(("grp", "patch"), ("head", "sub")),
        P(None, ("grp", "patch"), ("head", "sub")),
        P(None, "grp", ("head", "sub")),
        P(None, ("grp", "patch"), ("head", "sub")),
        P(("head", "sub"), "patch"),
        P(("grp", "patch", "head", "sub"), None),
        P(),
    )
    out_specs = P(("grp", "patch", "head", "sub"), None)
    return jax.shard_map(
        functools.partial(body, dict(mesh.shape)),
        mesh=mesh,
        in_specs=in_specs,
        out_specs=out_specs,
        check_vma=False,
    )
```

```python
import functools
import math

import jax
import jax.numpy as jnp
from jax import lax
from jax.experimental import pallas as pl
from jax.experimental.pallas import tpu as pltpu
from jax.sharding import PartitionSpec as P

HEAD_DIM = 128
SCALE_ROWS = 128
SATURATION = 448.0
PACK_ROWS = 64
VMEM_BYTES = 32 * 1024 * 1024
PACK_VMEM_BYTES = 60 * 1024 * 1024
ATTEND_FLOPS = 1
PROJECT_FLOPS = 1
OWN_FLOPS = 1
FETCHED = 4
ZERO_FLOPS = 6_000_000_000
HALF_FLOPS = 1

PATCH, NEAR, HEAD, SUB, INNER, GRP = range(6)


def spec(shape):
    return pl.BlockSpec(shape, lambda i, w: (0,) * len(shape))


def call(kernel, name, out_shape, grid, in_specs, out_specs, scratch=(), flops=1, vmem=VMEM_BYTES):
    return pl.pallas_call(
        kernel,
        out_shape=out_shape,
        grid_spec=pltpu.PrefetchScalarGridSpec(
            num_scalar_prefetch=1,
            grid=(grid,),
            in_specs=in_specs,
            out_specs=out_specs,
            scratch_shapes=list(scratch),
        ),
        compiler_params=pltpu.CompilerParams(vmem_limit_bytes=vmem),
        cost_estimate=pl.CostEstimate(flops=flops, bytes_accessed=0, transcendentals=0),
        name=name,
    )


def swap(x, axes, count, mask, only=None):
    pairs = [(at, at ^ mask) for at in range(count) if only is None or at in only]
    return lax.ppermute(x, axes, pairs)


def decode(fresh, cached, exponent):
    power = jnp.full((1, HEAD_DIM), exponent.astype(jnp.float32))
    cached = cached.astype(jnp.float32)
    residual = fresh.astype(jnp.float32) - cached
    codes = jnp.clip(residual * jnp.exp2(-power), -SATURATION, SATURATION).astype(jnp.bfloat16)
    return (cached + codes.astype(jnp.float32) * jnp.exp2(power)).astype(jnp.bfloat16)


def pack_kernel(split, per, exps_ref, q_ref, fresh_ref, cached_ref, *refs):
    outs, bufs = refs[: split - 1], refs[split - 1 : 2 * split - 2]
    q_buf, fresh_buf, cached_buf, sems, out_sems = refs[2 * split - 2 :]
    patch = lax.axis_index("patch")
    near = lax.rem(patch, split)
    tok = q_buf.shape[0]
    copies, sent = [], []
    for block in range(tok // PACK_ROWS):
        rows = pl.ds(block * PACK_ROWS, PACK_ROWS)
        there = pl.ds(pl.multiple_of(patch * tok + block * PACK_ROWS, PACK_ROWS), PACK_ROWS)
        copies.append(
            [
                pltpu.make_async_copy(q_ref.at[rows], q_buf.at[rows], sems.at[block, 0]),
                pltpu.make_async_copy(fresh_ref.at[:, rows], fresh_buf.at[:, rows], sems.at[block, 1]),
                pltpu.make_async_copy(cached_ref.at[:, there], cached_buf.at[:, rows], sems.at[block, 2]),
            ]
        )
        for copy in copies[-1]:
            copy.start()
    for block in range(tok // PACK_ROWS):
        rows = pl.ds(block * PACK_ROWS, PACK_ROWS)
        for copy in copies[block]:
            copy.wait()
        for rel in range(split - 1, 0, -1):
            buf = bufs[split - 1 - rel]
            for chunk in range(per):
                head = (near ^ rel) * per + chunk
                lanes = pl.ds(pl.multiple_of(head * HEAD_DIM, HEAD_DIM), HEAD_DIM)
                here = pl.ds(chunk * HEAD_DIM, HEAD_DIM)
                buf[0, rows, here] = q_buf[rows, lanes]
                for stacked in range(2):
                    buf[1 + stacked, rows, here] = decode(
                        fresh_buf[stacked, rows, lanes],
                        cached_buf[stacked, rows, lanes],
                        exps_ref[stacked, block * PACK_ROWS // SCALE_ROWS, head],
                    )
            sent.append(
                pltpu.make_async_copy(
                    buf.at[:, rows],
                    outs[split - 1 - rel].at[:, rows],
                    out_sems.at[block, rel - 1],
                )
            )
            sent[-1].start()
    for copy in sent:
        copy.wait()


def pack(split, exponents, queries, fresh_kv, cached_kv):
    tok, channels = queries.shape
    feat = channels // split
    blocks = tok // PACK_ROWS
    hbm = pl.BlockSpec(memory_space=pltpu.HBM)
    return pl.pallas_call(
        functools.partial(pack_kernel, split, feat // HEAD_DIM),
        out_shape=[jax.ShapeDtypeStruct((3, tok, feat), jnp.bfloat16)] * (split - 1),
        in_specs=[pl.BlockSpec(memory_space=pltpu.SMEM), hbm, hbm, hbm],
        out_specs=[hbm] * (split - 1),
        scratch_shapes=[pltpu.VMEM((3, tok, feat), jnp.bfloat16)] * (split - 1)
        + [
            pltpu.VMEM((tok, channels), jnp.bfloat16),
            pltpu.VMEM((2, tok, channels), jnp.bfloat16),
            pltpu.VMEM((2, tok, channels), jnp.bfloat16),
            pltpu.SemaphoreType.DMA((blocks, 3)),
            pltpu.SemaphoreType.DMA((blocks, split - 1)),
        ],
        compiler_params=pltpu.CompilerParams(vmem_limit_bytes=PACK_VMEM_BYTES),
        name="pack",
    )(exponents, queries, fresh_kv, cached_kv)


def own_kernel(per, where_ref, exps_ref, q_ref, fresh_ref, cached_ref, out_ref):
    out_ref[0] = q_ref[...]
    for chunk in range(per):
        lanes = pl.ds(chunk * HEAD_DIM, HEAD_DIM)
        for block in range(q_ref.shape[0] // SCALE_ROWS):
            rows = pl.ds(block * SCALE_ROWS, SCALE_ROWS)
            for stacked in range(2):
                out_ref[1 + stacked, rows, lanes] = decode(
                    fresh_ref[stacked, rows, lanes],
                    cached_ref[stacked, rows, lanes],
                    exps_ref[stacked, block, where_ref[NEAR] * per + chunk],
                )


def pack_own(split, where, exponents, queries, fresh_kv, cached_kv):
    tok, channels = queries.shape
    feat = channels // split
    out = jax.ShapeDtypeStruct((3, tok, feat), jnp.bfloat16)
    return call(
        functools.partial(own_kernel, feat // HEAD_DIM),
        "own",
        out,
        1,
        [
            pl.BlockSpec(memory_space=pltpu.SMEM),
            pl.BlockSpec((tok, feat), lambda i, w: (0, w[NEAR])),
            pl.BlockSpec((2, tok, feat), lambda i, w: (0, 0, w[NEAR])),
            pl.BlockSpec((2, tok, feat), lambda i, w: (0, w[PATCH], w[NEAR])),
        ],
        spec(out.shape),
    )(where, exponents, queries, fresh_kv, cached_kv)


def attend_kernel(split, part, where_ref, *refs):
    q_refs, kv_refs, out_ref = (refs[0], *refs[split - 1 : 0 : -1]), refs[:-1], refs[-1]
    factor = HEAD_DIM**-0.5 * math.log2(math.e)
    tok, feat = q_refs[0].shape[1:]
    count = out_ref.shape[1] // part[1]
    starts = [at * (tok // count) + part[0] for at in range(count)]
    for head in range(feat // HEAD_DIM):
        lanes = pl.ds(head * HEAD_DIM, HEAD_DIM)
        keys = jnp.concatenate([ref[1, :, lanes] for ref in kv_refs], axis=0)
        values = jnp.concatenate([ref[2, :, lanes] for ref in kv_refs], axis=0)
        values = jnp.concatenate([values, jnp.ones_like(values)], axis=1)
        for rel in range(split):
            rows = [q_refs[rel][0, start : start + part[1], lanes] for start in starts]
            query = jnp.concatenate(rows, axis=0) if len(rows) > 1 else rows[0]
            scores = lax.dot_general(
                query, keys, (((1,), (1,)), ((), ())), preferred_element_type=jnp.float32
            )
            peak = jnp.max(scores, axis=1, keepdims=True)
            expo = jnp.exp2((scores - peak) * factor).astype(jnp.bfloat16)
            mix = jnp.dot(expo, values, preferred_element_type=jnp.float32)
            mix = mix[:, :HEAD_DIM] / mix[:, HEAD_DIM:]
            out_ref[where_ref[NEAR] ^ rel, :, lanes] = mix.astype(jnp.bfloat16)


def attend(where, part, count, pieces, kv_pieces):
    split = len(pieces)
    _, tok, feat = pieces[0].shape
    out = jax.ShapeDtypeStruct((split, count * part[1], feat), jnp.bfloat16)
    return call(
        functools.partial(attend_kernel, split, part),
        "attend",
        out,
        1,
        [spec((3, tok, feat))] * len(kv_pieces),
        spec(out.shape),
        flops=ATTEND_FLOPS,
    )(where, *kv_pieces)


def project_kernel(split, n_slots, n_more, where_ref, *refs):
    slots, refs = refs[:n_slots], refs[n_slots:]
    more, weight_ref, refs = refs[:n_more], refs[n_more], refs[n_more + 1 :]
    outs, held_ref, acc_ref = refs[:-2], refs[-2], refs[-1]
    rows, feat = slots[0].shape
    n_sub, n_head = acc_ref.shape[3], acc_ref.shape[2]

    @pl.when(pl.program_id(0) == 0)
    def arrange():
        for at, slot in enumerate(slots):
            group, near = divmod(at, split)
            lane = (where_ref[NEAR] ^ near) * feat
            block = slot[...]
            if more and at == n_slots - 1:
                block = jnp.where(where_ref[INNER] == 1, block, more[0][...])
            held_ref[
                group * rows : (group + 1) * rows, pl.ds(pl.multiple_of(lane, HEAD_DIM), feat)
            ] = block

    acc = jnp.dot(held_ref[...], weight_ref[...], preferred_element_type=jnp.float32)
    acc_ref[...] = acc.reshape(acc_ref.shape)
    for sub in range(n_sub):
        for head in range(n_head):
            for at in range(n_slots):
                group, near = divmod(at, split)
                outs[sub][head, at] = acc_ref[
                    group, where_ref[NEAR] ^ near, where_ref[HEAD] ^ head, where_ref[SUB] ^ sub
                ].astype(jnp.bfloat16)


def project(split, where, slots, more, weight, n_head, n_sub):
    rows, feat = slots[0].shape
    n_patch = len(slots)
    total = rows * n_patch // split
    depth, cols = weight.shape
    wide = 640 if cols % 640 == 0 else cols
    piece = rows // (split * n_head * n_sub)
    return call(
        functools.partial(project_kernel, split, n_patch, len(more)),
        "project",
        [jax.ShapeDtypeStruct((n_head, n_patch, piece, cols), jnp.bfloat16)] * n_sub,
        cols // wide,
        [spec((rows, feat))] * (n_patch + len(more))
        + [pl.BlockSpec((depth, wide), lambda i, w: (0, i))],
        [pl.BlockSpec((n_head, n_patch, piece, wide), lambda i, w: (0, 0, 0, i))] * n_sub,
        [
            pltpu.VMEM((total, depth), jnp.bfloat16),
            pltpu.VMEM((n_patch // split, split, n_head, n_sub, piece, wide), jnp.float32),
        ],
        flops=PROJECT_FLOPS,
    )(where, *slots, *more, weight)


def mix_kernel(rels, where_ref, hidden_ref, gate_ref, *refs):
    blocks, out_ref = refs[:-1], refs[-1]
    piece, cols = blocks[0].shape
    for part in range(len(blocks) // len(rels)):
        rows = pl.ds(part * piece, piece)
        for at, rel in enumerate(rels):
            lanes = pl.ds(pl.multiple_of((where_ref[PATCH] ^ rel) * cols, HEAD_DIM), cols)
            mixed = hidden_ref[rows, lanes].astype(jnp.float32) + gate_ref[:, lanes] * blocks[
                part * len(rels) + at
            ][...].astype(jnp.float32)
            out_ref[rows, lanes] = mixed.astype(jnp.bfloat16)


def mix(where, hidden_in, attn_gate, blocks):
    rows, width = hidden_in.shape
    n_patch = len(blocks[0])
    piece, cols = blocks[0][0].shape
    if cols % HEAD_DIM:
        order = jnp.concatenate([jnp.stack(x) for x in blocks], axis=1)
        order = order[where[PATCH] ^ jnp.arange(n_patch)]
        projected = order.transpose(1, 0, 2).reshape(rows, width).astype(jnp.float32)
        return (hidden_in.astype(jnp.float32) + attn_gate * projected).astype(jnp.bfloat16)
    rels = [0, *range(n_patch - 1, 0, -1)]
    flat = [part[rel] for part in blocks for rel in rels]
    return call(
        functools.partial(mix_kernel, rels),
        "mix",
        jax.ShapeDtypeStruct((rows, width), jnp.bfloat16),
        1,
        [spec((rows, width)), spec((1, width))] + [spec((piece, cols))] * len(flat),
        spec((rows, width)),
    )(where, hidden_in, attn_gate[None], *flat)


def gather(parts, n_patch):
    if n_patch != 4:
        return [
            ([x] + [swap(x, "patch", n_patch, rel) for rel in range(1, n_patch)], [])
            for x in parts
        ]
    far = [swap(x, "patch", 4, 2) for x in parts]
    next_to = [swap(x, "patch", 4, 1) for x in parts]
    out = []
    for at, x in enumerate(parts):
        far[at], next_to[at], parts = lax.optimization_barrier((far[at], next_to[at], parts))
        middle = swap(parts[at], "patch", 4, 3, (1, 2))
        ends = lax.ppermute(far[at], "patch", [(1, 0), (2, 3)])
        if at + 1 < len(parts):
            ends, far[at + 1], next_to[at + 1] = lax.optimization_barrier(
                (ends, far[at + 1], next_to[at + 1])
            )
        out.append(([x, next_to[at], far[at], middle], [ends]))
    return out


def add_sub_kernel(n_sub, where_ref, *refs):
    terms, kept_ref, outs = refs[:n_sub], refs[n_sub], refs[n_sub + 1 :]
    for head in range(len(outs) + 1):
        total = terms[0][head].astype(jnp.float32)
        for term in terms[1:]:
            total += term[head].astype(jnp.float32)
        if head == 0:
            kept_ref[...] = total
        else:
            outs[head - 1][...] = total.astype(jnp.bfloat16)


def add_head_kernel(n_more, where_ref, kept_ref, *refs):
    for at, out in enumerate(refs[n_more:]):
        total = kept_ref[at]
        for term in refs[:n_more]:
            total += term[at].astype(jnp.float32)
        out[...] = total.astype(jnp.bfloat16)


def reduce_sub(sizes, where, terms):
    n_sub, n_head = sizes["sub"], sizes["head"]
    terms = [terms[0]] + [swap(terms[rel], "sub", n_sub, rel) for rel in range(1, n_sub)]
    shape = terms[0].shape[1:]
    return call(
        functools.partial(add_sub_kernel, n_sub),
        "add_sub",
        [jax.ShapeDtypeStruct(shape, jnp.float32)]
        + [jax.ShapeDtypeStruct(shape, jnp.bfloat16)] * (n_head - 1),
        1,
        [spec(terms[0].shape)] * n_sub,
        [spec(shape)] * n_head,
    )(where, *terms)


def reduce_head(sizes, where, sums):
    n_head = sizes["head"]
    shape = sums[0].shape
    sums = [sums[0]] + [swap(sums[rel], "head", n_head, rel) for rel in range(1, n_head)]
    return call(
        functools.partial(add_head_kernel, n_head - 1),
        "add_head",
        [jax.ShapeDtypeStruct(shape[1:], jnp.bfloat16)] * shape[0],
        1,
        [spec(shape)] * n_head,
        [spec(shape[1:])] * shape[0],
    )(where, *sums)


def sum_tail(sizes, where, pieces, kv_pieces, out_weight, hidden_in, attn_gate):
    n_patch, n_head, n_sub = sizes["patch"], sizes["head"], sizes["sub"]
    split, tok = len(pieces), pieces[0].shape[1]
    count = n_head * n_sub
    piece = tok // count
    parts = 2 if piece % 32 == 0 else 1
    attended = []
    for part in range(parts):
        rows = (part * (piece // parts), piece // parts)
        x = attend(where, rows, count, pieces, kv_pieces)
        attended.append(x.reshape(-1, x.shape[2]))
    slots = gather(attended, n_patch)
    blocks = []
    for part in range(parts):
        terms = project(split, where, *slots[part], out_weight, n_head, n_sub)
        total = reduce_head(sizes, where, reduce_sub(sizes, where, terms))
        blocks.append(
            [total[0]] + [swap(total[rel], "patch", n_patch, rel) for rel in range(1, n_patch)]
        )
    return mix(where, hidden_in, attn_gate, blocks)


def attend_half_kernel(half, where_ref, *refs):
    pieces, out = refs[:-1], refs[-1]
    factor = HEAD_DIM**-0.5 * math.log2(math.e)
    rows, feat = out.shape[1:]
    start = pl.multiple_of((where_ref[HEAD] ^ half) * rows, rows)
    for head in range(feat // HEAD_DIM):
        lanes = pl.ds(head * HEAD_DIM, HEAD_DIM)
        keys = jnp.concatenate([ref[1, :, lanes] for ref in pieces], axis=0)
        values = jnp.concatenate([ref[2, :, lanes] for ref in pieces], axis=0)
        values = jnp.concatenate([values, jnp.ones_like(values)], axis=1)
        query = jnp.concatenate([ref[0, pl.ds(start, rows), lanes] for ref in pieces], axis=0)
        scores = lax.dot_general(
            query, keys, (((1,), (1,)), ((), ())), preferred_element_type=jnp.float32
        )
        peak = jnp.max(scores, axis=1, keepdims=True)
        expo = jnp.exp2((scores - peak) * factor).astype(jnp.bfloat16)
        mix = jnp.dot(expo, values, preferred_element_type=jnp.float32)
        mix = (mix[:, :HEAD_DIM] / mix[:, HEAD_DIM:]).astype(jnp.bfloat16)
        for rel in range(len(pieces)):
            out[where_ref[NEAR] ^ rel, :, lanes] = mix[rel * rows : (rel + 1) * rows]


def attend_half(where, half, pieces):
    _, tok, feat = pieces[0].shape
    out = jax.ShapeDtypeStruct((len(pieces), tok // 2, feat), jnp.bfloat16)
    return call(
        functools.partial(attend_half_kernel, half),
        "attend",
        out,
        1,
        [spec((3, tok, feat))] * len(pieces),
        spec(out.shape),
        flops=HALF_FLOPS,
    )(where, *pieces).reshape(-1, feat)


def add_product_kernel(count, where_ref, *refs):
    total = refs[2 * count][...] if len(refs) > 2 * count + 1 else None
    for slot, weight in zip(refs[:count], refs[count : 2 * count]):
        term = jnp.dot(slot[...], weight[...], preferred_element_type=jnp.float32)
        total = term if total is None else total + term
    refs[-1][...] = total


def add_product(where, slots, weight, acc=None):
    rows, feat = next(iter(slots.values())).shape
    cols = weight.shape[1]
    wide = cols // 2
    whole = pl.BlockSpec((rows, wide), lambda i, w: (0, i))
    rels = list(slots)
    return call(
        functools.partial(add_product_kernel, len(rels)),
        "products",
        jax.ShapeDtypeStruct((rows, cols), jnp.float32),
        2,
        [spec((rows, feat))] * len(rels)
        + [pl.BlockSpec((feat, wide), lambda i, w, rel=rel: (w[NEAR] ^ rel, i)) for rel in rels]
        + ([] if acc is None else [whole]),
        whole,
        flops=ZERO_FLOPS if acc is None else 1,
    )(where, *slots.values(), *[weight] * len(rels), *([] if acc is None else [acc]))


def partner_place(where_ref, head):
    return (head + FETCHED * where_ref[GRP]) % 8


def first_kernel(where_ref, *refs):
    last, more, slots = refs[0], refs[1], refs[2:5]
    acc_ref, own_ref, fetched_ref, passed_ref, out_ref, held_ref = refs[5:]
    rows, feat = last.shape
    cut = fetched_ref.shape[0]

    def put(at, block):
        for head in range(2):
            there = partner_place(where_ref, 2 * (where_ref[NEAR] ^ at) + head)
            lanes = pl.ds(pl.multiple_of(there * HEAD_DIM, HEAD_DIM), HEAD_DIM)
            held_ref[:, lanes] = block[:, head * HEAD_DIM : (head + 1) * HEAD_DIM]

    @pl.when(pl.program_id(0) == 0)
    def arrange():
        for at, slot in zip((0, 2, 1), slots):
            put(at, slot[...])
        put(3, jnp.zeros((rows, feat), jnp.bfloat16))

    block = jnp.where(where_ref[INNER] == 1, last[...], more[...])
    acc = acc_ref[...]
    acc += jnp.dot(block, own_ref[...], preferred_element_type=jnp.float32)
    acc += jnp.dot(held_ref[:, :cut], fetched_ref[...], preferred_element_type=jnp.float32)
    acc += jnp.dot(held_ref[:, cut:], passed_ref[...], preferred_element_type=jnp.float32)
    out_ref[...] = acc


def first_product(where, last, more, slots, acc, weights):
    rows, feat = last.shape
    own, fetched, passed = weights
    wide = own.shape[1] // 2
    whole = pl.BlockSpec((rows, wide), lambda i, w: (0, i))
    return call(
        first_kernel,
        "first",
        jax.ShapeDtypeStruct(acc.shape, jnp.float32),
        2,
        [spec((rows, feat))] * 5
        + [whole, pl.BlockSpec((feat, wide), lambda i, w: (w[NEAR] ^ 3, i))]
        + [pl.BlockSpec((x.shape[0], wide), lambda i, w: (0, i)) for x in (fetched, passed)],
        whole,
        [pltpu.VMEM((rows, 4 * feat), jnp.bfloat16)],
    )(where, last, more, *slots, acc, own, fetched, passed)


def second_kernel(where_ref, slot, more, fetched_ref, passed_ref, acc_in, keep_ref, send_ref, acc_ref):
    weight = []
    for head in range(2):
        place = partner_place(where_ref, 2 * (where_ref[NEAR] ^ 3) + head)
        here = jnp.minimum(place, FETCHED - 1) * HEAD_DIM
        there = jnp.maximum(place - FETCHED, 0) * HEAD_DIM
        weight.append(
            jnp.where(
                place < FETCHED,
                fetched_ref[pl.ds(pl.multiple_of(here, HEAD_DIM), HEAD_DIM), :],
                passed_ref[pl.ds(pl.multiple_of(there, HEAD_DIM), HEAD_DIM), :],
            )
        )
    block = jnp.where(where_ref[INNER] == 1, slot[...], more[...])
    acc = acc_in[...] + jnp.dot(
        block, jnp.concatenate(weight, axis=0), preferred_element_type=jnp.float32
    )
    acc_ref[...] = acc.reshape(acc_ref.shape)
    for sub, out in enumerate((keep_ref, send_ref)):
        for at in range(4):
            out[at] = acc_ref[where_ref[NEAR] ^ at, where_ref[SUB] ^ sub].astype(jnp.bfloat16)


def second_product(where, chunk, slot, more, weights, acc):
    rows, feat = slot.shape
    cols = weights[0].shape[1]
    wide = cols // 2
    out = jax.ShapeDtypeStruct((4, rows // 8, wide), jnp.bfloat16)
    return call(
        second_kernel,
        "second",
        [out] * 2,
        1,
        [spec((rows, feat))] * 2
        + [pl.BlockSpec((x.shape[0], wide), lambda i, w: (0, chunk)) for x in weights]
        + [pl.BlockSpec((rows, wide), lambda i, w: (0, chunk))],
        [spec(out.shape)] * 2,
        [pltpu.VMEM((4, 2, rows // 8, wide), jnp.float32)],
    )(where, slot, more, *weights, acc)


def add_kernel(where_ref, keep_ref, term_ref, *outs):
    for at, out in enumerate(outs):
        total = keep_ref[at].astype(jnp.float32) + term_ref[at].astype(jnp.float32)
        out[...] = total.astype(jnp.bfloat16)


def add(where, keep, term):
    return call(
        add_kernel,
        "add",
        [jax.ShapeDtypeStruct(keep.shape[1:], jnp.bfloat16)] * keep.shape[0],
        1,
        [spec(keep.shape)] * 2,
        [spec(keep.shape[1:])] * keep.shape[0],
    )(where, keep, term)


def take_kernel(where_ref, weight_ref, out_ref):
    out_ref[...] = weight_ref[...]


def take_half(where, weight):
    rows, cols = weight.shape[0] // 2, weight.shape[1]
    return call(
        take_kernel,
        "take",
        jax.ShapeDtypeStruct((rows, cols), weight.dtype),
        2,
        [pl.BlockSpec((rows // 2, cols), lambda i, w: (2 * w[GRP] + i, 0))],
        pl.BlockSpec((rows // 2, cols), lambda i, w: (i, 0)),
    )(where, weight)


def share_tail(sizes, where, pieces, kv_pieces, out_weight, hidden_in, attn_gate):
    out_weight, where = lax.optimization_barrier((out_weight, where))
    fetched = swap(take_half(where, out_weight), "head", 2, 1)
    own, fetched = lax.optimization_barrier((pieces[0], fetched))
    pieces = [own, *pieces[1:]]
    passed = swap(fetched, "grp", 2, 1)

    pieces = [pieces[0], *pieces[:0:-1]]
    mine = attend_half(where, 0, pieces)
    where, mine = lax.optimization_barrier((where, mine))
    other = swap(attend_half(where, 1, pieces), "head", 2, 1)
    acc = add_product(where, {0: mine}, out_weight)
    other, acc = lax.optimization_barrier((other, acc))
    slots = []
    for at, x in enumerate((mine, other)):
        next_to, far = swap(x, "patch", 4, 1), swap(x, "patch", 4, 2)
        next_to, far, other, x = lax.optimization_barrier((next_to, far, other, x))
        if at == 1:
            acc = add_product(where, {2: slots[0][2], 1: slots[0][1]}, out_weight, acc)
            far, x, acc = lax.optimization_barrier((far, x, acc))
        middle = swap(x, "patch", 4, 3, (1, 2))
        ends = lax.ppermute(far, "patch", [(1, 0), (2, 3)])
        slots.append([x, next_to, far, middle, ends])
    weights = [out_weight, fetched, passed]
    partner = [slots[1][at] for at in (0, 2, 1)]
    acc = first_product(where, *slots[0][3:], partner, acc, weights)
    terms = [second_product(where, at, *slots[1][3:], [fetched, passed], acc) for at in range(2)]
    blocks = []
    for keep, send in terms:
        total = add(where, keep, swap(send, "sub", 2, 1))
        blocks.append([total[0]] + [swap(total[rel], "patch", 4, rel) for rel in range(3, 0, -1)])
    return mix_columns(where, hidden_in, attn_gate, blocks)


def mix_columns_kernel(where_ref, hidden_ref, gate_ref, *refs):
    blocks, out_ref = refs[:-1], refs[-1]
    cols = blocks[0].shape[1]
    for chunk in range(2):
        for at, rel in enumerate((0, 3, 2, 1)):
            start = (2 * (where_ref[PATCH] ^ rel) + chunk) * cols
            lanes = pl.ds(pl.multiple_of(start, HEAD_DIM), cols)
            mixed = hidden_ref[:, lanes].astype(jnp.float32) + gate_ref[:, lanes] * blocks[
                4 * chunk + at
            ][...].astype(jnp.float32)
            out_ref[:, lanes] = mixed.astype(jnp.bfloat16)


def mix_columns(where, hidden_in, attn_gate, blocks):
    rows, width = hidden_in.shape
    flat = [x for chunk in blocks for x in chunk]
    return call(
        mix_columns_kernel,
        "mix",
        jax.ShapeDtypeStruct((rows, width), jnp.bfloat16),
        2,
        [pl.BlockSpec((rows // 2, width), lambda i, w: (i, 0)), spec((1, width))]
        + [pl.BlockSpec((rows // 2, flat[0].shape[1]), lambda i, w: (i, 0))] * len(flat),
        pl.BlockSpec((rows // 2, width), lambda i, w: (i, 0)),
    )(where, hidden_in, attn_gate[None], *flat)


def body(sizes, queries, fresh_kv, cached_kv, exponents, out_weight, hidden_in, attn_gate):
    n_patch, n_head, n_sub = sizes["patch"], sizes["head"], sizes["sub"]
    tok, channels = queries.shape
    heads = channels // HEAD_DIM
    split = math.gcd(heads, n_patch)
    patch_at = lax.axis_index("patch")
    inner = (patch_at > 0) & (patch_at < n_patch - 1)
    where = jnp.stack(
        [
            patch_at,
            patch_at % split,
            lax.axis_index("head"),
            lax.axis_index("sub"),
            inner,
            lax.axis_index("grp"),
        ]
    ).astype(jnp.int32)

    arrays = (exponents, queries, fresh_kv, cached_kv)
    sent = pack(split, *arrays)
    far_first = [
        swap(x, "patch", n_patch, split - 1 - at) for at, x in enumerate(sent)
    ]
    where, sent = lax.optimization_barrier((where, sent))
    pieces = [pack_own(split, where, *arrays), *far_first]
    kv_pieces = list(pieces)
    for rel in range(split, n_patch, split):
        kv_pieces += [swap(x, "patch", n_patch, rel) for x in pieces]

    tail = (sizes, where, pieces, kv_pieces, out_weight, hidden_in, attn_gate)
    if (sizes["grp"], n_head, split, n_patch) == (2, 2, 4, 4):
        return share_tail(*tail)
    return sum_tail(*tail)


def solution(mesh):
    in_specs = (
        P(("grp", "patch"), ("head", "sub")),
        P(None, ("grp", "patch"), ("head", "sub")),
        P(None, "grp", ("head", "sub")),
        P(None, ("grp", "patch"), ("head", "sub")),
        P(("head", "sub"), "patch"),
        P(("grp", "patch", "head", "sub"), None),
        P(),
    )
    out_specs = P(("grp", "patch", "head", "sub"), None)
    return jax.shard_map(
        functools.partial(body, dict(mesh.shape)),
        mesh=mesh,
        in_specs=in_specs,
        out_specs=out_specs,
        check_vma=False,
    )
```

```python
import functools
import math

import jax
import jax.numpy as jnp
from jax import lax
from jax.experimental import pallas as pl
from jax.experimental.pallas import tpu as pltpu
from jax.sharding import PartitionSpec as P

HEAD_DIM = 128
SCALE_ROWS = 128
SATURATION = 448.0
PACK_ROWS = 64
VMEM_BYTES = 32 * 1024 * 1024
PACK_VMEM_BYTES = 60 * 1024 * 1024
ATTEND_FLOPS = 1
PROJECT_FLOPS = 1
OWN_FLOPS = 1
FETCHED = 4
ZERO_FLOPS = 6_000_000_000
HALF_FLOPS = 1

PATCH, NEAR, HEAD, SUB, INNER, GRP = range(6)


def spec(shape):
    return pl.BlockSpec(shape, lambda i, w: (0,) * len(shape))


def call(kernel, name, out_shape, grid, in_specs, out_specs, scratch=(), flops=1, vmem=VMEM_BYTES):
    return pl.pallas_call(
        kernel,
        out_shape=out_shape,
        grid_spec=pltpu.PrefetchScalarGridSpec(
            num_scalar_prefetch=1,
            grid=(grid,),
            in_specs=in_specs,
            out_specs=out_specs,
            scratch_shapes=list(scratch),
        ),
        compiler_params=pltpu.CompilerParams(vmem_limit_bytes=vmem),
        cost_estimate=pl.CostEstimate(flops=flops, bytes_accessed=0, transcendentals=0),
        name=name,
    )


def swap(x, axes, count, mask, only=None):
    pairs = [(at, at ^ mask) for at in range(count) if only is None or at in only]
    return lax.ppermute(x, axes, pairs)


def power_of_two(exponent):
    return lax.shift_left(jnp.int32(1), exponent + 15).astype(jnp.float32) * 2.0**-15


def decode(fresh, cached, exponent):
    cached = cached.astype(jnp.float32)
    residual = fresh.astype(jnp.float32) - cached
    scaled = residual * power_of_two(-exponent)
    codes = jnp.clip(scaled, -SATURATION, SATURATION).astype(jnp.bfloat16)
    return (cached + codes.astype(jnp.float32) * power_of_two(exponent)).astype(jnp.bfloat16)


def pack_kernel(split, per, shares, exps_ref, q_ref, fresh_ref, cached_ref, weight_ref, *refs):
    outs, part_ref, bufs = refs[: split - 1], refs[split - 1], refs[split : 2 * split - 1]
    q_buf, fresh_buf, cached_buf, sems, out_sems, part_sem = refs[2 * split - 1 :]
    patch = lax.axis_index("patch")
    count = part_ref.shape[0]
    start = lax.axis_index("grp") * count if shares == 2 else 0
    part = pltpu.make_async_copy(
        weight_ref.at[pl.ds(pl.multiple_of(start, HEAD_DIM), count)], part_ref, part_sem
    )
    near = lax.rem(patch, split)
    tok = q_buf.shape[0]
    copies, sent = [], []
    for block in range(tok // PACK_ROWS):
        rows = pl.ds(block * PACK_ROWS, PACK_ROWS)
        there = pl.ds(pl.multiple_of(patch * tok + block * PACK_ROWS, PACK_ROWS), PACK_ROWS)
        copies.append(
            [
                pltpu.make_async_copy(q_ref.at[rows], q_buf.at[rows], sems.at[block, 0]),
                pltpu.make_async_copy(fresh_ref.at[:, rows], fresh_buf.at[:, rows], sems.at[block, 1]),
                pltpu.make_async_copy(cached_ref.at[:, there], cached_buf.at[:, rows], sems.at[block, 2]),
            ]
        )
        for copy in copies[-1]:
            copy.start()
    part.start()
    for block in range(tok // PACK_ROWS):
        rows = pl.ds(block * PACK_ROWS, PACK_ROWS)
        for copy in copies[block]:
            copy.wait()
        for rel in range(split - 1, 0, -1):
            buf = bufs[split - 1 - rel]
            for chunk in range(per):
                head = (near ^ rel) * per + chunk
                lanes = pl.ds(pl.multiple_of(head * HEAD_DIM, HEAD_DIM), HEAD_DIM)
                here = pl.ds(chunk * HEAD_DIM, HEAD_DIM)
                buf[0, rows, here] = q_buf[rows, lanes]
                for stacked in range(2):
                    buf[1 + stacked, rows, here] = decode(
                        fresh_buf[stacked, rows, lanes],
                        cached_buf[stacked, rows, lanes],
                        exps_ref[stacked, block * PACK_ROWS // SCALE_ROWS, head],
                    )
            sent.append(
                pltpu.make_async_copy(
                    buf.at[:, rows],
                    outs[split - 1 - rel].at[:, rows],
                    out_sems.at[block, rel - 1],
                )
            )
            sent[-1].start()
    for copy in sent:
        copy.wait()
    part.wait()


def pack(split, shares, exponents, queries, fresh_kv, cached_kv, weight):
    tok, channels = queries.shape
    feat = channels // split
    blocks = tok // PACK_ROWS
    hbm = pl.BlockSpec(memory_space=pltpu.HBM)
    return pl.pallas_call(
        functools.partial(pack_kernel, split, feat // HEAD_DIM, shares),
        out_shape=[jax.ShapeDtypeStruct((3, tok, feat), jnp.bfloat16)] * (split - 1)
        + [jax.ShapeDtypeStruct((weight.shape[0] // shares, weight.shape[1]), weight.dtype)],
        in_specs=[pl.BlockSpec(memory_space=pltpu.SMEM), hbm, hbm, hbm, hbm],
        out_specs=[hbm] * split,
        scratch_shapes=[pltpu.VMEM((3, tok, feat), jnp.bfloat16)] * (split - 1)
        + [
            pltpu.VMEM((tok, channels), jnp.bfloat16),
            pltpu.VMEM((2, tok, channels), jnp.bfloat16),
            pltpu.VMEM((2, tok, channels), jnp.bfloat16),
            pltpu.SemaphoreType.DMA((blocks, 3)),
            pltpu.SemaphoreType.DMA((blocks, split - 1)),
            pltpu.SemaphoreType.DMA,
        ],
        compiler_params=pltpu.CompilerParams(vmem_limit_bytes=PACK_VMEM_BYTES),
        name="pack",
    )(exponents, queries, fresh_kv, cached_kv, weight)


def own_kernel(per, where_ref, exps_ref, q_ref, fresh_ref, cached_ref, out_ref):
    out_ref[0] = q_ref[...]
    for chunk in range(per):
        lanes = pl.ds(chunk * HEAD_DIM, HEAD_DIM)
        for block in range(q_ref.shape[0] // SCALE_ROWS):
            rows = pl.ds(block * SCALE_ROWS, SCALE_ROWS)
            for stacked in range(2):
                out_ref[1 + stacked, rows, lanes] = decode(
                    fresh_ref[stacked, rows, lanes],
                    cached_ref[stacked, rows, lanes],
                    exps_ref[stacked, block, where_ref[NEAR] * per + chunk],
                )


def pack_own(split, where, exponents, queries, fresh_kv, cached_kv):
    tok, channels = queries.shape
    feat = channels // split
    out = jax.ShapeDtypeStruct((3, tok, feat), jnp.bfloat16)
    return call(
        functools.partial(own_kernel, feat // HEAD_DIM),
        "own",
        out,
        1,
        [
            pl.BlockSpec(memory_space=pltpu.SMEM),
            pl.BlockSpec((tok, feat), lambda i, w: (0, w[NEAR])),
            pl.BlockSpec((2, tok, feat), lambda i, w: (0, 0, w[NEAR])),
            pl.BlockSpec((2, tok, feat), lambda i, w: (0, w[PATCH], w[NEAR])),
        ],
        spec(out.shape),
    )(where, exponents, queries, fresh_kv, cached_kv)


def attend_kernel(split, part, where_ref, *refs):
    q_refs, kv_refs, out_ref = (refs[0], *refs[split - 1 : 0 : -1]), refs[:-1], refs[-1]
    factor = HEAD_DIM**-0.5 * math.log2(math.e)
    tok, feat = q_refs[0].shape[1:]
    count = out_ref.shape[1] // part[1]
    starts = [at * (tok // count) + part[0] for at in range(count)]
    for head in range(feat // HEAD_DIM):
        lanes = pl.ds(head * HEAD_DIM, HEAD_DIM)
        keys = jnp.concatenate([ref[1, :, lanes] for ref in kv_refs], axis=0)
        values = jnp.concatenate([ref[2, :, lanes] for ref in kv_refs], axis=0)
        values = jnp.concatenate([values, jnp.ones_like(values)], axis=1)
        for rel in range(split):
            rows = [q_refs[rel][0, start : start + part[1], lanes] for start in starts]
            query = jnp.concatenate(rows, axis=0) if len(rows) > 1 else rows[0]
            scores = lax.dot_general(
                query, keys, (((1,), (1,)), ((), ())), preferred_element_type=jnp.float32
            )
            peak = jnp.max(scores, axis=1, keepdims=True)
            expo = jnp.exp2((scores - peak) * factor).astype(jnp.bfloat16)
            mix = jnp.dot(expo, values, preferred_element_type=jnp.float32)
            mix = mix[:, :HEAD_DIM] / mix[:, HEAD_DIM:]
            out_ref[where_ref[NEAR] ^ rel, :, lanes] = mix.astype(jnp.bfloat16)


def attend(where, part, count, pieces, kv_pieces):
    split = len(pieces)
    _, tok, feat = pieces[0].shape
    out = jax.ShapeDtypeStruct((split, count * part[1], feat), jnp.bfloat16)
    return call(
        functools.partial(attend_kernel, split, part),
        "attend",
        out,
        1,
        [spec((3, tok, feat))] * len(kv_pieces),
        spec(out.shape),
        flops=ATTEND_FLOPS,
    )(where, *kv_pieces)


def project_kernel(split, n_slots, n_more, where_ref, *refs):
    slots, refs = refs[:n_slots], refs[n_slots:]
    more, weight_ref, refs = refs[:n_more], refs[n_more], refs[n_more + 1 :]
    outs, held_ref, acc_ref = refs[:-2], refs[-2], refs[-1]
    rows, feat = slots[0].shape
    n_sub, n_head = acc_ref.shape[3], acc_ref.shape[2]

    @pl.when(pl.program_id(0) == 0)
    def arrange():
        for at, slot in enumerate(slots):
            group, near = divmod(at, split)
            lane = (where_ref[NEAR] ^ near) * feat
            block = slot[...]
            if more and at == n_slots - 1:
                block = jnp.where(where_ref[INNER] == 1, block, more[0][...])
            held_ref[
                group * rows : (group + 1) * rows, pl.ds(pl.multiple_of(lane, HEAD_DIM), feat)
            ] = block

    acc = jnp.dot(held_ref[...], weight_ref[...], preferred_element_type=jnp.float32)
    acc_ref[...] = acc.reshape(acc_ref.shape)
    for sub in range(n_sub):
        for head in range(n_head):
            for at in range(n_slots):
                group, near = divmod(at, split)
                outs[sub][head, at] = acc_ref[
                    group, where_ref[NEAR] ^ near, where_ref[HEAD] ^ head, where_ref[SUB] ^ sub
                ].astype(jnp.bfloat16)


def project(split, where, slots, more, weight, n_head, n_sub):
    rows, feat = slots[0].shape
    n_patch = len(slots)
    total = rows * n_patch // split
    depth, cols = weight.shape
    wide = 640 if cols % 640 == 0 else cols
    piece = rows // (split * n_head * n_sub)
    return call(
        functools.partial(project_kernel, split, n_patch, len(more)),
        "project",
        [jax.ShapeDtypeStruct((n_head, n_patch, piece, cols), jnp.bfloat16)] * n_sub,
        cols // wide,
        [spec((rows, feat))] * (n_patch + len(more))
        + [pl.BlockSpec((depth, wide), lambda i, w: (0, i))],
        [pl.BlockSpec((n_head, n_patch, piece, wide), lambda i, w: (0, 0, 0, i))] * n_sub,
        [
            pltpu.VMEM((total, depth), jnp.bfloat16),
            pltpu.VMEM((n_patch // split, split, n_head, n_sub, piece, wide), jnp.float32),
        ],
        flops=PROJECT_FLOPS,
    )(where, *slots, *more, weight)


def mix_kernel(rels, where_ref, hidden_ref, gate_ref, *refs):
    blocks, out_ref = refs[:-1], refs[-1]
    piece, cols = blocks[0].shape
    for part in range(len(blocks) // len(rels)):
        rows = pl.ds(part * piece, piece)
        for at, rel in enumerate(rels):
            lanes = pl.ds(pl.multiple_of((where_ref[PATCH] ^ rel) * cols, HEAD_DIM), cols)
            mixed = hidden_ref[rows, lanes].astype(jnp.float32) + gate_ref[:, lanes] * blocks[
                part * len(rels) + at
            ][...].astype(jnp.float32)
            out_ref[rows, lanes] = mixed.astype(jnp.bfloat16)


def mix(where, hidden_in, attn_gate, blocks):
    rows, width = hidden_in.shape
    n_patch = len(blocks[0])
    piece, cols = blocks[0][0].shape
    if cols % HEAD_DIM:
        order = jnp.concatenate([jnp.stack(x) for x in blocks], axis=1)
        order = order[where[PATCH] ^ jnp.arange(n_patch)]
        projected = order.transpose(1, 0, 2).reshape(rows, width).astype(jnp.float32)
        return (hidden_in.astype(jnp.float32) + attn_gate * projected).astype(jnp.bfloat16)
    rels = [0, *range(n_patch - 1, 0, -1)]
    flat = [part[rel] for part in blocks for rel in rels]
    return call(
        functools.partial(mix_kernel, rels),
        "mix",
        jax.ShapeDtypeStruct((rows, width), jnp.bfloat16),
        1,
        [spec((rows, width)), spec((1, width))] + [spec((piece, cols))] * len(flat),
        spec((rows, width)),
    )(where, hidden_in, attn_gate[None], *flat)


def gather(parts, n_patch):
    if n_patch != 4:
        return [
            ([x] + [swap(x, "patch", n_patch, rel) for rel in range(1, n_patch)], [])
            for x in parts
        ]
    far = [swap(x, "patch", 4, 2) for x in parts]
    next_to = [swap(x, "patch", 4, 1) for x in parts]
    out = []
    for at, x in enumerate(parts):
        far[at], next_to[at], parts = lax.optimization_barrier((far[at], next_to[at], parts))
        middle = swap(parts[at], "patch", 4, 3, (1, 2))
        ends = lax.ppermute(far[at], "patch", [(1, 0), (2, 3)])
        if at + 1 < len(parts):
            ends, far[at + 1], next_to[at + 1] = lax.optimization_barrier(
                (ends, far[at + 1], next_to[at + 1])
            )
        out.append(([x, next_to[at], far[at], middle], [ends]))
    return out


def add_sub_kernel(n_sub, where_ref, *refs):
    terms, kept_ref, outs = refs[:n_sub], refs[n_sub], refs[n_sub + 1 :]
    for head in range(len(outs) + 1):
        total = terms[0][head].astype(jnp.float32)
        for term in terms[1:]:
            total += term[head].astype(jnp.float32)
        if head == 0:
            kept_ref[...] = total
        else:
            outs[head - 1][...] = total.astype(jnp.bfloat16)


def add_head_kernel(n_more, where_ref, kept_ref, *refs):
    for at, out in enumerate(refs[n_more:]):
        total = kept_ref[at]
        for term in refs[:n_more]:
            total += term[at].astype(jnp.float32)
        out[...] = total.astype(jnp.bfloat16)


def reduce_sub(sizes, where, terms):
    n_sub, n_head = sizes["sub"], sizes["head"]
    terms = [terms[0]] + [swap(terms[rel], "sub", n_sub, rel) for rel in range(1, n_sub)]
    shape = terms[0].shape[1:]
    return call(
        functools.partial(add_sub_kernel, n_sub),
        "add_sub",
        [jax.ShapeDtypeStruct(shape, jnp.float32)]
        + [jax.ShapeDtypeStruct(shape, jnp.bfloat16)] * (n_head - 1),
        1,
        [spec(terms[0].shape)] * n_sub,
        [spec(shape)] * n_head,
    )(where, *terms)


def reduce_head(sizes, where, sums):
    n_head = sizes["head"]
    shape = sums[0].shape
    sums = [sums[0]] + [swap(sums[rel], "head", n_head, rel) for rel in range(1, n_head)]
    return call(
        functools.partial(add_head_kernel, n_head - 1),
        "add_head",
        [jax.ShapeDtypeStruct(shape[1:], jnp.bfloat16)] * shape[0],
        1,
        [spec(shape)] * n_head,
        [spec(shape[1:])] * shape[0],
    )(where, *sums)


def sum_tail(sizes, where, pieces, kv_pieces, out_weight, hidden_in, attn_gate):
    n_patch, n_head, n_sub = sizes["patch"], sizes["head"], sizes["sub"]
    split, tok = len(pieces), pieces[0].shape[1]
    count = n_head * n_sub
    piece = tok // count
    parts = 2 if piece % 32 == 0 else 1
    attended = []
    for part in range(parts):
        rows = (part * (piece // parts), piece // parts)
        x = attend(where, rows, count, pieces, kv_pieces)
        attended.append(x.reshape(-1, x.shape[2]))
    slots = gather(attended, n_patch)
    blocks = []
    for part in range(parts):
        terms = project(split, where, *slots[part], out_weight, n_head, n_sub)
        total = reduce_head(sizes, where, reduce_sub(sizes, where, terms))
        blocks.append(
            [total[0]] + [swap(total[rel], "patch", n_patch, rel) for rel in range(1, n_patch)]
        )
    return mix(where, hidden_in, attn_gate, blocks)


def attend_half_kernel(half, where_ref, *refs):
    pieces, out = refs[:-1], refs[-1]
    factor = HEAD_DIM**-0.5 * math.log2(math.e)
    rows, feat = out.shape[1:]
    start = pl.multiple_of((where_ref[HEAD] ^ half) * rows, rows)
    for head in range(feat // HEAD_DIM):
        lanes = pl.ds(head * HEAD_DIM, HEAD_DIM)
        keys = jnp.concatenate([ref[1, :, lanes] for ref in pieces], axis=0)
        values = jnp.concatenate([ref[2, :, lanes] for ref in pieces], axis=0)
        values = jnp.concatenate([values, jnp.ones_like(values)], axis=1)
        query = jnp.concatenate([ref[0, pl.ds(start, rows), lanes] for ref in pieces], axis=0)
        scores = lax.dot_general(
            query, keys, (((1,), (1,)), ((), ())), preferred_element_type=jnp.float32
        )
        peak = jnp.max(scores, axis=1, keepdims=True)
        expo = jnp.exp2((scores - peak) * factor).astype(jnp.bfloat16)
        mix = jnp.dot(expo, values, preferred_element_type=jnp.float32)
        mix = (mix[:, :HEAD_DIM] / mix[:, HEAD_DIM:]).astype(jnp.bfloat16)
        for rel in range(len(pieces)):
            out[where_ref[NEAR] ^ rel, :, lanes] = mix[rel * rows : (rel + 1) * rows]


def attend_half(where, half, pieces):
    _, tok, feat = pieces[0].shape
    out = jax.ShapeDtypeStruct((len(pieces), tok // 2, feat), jnp.bfloat16)
    return call(
        functools.partial(attend_half_kernel, half),
        "attend",
        out,
        1,
        [spec((3, tok, feat))] * len(pieces),
        spec(out.shape),
        flops=HALF_FLOPS,
    )(where, *pieces).reshape(-1, feat)


def add_product_kernel(count, where_ref, *refs):
    total = refs[2 * count][...] if len(refs) > 2 * count + 1 else None
    for slot, weight in zip(refs[:count], refs[count : 2 * count]):
        term = jnp.dot(slot[...], weight[...], preferred_element_type=jnp.float32)
        total = term if total is None else total + term
    refs[-1][...] = total


def add_product(where, slots, weight, acc=None):
    rows, feat = next(iter(slots.values())).shape
    cols = weight.shape[1]
    wide = cols // 2
    whole = pl.BlockSpec((rows, wide), lambda i, w: (0, i))
    rels = list(slots)
    return call(
        functools.partial(add_product_kernel, len(rels)),
        "products",
        jax.ShapeDtypeStruct((rows, cols), jnp.float32),
        2,
        [spec((rows, feat))] * len(rels)
        + [pl.BlockSpec((feat, wide), lambda i, w, rel=rel: (w[NEAR] ^ rel, i)) for rel in rels]
        + ([] if acc is None else [whole]),
        whole,
        flops=ZERO_FLOPS if acc is None else 1,
    )(where, *slots.values(), *[weight] * len(rels), *([] if acc is None else [acc]))


def partner_place(where_ref, head):
    return (head + FETCHED * where_ref[GRP]) % 8


def first_kernel(where_ref, *refs):
    last, more, slots = refs[0], refs[1], refs[2:5]
    acc_ref, own_ref, fetched_ref, passed_ref, out_ref, held_ref = refs[5:]
    rows, feat = last.shape
    cut = fetched_ref.shape[0]

    def put(at, block):
        for head in range(2):
            there = partner_place(where_ref, 2 * (where_ref[NEAR] ^ at) + head)
            lanes = pl.ds(pl.multiple_of(there * HEAD_DIM, HEAD_DIM), HEAD_DIM)
            held_ref[:, lanes] = block[:, head * HEAD_DIM : (head + 1) * HEAD_DIM]

    @pl.when(pl.program_id(0) == 0)
    def arrange():
        for at, slot in zip((0, 2, 1), slots):
            put(at, slot[...])
        put(3, jnp.zeros((rows, feat), jnp.bfloat16))

    block = jnp.where(where_ref[INNER] == 1, last[...], more[...])
    acc = acc_ref[...]
    acc += jnp.dot(block, own_ref[...], preferred_element_type=jnp.float32)
    acc += jnp.dot(held_ref[:, :cut], fetched_ref[...], preferred_element_type=jnp.float32)
    acc += jnp.dot(held_ref[:, cut:], passed_ref[...], preferred_element_type=jnp.float32)
    out_ref[...] = acc


def first_product(where, last, more, slots, acc, weights):
    rows, feat = last.shape
    own, fetched, passed = weights
    wide = own.shape[1] // 2
    whole = pl.BlockSpec((rows, wide), lambda i, w: (0, i))
    return call(
        first_kernel,
        "first",
        jax.ShapeDtypeStruct(acc.shape, jnp.float32),
        2,
        [spec((rows, feat))] * 5
        + [whole, pl.BlockSpec((feat, wide), lambda i, w: (w[NEAR] ^ 3, i))]
        + [pl.BlockSpec((x.shape[0], wide), lambda i, w: (0, i)) for x in (fetched, passed)],
        whole,
        [pltpu.VMEM((rows, 4 * feat), jnp.bfloat16)],
    )(where, last, more, *slots, acc, own, fetched, passed)


def second_kernel(where_ref, slot, more, fetched_ref, passed_ref, acc_in, keep_ref, send_ref, acc_ref):
    weight = []
    for head in range(2):
        place = partner_place(where_ref, 2 * (where_ref[NEAR] ^ 3) + head)
        here = jnp.minimum(place, FETCHED - 1) * HEAD_DIM
        there = jnp.maximum(place - FETCHED, 0) * HEAD_DIM
        weight.append(
            jnp.where(
                place < FETCHED,
                fetched_ref[pl.ds(pl.multiple_of(here, HEAD_DIM), HEAD_DIM), :],
                passed_ref[pl.ds(pl.multiple_of(there, HEAD_DIM), HEAD_DIM), :],
            )
        )
    block = jnp.where(where_ref[INNER] == 1, slot[...], more[...])
    acc = acc_in[...] + jnp.dot(
        block, jnp.concatenate(weight, axis=0), preferred_element_type=jnp.float32
    )
    acc_ref[...] = acc.reshape(acc_ref.shape)
    for sub, out in enumerate((keep_ref, send_ref)):
        for at in range(4):
            out[at] = acc_ref[where_ref[NEAR] ^ at, where_ref[SUB] ^ sub].astype(jnp.bfloat16)


def second_product(where, chunk, slot, more, weights, acc):
    rows, feat = slot.shape
    cols = weights[0].shape[1]
    wide = cols // 2
    out = jax.ShapeDtypeStruct((4, rows // 8, wide), jnp.bfloat16)
    return call(
        second_kernel,
        "second",
        [out] * 2,
        1,
        [spec((rows, feat))] * 2
        + [pl.BlockSpec((x.shape[0], wide), lambda i, w: (0, chunk)) for x in weights]
        + [pl.BlockSpec((rows, wide), lambda i, w: (0, chunk))],
        [spec(out.shape)] * 2,
        [pltpu.VMEM((4, 2, rows // 8, wide), jnp.float32)],
    )(where, slot, more, *weights, acc)


def add_kernel(where_ref, keep_ref, term_ref, *outs):
    for at, out in enumerate(outs):
        total = keep_ref[at].astype(jnp.float32) + term_ref[at].astype(jnp.float32)
        out[...] = total.astype(jnp.bfloat16)


def add(where, keep, term):
    return call(
        add_kernel,
        "add",
        [jax.ShapeDtypeStruct(keep.shape[1:], jnp.bfloat16)] * keep.shape[0],
        1,
        [spec(keep.shape)] * 2,
        [spec(keep.shape[1:])] * keep.shape[0],
    )(where, keep, term)


def share_tail(sizes, where, pieces, out_weight, part, hidden_in, attn_gate):
    fetched = swap(part, "head", 2, 1)
    own, fetched = lax.optimization_barrier((pieces[0], fetched))
    pieces = [own, *pieces[1:]]
    passed = swap(fetched, "grp", 2, 1)

    pieces = [pieces[0], *pieces[:0:-1]]
    mine = attend_half(where, 0, pieces)
    where, mine = lax.optimization_barrier((where, mine))
    other = swap(attend_half(where, 1, pieces), "head", 2, 1)
    acc = add_product(where, {0: mine}, out_weight)
    other, acc = lax.optimization_barrier((other, acc))
    slots = []
    for at, x in enumerate((mine, other)):
        next_to, far = swap(x, "patch", 4, 1), swap(x, "patch", 4, 2)
        next_to, far, other, x = lax.optimization_barrier((next_to, far, other, x))
        if at == 1:
            acc = add_product(where, {2: slots[0][2], 1: slots[0][1]}, out_weight, acc)
            far, x, acc = lax.optimization_barrier((far, x, acc))
        middle = swap(x, "patch", 4, 3, (1, 2))
        ends = lax.ppermute(far, "patch", [(1, 0), (2, 3)])
        slots.append([x, next_to, far, middle, ends])
    weights = [out_weight, fetched, passed]
    partner = [slots[1][at] for at in (0, 2, 1)]
    acc = first_product(where, *slots[0][3:], partner, acc, weights)
    terms = [second_product(where, at, *slots[1][3:], [fetched, passed], acc) for at in range(2)]
    blocks = []
    for keep, send in terms:
        total = add(where, keep, swap(send, "sub", 2, 1))
        blocks.append([total[0]] + [swap(total[rel], "patch", 4, rel) for rel in range(3, 0, -1)])
    return mix_columns(where, hidden_in, attn_gate, blocks)


def mix_columns_kernel(where_ref, hidden_ref, gate_ref, *refs):
    blocks, out_ref = refs[:-1], refs[-1]
    cols = blocks[0].shape[1]
    for chunk in range(2):
        for at, rel in enumerate((0, 3, 2, 1)):
            start = (2 * (where_ref[PATCH] ^ rel) + chunk) * cols
            lanes = pl.ds(pl.multiple_of(start, HEAD_DIM), cols)
            mixed = hidden_ref[:, lanes].astype(jnp.float32) + gate_ref[:, lanes] * blocks[
                4 * chunk + at
            ][...].astype(jnp.float32)
            out_ref[:, lanes] = mixed.astype(jnp.bfloat16)


def mix_columns(where, hidden_in, attn_gate, blocks):
    rows, width = hidden_in.shape
    flat = [x for chunk in blocks for x in chunk]
    return call(
        mix_columns_kernel,
        "mix",
        jax.ShapeDtypeStruct((rows, width), jnp.bfloat16),
        2,
        [pl.BlockSpec((rows // 2, width), lambda i, w: (i, 0)), spec((1, width))]
        + [pl.BlockSpec((rows // 2, flat[0].shape[1]), lambda i, w: (i, 0))] * len(flat),
        pl.BlockSpec((rows // 2, width), lambda i, w: (i, 0)),
    )(where, hidden_in, attn_gate[None], *flat)


def body(sizes, queries, fresh_kv, cached_kv, exponents, out_weight, hidden_in, attn_gate):
    n_patch, n_head, n_sub = sizes["patch"], sizes["head"], sizes["sub"]
    tok, channels = queries.shape
    heads = channels // HEAD_DIM
    split = math.gcd(heads, n_patch)
    patch_at = lax.axis_index("patch")
    inner = (patch_at > 0) & (patch_at < n_patch - 1)
    where = jnp.stack(
        [
            patch_at,
            patch_at % split,
            lax.axis_index("head"),
            lax.axis_index("sub"),
            inner,
            lax.axis_index("grp"),
        ]
    ).astype(jnp.int32)

    arrays = (exponents, queries, fresh_kv, cached_kv)
    shared = (sizes["grp"], n_head, split, n_patch, heads) == (2, 2, 4, 4, 8)
    shares = 2 if shared else out_weight.shape[0] // HEAD_DIM
    *sent, part = pack(split, shares, *arrays, out_weight)
    far_first = [
        swap(x, "patch", n_patch, split - 1 - at) for at, x in enumerate(sent)
    ]
    where, sent = lax.optimization_barrier((where, sent))
    pieces = [pack_own(split, where, *arrays), *far_first]
    if shared:
        return share_tail(sizes, where, pieces, out_weight, part, hidden_in, attn_gate)
    kv_pieces = list(pieces)
    for rel in range(split, n_patch, split):
        kv_pieces += [swap(x, "patch", n_patch, rel) for x in pieces]
    return sum_tail(sizes, where, pieces, kv_pieces, out_weight, hidden_in, attn_gate)


def solution(mesh):
    in_specs = (
        P(("grp", "patch"), ("head", "sub")),
        P(None, ("grp", "patch"), ("head", "sub")),
        P(None, "grp", ("head", "sub")),
        P(None, ("grp", "patch"), ("head", "sub")),
        P(("head", "sub"), "patch"),
        P(("grp", "patch", "head", "sub"), None),
        P(),
    )
    out_specs = P(("grp", "patch", "head", "sub"), None)
    return jax.shard_map(
        functools.partial(body, dict(mesh.shape)),
        mesh=mesh,
        in_specs=in_specs,
        out_specs=out_specs,
        check_vma=False,
    )
```

```python
import functools
import math

import jax
import jax.numpy as jnp
from jax import lax
from jax.experimental import pallas as pl
from jax.experimental.pallas import tpu as pltpu
from jax.sharding import PartitionSpec as P

HEAD_DIM = 128
SCALE_ROWS = 128
SATURATION = 448.0
PACK_ROWS = 64
VMEM_BYTES = 32 * 1024 * 1024
PACK_VMEM_BYTES = 60 * 1024 * 1024
ATTEND_FLOPS = 1
PROJECT_FLOPS = 1
OWN_FLOPS = 1
FETCHED = 4
ZERO_FLOPS = 6_000_000_000
HALF_FLOPS = 1

PATCH, NEAR, HEAD, SUB, INNER, GRP = range(6)


def spec(shape):
    return pl.BlockSpec(shape, lambda i, w: (0,) * len(shape))


def call(kernel, name, out_shape, grid, in_specs, out_specs, scratch=(), flops=1, vmem=VMEM_BYTES):
    return pl.pallas_call(
        kernel,
        out_shape=out_shape,
        grid_spec=pltpu.PrefetchScalarGridSpec(
            num_scalar_prefetch=1,
            grid=(grid,),
            in_specs=in_specs,
            out_specs=out_specs,
            scratch_shapes=list(scratch),
        ),
        compiler_params=pltpu.CompilerParams(vmem_limit_bytes=vmem),
        cost_estimate=pl.CostEstimate(flops=flops, bytes_accessed=0, transcendentals=0),
        name=name,
    )


def swap(x, axes, count, mask, only=None):
    pairs = [(at, at ^ mask) for at in range(count) if only is None or at in only]
    return lax.ppermute(x, axes, pairs)


def power_of_two(exponent):
    return lax.shift_left(jnp.int32(1), exponent + 15).astype(jnp.float32) * 2.0**-15


def decode(fresh, cached, exponent):
    cached = cached.astype(jnp.float32)
    residual = fresh.astype(jnp.float32) - cached
    scaled = residual * power_of_two(-exponent)
    codes = jnp.clip(scaled, -SATURATION, SATURATION).astype(jnp.bfloat16)
    return (cached + codes.astype(jnp.float32) * power_of_two(exponent)).astype(jnp.bfloat16)


def pack_kernel(split, per, shares, exps_ref, q_ref, fresh_ref, cached_ref, weight_ref, *refs):
    outs, part_ref, bufs = refs[: split - 1], refs[split - 1], refs[split : 2 * split - 1]
    q_buf, fresh_buf, cached_buf, part_buf, sems, out_sems, part_sems = refs[2 * split - 1 :]
    patch = lax.axis_index("patch")
    count = part_ref.shape[0]
    start = lax.axis_index("grp") * count if shares == 2 else 0
    part_in = pltpu.make_async_copy(
        weight_ref.at[pl.ds(pl.multiple_of(start, HEAD_DIM), count)], part_buf, part_sems.at[0]
    )
    part_out = pltpu.make_async_copy(part_buf, part_ref, part_sems.at[1])
    near = lax.rem(patch, split)
    tok = q_buf.shape[0]
    copies, sent = [], []
    for block in range(tok // PACK_ROWS):
        rows = pl.ds(block * PACK_ROWS, PACK_ROWS)
        there = pl.ds(pl.multiple_of(patch * tok + block * PACK_ROWS, PACK_ROWS), PACK_ROWS)
        copies.append(
            [
                pltpu.make_async_copy(q_ref.at[rows], q_buf.at[rows], sems.at[block, 0]),
                pltpu.make_async_copy(fresh_ref.at[:, rows], fresh_buf.at[:, rows], sems.at[block, 1]),
                pltpu.make_async_copy(cached_ref.at[:, there], cached_buf.at[:, rows], sems.at[block, 2]),
            ]
        )
        for copy in copies[-1]:
            copy.start()
    part_in.start()
    for block in range(tok // PACK_ROWS):
        rows = pl.ds(block * PACK_ROWS, PACK_ROWS)
        for copy in copies[block]:
            copy.wait()
        for rel in range(split - 1, 0, -1):
            buf = bufs[split - 1 - rel]
            for chunk in range(per):
                head = (near ^ rel) * per + chunk
                lanes = pl.ds(pl.multiple_of(head * HEAD_DIM, HEAD_DIM), HEAD_DIM)
                here = pl.ds(chunk * HEAD_DIM, HEAD_DIM)
                buf[0, rows, here] = q_buf[rows, lanes]
                for stacked in range(2):
                    buf[1 + stacked, rows, here] = decode(
                        fresh_buf[stacked, rows, lanes],
                        cached_buf[stacked, rows, lanes],
                        exps_ref[stacked, block * PACK_ROWS // SCALE_ROWS, head],
                    )
            sent.append(
                pltpu.make_async_copy(
                    buf.at[:, rows],
                    outs[split - 1 - rel].at[:, rows],
                    out_sems.at[block, rel - 1],
                )
            )
            sent[-1].start()
        if block == tok // PACK_ROWS - 2:
            part_in.wait()
            part_out.start()
    for copy in sent:
        copy.wait()
    part_out.wait()


def pack(split, shares, exponents, queries, fresh_kv, cached_kv, weight):
    tok, channels = queries.shape
    feat = channels // split
    blocks = tok // PACK_ROWS
    hbm = pl.BlockSpec(memory_space=pltpu.HBM)
    return pl.pallas_call(
        functools.partial(pack_kernel, split, feat // HEAD_DIM, shares),
        out_shape=[jax.ShapeDtypeStruct((3, tok, feat), jnp.bfloat16)] * (split - 1)
        + [jax.ShapeDtypeStruct((weight.shape[0] // shares, weight.shape[1]), weight.dtype)],
        in_specs=[pl.BlockSpec(memory_space=pltpu.SMEM), hbm, hbm, hbm, hbm],
        out_specs=[hbm] * split,
        scratch_shapes=[pltpu.VMEM((3, tok, feat), jnp.bfloat16)] * (split - 1)
        + [
            pltpu.VMEM((tok, channels), jnp.bfloat16),
            pltpu.VMEM((2, tok, channels), jnp.bfloat16),
            pltpu.VMEM((2, tok, channels), jnp.bfloat16),
            pltpu.VMEM((weight.shape[0] // shares, weight.shape[1]), weight.dtype),
            pltpu.SemaphoreType.DMA((blocks, 3)),
            pltpu.SemaphoreType.DMA((blocks, split - 1)),
            pltpu.SemaphoreType.DMA((2,)),
        ],
        compiler_params=pltpu.CompilerParams(vmem_limit_bytes=PACK_VMEM_BYTES),
        name="pack",
    )(exponents, queries, fresh_kv, cached_kv, weight)


def own_kernel(per, where_ref, exps_ref, q_ref, fresh_ref, cached_ref, out_ref):
    out_ref[0] = q_ref[...]
    for chunk in range(per):
        lanes = pl.ds(chunk * HEAD_DIM, HEAD_DIM)
        for block in range(q_ref.shape[0] // SCALE_ROWS):
            rows = pl.ds(block * SCALE_ROWS, SCALE_ROWS)
            for stacked in range(2):
                out_ref[1 + stacked, rows, lanes] = decode(
                    fresh_ref[stacked, rows, lanes],
                    cached_ref[stacked, rows, lanes],
                    exps_ref[stacked, block, where_ref[NEAR] * per + chunk],
                )


def pack_own(split, where, exponents, queries, fresh_kv, cached_kv):
    tok, channels = queries.shape
    feat = channels // split
    out = jax.ShapeDtypeStruct((3, tok, feat), jnp.bfloat16)
    return call(
        functools.partial(own_kernel, feat // HEAD_DIM),
        "own",
        out,
        1,
        [
            pl.BlockSpec(memory_space=pltpu.SMEM),
            pl.BlockSpec((tok, feat), lambda i, w: (0, w[NEAR])),
            pl.BlockSpec((2, tok, feat), lambda i, w: (0, 0, w[NEAR])),
            pl.BlockSpec((2, tok, feat), lambda i, w: (0, w[PATCH], w[NEAR])),
        ],
        spec(out.shape),
    )(where, exponents, queries, fresh_kv, cached_kv)


def attend_kernel(split, part, where_ref, *refs):
    q_refs, kv_refs, out_ref = (refs[0], *refs[split - 1 : 0 : -1]), refs[:-1], refs[-1]
    factor = HEAD_DIM**-0.5 * math.log2(math.e)
    tok, feat = q_refs[0].shape[1:]
    count = out_ref.shape[1] // part[1]
    starts = [at * (tok // count) + part[0] for at in range(count)]
    for head in range(feat // HEAD_DIM):
        lanes = pl.ds(head * HEAD_DIM, HEAD_DIM)
        keys = jnp.concatenate([ref[1, :, lanes] for ref in kv_refs], axis=0)
        values = jnp.concatenate([ref[2, :, lanes] for ref in kv_refs], axis=0)
        values = jnp.concatenate([values, jnp.ones_like(values)], axis=1)
        for rel in range(split):
            rows = [q_refs[rel][0, start : start + part[1], lanes] for start in starts]
            query = jnp.concatenate(rows, axis=0) if len(rows) > 1 else rows[0]
            scores = lax.dot_general(
                query, keys, (((1,), (1,)), ((), ())), preferred_element_type=jnp.float32
            )
            peak = jnp.max(scores, axis=1, keepdims=True)
            expo = jnp.exp2((scores - peak) * factor).astype(jnp.bfloat16)
            mix = jnp.dot(expo, values, preferred_element_type=jnp.float32)
            mix = mix[:, :HEAD_DIM] / mix[:, HEAD_DIM:]
            out_ref[where_ref[NEAR] ^ rel, :, lanes] = mix.astype(jnp.bfloat16)


def attend(where, part, count, pieces, kv_pieces):
    split = len(pieces)
    _, tok, feat = pieces[0].shape
    out = jax.ShapeDtypeStruct((split, count * part[1], feat), jnp.bfloat16)
    return call(
        functools.partial(attend_kernel, split, part),
        "attend",
        out,
        1,
        [spec((3, tok, feat))] * len(kv_pieces),
        spec(out.shape),
        flops=ATTEND_FLOPS,
    )(where, *kv_pieces)


def project_kernel(split, n_slots, n_more, where_ref, *refs):
    slots, refs = refs[:n_slots], refs[n_slots:]
    more, weight_ref, refs = refs[:n_more], refs[n_more], refs[n_more + 1 :]
    outs, held_ref, acc_ref = refs[:-2], refs[-2], refs[-1]
    rows, feat = slots[0].shape
    n_sub, n_head = acc_ref.shape[3], acc_ref.shape[2]

    @pl.when(pl.program_id(0) == 0)
    def arrange():
        for at, slot in enumerate(slots):
            group, near = divmod(at, split)
            lane = (where_ref[NEAR] ^ near) * feat
            block = slot[...]
            if more and at == n_slots - 1:
                block = jnp.where(where_ref[INNER] == 1, block, more[0][...])
            held_ref[
                group * rows : (group + 1) * rows, pl.ds(pl.multiple_of(lane, HEAD_DIM), feat)
            ] = block

    acc = jnp.dot(held_ref[...], weight_ref[...], preferred_element_type=jnp.float32)
    acc_ref[...] = acc.reshape(acc_ref.shape)
    for sub in range(n_sub):
        for head in range(n_head):
            for at in range(n_slots):
                group, near = divmod(at, split)
                outs[sub][head, at] = acc_ref[
                    group, where_ref[NEAR] ^ near, where_ref[HEAD] ^ head, where_ref[SUB] ^ sub
                ].astype(jnp.bfloat16)


def project(split, where, slots, more, weight, n_head, n_sub):
    rows, feat = slots[0].shape
    n_patch = len(slots)
    total = rows * n_patch // split
    depth, cols = weight.shape
    wide = 640 if cols % 640 == 0 else cols
    piece = rows // (split * n_head * n_sub)
    return call(
        functools.partial(project_kernel, split, n_patch, len(more)),
        "project",
        [jax.ShapeDtypeStruct((n_head, n_patch, piece, cols), jnp.bfloat16)] * n_sub,
        cols // wide,
        [spec((rows, feat))] * (n_patch + len(more))
        + [pl.BlockSpec((depth, wide), lambda i, w: (0, i))],
        [pl.BlockSpec((n_head, n_patch, piece, wide), lambda i, w: (0, 0, 0, i))] * n_sub,
        [
            pltpu.VMEM((total, depth), jnp.bfloat16),
            pltpu.VMEM((n_patch // split, split, n_head, n_sub, piece, wide), jnp.float32),
        ],
        flops=PROJECT_FLOPS,
    )(where, *slots, *more, weight)


def mix_kernel(rels, where_ref, hidden_ref, gate_ref, *refs):
    blocks, out_ref = refs[:-1], refs[-1]
    piece, cols = blocks[0].shape
    for part in range(len(blocks) // len(rels)):
        rows = pl.ds(part * piece, piece)
        for at, rel in enumerate(rels):
            lanes = pl.ds(pl.multiple_of((where_ref[PATCH] ^ rel) * cols, HEAD_DIM), cols)
            mixed = hidden_ref[rows, lanes].astype(jnp.float32) + gate_ref[:, lanes] * blocks[
                part * len(rels) + at
            ][...].astype(jnp.float32)
            out_ref[rows, lanes] = mixed.astype(jnp.bfloat16)


def mix(where, hidden_in, attn_gate, blocks):
    rows, width = hidden_in.shape
    n_patch = len(blocks[0])
    piece, cols = blocks[0][0].shape
    if cols % HEAD_DIM:
        order = jnp.concatenate([jnp.stack(x) for x in blocks], axis=1)
        order = order[where[PATCH] ^ jnp.arange(n_patch)]
        projected = order.transpose(1, 0, 2).reshape(rows, width).astype(jnp.float32)
        return (hidden_in.astype(jnp.float32) + attn_gate * projected).astype(jnp.bfloat16)
    rels = [0, *range(n_patch - 1, 0, -1)]
    flat = [part[rel] for part in blocks for rel in rels]
    return call(
        functools.partial(mix_kernel, rels),
        "mix",
        jax.ShapeDtypeStruct((rows, width), jnp.bfloat16),
        1,
        [spec((rows, width)), spec((1, width))] + [spec((piece, cols))] * len(flat),
        spec((rows, width)),
    )(where, hidden_in, attn_gate[None], *flat)


def gather(parts, n_patch):
    if n_patch != 4:
        return [
            ([x] + [swap(x, "patch", n_patch, rel) for rel in range(1, n_patch)], [])
            for x in parts
        ]
    far = [swap(x, "patch", 4, 2) for x in parts]
    next_to = [swap(x, "patch", 4, 1) for x in parts]
    out = []
    for at, x in enumerate(parts):
        far[at], next_to[at], parts = lax.optimization_barrier((far[at], next_to[at], parts))
        middle = swap(parts[at], "patch", 4, 3, (1, 2))
        ends = lax.ppermute(far[at], "patch", [(1, 0), (2, 3)])
        if at + 1 < len(parts):
            ends, far[at + 1], next_to[at + 1] = lax.optimization_barrier(
                (ends, far[at + 1], next_to[at + 1])
            )
        out.append(([x, next_to[at], far[at], middle], [ends]))
    return out


def add_sub_kernel(n_sub, where_ref, *refs):
    terms, kept_ref, outs = refs[:n_sub], refs[n_sub], refs[n_sub + 1 :]
    for head in range(len(outs) + 1):
        total = terms[0][head].astype(jnp.float32)
        for term in terms[1:]:
            total += term[head].astype(jnp.float32)
        if head == 0:
            kept_ref[...] = total
        else:
            outs[head - 1][...] = total.astype(jnp.bfloat16)


def add_head_kernel(n_more, where_ref, kept_ref, *refs):
    for at, out in enumerate(refs[n_more:]):
        total = kept_ref[at]
        for term in refs[:n_more]:
            total += term[at].astype(jnp.float32)
        out[...] = total.astype(jnp.bfloat16)


def reduce_sub(sizes, where, terms):
    n_sub, n_head = sizes["sub"], sizes["head"]
    terms = [terms[0]] + [swap(terms[rel], "sub", n_sub, rel) for rel in range(1, n_sub)]
    shape = terms[0].shape[1:]
    return call(
        functools.partial(add_sub_kernel, n_sub),
        "add_sub",
        [jax.ShapeDtypeStruct(shape, jnp.float32)]
        + [jax.ShapeDtypeStruct(shape, jnp.bfloat16)] * (n_head - 1),
        1,
        [spec(terms[0].shape)] * n_sub,
        [spec(shape)] * n_head,
    )(where, *terms)


def reduce_head(sizes, where, sums):
    n_head = sizes["head"]
    shape = sums[0].shape
    sums = [sums[0]] + [swap(sums[rel], "head", n_head, rel) for rel in range(1, n_head)]
    return call(
        functools.partial(add_head_kernel, n_head - 1),
        "add_head",
        [jax.ShapeDtypeStruct(shape[1:], jnp.bfloat16)] * shape[0],
        1,
        [spec(shape)] * n_head,
        [spec(shape[1:])] * shape[0],
    )(where, *sums)


def sum_tail(sizes, where, pieces, kv_pieces, out_weight, hidden_in, attn_gate):
    n_patch, n_head, n_sub = sizes["patch"], sizes["head"], sizes["sub"]
    split, tok = len(pieces), pieces[0].shape[1]
    count = n_head * n_sub
    piece = tok // count
    parts = 2 if piece % 32 == 0 else 1
    attended = []
    for part in range(parts):
        rows = (part * (piece // parts), piece // parts)
        x = attend(where, rows, count, pieces, kv_pieces)
        attended.append(x.reshape(-1, x.shape[2]))
    slots = gather(attended, n_patch)
    blocks = []
    for part in range(parts):
        terms = project(split, where, *slots[part], out_weight, n_head, n_sub)
        total = reduce_head(sizes, where, reduce_sub(sizes, where, terms))
        blocks.append(
            [total[0]] + [swap(total[rel], "patch", n_patch, rel) for rel in range(1, n_patch)]
        )
    return mix(where, hidden_in, attn_gate, blocks)


def attend_half_kernel(half, where_ref, *refs):
    pieces, out = refs[:-1], refs[-1]
    factor = HEAD_DIM**-0.5 * math.log2(math.e)
    rows, feat = out.shape[1:]
    start = pl.multiple_of((where_ref[HEAD] ^ half) * rows, rows)
    for head in range(feat // HEAD_DIM):
        lanes = pl.ds(head * HEAD_DIM, HEAD_DIM)
        keys = jnp.concatenate([ref[1, :, lanes] for ref in pieces], axis=0)
        values = jnp.concatenate([ref[2, :, lanes] for ref in pieces], axis=0)
        values = jnp.concatenate([values, jnp.ones_like(values)], axis=1)
        query = jnp.concatenate([ref[0, pl.ds(start, rows), lanes] for ref in pieces], axis=0)
        scores = lax.dot_general(
            query, keys, (((1,), (1,)), ((), ())), preferred_element_type=jnp.float32
        )
        peak = jnp.max(scores, axis=1, keepdims=True)
        expo = jnp.exp2((scores - peak) * factor).astype(jnp.bfloat16)
        mix = jnp.dot(expo, values, preferred_element_type=jnp.float32)
        mix = (mix[:, :HEAD_DIM] / mix[:, HEAD_DIM:]).astype(jnp.bfloat16)
        for rel in range(len(pieces)):
            out[where_ref[NEAR] ^ rel, :, lanes] = mix[rel * rows : (rel + 1) * rows]


def attend_half(where, half, pieces):
    _, tok, feat = pieces[0].shape
    out = jax.ShapeDtypeStruct((len(pieces), tok // 2, feat), jnp.bfloat16)
    return call(
        functools.partial(attend_half_kernel, half),
        "attend",
        out,
        1,
        [spec((3, tok, feat))] * len(pieces),
        spec(out.shape),
        flops=HALF_FLOPS,
    )(where, *pieces).reshape(-1, feat)


def add_product_kernel(count, where_ref, *refs):
    total = refs[2 * count][...] if len(refs) > 2 * count + 1 else None
    for slot, weight in zip(refs[:count], refs[count : 2 * count]):
        term = jnp.dot(slot[...], weight[...], preferred_element_type=jnp.float32)
        total = term if total is None else total + term
    refs[-1][...] = total


def add_product(where, slots, weight, acc=None):
    rows, feat = next(iter(slots.values())).shape
    cols = weight.shape[1]
    wide = cols // 2
    whole = pl.BlockSpec((rows, wide), lambda i, w: (0, i))
    rels = list(slots)
    return call(
        functools.partial(add_product_kernel, len(rels)),
        "products",
        jax.ShapeDtypeStruct((rows, cols), jnp.float32),
        2,
        [spec((rows, feat))] * len(rels)
        + [pl.BlockSpec((feat, wide), lambda i, w, rel=rel: (w[NEAR] ^ rel, i)) for rel in rels]
        + ([] if acc is None else [whole]),
        whole,
        flops=ZERO_FLOPS if acc is None else 1,
    )(where, *slots.values(), *[weight] * len(rels), *([] if acc is None else [acc]))


def partner_place(where_ref, head):
    return (head + FETCHED * where_ref[GRP]) % 8


def first_kernel(where_ref, *refs):
    last, more, slots = refs[0], refs[1], refs[2:5]
    acc_ref, own_ref, fetched_ref, passed_ref, out_ref, held_ref = refs[5:]
    rows, feat = last.shape
    cut = fetched_ref.shape[0]

    def put(at, block):
        for head in range(2):
            there = partner_place(where_ref, 2 * (where_ref[NEAR] ^ at) + head)
            lanes = pl.ds(pl.multiple_of(there * HEAD_DIM, HEAD_DIM), HEAD_DIM)
            held_ref[:, lanes] = block[:, head * HEAD_DIM : (head + 1) * HEAD_DIM]

    @pl.when(pl.program_id(0) == 0)
    def arrange():
        for at, slot in zip((0, 2, 1), slots):
            put(at, slot[...])
        put(3, jnp.zeros((rows, feat), jnp.bfloat16))

    block = jnp.where(where_ref[INNER] == 1, last[...], more[...])
    acc = acc_ref[...]
    acc += jnp.dot(block, own_ref[...], preferred_element_type=jnp.float32)
    acc += jnp.dot(held_ref[:, :cut], fetched_ref[...], preferred_element_type=jnp.float32)
    acc += jnp.dot(held_ref[:, cut:], passed_ref[...], preferred_element_type=jnp.float32)
    out_ref[...] = acc


def first_product(where, last, more, slots, acc, weights):
    rows, feat = last.shape
    own, fetched, passed = weights
    wide = own.shape[1] // 2
    whole = pl.BlockSpec((rows, wide), lambda i, w: (0, i))
    return call(
        first_kernel,
        "first",
        jax.ShapeDtypeStruct(acc.shape, jnp.float32),
        2,
        [spec((rows, feat))] * 5
        + [whole, pl.BlockSpec((feat, wide), lambda i, w: (w[NEAR] ^ 3, i))]
        + [pl.BlockSpec((x.shape[0], wide), lambda i, w: (0, i)) for x in (fetched, passed)],
        whole,
        [pltpu.VMEM((rows, 4 * feat), jnp.bfloat16)],
    )(where, last, more, *slots, acc, own, fetched, passed)


def second_kernel(where_ref, slot, more, fetched_ref, passed_ref, acc_in, keep_ref, send_ref, acc_ref):
    weight = []
    for head in range(2):
        place = partner_place(where_ref, 2 * (where_ref[NEAR] ^ 3) + head)
        here = jnp.minimum(place, FETCHED - 1) * HEAD_DIM
        there = jnp.maximum(place - FETCHED, 0) * HEAD_DIM
        weight.append(
            jnp.where(
                place < FETCHED,
                fetched_ref[pl.ds(pl.multiple_of(here, HEAD_DIM), HEAD_DIM), :],
                passed_ref[pl.ds(pl.multiple_of(there, HEAD_DIM), HEAD_DIM), :],
            )
        )
    block = jnp.where(where_ref[INNER] == 1, slot[...], more[...])
    acc = acc_in[...] + jnp.dot(
        block, jnp.concatenate(weight, axis=0), preferred_element_type=jnp.float32
    )
    acc_ref[...] = acc.reshape(acc_ref.shape)
    for sub, out in enumerate((keep_ref, send_ref)):
        for at in range(4):
            out[at] = acc_ref[where_ref[NEAR] ^ at, where_ref[SUB] ^ sub].astype(jnp.bfloat16)


def second_product(where, chunk, slot, more, weights, acc):
    rows, feat = slot.shape
    cols = weights[0].shape[1]
    wide = cols // 2
    out = jax.ShapeDtypeStruct((4, rows // 8, wide), jnp.bfloat16)
    return call(
        second_kernel,
        "second",
        [out] * 2,
        1,
        [spec((rows, feat))] * 2
        + [pl.BlockSpec((x.shape[0], wide), lambda i, w: (0, chunk)) for x in weights]
        + [pl.BlockSpec((rows, wide), lambda i, w: (0, chunk))],
        [spec(out.shape)] * 2,
        [pltpu.VMEM((4, 2, rows // 8, wide), jnp.float32)],
    )(where, slot, more, *weights, acc)


def add_kernel(where_ref, keep_ref, term_ref, *outs):
    for at, out in enumerate(outs):
        total = keep_ref[at].astype(jnp.float32) + term_ref[at].astype(jnp.float32)
        out[...] = total.astype(jnp.bfloat16)


def add(where, keep, term):
    return call(
        add_kernel,
        "add",
        [jax.ShapeDtypeStruct(keep.shape[1:], jnp.bfloat16)] * keep.shape[0],
        1,
        [spec(keep.shape)] * 2,
        [spec(keep.shape[1:])] * keep.shape[0],
    )(where, keep, term)


def share_tail(sizes, where, pieces, out_weight, part, hidden_in, attn_gate):
    fetched = swap(part, "head", 2, 1)
    own, fetched = lax.optimization_barrier((pieces[0], fetched))
    pieces = [own, *pieces[1:]]
    passed = swap(fetched, "grp", 2, 1)

    pieces = [pieces[0], *pieces[:0:-1]]
    mine = attend_half(where, 0, pieces)
    where, mine = lax.optimization_barrier((where, mine))
    other = swap(attend_half(where, 1, pieces), "head", 2, 1)
    acc = add_product(where, {0: mine}, out_weight)
    other, acc = lax.optimization_barrier((other, acc))
    slots = []
    for at, x in enumerate((mine, other)):
        next_to, far = swap(x, "patch", 4, 1), swap(x, "patch", 4, 2)
        next_to, far, other, x = lax.optimization_barrier((next_to, far, other, x))
        if at == 1:
            acc = add_product(where, {2: slots[0][2], 1: slots[0][1]}, out_weight, acc)
            far, x, acc = lax.optimization_barrier((far, x, acc))
        middle = swap(x, "patch", 4, 3, (1, 2))
        ends = lax.ppermute(far, "patch", [(1, 0), (2, 3)])
        slots.append([x, next_to, far, middle, ends])
    weights = [out_weight, fetched, passed]
    partner = [slots[1][at] for at in (0, 2, 1)]
    acc = first_product(where, *slots[0][3:], partner, acc, weights)
    terms = [second_product(where, at, *slots[1][3:], [fetched, passed], acc) for at in range(2)]
    blocks = []
    for keep, send in terms:
        total = add(where, keep, swap(send, "sub", 2, 1))
        blocks.append([total[0]] + [swap(total[rel], "patch", 4, rel) for rel in range(3, 0, -1)])
    return mix_columns(where, hidden_in, attn_gate, blocks)


def mix_columns_kernel(where_ref, hidden_ref, gate_ref, *refs):
    blocks, out_ref = refs[:-1], refs[-1]
    cols = blocks[0].shape[1]
    for chunk in range(2):
        for at, rel in enumerate((0, 3, 2, 1)):
            start = (2 * (where_ref[PATCH] ^ rel) + chunk) * cols
            lanes = pl.ds(pl.multiple_of(start, HEAD_DIM), cols)
            mixed = hidden_ref[:, lanes].astype(jnp.float32) + gate_ref[:, lanes] * blocks[
                4 * chunk + at
            ][...].astype(jnp.float32)
            out_ref[:, lanes] = mixed.astype(jnp.bfloat16)


def mix_columns(where, hidden_in, attn_gate, blocks):
    rows, width = hidden_in.shape
    flat = [x for chunk in blocks for x in chunk]
    return call(
        mix_columns_kernel,
        "mix",
        jax.ShapeDtypeStruct((rows, width), jnp.bfloat16),
        2,
        [pl.BlockSpec((rows // 2, width), lambda i, w: (i, 0)), spec((1, width))]
        + [pl.BlockSpec((rows // 2, flat[0].shape[1]), lambda i, w: (i, 0))] * len(flat),
        pl.BlockSpec((rows // 2, width), lambda i, w: (i, 0)),
    )(where, hidden_in, attn_gate[None], *flat)


def body(sizes, queries, fresh_kv, cached_kv, exponents, out_weight, hidden_in, attn_gate):
    n_patch, n_head, n_sub = sizes["patch"], sizes["head"], sizes["sub"]
    tok, channels = queries.shape
    heads = channels // HEAD_DIM
    split = math.gcd(heads, n_patch)
    patch_at = lax.axis_index("patch")
    inner = (patch_at > 0) & (patch_at < n_patch - 1)
    where = jnp.stack(
        [
            patch_at,
            patch_at % split,
            lax.axis_index("head"),
            lax.axis_index("sub"),
            inner,
            lax.axis_index("grp"),
        ]
    ).astype(jnp.int32)

    arrays = (exponents, queries, fresh_kv, cached_kv)
    shared = (sizes["grp"], n_head, split, n_patch, heads) == (2, 2, 4, 4, 8)
    shares = 2 if shared else out_weight.shape[0] // HEAD_DIM
    *sent, part = pack(split, shares, *arrays, out_weight)
    far_first = [
        swap(x, "patch", n_patch, split - 1 - at) for at, x in enumerate(sent)
    ]
    where, sent = lax.optimization_barrier((where, sent))
    pieces = [pack_own(split, where, *arrays), *far_first]
    if shared:
        return share_tail(sizes, where, pieces, out_weight, part, hidden_in, attn_gate)
    kv_pieces = list(pieces)
    for rel in range(split, n_patch, split):
        kv_pieces += [swap(x, "patch", n_patch, rel) for x in pieces]
    return sum_tail(sizes, where, pieces, kv_pieces, out_weight, hidden_in, attn_gate)


def solution(mesh):
    in_specs = (
        P(("grp", "patch"), ("head", "sub")),
        P(None, ("grp", "patch"), ("head", "sub")),
        P(None, "grp", ("head", "sub")),
        P(None, ("grp", "patch"), ("head", "sub")),
        P(("head", "sub"), "patch"),
        P(("grp", "patch", "head", "sub"), None),
        P(),
    )
    out_specs = P(("grp", "patch", "head", "sub"), None)
    return jax.shard_map(
        functools.partial(body, dict(mesh.shape)),
        mesh=mesh,
        in_specs=in_specs,
        out_specs=out_specs,
        check_vma=False,
    )
```

```python
import functools
import math

import jax
import jax.numpy as jnp
from jax import lax
from jax.experimental import pallas as pl
from jax.experimental.pallas import tpu as pltpu
from jax.sharding import PartitionSpec as P

HEAD_DIM = 128
SCALE_ROWS = 128
SATURATION = 448.0
PACK_ROWS = 64
VMEM_BYTES = 32 * 1024 * 1024
PACK_VMEM_BYTES = 60 * 1024 * 1024
ATTEND_FLOPS = 1
PROJECT_FLOPS = 1
OWN_FLOPS = 1
FETCHED = 4
ZERO_FLOPS = 6_000_000_000
HALF_FLOPS = 1

PATCH, NEAR, HEAD, SUB, INNER, GRP = range(6)


def spec(shape):
    return pl.BlockSpec(shape, lambda i, w: (0,) * len(shape))


def call(kernel, name, out_shape, grid, in_specs, out_specs, scratch=(), flops=1, vmem=VMEM_BYTES):
    return pl.pallas_call(
        kernel,
        out_shape=out_shape,
        grid_spec=pltpu.PrefetchScalarGridSpec(
            num_scalar_prefetch=1,
            grid=(grid,),
            in_specs=in_specs,
            out_specs=out_specs,
            scratch_shapes=list(scratch),
        ),
        compiler_params=pltpu.CompilerParams(vmem_limit_bytes=vmem),
        cost_estimate=pl.CostEstimate(flops=flops, bytes_accessed=0, transcendentals=0),
        name=name,
    )


def swap(x, axes, count, mask, only=None):
    pairs = [(at, at ^ mask) for at in range(count) if only is None or at in only]
    return lax.ppermute(x, axes, pairs)


def decode(fresh, cached, exponent):
    power = jnp.full((1, HEAD_DIM), exponent.astype(jnp.float32))
    cached = cached.astype(jnp.float32)
    residual = fresh.astype(jnp.float32) - cached
    codes = jnp.clip(residual * jnp.exp2(-power), -SATURATION, SATURATION).astype(jnp.bfloat16)
    return (cached + codes.astype(jnp.float32) * jnp.exp2(power)).astype(jnp.bfloat16)


def send_order(split):
    return sorted(range(1, split), key=lambda rel: (rel != split // 2, -rel))


def pack_kernel(split, per, exps_ref, q_ref, fresh_ref, cached_ref, *refs):
    outs, bufs = refs[: split - 1], refs[split - 1 : 2 * split - 2]
    q_buf, fresh_buf, cached_buf, sems, out_sems = refs[2 * split - 2 :]
    patch = lax.axis_index("patch")
    near = lax.rem(patch, split)
    tok = q_buf.shape[0]
    copies, sent = [], []
    for block in range(tok // PACK_ROWS):
        rows = pl.ds(block * PACK_ROWS, PACK_ROWS)
        there = pl.ds(pl.multiple_of(patch * tok + block * PACK_ROWS, PACK_ROWS), PACK_ROWS)
        copies.append(
            [
                pltpu.make_async_copy(q_ref.at[rows], q_buf.at[rows], sems.at[block, 0]),
                pltpu.make_async_copy(fresh_ref.at[:, rows], fresh_buf.at[:, rows], sems.at[block, 1]),
                pltpu.make_async_copy(cached_ref.at[:, there], cached_buf.at[:, rows], sems.at[block, 2]),
            ]
        )
        for copy in copies[-1]:
            copy.start()
    for block in range(tok // PACK_ROWS):
        rows = pl.ds(block * PACK_ROWS, PACK_ROWS)
        for copy in copies[block]:
            copy.wait()
        for number, rel in enumerate(send_order(split)):
            buf = bufs[number]
            for chunk in range(per):
                head = (near ^ rel) * per + chunk
                lanes = pl.ds(pl.multiple_of(head * HEAD_DIM, HEAD_DIM), HEAD_DIM)
                here = pl.ds(chunk * HEAD_DIM, HEAD_DIM)
                buf[0, rows, here] = q_buf[rows, lanes]
                for stacked in range(2):
                    buf[1 + stacked, rows, here] = decode(
                        fresh_buf[stacked, rows, lanes],
                        cached_buf[stacked, rows, lanes],
                        exps_ref[stacked, block * PACK_ROWS // SCALE_ROWS, head],
                    )
            sent.append(
                pltpu.make_async_copy(
                    buf.at[:, rows], outs[number].at[:, rows], out_sems.at[block, number]
                )
            )
            sent[-1].start()
    for copy in sent:
        copy.wait()


def pack(split, exponents, queries, fresh_kv, cached_kv):
    tok, channels = queries.shape
    feat = channels // split
    blocks = tok // PACK_ROWS
    hbm = pl.BlockSpec(memory_space=pltpu.HBM)
    return pl.pallas_call(
        functools.partial(pack_kernel, split, feat // HEAD_DIM),
        out_shape=[jax.ShapeDtypeStruct((3, tok, feat), jnp.bfloat16)] * (split - 1),
        in_specs=[pl.BlockSpec(memory_space=pltpu.SMEM), hbm, hbm, hbm],
        out_specs=[hbm] * (split - 1),
        scratch_shapes=[pltpu.VMEM((3, tok, feat), jnp.bfloat16)] * (split - 1)
        + [
            pltpu.VMEM((tok, channels), jnp.bfloat16),
            pltpu.VMEM((2, tok, channels), jnp.bfloat16),
            pltpu.VMEM((2, tok, channels), jnp.bfloat16),
            pltpu.SemaphoreType.DMA((blocks, 3)),
            pltpu.SemaphoreType.DMA((blocks, split - 1)),
        ],
        compiler_params=pltpu.CompilerParams(vmem_limit_bytes=PACK_VMEM_BYTES),
        name="pack",
    )(exponents, queries, fresh_kv, cached_kv)


def own_kernel(per, where_ref, exps_ref, q_ref, fresh_ref, cached_ref, out_ref):
    out_ref[0] = q_ref[...]
    for chunk in range(per):
        lanes = pl.ds(chunk * HEAD_DIM, HEAD_DIM)
        for block in range(q_ref.shape[0] // SCALE_ROWS):
            rows = pl.ds(block * SCALE_ROWS, SCALE_ROWS)
            for stacked in range(2):
                out_ref[1 + stacked, rows, lanes] = decode(
                    fresh_ref[stacked, rows, lanes],
                    cached_ref[stacked, rows, lanes],
                    exps_ref[stacked, block, where_ref[NEAR] * per + chunk],
                )


def pack_own(split, where, exponents, queries, fresh_kv, cached_kv):
    tok, channels = queries.shape
    feat = channels // split
    out = jax.ShapeDtypeStruct((3, tok, feat), jnp.bfloat16)
    return call(
        functools.partial(own_kernel, feat // HEAD_DIM),
        "own",
        out,
        1,
        [
            pl.BlockSpec(memory_space=pltpu.SMEM),
            pl.BlockSpec((tok, feat), lambda i, w: (0, w[NEAR])),
            pl.BlockSpec((2, tok, feat), lambda i, w: (0, 0, w[NEAR])),
            pl.BlockSpec((2, tok, feat), lambda i, w: (0, w[PATCH], w[NEAR])),
        ],
        spec(out.shape),
    )(where, exponents, queries, fresh_kv, cached_kv)


def attend_kernel(split, part, where_ref, *refs):
    q_refs, kv_refs, out_ref = (refs[0], *refs[split - 1 : 0 : -1]), refs[:-1], refs[-1]
    factor = HEAD_DIM**-0.5 * math.log2(math.e)
    tok, feat = q_refs[0].shape[1:]
    count = out_ref.shape[1] // part[1]
    starts = [at * (tok // count) + part[0] for at in range(count)]
    for head in range(feat // HEAD_DIM):
        lanes = pl.ds(head * HEAD_DIM, HEAD_DIM)
        keys = jnp.concatenate([ref[1, :, lanes] for ref in kv_refs], axis=0)
        values = jnp.concatenate([ref[2, :, lanes] for ref in kv_refs], axis=0)
        values = jnp.concatenate([values, jnp.ones_like(values)], axis=1)
        for rel in range(split):
            rows = [q_refs[rel][0, start : start + part[1], lanes] for start in starts]
            query = jnp.concatenate(rows, axis=0) if len(rows) > 1 else rows[0]
            scores = lax.dot_general(
                query, keys, (((1,), (1,)), ((), ())), preferred_element_type=jnp.float32
            )
            peak = jnp.max(scores, axis=1, keepdims=True)
            expo = jnp.exp2((scores - peak) * factor).astype(jnp.bfloat16)
            mix = jnp.dot(expo, values, preferred_element_type=jnp.float32)
            mix = mix[:, :HEAD_DIM] / mix[:, HEAD_DIM:]
            out_ref[where_ref[NEAR] ^ rel, :, lanes] = mix.astype(jnp.bfloat16)


def attend(where, part, count, pieces, kv_pieces):
    split = len(pieces)
    _, tok, feat = pieces[0].shape
    out = jax.ShapeDtypeStruct((split, count * part[1], feat), jnp.bfloat16)
    return call(
        functools.partial(attend_kernel, split, part),
        "attend",
        out,
        1,
        [spec((3, tok, feat))] * len(kv_pieces),
        spec(out.shape),
        flops=ATTEND_FLOPS,
    )(where, *kv_pieces)


def project_kernel(split, n_slots, n_more, where_ref, *refs):
    slots, refs = refs[:n_slots], refs[n_slots:]
    more, weight_ref, refs = refs[:n_more], refs[n_more], refs[n_more + 1 :]
    outs, held_ref, acc_ref = refs[:-2], refs[-2], refs[-1]
    rows, feat = slots[0].shape
    n_sub, n_head = acc_ref.shape[3], acc_ref.shape[2]

    @pl.when(pl.program_id(0) == 0)
    def arrange():
        for at, slot in enumerate(slots):
            group, near = divmod(at, split)
            lane = (where_ref[NEAR] ^ near) * feat
            block = slot[...]
            if more and at == n_slots - 1:
                block = jnp.where(where_ref[INNER] == 1, block, more[0][...])
            held_ref[
                group * rows : (group + 1) * rows, pl.ds(pl.multiple_of(lane, HEAD_DIM), feat)
            ] = block

    acc = jnp.dot(held_ref[...], weight_ref[...], preferred_element_type=jnp.float32)
    acc_ref[...] = acc.reshape(acc_ref.shape)
    for sub in range(n_sub):
        for head in range(n_head):
            for at in range(n_slots):
                group, near = divmod(at, split)
                outs[sub][head, at] = acc_ref[
                    group, where_ref[NEAR] ^ near, where_ref[HEAD] ^ head, where_ref[SUB] ^ sub
                ].astype(jnp.bfloat16)


def project(split, where, slots, more, weight, n_head, n_sub):
    rows, feat = slots[0].shape
    n_patch = len(slots)
    total = rows * n_patch // split
    depth, cols = weight.shape
    wide = 640 if cols % 640 == 0 else cols
    piece = rows // (split * n_head * n_sub)
    return call(
        functools.partial(project_kernel, split, n_patch, len(more)),
        "project",
        [jax.ShapeDtypeStruct((n_head, n_patch, piece, cols), jnp.bfloat16)] * n_sub,
        cols // wide,
        [spec((rows, feat))] * (n_patch + len(more))
        + [pl.BlockSpec((depth, wide), lambda i, w: (0, i))],
        [pl.BlockSpec((n_head, n_patch, piece, wide), lambda i, w: (0, 0, 0, i))] * n_sub,
        [
            pltpu.VMEM((total, depth), jnp.bfloat16),
            pltpu.VMEM((n_patch // split, split, n_head, n_sub, piece, wide), jnp.float32),
        ],
        flops=PROJECT_FLOPS,
    )(where, *slots, *more, weight)


def mix_kernel(rels, where_ref, hidden_ref, gate_ref, *refs):
    blocks, out_ref = refs[:-1], refs[-1]
    piece, cols = blocks[0].shape
    for part in range(len(blocks) // len(rels)):
        rows = pl.ds(part * piece, piece)
        for at, rel in enumerate(rels):
            lanes = pl.ds(pl.multiple_of((where_ref[PATCH] ^ rel) * cols, HEAD_DIM), cols)
            mixed = hidden_ref[rows, lanes].astype(jnp.float32) + gate_ref[:, lanes] * blocks[
                part * len(rels) + at
            ][...].astype(jnp.float32)
            out_ref[rows, lanes] = mixed.astype(jnp.bfloat16)


def mix(where, hidden_in, attn_gate, blocks):
    rows, width = hidden_in.shape
    n_patch = len(blocks[0])
    piece, cols = blocks[0][0].shape
    if cols % HEAD_DIM:
        order = jnp.concatenate([jnp.stack(x) for x in blocks], axis=1)
        order = order[where[PATCH] ^ jnp.arange(n_patch)]
        projected = order.transpose(1, 0, 2).reshape(rows, width).astype(jnp.float32)
        return (hidden_in.astype(jnp.float32) + attn_gate * projected).astype(jnp.bfloat16)
    rels = [0, *range(n_patch - 1, 0, -1)]
    flat = [part[rel] for part in blocks for rel in rels]
    return call(
        functools.partial(mix_kernel, rels),
        "mix",
        jax.ShapeDtypeStruct((rows, width), jnp.bfloat16),
        1,
        [spec((rows, width)), spec((1, width))] + [spec((piece, cols))] * len(flat),
        spec((rows, width)),
    )(where, hidden_in, attn_gate[None], *flat)


def gather(parts, n_patch):
    if n_patch != 4:
        return [
            ([x] + [swap(x, "patch", n_patch, rel) for rel in range(1, n_patch)], [])
            for x in parts
        ]
    far = [swap(x, "patch", 4, 2) for x in parts]
    next_to = [swap(x, "patch", 4, 1) for x in parts]
    out = []
    for at, x in enumerate(parts):
        far[at], next_to[at], parts = lax.optimization_barrier((far[at], next_to[at], parts))
        middle = swap(parts[at], "patch", 4, 3, (1, 2))
        ends = lax.ppermute(far[at], "patch", [(1, 0), (2, 3)])
        if at + 1 < len(parts):
            ends, far[at + 1], next_to[at + 1] = lax.optimization_barrier(
                (ends, far[at + 1], next_to[at + 1])
            )
        out.append(([x, next_to[at], far[at], middle], [ends]))
    return out


def add_sub_kernel(n_sub, where_ref, *refs):
    terms, kept_ref, outs = refs[:n_sub], refs[n_sub], refs[n_sub + 1 :]
    for head in range(len(outs) + 1):
        total = terms[0][head].astype(jnp.float32)
        for term in terms[1:]:
            total += term[head].astype(jnp.float32)
        if head == 0:
            kept_ref[...] = total
        else:
            outs[head - 1][...] = total.astype(jnp.bfloat16)


def add_head_kernel(n_more, where_ref, kept_ref, *refs):
    for at, out in enumerate(refs[n_more:]):
        total = kept_ref[at]
        for term in refs[:n_more]:
            total += term[at].astype(jnp.float32)
        out[...] = total.astype(jnp.bfloat16)


def reduce_sub(sizes, where, terms):
    n_sub, n_head = sizes["sub"], sizes["head"]
    terms = [terms[0]] + [swap(terms[rel], "sub", n_sub, rel) for rel in range(1, n_sub)]
    shape = terms[0].shape[1:]
    return call(
        functools.partial(add_sub_kernel, n_sub),
        "add_sub",
        [jax.ShapeDtypeStruct(shape, jnp.float32)]
        + [jax.ShapeDtypeStruct(shape, jnp.bfloat16)] * (n_head - 1),
        1,
        [spec(terms[0].shape)] * n_sub,
        [spec(shape)] * n_head,
    )(where, *terms)


def reduce_head(sizes, where, sums):
    n_head = sizes["head"]
    shape = sums[0].shape
    sums = [sums[0]] + [swap(sums[rel], "head", n_head, rel) for rel in range(1, n_head)]
    return call(
        functools.partial(add_head_kernel, n_head - 1),
        "add_head",
        [jax.ShapeDtypeStruct(shape[1:], jnp.bfloat16)] * shape[0],
        1,
        [spec(shape)] * n_head,
        [spec(shape[1:])] * shape[0],
    )(where, *sums)


def sum_tail(sizes, where, pieces, kv_pieces, out_weight, hidden_in, attn_gate):
    n_patch, n_head, n_sub = sizes["patch"], sizes["head"], sizes["sub"]
    split, tok = len(pieces), pieces[0].shape[1]
    count = n_head * n_sub
    piece = tok // count
    parts = 2 if piece % 32 == 0 else 1
    attended = []
    for part in range(parts):
        rows = (part * (piece // parts), piece // parts)
        x = attend(where, rows, count, pieces, kv_pieces)
        attended.append(x.reshape(-1, x.shape[2]))
    slots = gather(attended, n_patch)
    blocks = []
    for part in range(parts):
        terms = project(split, where, *slots[part], out_weight, n_head, n_sub)
        total = reduce_head(sizes, where, reduce_sub(sizes, where, terms))
        blocks.append(
            [total[0]] + [swap(total[rel], "patch", n_patch, rel) for rel in range(1, n_patch)]
        )
    return mix(where, hidden_in, attn_gate, blocks)


def attend_half_kernel(half, where_ref, *refs):
    pieces, out = refs[:-1], refs[-1]
    factor = HEAD_DIM**-0.5 * math.log2(math.e)
    rows, feat = out.shape[1:]
    start = pl.multiple_of((where_ref[HEAD] ^ half) * rows, rows)
    for head in range(feat // HEAD_DIM):
        lanes = pl.ds(head * HEAD_DIM, HEAD_DIM)
        keys = jnp.concatenate([ref[1, :, lanes] for ref in pieces], axis=0)
        values = jnp.concatenate([ref[2, :, lanes] for ref in pieces], axis=0)
        values = jnp.concatenate([values, jnp.ones_like(values)], axis=1)
        query = jnp.concatenate([ref[0, pl.ds(start, rows), lanes] for ref in pieces], axis=0)
        scores = lax.dot_general(
            query, keys, (((1,), (1,)), ((), ())), preferred_element_type=jnp.float32
        )
        peak = jnp.max(scores, axis=1, keepdims=True)
        expo = jnp.exp2((scores - peak) * factor).astype(jnp.bfloat16)
        mix = jnp.dot(expo, values, preferred_element_type=jnp.float32)
        mix = (mix[:, :HEAD_DIM] / mix[:, HEAD_DIM:]).astype(jnp.bfloat16)
        for rel in range(len(pieces)):
            out[where_ref[NEAR] ^ rel, :, lanes] = mix[rel * rows : (rel + 1) * rows]


def attend_half(where, half, pieces):
    _, tok, feat = pieces[0].shape
    out = jax.ShapeDtypeStruct((len(pieces), tok // 2, feat), jnp.bfloat16)
    return call(
        functools.partial(attend_half_kernel, half),
        "attend",
        out,
        1,
        [spec((3, tok, feat))] * len(pieces),
        spec(out.shape),
        flops=HALF_FLOPS,
    )(where, *pieces).reshape(-1, feat)


def add_product_kernel(count, where_ref, *refs):
    total = refs[2 * count][...] if len(refs) > 2 * count + 1 else None
    for slot, weight in zip(refs[:count], refs[count : 2 * count]):
        term = jnp.dot(slot[...], weight[...], preferred_element_type=jnp.float32)
        total = term if total is None else total + term
    refs[-1][...] = total


def add_product(where, slots, weight, acc=None):
    rows, feat = next(iter(slots.values())).shape
    cols = weight.shape[1]
    wide = cols // 2
    whole = pl.BlockSpec((rows, wide), lambda i, w: (0, i))
    rels = list(slots)
    return call(
        functools.partial(add_product_kernel, len(rels)),
        "products",
        jax.ShapeDtypeStruct((rows, cols), jnp.float32),
        2,
        [spec((rows, feat))] * len(rels)
        + [pl.BlockSpec((feat, wide), lambda i, w, rel=rel: (w[NEAR] ^ rel, i)) for rel in rels]
        + ([] if acc is None else [whole]),
        whole,
        flops=ZERO_FLOPS if acc is None else 1,
    )(where, *slots.values(), *[weight] * len(rels), *([] if acc is None else [acc]))


def partner_place(where_ref, head):
    return (head + FETCHED * where_ref[GRP]) % 8


def first_kernel(where_ref, *refs):
    last, more, slots = refs[0], refs[1], refs[2:5]
    acc_ref, own_ref, fetched_ref, passed_ref, out_ref, held_ref = refs[5:]
    rows, feat = last.shape
    cut = fetched_ref.shape[0]

    def put(at, block):
        for head in range(2):
            there = partner_place(where_ref, 2 * (where_ref[NEAR] ^ at) + head)
            lanes = pl.ds(pl.multiple_of(there * HEAD_DIM, HEAD_DIM), HEAD_DIM)
            held_ref[:, lanes] = block[:, head * HEAD_DIM : (head + 1) * HEAD_DIM]

    @pl.when(pl.program_id(0) == 0)
    def arrange():
        for at, slot in zip((0, 2, 1), slots):
            put(at, slot[...])
        put(3, jnp.zeros((rows, feat), jnp.bfloat16))

    block = jnp.where(where_ref[INNER] == 1, last[...], more[...])
    acc = acc_ref[...]
    acc += jnp.dot(block, own_ref[...], preferred_element_type=jnp.float32)
    acc += jnp.dot(held_ref[:, :cut], fetched_ref[...], preferred_element_type=jnp.float32)
    acc += jnp.dot(held_ref[:, cut:], passed_ref[...], preferred_element_type=jnp.float32)
    out_ref[...] = acc


def first_product(where, last, more, slots, acc, weights):
    rows, feat = last.shape
    own, fetched, passed = weights
    wide = own.shape[1] // 2
    whole = pl.BlockSpec((rows, wide), lambda i, w: (0, i))
    return call(
        first_kernel,
        "first",
        jax.ShapeDtypeStruct(acc.shape, jnp.float32),
        2,
        [spec((rows, feat))] * 5
        + [whole, pl.BlockSpec((feat, wide), lambda i, w: (w[NEAR] ^ 3, i))]
        + [pl.BlockSpec((x.shape[0], wide), lambda i, w: (0, i)) for x in (fetched, passed)],
        whole,
        [pltpu.VMEM((rows, 4 * feat), jnp.bfloat16)],
    )(where, last, more, *slots, acc, own, fetched, passed)


def second_kernel(where_ref, slot, more, fetched_ref, passed_ref, acc_in, keep_ref, send_ref, acc_ref):
    weight = []
    for head in range(2):
        place = partner_place(where_ref, 2 * (where_ref[NEAR] ^ 3) + head)
        here = jnp.minimum(place, FETCHED - 1) * HEAD_DIM
        there = jnp.maximum(place - FETCHED, 0) * HEAD_DIM
        weight.append(
            jnp.where(
                place < FETCHED,
                fetched_ref[pl.ds(pl.multiple_of(here, HEAD_DIM), HEAD_DIM), :],
                passed_ref[pl.ds(pl.multiple_of(there, HEAD_DIM), HEAD_DIM), :],
            )
        )
    block = jnp.where(where_ref[INNER] == 1, slot[...], more[...])
    acc = acc_in[...] + jnp.dot(
        block, jnp.concatenate(weight, axis=0), preferred_element_type=jnp.float32
    )
    acc_ref[...] = acc.reshape(acc_ref.shape)
    for sub, out in enumerate((keep_ref, send_ref)):
        for at in range(4):
            out[at] = acc_ref[where_ref[NEAR] ^ at, where_ref[SUB] ^ sub].astype(jnp.bfloat16)


def second_product(where, chunk, slot, more, weights, acc):
    rows, feat = slot.shape
    cols = weights[0].shape[1]
    wide = cols // 2
    out = jax.ShapeDtypeStruct((4, rows // 8, wide), jnp.bfloat16)
    return call(
        second_kernel,
        "second",
        [out] * 2,
        1,
        [spec((rows, feat))] * 2
        + [pl.BlockSpec((x.shape[0], wide), lambda i, w: (0, chunk)) for x in weights]
        + [pl.BlockSpec((rows, wide), lambda i, w: (0, chunk))],
        [spec(out.shape)] * 2,
        [pltpu.VMEM((4, 2, rows // 8, wide), jnp.float32)],
    )(where, slot, more, *weights, acc)


def add_kernel(where_ref, keep_ref, term_ref, *outs):
    for at, out in enumerate(outs):
        total = keep_ref[at].astype(jnp.float32) + term_ref[at].astype(jnp.float32)
        out[...] = total.astype(jnp.bfloat16)


def add(where, keep, term):
    return call(
        add_kernel,
        "add",
        [jax.ShapeDtypeStruct(keep.shape[1:], jnp.bfloat16)] * keep.shape[0],
        1,
        [spec(keep.shape)] * 2,
        [spec(keep.shape[1:])] * keep.shape[0],
    )(where, keep, term)


def take_kernel(where_ref, weight_ref, out_ref):
    out_ref[...] = weight_ref[...]


def take_half(where, weight):
    rows, cols = weight.shape[0] // 2, weight.shape[1]
    return call(
        take_kernel,
        "take",
        jax.ShapeDtypeStruct((rows, cols), weight.dtype),
        2,
        [pl.BlockSpec((rows // 2, cols), lambda i, w: (2 * w[GRP] + i, 0))],
        pl.BlockSpec((rows // 2, cols), lambda i, w: (i, 0)),
    )(where, weight)


def share_tail(sizes, where, pieces, kv_pieces, out_weight, hidden_in, attn_gate):
    out_weight, where = lax.optimization_barrier((out_weight, where))
    fetched = swap(take_half(where, out_weight), "head", 2, 1)
    own, fetched = lax.optimization_barrier((pieces[0], fetched))
    pieces = [own, *pieces[1:]]
    passed = swap(fetched, "grp", 2, 1)

    pieces = [pieces[0], *pieces[:0:-1]]
    mine = attend_half(where, 0, pieces)
    where, mine = lax.optimization_barrier((where, mine))
    other = swap(attend_half(where, 1, pieces), "head", 2, 1)
    acc = add_product(where, {0: mine}, out_weight)
    other, acc = lax.optimization_barrier((other, acc))
    slots = []
    for at, x in enumerate((mine, other)):
        next_to, far = swap(x, "patch", 4, 1), swap(x, "patch", 4, 2)
        next_to, far, other, x = lax.optimization_barrier((next_to, far, other, x))
        if at == 1:
            acc = add_product(where, {2: slots[0][2], 1: slots[0][1]}, out_weight, acc)
            far, x, acc = lax.optimization_barrier((far, x, acc))
        middle = swap(x, "patch", 4, 3, (1, 2))
        ends = lax.ppermute(far, "patch", [(1, 0), (2, 3)])
        slots.append([x, next_to, far, middle, ends])
    weights = [out_weight, fetched, passed]
    partner = [slots[1][at] for at in (0, 2, 1)]
    acc = first_product(where, *slots[0][3:], partner, acc, weights)
    terms = [second_product(where, at, *slots[1][3:], [fetched, passed], acc) for at in range(2)]
    blocks = []
    for keep, send in terms:
        total = add(where, keep, swap(send, "sub", 2, 1))
        blocks.append([total[0]] + [swap(total[rel], "patch", 4, rel) for rel in (2, 3, 1)])
    return mix_columns(where, hidden_in, attn_gate, blocks)


def mix_columns_kernel(where_ref, hidden_ref, gate_ref, *refs):
    blocks, out_ref = refs[:-1], refs[-1]
    cols = blocks[0].shape[1]
    for chunk in range(2):
        for at, rel in enumerate((0, 2, 3, 1)):
            start = (2 * (where_ref[PATCH] ^ rel) + chunk) * cols
            lanes = pl.ds(pl.multiple_of(start, HEAD_DIM), cols)
            mixed = hidden_ref[:, lanes].astype(jnp.float32) + gate_ref[:, lanes] * blocks[
                4 * chunk + at
            ][...].astype(jnp.float32)
            out_ref[:, lanes] = mixed.astype(jnp.bfloat16)


def mix_columns(where, hidden_in, attn_gate, blocks):
    rows, width = hidden_in.shape
    flat = [x for chunk in blocks for x in chunk]
    return call(
        mix_columns_kernel,
        "mix",
        jax.ShapeDtypeStruct((rows, width), jnp.bfloat16),
        2,
        [pl.BlockSpec((rows // 2, width), lambda i, w: (i, 0)), spec((1, width))]
        + [pl.BlockSpec((rows // 2, flat[0].shape[1]), lambda i, w: (i, 0))] * len(flat),
        pl.BlockSpec((rows // 2, width), lambda i, w: (i, 0)),
    )(where, hidden_in, attn_gate[None], *flat)


def body(sizes, queries, fresh_kv, cached_kv, exponents, out_weight, hidden_in, attn_gate):
    n_patch, n_head, n_sub = sizes["patch"], sizes["head"], sizes["sub"]
    tok, channels = queries.shape
    heads = channels // HEAD_DIM
    split = math.gcd(heads, n_patch)
    patch_at = lax.axis_index("patch")
    inner = (patch_at > 0) & (patch_at < n_patch - 1)
    where = jnp.stack(
        [
            patch_at,
            patch_at % split,
            lax.axis_index("head"),
            lax.axis_index("sub"),
            inner,
            lax.axis_index("grp"),
        ]
    ).astype(jnp.int32)

    arrays = (exponents, queries, fresh_kv, cached_kv)
    sent = pack(split, *arrays)
    arrived = {rel: swap(x, "patch", n_patch, rel) for rel, x in zip(send_order(split), sent)}
    where, sent = lax.optimization_barrier((where, sent))
    pieces = [pack_own(split, where, *arrays), *[arrived[rel] for rel in range(split - 1, 0, -1)]]
    kv_pieces = list(pieces)
    for rel in range(split, n_patch, split):
        kv_pieces += [swap(x, "patch", n_patch, rel) for x in pieces]

    tail = (sizes, where, pieces, kv_pieces, out_weight, hidden_in, attn_gate)
    if (sizes["grp"], n_head, split, n_patch) == (2, 2, 4, 4):
        return share_tail(*tail)
    return sum_tail(*tail)


def solution(mesh):
    in_specs = (
        P(("grp", "patch"), ("head", "sub")),
        P(None, ("grp", "patch"), ("head", "sub")),
        P(None, "grp", ("head", "sub")),
        P(None, ("grp", "patch"), ("head", "sub")),
        P(("head", "sub"), "patch"),
        P(("grp", "patch", "head", "sub"), None),
        P(),
    )
    out_specs = P(("grp", "patch", "head", "sub"), None)
    return jax.shard_map(
        functools.partial(body, dict(mesh.shape)),
        mesh=mesh,
        in_specs=in_specs,
        out_specs=out_specs,
        check_vma=False,
    )
```

```python
import functools
import math

import jax
import jax.numpy as jnp
from jax import lax
from jax.experimental import pallas as pl
from jax.experimental.pallas import tpu as pltpu
from jax.sharding import PartitionSpec as P

HEAD_DIM = 128
SCALE_ROWS = 128
SATURATION = 448.0
PACK_ROWS = 64
VMEM_BYTES = 32 * 1024 * 1024
PACK_VMEM_BYTES = 60 * 1024 * 1024
ATTEND_FLOPS = 1
PROJECT_FLOPS = 1
OWN_FLOPS = 1
FETCHED = 4
ZERO_FLOPS = 6_000_000_000
HALF_FLOPS = 1

PATCH, NEAR, HEAD, SUB, INNER, GRP = range(6)


def spec(shape):
    return pl.BlockSpec(shape, lambda i, w: (0,) * len(shape))


def call(kernel, name, out_shape, grid, in_specs, out_specs, scratch=(), flops=1, vmem=VMEM_BYTES):
    return pl.pallas_call(
        kernel,
        out_shape=out_shape,
        grid_spec=pltpu.PrefetchScalarGridSpec(
            num_scalar_prefetch=1,
            grid=(grid,),
            in_specs=in_specs,
            out_specs=out_specs,
            scratch_shapes=list(scratch),
        ),
        compiler_params=pltpu.CompilerParams(vmem_limit_bytes=vmem),
        cost_estimate=pl.CostEstimate(flops=flops, bytes_accessed=0, transcendentals=0),
        name=name,
    )


def swap(x, axes, count, mask, only=None):
    pairs = [(at, at ^ mask) for at in range(count) if only is None or at in only]
    return lax.ppermute(x, axes, pairs)


def decode(fresh, cached, exponent):
    power = jnp.full((1, HEAD_DIM), exponent.astype(jnp.float32))
    cached = cached.astype(jnp.float32)
    residual = fresh.astype(jnp.float32) - cached
    codes = jnp.clip(residual * jnp.exp2(-power), -SATURATION, SATURATION).astype(jnp.bfloat16)
    return (cached + codes.astype(jnp.float32) * jnp.exp2(power)).astype(jnp.bfloat16)


def send_order(split):
    return sorted(range(1, split), key=lambda rel: (rel != split // 2, -rel))


def pack_kernel(split, per, exps_ref, q_ref, fresh_ref, cached_ref, *refs):
    outs, bufs = refs[: split - 1], refs[split - 1 : 2 * split - 2]
    q_buf, fresh_buf, cached_buf, sems, out_sems = refs[2 * split - 2 :]
    patch = lax.axis_index("patch")
    near = lax.rem(patch, split)
    tok = q_buf.shape[0]
    copies, sent = [], []
    for block in range(tok // PACK_ROWS):
        rows = pl.ds(block * PACK_ROWS, PACK_ROWS)
        there = pl.ds(pl.multiple_of(patch * tok + block * PACK_ROWS, PACK_ROWS), PACK_ROWS)
        copies.append(
            [
                pltpu.make_async_copy(q_ref.at[rows], q_buf.at[rows], sems.at[block, 0]),
                pltpu.make_async_copy(fresh_ref.at[:, rows], fresh_buf.at[:, rows], sems.at[block, 1]),
                pltpu.make_async_copy(cached_ref.at[:, there], cached_buf.at[:, rows], sems.at[block, 2]),
            ]
        )
        for copy in copies[-1]:
            copy.start()
    for block in range(tok // PACK_ROWS):
        rows = pl.ds(block * PACK_ROWS, PACK_ROWS)
        for copy in copies[block]:
            copy.wait()
        for number, rel in enumerate(send_order(split)):
            buf = bufs[number]
            for chunk in range(per):
                head = (near ^ rel) * per + chunk
                lanes = pl.ds(pl.multiple_of(head * HEAD_DIM, HEAD_DIM), HEAD_DIM)
                here = pl.ds(chunk * HEAD_DIM, HEAD_DIM)
                buf[0, rows, here] = q_buf[rows, lanes]
                for stacked in range(2):
                    buf[1 + stacked, rows, here] = decode(
                        fresh_buf[stacked, rows, lanes],
                        cached_buf[stacked, rows, lanes],
                        exps_ref[stacked, block * PACK_ROWS // SCALE_ROWS, head],
                    )
            sent.append(
                pltpu.make_async_copy(
                    buf.at[:, rows], outs[number].at[:, rows], out_sems.at[block, number]
                )
            )
            sent[-1].start()
    for copy in sent:
        copy.wait()


def pack(split, exponents, queries, fresh_kv, cached_kv):
    tok, channels = queries.shape
    feat = channels // split
    blocks = tok // PACK_ROWS
    hbm = pl.BlockSpec(memory_space=pltpu.HBM)
    return pl.pallas_call(
        functools.partial(pack_kernel, split, feat // HEAD_DIM),
        out_shape=[jax.ShapeDtypeStruct((3, tok, feat), jnp.bfloat16)] * (split - 1),
        in_specs=[pl.BlockSpec(memory_space=pltpu.SMEM), hbm, hbm, hbm],
        out_specs=[hbm] * (split - 1),
        scratch_shapes=[pltpu.VMEM((3, tok, feat), jnp.bfloat16)] * (split - 1)
        + [
            pltpu.VMEM((tok, channels), jnp.bfloat16),
            pltpu.VMEM((2, tok, channels), jnp.bfloat16),
            pltpu.VMEM((2, tok, channels), jnp.bfloat16),
            pltpu.SemaphoreType.DMA((blocks, 3)),
            pltpu.SemaphoreType.DMA((blocks, split - 1)),
        ],
        compiler_params=pltpu.CompilerParams(vmem_limit_bytes=PACK_VMEM_BYTES),
        name="pack",
    )(exponents, queries, fresh_kv, cached_kv)


def own_kernel(per, where_ref, exps_ref, q_ref, fresh_ref, cached_ref, out_ref):
    out_ref[0] = q_ref[...]
    for chunk in range(per):
        lanes = pl.ds(chunk * HEAD_DIM, HEAD_DIM)
        for block in range(q_ref.shape[0] // SCALE_ROWS):
            rows = pl.ds(block * SCALE_ROWS, SCALE_ROWS)
            for stacked in range(2):
                out_ref[1 + stacked, rows, lanes] = decode(
                    fresh_ref[stacked, rows, lanes],
                    cached_ref[stacked, rows, lanes],
                    exps_ref[stacked, block, where_ref[NEAR] * per + chunk],
                )


def pack_own(split, where, exponents, queries, fresh_kv, cached_kv):
    tok, channels = queries.shape
    feat = channels // split
    out = jax.ShapeDtypeStruct((3, tok, feat), jnp.bfloat16)
    return call(
        functools.partial(own_kernel, feat // HEAD_DIM),
        "own",
        out,
        1,
        [
            pl.BlockSpec(memory_space=pltpu.SMEM),
            pl.BlockSpec((tok, feat), lambda i, w: (0, w[NEAR])),
            pl.BlockSpec((2, tok, feat), lambda i, w: (0, 0, w[NEAR])),
            pl.BlockSpec((2, tok, feat), lambda i, w: (0, w[PATCH], w[NEAR])),
        ],
        spec(out.shape),
    )(where, exponents, queries, fresh_kv, cached_kv)


def attend_kernel(split, part, where_ref, *refs):
    q_refs, kv_refs, out_ref = (refs[0], *refs[split - 1 : 0 : -1]), refs[:-1], refs[-1]
    factor = HEAD_DIM**-0.5 * math.log2(math.e)
    tok, feat = q_refs[0].shape[1:]
    count = out_ref.shape[1] // part[1]
    starts = [at * (tok // count) + part[0] for at in range(count)]
    for head in range(feat // HEAD_DIM):
        lanes = pl.ds(head * HEAD_DIM, HEAD_DIM)
        keys = jnp.concatenate([ref[1, :, lanes] for ref in kv_refs], axis=0)
        values = jnp.concatenate([ref[2, :, lanes] for ref in kv_refs], axis=0)
        values = jnp.concatenate([values, jnp.ones_like(values)], axis=1)
        for rel in range(split):
            rows = [q_refs[rel][0, start : start + part[1], lanes] for start in starts]
            query = jnp.concatenate(rows, axis=0) if len(rows) > 1 else rows[0]
            scores = lax.dot_general(
                query, keys, (((1,), (1,)), ((), ())), preferred_element_type=jnp.float32
            )
            peak = jnp.max(scores, axis=1, keepdims=True)
            expo = jnp.exp2((scores - peak) * factor).astype(jnp.bfloat16)
            mix = jnp.dot(expo, values, preferred_element_type=jnp.float32)
            mix = mix[:, :HEAD_DIM] / mix[:, HEAD_DIM:]
            out_ref[where_ref[NEAR] ^ rel, :, lanes] = mix.astype(jnp.bfloat16)


def attend(where, part, count, pieces, kv_pieces):
    split = len(pieces)
    _, tok, feat = pieces[0].shape
    out = jax.ShapeDtypeStruct((split, count * part[1], feat), jnp.bfloat16)
    return call(
        functools.partial(attend_kernel, split, part),
        "attend",
        out,
        1,
        [spec((3, tok, feat))] * len(kv_pieces),
        spec(out.shape),
        flops=ATTEND_FLOPS,
    )(where, *kv_pieces)


def project_kernel(split, n_slots, n_more, where_ref, *refs):
    slots, refs = refs[:n_slots], refs[n_slots:]
    more, weight_ref, refs = refs[:n_more], refs[n_more], refs[n_more + 1 :]
    outs, held_ref, acc_ref = refs[:-2], refs[-2], refs[-1]
    rows, feat = slots[0].shape
    n_sub, n_head = acc_ref.shape[3], acc_ref.shape[2]

    @pl.when(pl.program_id(0) == 0)
    def arrange():
        for at, slot in enumerate(slots):
            group, near = divmod(at, split)
            lane = (where_ref[NEAR] ^ near) * feat
            block = slot[...]
            if more and at == n_slots - 1:
                block = jnp.where(where_ref[INNER] == 1, block, more[0][...])
            held_ref[
                group * rows : (group + 1) * rows, pl.ds(pl.multiple_of(lane, HEAD_DIM), feat)
            ] = block

    acc = jnp.dot(held_ref[...], weight_ref[...], preferred_element_type=jnp.float32)
    acc_ref[...] = acc.reshape(acc_ref.shape)
    for sub in range(n_sub):
        for head in range(n_head):
            for at in range(n_slots):
                group, near = divmod(at, split)
                outs[sub][head, at] = acc_ref[
                    group, where_ref[NEAR] ^ near, where_ref[HEAD] ^ head, where_ref[SUB] ^ sub
                ].astype(jnp.bfloat16)


def project(split, where, slots, more, weight, n_head, n_sub):
    rows, feat = slots[0].shape
    n_patch = len(slots)
    total = rows * n_patch // split
    depth, cols = weight.shape
    wide = 640 if cols % 640 == 0 else cols
    piece = rows // (split * n_head * n_sub)
    return call(
        functools.partial(project_kernel, split, n_patch, len(more)),
        "project",
        [jax.ShapeDtypeStruct((n_head, n_patch, piece, cols), jnp.bfloat16)] * n_sub,
        cols // wide,
        [spec((rows, feat))] * (n_patch + len(more))
        + [pl.BlockSpec((depth, wide), lambda i, w: (0, i))],
        [pl.BlockSpec((n_head, n_patch, piece, wide), lambda i, w: (0, 0, 0, i))] * n_sub,
        [
            pltpu.VMEM((total, depth), jnp.bfloat16),
            pltpu.VMEM((n_patch // split, split, n_head, n_sub, piece, wide), jnp.float32),
        ],
        flops=PROJECT_FLOPS,
    )(where, *slots, *more, weight)


def mix_kernel(rels, where_ref, hidden_ref, gate_ref, *refs):
    blocks, out_ref = refs[:-1], refs[-1]
    piece, cols = blocks[0].shape
    for part in range(len(blocks) // len(rels)):
        rows = pl.ds(part * piece, piece)
        for at, rel in enumerate(rels):
            lanes = pl.ds(pl.multiple_of((where_ref[PATCH] ^ rel) * cols, HEAD_DIM), cols)
            mixed = hidden_ref[rows, lanes].astype(jnp.float32) + gate_ref[:, lanes] * blocks[
                part * len(rels) + at
            ][...].astype(jnp.float32)
            out_ref[rows, lanes] = mixed.astype(jnp.bfloat16)


def mix(where, hidden_in, attn_gate, blocks):
    rows, width = hidden_in.shape
    n_patch = len(blocks[0])
    piece, cols = blocks[0][0].shape
    if cols % HEAD_DIM:
        order = jnp.concatenate([jnp.stack(x) for x in blocks], axis=1)
        order = order[where[PATCH] ^ jnp.arange(n_patch)]
        projected = order.transpose(1, 0, 2).reshape(rows, width).astype(jnp.float32)
        return (hidden_in.astype(jnp.float32) + attn_gate * projected).astype(jnp.bfloat16)
    rels = [0, *range(n_patch - 1, 0, -1)]
    flat = [part[rel] for part in blocks for rel in rels]
    return call(
        functools.partial(mix_kernel, rels),
        "mix",
        jax.ShapeDtypeStruct((rows, width), jnp.bfloat16),
        1,
        [spec((rows, width)), spec((1, width))] + [spec((piece, cols))] * len(flat),
        spec((rows, width)),
    )(where, hidden_in, attn_gate[None], *flat)


def gather(parts, n_patch):
    if n_patch != 4:
        return [
            ([x] + [swap(x, "patch", n_patch, rel) for rel in range(1, n_patch)], [])
            for x in parts
        ]
    far = [swap(x, "patch", 4, 2) for x in parts]
    next_to = [swap(x, "patch", 4, 1) for x in parts]
    out = []
    for at, x in enumerate(parts):
        far[at], next_to[at], parts = lax.optimization_barrier((far[at], next_to[at], parts))
        middle = swap(parts[at], "patch", 4, 3, (1, 2))
        ends = lax.ppermute(far[at], "patch", [(1, 0), (2, 3)])
        if at + 1 < len(parts):
            ends, far[at + 1], next_to[at + 1] = lax.optimization_barrier(
                (ends, far[at + 1], next_to[at + 1])
            )
        out.append(([x, next_to[at], far[at], middle], [ends]))
    return out


def add_sub_kernel(n_sub, where_ref, *refs):
    terms, kept_ref, outs = refs[:n_sub], refs[n_sub], refs[n_sub + 1 :]
    for head in range(len(outs) + 1):
        total = terms[0][head].astype(jnp.float32)
        for term in terms[1:]:
            total += term[head].astype(jnp.float32)
        if head == 0:
            kept_ref[...] = total
        else:
            outs[head - 1][...] = total.astype(jnp.bfloat16)


def add_head_kernel(n_more, where_ref, kept_ref, *refs):
    for at, out in enumerate(refs[n_more:]):
        total = kept_ref[at]
        for term in refs[:n_more]:
            total += term[at].astype(jnp.float32)
        out[...] = total.astype(jnp.bfloat16)


def reduce_sub(sizes, where, terms):
    n_sub, n_head = sizes["sub"], sizes["head"]
    terms = [terms[0]] + [swap(terms[rel], "sub", n_sub, rel) for rel in range(1, n_sub)]
    shape = terms[0].shape[1:]
    return call(
        functools.partial(add_sub_kernel, n_sub),
        "add_sub",
        [jax.ShapeDtypeStruct(shape, jnp.float32)]
        + [jax.ShapeDtypeStruct(shape, jnp.bfloat16)] * (n_head - 1),
        1,
        [spec(terms[0].shape)] * n_sub,
        [spec(shape)] * n_head,
    )(where, *terms)


def reduce_head(sizes, where, sums):
    n_head = sizes["head"]
    shape = sums[0].shape
    sums = [sums[0]] + [swap(sums[rel], "head", n_head, rel) for rel in range(1, n_head)]
    return call(
        functools.partial(add_head_kernel, n_head - 1),
        "add_head",
        [jax.ShapeDtypeStruct(shape[1:], jnp.bfloat16)] * shape[0],
        1,
        [spec(shape)] * n_head,
        [spec(shape[1:])] * shape[0],
    )(where, *sums)


def sum_tail(sizes, where, pieces, kv_pieces, out_weight, hidden_in, attn_gate):
    n_patch, n_head, n_sub = sizes["patch"], sizes["head"], sizes["sub"]
    split, tok = len(pieces), pieces[0].shape[1]
    count = n_head * n_sub
    piece = tok // count
    parts = 2 if piece % 32 == 0 else 1
    attended = []
    for part in range(parts):
        rows = (part * (piece // parts), piece // parts)
        x = attend(where, rows, count, pieces, kv_pieces)
        attended.append(x.reshape(-1, x.shape[2]))
    slots = gather(attended, n_patch)
    blocks = []
    for part in range(parts):
        terms = project(split, where, *slots[part], out_weight, n_head, n_sub)
        total = reduce_head(sizes, where, reduce_sub(sizes, where, terms))
        blocks.append(
            [total[0]] + [swap(total[rel], "patch", n_patch, rel) for rel in range(1, n_patch)]
        )
    return mix(where, hidden_in, attn_gate, blocks)


def attend_half_kernel(half, where_ref, *refs):
    pieces, out = refs[:-1], refs[-1]
    factor = HEAD_DIM**-0.5 * math.log2(math.e)
    rows, feat = out.shape[1:]
    start = pl.multiple_of((where_ref[HEAD] ^ half) * rows, rows)
    for head in range(feat // HEAD_DIM):
        lanes = pl.ds(head * HEAD_DIM, HEAD_DIM)
        keys = jnp.concatenate([ref[1, :, lanes] for ref in pieces], axis=0)
        values = jnp.concatenate([ref[2, :, lanes] for ref in pieces], axis=0)
        values = jnp.concatenate([values, jnp.ones_like(values)], axis=1)
        for first in range(0, len(pieces), 2):
            query = [ref[0, pl.ds(start, rows), lanes] for ref in pieces[first : first + 2]]
            scores = lax.dot_general(
                jnp.concatenate(query, axis=0),
                keys,
                (((1,), (1,)), ((), ())),
                preferred_element_type=jnp.float32,
            )
            peak = jnp.max(scores, axis=1, keepdims=True)
            expo = jnp.exp2((scores - peak) * factor).astype(jnp.bfloat16)
            mix = jnp.dot(expo, values, preferred_element_type=jnp.float32)
            mix = (mix[:, :HEAD_DIM] / mix[:, HEAD_DIM:]).astype(jnp.bfloat16)
            for at in range(len(query)):
                block = mix[at * rows : (at + 1) * rows]
                out[where_ref[NEAR] ^ (first + at), :, lanes] = block


def attend_half(where, half, pieces):
    _, tok, feat = pieces[0].shape
    out = jax.ShapeDtypeStruct((len(pieces), tok // 2, feat), jnp.bfloat16)
    return call(
        functools.partial(attend_half_kernel, half),
        "attend",
        out,
        1,
        [spec((3, tok, feat))] * len(pieces),
        spec(out.shape),
        flops=HALF_FLOPS,
    )(where, *pieces).reshape(-1, feat)


def add_product_kernel(count, where_ref, *refs):
    total = refs[2 * count][...] if len(refs) > 2 * count + 1 else None
    for slot, weight in zip(refs[:count], refs[count : 2 * count]):
        term = jnp.dot(slot[...], weight[...], preferred_element_type=jnp.float32)
        total = term if total is None else total + term
    refs[-1][...] = total


def add_product(where, slots, weight, acc=None):
    rows, feat = next(iter(slots.values())).shape
    cols = weight.shape[1]
    wide = cols // 2
    whole = pl.BlockSpec((rows, wide), lambda i, w: (0, i))
    rels = list(slots)
    return call(
        functools.partial(add_product_kernel, len(rels)),
        "products",
        jax.ShapeDtypeStruct((rows, cols), jnp.float32),
        2,
        [spec((rows, feat))] * len(rels)
        + [pl.BlockSpec((feat, wide), lambda i, w, rel=rel: (w[NEAR] ^ rel, i)) for rel in rels]
        + ([] if acc is None else [whole]),
        whole,
        flops=ZERO_FLOPS if acc is None else 1,
    )(where, *slots.values(), *[weight] * len(rels), *([] if acc is None else [acc]))


def partner_place(where_ref, head):
    return (head + FETCHED * where_ref[GRP]) % 8


def first_kernel(where_ref, *refs):
    last, more, slots = refs[0], refs[1], refs[2:5]
    acc_ref, own_ref, fetched_ref, passed_ref, out_ref, held_ref = refs[5:]
    rows, feat = last.shape
    cut = fetched_ref.shape[0]

    def put(at, block):
        for head in range(2):
            there = partner_place(where_ref, 2 * (where_ref[NEAR] ^ at) + head)
            lanes = pl.ds(pl.multiple_of(there * HEAD_DIM, HEAD_DIM), HEAD_DIM)
            held_ref[:, lanes] = block[:, head * HEAD_DIM : (head + 1) * HEAD_DIM]

    @pl.when(pl.program_id(0) == 0)
    def arrange():
        for at, slot in zip((0, 2, 1), slots):
            put(at, slot[...])
        put(3, jnp.zeros((rows, feat), jnp.bfloat16))

    block = jnp.where(where_ref[INNER] == 1, last[...], more[...])
    acc = acc_ref[...]
    acc += jnp.dot(block, own_ref[...], preferred_element_type=jnp.float32)
    acc += jnp.dot(held_ref[:, :cut], fetched_ref[...], preferred_element_type=jnp.float32)
    acc += jnp.dot(held_ref[:, cut:], passed_ref[...], preferred_element_type=jnp.float32)
    out_ref[...] = acc


def first_product(where, last, more, slots, acc, weights):
    rows, feat = last.shape
    own, fetched, passed = weights
    wide = own.shape[1] // 2
    whole = pl.BlockSpec((rows, wide), lambda i, w: (0, i))
    return call(
        first_kernel,
        "first",
        jax.ShapeDtypeStruct(acc.shape, jnp.float32),
        2,
        [spec((rows, feat))] * 5
        + [whole, pl.BlockSpec((feat, wide), lambda i, w: (w[NEAR] ^ 3, i))]
        + [pl.BlockSpec((x.shape[0], wide), lambda i, w: (0, i)) for x in (fetched, passed)],
        whole,
        [pltpu.VMEM((rows, 4 * feat), jnp.bfloat16)],
    )(where, last, more, *slots, acc, own, fetched, passed)


def second_kernel(where_ref, slot, more, fetched_ref, passed_ref, acc_in, keep_ref, send_ref, acc_ref):
    weight = []
    for head in range(2):
        place = partner_place(where_ref, 2 * (where_ref[NEAR] ^ 3) + head)
        here = jnp.minimum(place, FETCHED - 1) * HEAD_DIM
        there = jnp.maximum(place - FETCHED, 0) * HEAD_DIM
        weight.append(
            jnp.where(
                place < FETCHED,
                fetched_ref[pl.ds(pl.multiple_of(here, HEAD_DIM), HEAD_DIM), :],
                passed_ref[pl.ds(pl.multiple_of(there, HEAD_DIM), HEAD_DIM), :],
            )
        )
    block = jnp.where(where_ref[INNER] == 1, slot[...], more[...])
    acc = acc_in[...] + jnp.dot(
        block, jnp.concatenate(weight, axis=0), preferred_element_type=jnp.float32
    )
    acc_ref[...] = acc.reshape(acc_ref.shape)
    for sub, out in enumerate((keep_ref, send_ref)):
        for at in range(4):
            out[at] = acc_ref[where_ref[NEAR] ^ at, where_ref[SUB] ^ sub].astype(jnp.bfloat16)


def second_product(where, chunk, slot, more, weights, acc):
    rows, feat = slot.shape
    cols = weights[0].shape[1]
    wide = cols // 2
    out = jax.ShapeDtypeStruct((4, rows // 8, wide), jnp.bfloat16)
    return call(
        second_kernel,
        "second",
        [out] * 2,
        1,
        [spec((rows, feat))] * 2
        + [pl.BlockSpec((x.shape[0], wide), lambda i, w: (0, chunk)) for x in weights]
        + [pl.BlockSpec((rows, wide), lambda i, w: (0, chunk))],
        [spec(out.shape)] * 2,
        [pltpu.VMEM((4, 2, rows // 8, wide), jnp.float32)],
    )(where, slot, more, *weights, acc)


def add_kernel(where_ref, keep_ref, term_ref, *outs):
    for at, out in enumerate(outs):
        total = keep_ref[at].astype(jnp.float32) + term_ref[at].astype(jnp.float32)
        out[...] = total.astype(jnp.bfloat16)


def add(where, keep, term):
    return call(
        add_kernel,
        "add",
        [jax.ShapeDtypeStruct(keep.shape[1:], jnp.bfloat16)] * keep.shape[0],
        1,
        [spec(keep.shape)] * 2,
        [spec(keep.shape[1:])] * keep.shape[0],
    )(where, keep, term)


def take_kernel(where_ref, weight_ref, out_ref):
    out_ref[...] = weight_ref[...]


def take_half(where, weight):
    rows, cols = weight.shape[0] // 2, weight.shape[1]
    return call(
        take_kernel,
        "take",
        jax.ShapeDtypeStruct((rows, cols), weight.dtype),
        2,
        [pl.BlockSpec((rows // 2, cols), lambda i, w: (2 * w[GRP] + i, 0))],
        pl.BlockSpec((rows // 2, cols), lambda i, w: (i, 0)),
    )(where, weight)


def share_tail(sizes, where, pieces, kv_pieces, out_weight, hidden_in, attn_gate):
    out_weight, where = lax.optimization_barrier((out_weight, where))
    fetched = swap(take_half(where, out_weight), "head", 2, 1)
    own, fetched = lax.optimization_barrier((pieces[0], fetched))
    pieces = [own, *pieces[1:]]
    passed = swap(fetched, "grp", 2, 1)

    pieces = [pieces[0], *pieces[:0:-1]]
    mine = attend_half(where, 0, pieces)
    where, mine = lax.optimization_barrier((where, mine))
    other = swap(attend_half(where, 1, pieces), "head", 2, 1)
    acc = add_product(where, {0: mine}, out_weight)
    other, acc = lax.optimization_barrier((other, acc))
    slots = []
    for at, x in enumerate((mine, other)):
        next_to, far = swap(x, "patch", 4, 1), swap(x, "patch", 4, 2)
        next_to, far, other, x = lax.optimization_barrier((next_to, far, other, x))
        if at == 1:
            acc = add_product(where, {2: slots[0][2], 1: slots[0][1]}, out_weight, acc)
            far, x, acc = lax.optimization_barrier((far, x, acc))
        middle = swap(x, "patch", 4, 3, (1, 2))
        ends = lax.ppermute(far, "patch", [(1, 0), (2, 3)])
        slots.append([x, next_to, far, middle, ends])
    weights = [out_weight, fetched, passed]
    partner = [slots[1][at] for at in (0, 2, 1)]
    acc = first_product(where, *slots[0][3:], partner, acc, weights)
    terms = [second_product(where, at, *slots[1][3:], [fetched, passed], acc) for at in range(2)]
    blocks = []
    for keep, send in terms:
        total = add(where, keep, swap(send, "sub", 2, 1))
        blocks.append([total[0]] + [swap(total[rel], "patch", 4, rel) for rel in range(3, 0, -1)])
    return mix_columns(where, hidden_in, attn_gate, blocks)


def mix_columns_kernel(where_ref, hidden_ref, gate_ref, *refs):
    blocks, out_ref = refs[:-1], refs[-1]
    cols = blocks[0].shape[1]
    for chunk in range(2):
        for at, rel in enumerate((0, 3, 2, 1)):
            start = (2 * (where_ref[PATCH] ^ rel) + chunk) * cols
            lanes = pl.ds(pl.multiple_of(start, HEAD_DIM), cols)
            mixed = hidden_ref[:, lanes].astype(jnp.float32) + gate_ref[:, lanes] * blocks[
                4 * chunk + at
            ][...].astype(jnp.float32)
            out_ref[:, lanes] = mixed.astype(jnp.bfloat16)


def mix_columns(where, hidden_in, attn_gate, blocks):
    rows, width = hidden_in.shape
    flat = [x for chunk in blocks for x in chunk]
    return call(
        mix_columns_kernel,
        "mix",
        jax.ShapeDtypeStruct((rows, width), jnp.bfloat16),
        2,
        [pl.BlockSpec((rows // 2, width), lambda i, w: (i, 0)), spec((1, width))]
        + [pl.BlockSpec((rows // 2, flat[0].shape[1]), lambda i, w: (i, 0))] * len(flat),
        pl.BlockSpec((rows // 2, width), lambda i, w: (i, 0)),
    )(where, hidden_in, attn_gate[None], *flat)


def body(sizes, queries, fresh_kv, cached_kv, exponents, out_weight, hidden_in, attn_gate):
    n_patch, n_head, n_sub = sizes["patch"], sizes["head"], sizes["sub"]
    tok, channels = queries.shape
    heads = channels // HEAD_DIM
    split = math.gcd(heads, n_patch)
    patch_at = lax.axis_index("patch")
    inner = (patch_at > 0) & (patch_at < n_patch - 1)
    where = jnp.stack(
        [
            patch_at,
            patch_at % split,
            lax.axis_index("head"),
            lax.axis_index("sub"),
            inner,
            lax.axis_index("grp"),
        ]
    ).astype(jnp.int32)

    arrays = (exponents, queries, fresh_kv, cached_kv)
    sent = pack(split, *arrays)
    arrived = {rel: swap(x, "patch", n_patch, rel) for rel, x in zip(send_order(split), sent)}
    where, sent = lax.optimization_barrier((where, sent))
    pieces = [pack_own(split, where, *arrays), *[arrived[rel] for rel in range(split - 1, 0, -1)]]
    kv_pieces = list(pieces)
    for rel in range(split, n_patch, split):
        kv_pieces += [swap(x, "patch", n_patch, rel) for x in pieces]

    tail = (sizes, where, pieces, kv_pieces, out_weight, hidden_in, attn_gate)
    if (sizes["grp"], n_head, split, n_patch) == (2, 2, 4, 4):
        return share_tail(*tail)
    return sum_tail(*tail)


def solution(mesh):
    in_specs = (
        P(("grp", "patch"), ("head", "sub")),
        P(None, ("grp", "patch"), ("head", "sub")),
        P(None, "grp", ("head", "sub")),
        P(None, ("grp", "patch"), ("head", "sub")),
        P(("head", "sub"), "patch"),
        P(("grp", "patch", "head", "sub"), None),
        P(),
    )
    out_specs = P(("grp", "patch", "head", "sub"), None)
    return jax.shard_map(
        functools.partial(body, dict(mesh.shape)),
        mesh=mesh,
        in_specs=in_specs,
        out_specs=out_specs,
        check_vma=False,
    )
```

```python
import functools
import math

import jax
import jax.numpy as jnp
from jax import lax
from jax.experimental import pallas as pl
from jax.experimental.pallas import tpu as pltpu
from jax.sharding import PartitionSpec as P

HEAD_DIM = 128
SCALE_ROWS = 128
SATURATION = 448.0
PACK_ROWS = 32
VMEM_BYTES = 32 * 1024 * 1024
PACK_VMEM_BYTES = 60 * 1024 * 1024
ATTEND_FLOPS = 1
PROJECT_FLOPS = 1
OWN_FLOPS = 1
FETCHED = 4
ZERO_FLOPS = 6_000_000_000
HALF_FLOPS = 1

PATCH, NEAR, HEAD, SUB, INNER, GRP = range(6)


def spec(shape):
    return pl.BlockSpec(shape, lambda i, w: (0,) * len(shape))


def call(kernel, name, out_shape, grid, in_specs, out_specs, scratch=(), flops=1, vmem=VMEM_BYTES):
    return pl.pallas_call(
        kernel,
        out_shape=out_shape,
        grid_spec=pltpu.PrefetchScalarGridSpec(
            num_scalar_prefetch=1,
            grid=(grid,),
            in_specs=in_specs,
            out_specs=out_specs,
            scratch_shapes=list(scratch),
        ),
        compiler_params=pltpu.CompilerParams(vmem_limit_bytes=vmem),
        cost_estimate=pl.CostEstimate(flops=flops, bytes_accessed=0, transcendentals=0),
        name=name,
    )


def swap(x, axes, count, mask, only=None):
    pairs = [(at, at ^ mask) for at in range(count) if only is None or at in only]
    return lax.ppermute(x, axes, pairs)


def decode(fresh, cached, exponent):
    power = jnp.full((1, HEAD_DIM), exponent.astype(jnp.float32))
    cached = cached.astype(jnp.float32)
    residual = fresh.astype(jnp.float32) - cached
    codes = jnp.clip(residual * jnp.exp2(-power), -SATURATION, SATURATION).astype(jnp.bfloat16)
    return (cached + codes.astype(jnp.float32) * jnp.exp2(power)).astype(jnp.bfloat16)


def pack_kernel(split, per, exps_ref, q_ref, fresh_ref, cached_ref, *refs):
    outs, bufs = refs[: split - 1], refs[split - 1 : 2 * split - 2]
    q_buf, fresh_buf, cached_buf, sems, out_sems = refs[2 * split - 2 :]
    patch = lax.axis_index("patch")
    near = lax.rem(patch, split)
    tok = q_buf.shape[0]
    copies, sent = [], []
    for block in range(tok // PACK_ROWS):
        rows = pl.ds(block * PACK_ROWS, PACK_ROWS)
        there = pl.ds(pl.multiple_of(patch * tok + block * PACK_ROWS, PACK_ROWS), PACK_ROWS)
        copies.append(
            [
                pltpu.make_async_copy(q_ref.at[rows], q_buf.at[rows], sems.at[block, 0]),
                pltpu.make_async_copy(fresh_ref.at[:, rows], fresh_buf.at[:, rows], sems.at[block, 1]),
                pltpu.make_async_copy(cached_ref.at[:, there], cached_buf.at[:, rows], sems.at[block, 2]),
            ]
        )
        for copy in copies[-1]:
            copy.start()
    for block in range(tok // PACK_ROWS):
        rows = pl.ds(block * PACK_ROWS, PACK_ROWS)
        for copy in copies[block]:
            copy.wait()
        for rel in range(split - 1, 0, -1):
            buf = bufs[split - 1 - rel]
            for chunk in range(per):
                head = (near ^ rel) * per + chunk
                lanes = pl.ds(pl.multiple_of(head * HEAD_DIM, HEAD_DIM), HEAD_DIM)
                here = pl.ds(chunk * HEAD_DIM, HEAD_DIM)
                buf[0, rows, here] = q_buf[rows, lanes]
                for stacked in range(2):
                    buf[1 + stacked, rows, here] = decode(
                        fresh_buf[stacked, rows, lanes],
                        cached_buf[stacked, rows, lanes],
                        exps_ref[stacked, block * PACK_ROWS // SCALE_ROWS, head],
                    )
            sent.append(
                pltpu.make_async_copy(
                    buf.at[:, rows],
                    outs[split - 1 - rel].at[:, rows],
                    out_sems.at[block, rel - 1],
                )
            )
            sent[-1].start()
    for copy in sent:
        copy.wait()


def pack(split, exponents, queries, fresh_kv, cached_kv):
    tok, channels = queries.shape
    feat = channels // split
    blocks = tok // PACK_ROWS
    hbm = pl.BlockSpec(memory_space=pltpu.HBM)
    return pl.pallas_call(
        functools.partial(pack_kernel, split, feat // HEAD_DIM),
        out_shape=[jax.ShapeDtypeStruct((3, tok, feat), jnp.bfloat16)] * (split - 1),
        in_specs=[pl.BlockSpec(memory_space=pltpu.SMEM), hbm, hbm, hbm],
        out_specs=[hbm] * (split - 1),
        scratch_shapes=[pltpu.VMEM((3, tok, feat), jnp.bfloat16)] * (split - 1)
        + [
            pltpu.VMEM((tok, channels), jnp.bfloat16),
            pltpu.VMEM((2, tok, channels), jnp.bfloat16),
            pltpu.VMEM((2, tok, channels), jnp.bfloat16),
            pltpu.SemaphoreType.DMA((blocks, 3)),
            pltpu.SemaphoreType.DMA((blocks, split - 1)),
        ],
        compiler_params=pltpu.CompilerParams(vmem_limit_bytes=PACK_VMEM_BYTES),
        name="pack",
    )(exponents, queries, fresh_kv, cached_kv)


def own_kernel(per, where_ref, exps_ref, q_ref, fresh_ref, cached_ref, out_ref):
    out_ref[0] = q_ref[...]
    for chunk in range(per):
        lanes = pl.ds(chunk * HEAD_DIM, HEAD_DIM)
        for block in range(q_ref.shape[0] // SCALE_ROWS):
            rows = pl.ds(block * SCALE_ROWS, SCALE_ROWS)
            for stacked in range(2):
                out_ref[1 + stacked, rows, lanes] = decode(
                    fresh_ref[stacked, rows, lanes],
                    cached_ref[stacked, rows, lanes],
                    exps_ref[stacked, block, where_ref[NEAR] * per + chunk],
                )


def pack_own(split, where, exponents, queries, fresh_kv, cached_kv):
    tok, channels = queries.shape
    feat = channels // split
    out = jax.ShapeDtypeStruct((3, tok, feat), jnp.bfloat16)
    return call(
        functools.partial(own_kernel, feat // HEAD_DIM),
        "own",
        out,
        1,
        [
            pl.BlockSpec(memory_space=pltpu.SMEM),
            pl.BlockSpec((tok, feat), lambda i, w: (0, w[NEAR])),
            pl.BlockSpec((2, tok, feat), lambda i, w: (0, 0, w[NEAR])),
            pl.BlockSpec((2, tok, feat), lambda i, w: (0, w[PATCH], w[NEAR])),
        ],
        spec(out.shape),
    )(where, exponents, queries, fresh_kv, cached_kv)


def attend_kernel(split, part, where_ref, *refs):
    q_refs, kv_refs, out_ref = (refs[0], *refs[split - 1 : 0 : -1]), refs[:-1], refs[-1]
    factor = HEAD_DIM**-0.5 * math.log2(math.e)
    tok, feat = q_refs[0].shape[1:]
    count = out_ref.shape[1] // part[1]
    starts = [at * (tok // count) + part[0] for at in range(count)]
    for head in range(feat // HEAD_DIM):
        lanes = pl.ds(head * HEAD_DIM, HEAD_DIM)
        keys = jnp.concatenate([ref[1, :, lanes] for ref in kv_refs], axis=0)
        values = jnp.concatenate([ref[2, :, lanes] for ref in kv_refs], axis=0)
        values = jnp.concatenate([values, jnp.ones_like(values)], axis=1)
        for rel in range(split):
            rows = [q_refs[rel][0, start : start + part[1], lanes] for start in starts]
            query = jnp.concatenate(rows, axis=0) if len(rows) > 1 else rows[0]
            scores = lax.dot_general(
                query, keys, (((1,), (1,)), ((), ())), preferred_element_type=jnp.float32
            )
            peak = jnp.max(scores, axis=1, keepdims=True)
            expo = jnp.exp2((scores - peak) * factor).astype(jnp.bfloat16)
            mix = jnp.dot(expo, values, preferred_element_type=jnp.float32)
            mix = mix[:, :HEAD_DIM] / mix[:, HEAD_DIM:]
            out_ref[where_ref[NEAR] ^ rel, :, lanes] = mix.astype(jnp.bfloat16)


def attend(where, part, count, pieces, kv_pieces):
    split = len(pieces)
    _, tok, feat = pieces[0].shape
    out = jax.ShapeDtypeStruct((split, count * part[1], feat), jnp.bfloat16)
    return call(
        functools.partial(attend_kernel, split, part),
        "attend",
        out,
        1,
        [spec((3, tok, feat))] * len(kv_pieces),
        spec(out.shape),
        flops=ATTEND_FLOPS,
    )(where, *kv_pieces)


def project_kernel(split, n_slots, n_more, where_ref, *refs):
    slots, refs = refs[:n_slots], refs[n_slots:]
    more, weight_ref, refs = refs[:n_more], refs[n_more], refs[n_more + 1 :]
    outs, held_ref, acc_ref = refs[:-2], refs[-2], refs[-1]
    rows, feat = slots[0].shape
    n_sub, n_head = acc_ref.shape[3], acc_ref.shape[2]

    @pl.when(pl.program_id(0) == 0)
    def arrange():
        for at, slot in enumerate(slots):
            group, near = divmod(at, split)
            lane = (where_ref[NEAR] ^ near) * feat
            block = slot[...]
            if more and at == n_slots - 1:
                block = jnp.where(where_ref[INNER] == 1, block, more[0][...])
            held_ref[
                group * rows : (group + 1) * rows, pl.ds(pl.multiple_of(lane, HEAD_DIM), feat)
            ] = block

    acc = jnp.dot(held_ref[...], weight_ref[...], preferred_element_type=jnp.float32)
    acc_ref[...] = acc.reshape(acc_ref.shape)
    for sub in range(n_sub):
        for head in range(n_head):
            for at in range(n_slots):
                group, near = divmod(at, split)
                outs[sub][head, at] = acc_ref[
                    group, where_ref[NEAR] ^ near, where_ref[HEAD] ^ head, where_ref[SUB] ^ sub
                ].astype(jnp.bfloat16)


def project(split, where, slots, more, weight, n_head, n_sub):
    rows, feat = slots[0].shape
    n_patch = len(slots)
    total = rows * n_patch // split
    depth, cols = weight.shape
    wide = 640 if cols % 640 == 0 else cols
    piece = rows // (split * n_head * n_sub)
    return call(
        functools.partial(project_kernel, split, n_patch, len(more)),
        "project",
        [jax.ShapeDtypeStruct((n_head, n_patch, piece, cols), jnp.bfloat16)] * n_sub,
        cols // wide,
        [spec((rows, feat))] * (n_patch + len(more))
        + [pl.BlockSpec((depth, wide), lambda i, w: (0, i))],
        [pl.BlockSpec((n_head, n_patch, piece, wide), lambda i, w: (0, 0, 0, i))] * n_sub,
        [
            pltpu.VMEM((total, depth), jnp.bfloat16),
            pltpu.VMEM((n_patch // split, split, n_head, n_sub, piece, wide), jnp.float32),
        ],
        flops=PROJECT_FLOPS,
    )(where, *slots, *more, weight)


def mix_kernel(rels, where_ref, hidden_ref, gate_ref, *refs):
    blocks, out_ref = refs[:-1], refs[-1]
    piece, cols = blocks[0].shape
    for part in range(len(blocks) // len(rels)):
        rows = pl.ds(part * piece, piece)
        for at, rel in enumerate(rels):
            lanes = pl.ds(pl.multiple_of((where_ref[PATCH] ^ rel) * cols, HEAD_DIM), cols)
            mixed = hidden_ref[rows, lanes].astype(jnp.float32) + gate_ref[:, lanes] * blocks[
                part * len(rels) + at
            ][...].astype(jnp.float32)
            out_ref[rows, lanes] = mixed.astype(jnp.bfloat16)


def mix(where, hidden_in, attn_gate, blocks):
    rows, width = hidden_in.shape
    n_patch = len(blocks[0])
    piece, cols = blocks[0][0].shape
    if cols % HEAD_DIM:
        order = jnp.concatenate([jnp.stack(x) for x in blocks], axis=1)
        order = order[where[PATCH] ^ jnp.arange(n_patch)]
        projected = order.transpose(1, 0, 2).reshape(rows, width).astype(jnp.float32)
        return (hidden_in.astype(jnp.float32) + attn_gate * projected).astype(jnp.bfloat16)
    rels = [0, *range(n_patch - 1, 0, -1)]
    flat = [part[rel] for part in blocks for rel in rels]
    return call(
        functools.partial(mix_kernel, rels),
        "mix",
        jax.ShapeDtypeStruct((rows, width), jnp.bfloat16),
        1,
        [spec((rows, width)), spec((1, width))] + [spec((piece, cols))] * len(flat),
        spec((rows, width)),
    )(where, hidden_in, attn_gate[None], *flat)


def gather(parts, n_patch):
    if n_patch != 4:
        return [
            ([x] + [swap(x, "patch", n_patch, rel) for rel in range(1, n_patch)], [])
            for x in parts
        ]
    far = [swap(x, "patch", 4, 2) for x in parts]
    next_to = [swap(x, "patch", 4, 1) for x in parts]
    out = []
    for at, x in enumerate(parts):
        far[at], next_to[at], parts = lax.optimization_barrier((far[at], next_to[at], parts))
        middle = swap(parts[at], "patch", 4, 3, (1, 2))
        ends = lax.ppermute(far[at], "patch", [(1, 0), (2, 3)])
        if at + 1 < len(parts):
            ends, far[at + 1], next_to[at + 1] = lax.optimization_barrier(
                (ends, far[at + 1], next_to[at + 1])
            )
        out.append(([x, next_to[at], far[at], middle], [ends]))
    return out


def add_sub_kernel(n_sub, where_ref, *refs):
    terms, kept_ref, outs = refs[:n_sub], refs[n_sub], refs[n_sub + 1 :]
    for head in range(len(outs) + 1):
        total = terms[0][head].astype(jnp.float32)
        for term in terms[1:]:
            total += term[head].astype(jnp.float32)
        if head == 0:
            kept_ref[...] = total
        else:
            outs[head - 1][...] = total.astype(jnp.bfloat16)


def add_head_kernel(n_more, where_ref, kept_ref, *refs):
    for at, out in enumerate(refs[n_more:]):
        total = kept_ref[at]
        for term in refs[:n_more]:
            total += term[at].astype(jnp.float32)
        out[...] = total.astype(jnp.bfloat16)


def reduce_sub(sizes, where, terms):
    n_sub, n_head = sizes["sub"], sizes["head"]
    terms = [terms[0]] + [swap(terms[rel], "sub", n_sub, rel) for rel in range(1, n_sub)]
    shape = terms[0].shape[1:]
    return call(
        functools.partial(add_sub_kernel, n_sub),
        "add_sub",
        [jax.ShapeDtypeStruct(shape, jnp.float32)]
        + [jax.ShapeDtypeStruct(shape, jnp.bfloat16)] * (n_head - 1),
        1,
        [spec(terms[0].shape)] * n_sub,
        [spec(shape)] * n_head,
    )(where, *terms)


def reduce_head(sizes, where, sums):
    n_head = sizes["head"]
    shape = sums[0].shape
    sums = [sums[0]] + [swap(sums[rel], "head", n_head, rel) for rel in range(1, n_head)]
    return call(
        functools.partial(add_head_kernel, n_head - 1),
        "add_head",
        [jax.ShapeDtypeStruct(shape[1:], jnp.bfloat16)] * shape[0],
        1,
        [spec(shape)] * n_head,
        [spec(shape[1:])] * shape[0],
    )(where, *sums)


def sum_tail(sizes, where, pieces, kv_pieces, out_weight, hidden_in, attn_gate):
    n_patch, n_head, n_sub = sizes["patch"], sizes["head"], sizes["sub"]
    split, tok = len(pieces), pieces[0].shape[1]
    count = n_head * n_sub
    piece = tok // count
    parts = 2 if piece % 32 == 0 else 1
    attended = []
    for part in range(parts):
        rows = (part * (piece // parts), piece // parts)
        x = attend(where, rows, count, pieces, kv_pieces)
        attended.append(x.reshape(-1, x.shape[2]))
    slots = gather(attended, n_patch)
    blocks = []
    for part in range(parts):
        terms = project(split, where, *slots[part], out_weight, n_head, n_sub)
        total = reduce_head(sizes, where, reduce_sub(sizes, where, terms))
        blocks.append(
            [total[0]] + [swap(total[rel], "patch", n_patch, rel) for rel in range(1, n_patch)]
        )
    return mix(where, hidden_in, attn_gate, blocks)


def attend_half_kernel(half, where_ref, *refs):
    pieces, out = refs[:-1], refs[-1]
    factor = HEAD_DIM**-0.5 * math.log2(math.e)
    rows, feat = out.shape[1:]
    start = pl.multiple_of((where_ref[HEAD] ^ half) * rows, rows)
    for head in range(feat // HEAD_DIM):
        lanes = pl.ds(head * HEAD_DIM, HEAD_DIM)
        keys = jnp.concatenate([ref[1, :, lanes] for ref in pieces], axis=0)
        values = jnp.concatenate([ref[2, :, lanes] for ref in pieces], axis=0)
        values = jnp.concatenate([values, jnp.ones_like(values)], axis=1)
        for rel, ref in enumerate(pieces):
            scores = lax.dot_general(
                ref[0, pl.ds(start, rows), lanes],
                keys,
                (((1,), (1,)), ((), ())),
                preferred_element_type=jnp.float32,
            )
            peak = jnp.max(scores, axis=1, keepdims=True)
            expo = jnp.exp2((scores - peak) * factor).astype(jnp.bfloat16)
            mix = jnp.dot(expo, values, preferred_element_type=jnp.float32)
            mix = (mix[:, :HEAD_DIM] / mix[:, HEAD_DIM:]).astype(jnp.bfloat16)
            out[where_ref[NEAR] ^ rel, :, lanes] = mix


def attend_half(where, half, pieces):
    _, tok, feat = pieces[0].shape
    out = jax.ShapeDtypeStruct((len(pieces), tok // 2, feat), jnp.bfloat16)
    return call(
        functools.partial(attend_half_kernel, half),
        "attend",
        out,
        1,
        [spec((3, tok, feat))] * len(pieces),
        spec(out.shape),
        flops=HALF_FLOPS,
    )(where, *pieces).reshape(-1, feat)


def add_product_kernel(count, where_ref, *refs):
    total = refs[2 * count][...] if len(refs) > 2 * count + 1 else None
    for slot, weight in zip(refs[:count], refs[count : 2 * count]):
        term = jnp.dot(slot[...], weight[...], preferred_element_type=jnp.float32)
        total = term if total is None else total + term
    refs[-1][...] = total


def add_product(where, slots, weight, acc=None):
    rows, feat = next(iter(slots.values())).shape
    cols = weight.shape[1]
    wide = cols // 2
    whole = pl.BlockSpec((rows, wide), lambda i, w: (0, i))
    rels = list(slots)
    return call(
        functools.partial(add_product_kernel, len(rels)),
        "products",
        jax.ShapeDtypeStruct((rows, cols), jnp.float32),
        2,
        [spec((rows, feat))] * len(rels)
        + [pl.BlockSpec((feat, wide), lambda i, w, rel=rel: (w[NEAR] ^ rel, i)) for rel in rels]
        + ([] if acc is None else [whole]),
        whole,
        flops=ZERO_FLOPS if acc is None else 1,
    )(where, *slots.values(), *[weight] * len(rels), *([] if acc is None else [acc]))


def partner_place(where_ref, head):
    return (head + FETCHED * where_ref[GRP]) % 8


def first_kernel(where_ref, *refs):
    last, more, slots = refs[0], refs[1], refs[2:5]
    acc_ref, own_ref, fetched_ref, passed_ref, out_ref, held_ref = refs[5:]
    rows, feat = last.shape
    cut = fetched_ref.shape[0]

    def put(at, block):
        for head in range(2):
            there = partner_place(where_ref, 2 * (where_ref[NEAR] ^ at) + head)
            lanes = pl.ds(pl.multiple_of(there * HEAD_DIM, HEAD_DIM), HEAD_DIM)
            held_ref[:, lanes] = block[:, head * HEAD_DIM : (head + 1) * HEAD_DIM]

    @pl.when(pl.program_id(0) == 0)
    def arrange():
        for at, slot in zip((0, 2, 1), slots):
            put(at, slot[...])
        put(3, jnp.zeros((rows, feat), jnp.bfloat16))

    block = jnp.where(where_ref[INNER] == 1, last[...], more[...])
    acc = acc_ref[...]
    acc += jnp.dot(block, own_ref[...], preferred_element_type=jnp.float32)
    acc += jnp.dot(held_ref[:, :cut], fetched_ref[...], preferred_element_type=jnp.float32)
    acc += jnp.dot(held_ref[:, cut:], passed_ref[...], preferred_element_type=jnp.float32)
    out_ref[...] = acc


def first_product(where, last, more, slots, acc, weights):
    rows, feat = last.shape
    own, fetched, passed = weights
    wide = own.shape[1] // 2
    whole = pl.BlockSpec((rows, wide), lambda i, w: (0, i))
    return call(
        first_kernel,
        "first",
        jax.ShapeDtypeStruct(acc.shape, jnp.float32),
        2,
        [spec((rows, feat))] * 5
        + [whole, pl.BlockSpec((feat, wide), lambda i, w: (w[NEAR] ^ 3, i))]
        + [pl.BlockSpec((x.shape[0], wide), lambda i, w: (0, i)) for x in (fetched, passed)],
        whole,
        [pltpu.VMEM((rows, 4 * feat), jnp.bfloat16)],
    )(where, last, more, *slots, acc, own, fetched, passed)


def second_kernel(where_ref, slot, more, fetched_ref, passed_ref, acc_in, keep_ref, send_ref, acc_ref):
    weight = []
    for head in range(2):
        place = partner_place(where_ref, 2 * (where_ref[NEAR] ^ 3) + head)
        here = jnp.minimum(place, FETCHED - 1) * HEAD_DIM
        there = jnp.maximum(place - FETCHED, 0) * HEAD_DIM
        weight.append(
            jnp.where(
                place < FETCHED,
                fetched_ref[pl.ds(pl.multiple_of(here, HEAD_DIM), HEAD_DIM), :],
                passed_ref[pl.ds(pl.multiple_of(there, HEAD_DIM), HEAD_DIM), :],
            )
        )
    block = jnp.where(where_ref[INNER] == 1, slot[...], more[...])
    acc = acc_in[...] + jnp.dot(
        block, jnp.concatenate(weight, axis=0), preferred_element_type=jnp.float32
    )
    acc_ref[...] = acc.reshape(acc_ref.shape)
    for sub, out in enumerate((keep_ref, send_ref)):
        for at in range(4):
            out[at] = acc_ref[where_ref[NEAR] ^ at, where_ref[SUB] ^ sub].astype(jnp.bfloat16)


def second_product(where, chunk, slot, more, weights, acc):
    rows, feat = slot.shape
    cols = weights[0].shape[1]
    wide = cols // 2
    out = jax.ShapeDtypeStruct((4, rows // 8, wide), jnp.bfloat16)
    return call(
        second_kernel,
        "second",
        [out] * 2,
        1,
        [spec((rows, feat))] * 2
        + [pl.BlockSpec((x.shape[0], wide), lambda i, w: (0, chunk)) for x in weights]
        + [pl.BlockSpec((rows, wide), lambda i, w: (0, chunk))],
        [spec(out.shape)] * 2,
        [pltpu.VMEM((4, 2, rows // 8, wide), jnp.float32)],
    )(where, slot, more, *weights, acc)


def add_kernel(where_ref, keep_ref, term_ref, *outs):
    for at, out in enumerate(outs):
        total = keep_ref[at].astype(jnp.float32) + term_ref[at].astype(jnp.float32)
        out[...] = total.astype(jnp.bfloat16)


def add(where, keep, term):
    return call(
        add_kernel,
        "add",
        [jax.ShapeDtypeStruct(keep.shape[1:], jnp.bfloat16)] * keep.shape[0],
        1,
        [spec(keep.shape)] * 2,
        [spec(keep.shape[1:])] * keep.shape[0],
    )(where, keep, term)


def take_kernel(where_ref, weight_ref, out_ref):
    out_ref[...] = weight_ref[...]


def take_half(where, weight):
    rows, cols = weight.shape[0] // 2, weight.shape[1]
    return call(
        take_kernel,
        "take",
        jax.ShapeDtypeStruct((rows, cols), weight.dtype),
        2,
        [pl.BlockSpec((rows // 2, cols), lambda i, w: (2 * w[GRP] + i, 0))],
        pl.BlockSpec((rows // 2, cols), lambda i, w: (i, 0)),
    )(where, weight)


def share_tail(sizes, where, pieces, kv_pieces, out_weight, hidden_in, attn_gate):
    out_weight, where = lax.optimization_barrier((out_weight, where))
    fetched = swap(take_half(where, out_weight), "head", 2, 1)
    own, fetched = lax.optimization_barrier((pieces[0], fetched))
    pieces = [own, *pieces[1:]]
    passed = swap(fetched, "grp", 2, 1)

    pieces = [pieces[0], *pieces[:0:-1]]
    mine = attend_half(where, 0, pieces)
    where, mine = lax.optimization_barrier((where, mine))
    other = swap(attend_half(where, 1, pieces), "head", 2, 1)
    acc = add_product(where, {0: mine}, out_weight)
    other, acc = lax.optimization_barrier((other, acc))
    slots = []
    for at, x in enumerate((mine, other)):
        next_to, far = swap(x, "patch", 4, 1), swap(x, "patch", 4, 2)
        next_to, far, other, x = lax.optimization_barrier((next_to, far, other, x))
        if at == 1:
            acc = add_product(where, {2: slots[0][2], 1: slots[0][1]}, out_weight, acc)
            far, x, acc = lax.optimization_barrier((far, x, acc))
        middle = swap(x, "patch", 4, 3, (1, 2))
        ends = lax.ppermute(far, "patch", [(1, 0), (2, 3)])
        slots.append([x, next_to, far, middle, ends])
    weights = [out_weight, fetched, passed]
    partner = [slots[1][at] for at in (0, 2, 1)]
    acc = first_product(where, *slots[0][3:], partner, acc, weights)
    terms = [second_product(where, at, *slots[1][3:], [fetched, passed], acc) for at in range(2)]
    blocks = []
    for keep, send in terms:
        total = add(where, keep, swap(send, "sub", 2, 1))
        blocks.append([total[0]] + [swap(total[rel], "patch", 4, rel) for rel in range(3, 0, -1)])
    return mix_columns(where, hidden_in, attn_gate, blocks)


def mix_columns_kernel(where_ref, hidden_ref, gate_ref, *refs):
    blocks, out_ref = refs[:-1], refs[-1]
    cols = blocks[0].shape[1]
    for chunk in range(2):
        for at, rel in enumerate((0, 3, 2, 1)):
            start = (2 * (where_ref[PATCH] ^ rel) + chunk) * cols
            lanes = pl.ds(pl.multiple_of(start, HEAD_DIM), cols)
            mixed = hidden_ref[:, lanes].astype(jnp.float32) + gate_ref[:, lanes] * blocks[
                4 * chunk + at
            ][...].astype(jnp.float32)
            out_ref[:, lanes] = mixed.astype(jnp.bfloat16)


def mix_columns(where, hidden_in, attn_gate, blocks):
    rows, width = hidden_in.shape
    flat = [x for chunk in blocks for x in chunk]
    return call(
        mix_columns_kernel,
        "mix",
        jax.ShapeDtypeStruct((rows, width), jnp.bfloat16),
        2,
        [pl.BlockSpec((rows // 2, width), lambda i, w: (i, 0)), spec((1, width))]
        + [pl.BlockSpec((rows // 2, flat[0].shape[1]), lambda i, w: (i, 0))] * len(flat),
        pl.BlockSpec((rows // 2, width), lambda i, w: (i, 0)),
    )(where, hidden_in, attn_gate[None], *flat)


def body(sizes, queries, fresh_kv, cached_kv, exponents, out_weight, hidden_in, attn_gate):
    n_patch, n_head, n_sub = sizes["patch"], sizes["head"], sizes["sub"]
    tok, channels = queries.shape
    heads = channels // HEAD_DIM
    split = math.gcd(heads, n_patch)
    patch_at = lax.axis_index("patch")
    inner = (patch_at > 0) & (patch_at < n_patch - 1)
    where = jnp.stack(
        [
            patch_at,
            patch_at % split,
            lax.axis_index("head"),
            lax.axis_index("sub"),
            inner,
            lax.axis_index("grp"),
        ]
    ).astype(jnp.int32)

    arrays = (exponents, queries, fresh_kv, cached_kv)
    sent = pack(split, *arrays)
    far_first = [
        swap(x, "patch", n_patch, split - 1 - at) for at, x in enumerate(sent)
    ]
    where, sent = lax.optimization_barrier((where, sent))
    pieces = [pack_own(split, where, *arrays), *far_first]
    kv_pieces = list(pieces)
    for rel in range(split, n_patch, split):
        kv_pieces += [swap(x, "patch", n_patch, rel) for x in pieces]

    tail = (sizes, where, pieces, kv_pieces, out_weight, hidden_in, attn_gate)
    if (sizes["grp"], n_head, split, n_patch) == (2, 2, 4, 4):
        return share_tail(*tail)
    return sum_tail(*tail)


def solution(mesh):
    in_specs = (
        P(("grp", "patch"), ("head", "sub")),
        P(None, ("grp", "patch"), ("head", "sub")),
        P(None, "grp", ("head", "sub")),
        P(None, ("grp", "patch"), ("head", "sub")),
        P(("head", "sub"), "patch"),
        P(("grp", "patch", "head", "sub"), None),
        P(),
    )
    out_specs = P(("grp", "patch", "head", "sub"), None)
    return jax.shard_map(
        functools.partial(body, dict(mesh.shape)),
        mesh=mesh,
        in_specs=in_specs,
        out_specs=out_specs,
        check_vma=False,
    )
```

```python
import functools
import math

import jax
import jax.numpy as jnp
from jax import lax
from jax.experimental import pallas as pl
from jax.experimental.pallas import tpu as pltpu
from jax.sharding import PartitionSpec as P

HEAD_DIM = 128
SCALE_ROWS = 128
SATURATION = 448.0
PACK_ROWS = 64
VMEM_BYTES = 32 * 1024 * 1024
PACK_VMEM_BYTES = 60 * 1024 * 1024
ATTEND_FLOPS = 1
PROJECT_FLOPS = 1
OWN_FLOPS = 1
FETCHED = 4
ZERO_FLOPS = 6_000_000_000
HALF_FLOPS = 1

PATCH, NEAR, HEAD, SUB, INNER, GRP = range(6)


def spec(shape):
    return pl.BlockSpec(shape, lambda i, w: (0,) * len(shape))


def call(kernel, name, out_shape, grid, in_specs, out_specs, scratch=(), flops=1, vmem=VMEM_BYTES):
    return pl.pallas_call(
        kernel,
        out_shape=out_shape,
        grid_spec=pltpu.PrefetchScalarGridSpec(
            num_scalar_prefetch=1,
            grid=(grid,),
            in_specs=in_specs,
            out_specs=out_specs,
            scratch_shapes=list(scratch),
        ),
        compiler_params=pltpu.CompilerParams(vmem_limit_bytes=vmem),
        cost_estimate=pl.CostEstimate(flops=flops, bytes_accessed=0, transcendentals=0),
        name=name,
    )


def swap(x, axes, count, mask, only=None):
    pairs = [(at, at ^ mask) for at in range(count) if only is None or at in only]
    return lax.ppermute(x, axes, pairs)


def decode(fresh, cached, exponent):
    power = jnp.full((1, HEAD_DIM), exponent.astype(jnp.float32))
    cached = cached.astype(jnp.float32)
    residual = fresh.astype(jnp.float32) - cached
    codes = jnp.clip(residual * jnp.exp2(-power), -SATURATION, SATURATION).astype(jnp.bfloat16)
    return (cached + codes.astype(jnp.float32) * jnp.exp2(power)).astype(jnp.bfloat16)


def send_order(split):
    return sorted(range(1, split), key=lambda rel: (rel != split // 2, -rel))


def pack_kernel(split, per, exps_ref, q_ref, fresh_ref, cached_ref, *refs):
    outs, bufs = refs[: split - 1], refs[split - 1 : 2 * split - 2]
    q_buf, fresh_buf, cached_buf, sems, out_sems = refs[2 * split - 2 :]
    patch = lax.axis_index("patch")
    near = lax.rem(patch, split)
    tok = q_buf.shape[0]
    copies, sent = [], []
    for block in range(tok // PACK_ROWS):
        rows = pl.ds(block * PACK_ROWS, PACK_ROWS)
        there = pl.ds(pl.multiple_of(patch * tok + block * PACK_ROWS, PACK_ROWS), PACK_ROWS)
        copies.append(
            [
                pltpu.make_async_copy(q_ref.at[rows], q_buf.at[rows], sems.at[block, 0]),
                pltpu.make_async_copy(fresh_ref.at[:, rows], fresh_buf.at[:, rows], sems.at[block, 1]),
                pltpu.make_async_copy(cached_ref.at[:, there], cached_buf.at[:, rows], sems.at[block, 2]),
            ]
        )
        for copy in copies[-1]:
            copy.start()
    for block in range(tok // PACK_ROWS):
        rows = pl.ds(block * PACK_ROWS, PACK_ROWS)
        for copy in copies[block]:
            copy.wait()
        for number, rel in enumerate(send_order(split)):
            buf = bufs[number]
            for chunk in range(per):
                head = (near ^ rel) * per + chunk
                lanes = pl.ds(pl.multiple_of(head * HEAD_DIM, HEAD_DIM), HEAD_DIM)
                here = pl.ds(chunk * HEAD_DIM, HEAD_DIM)
                buf[0, rows, here] = q_buf[rows, lanes]
                for stacked in range(2):
                    buf[1 + stacked, rows, here] = decode(
                        fresh_buf[stacked, rows, lanes],
                        cached_buf[stacked, rows, lanes],
                        exps_ref[stacked, block * PACK_ROWS // SCALE_ROWS, head],
                    )
            sent.append(
                pltpu.make_async_copy(
                    buf.at[:, rows], outs[number].at[:, rows], out_sems.at[block, number]
                )
            )
            sent[-1].start()
    for copy in sent:
        copy.wait()


def pack(split, exponents, queries, fresh_kv, cached_kv):
    tok, channels = queries.shape
    feat = channels // split
    blocks = tok // PACK_ROWS
    hbm = pl.BlockSpec(memory_space=pltpu.HBM)
    return pl.pallas_call(
        functools.partial(pack_kernel, split, feat // HEAD_DIM),
        out_shape=[jax.ShapeDtypeStruct((3, tok, feat), jnp.bfloat16)] * (split - 1),
        in_specs=[pl.BlockSpec(memory_space=pltpu.SMEM), hbm, hbm, hbm],
        out_specs=[hbm] * (split - 1),
        scratch_shapes=[pltpu.VMEM((3, tok, feat), jnp.bfloat16)] * (split - 1)
        + [
            pltpu.VMEM((tok, channels), jnp.bfloat16),
            pltpu.VMEM((2, tok, channels), jnp.bfloat16),
            pltpu.VMEM((2, tok, channels), jnp.bfloat16),
            pltpu.SemaphoreType.DMA((blocks, 3)),
            pltpu.SemaphoreType.DMA((blocks, split - 1)),
        ],
        compiler_params=pltpu.CompilerParams(vmem_limit_bytes=PACK_VMEM_BYTES),
        name="pack",
    )(exponents, queries, fresh_kv, cached_kv)


def own_kernel(per, where_ref, exps_ref, q_ref, fresh_ref, cached_ref, out_ref):
    out_ref[0] = q_ref[...]
    for chunk in range(per):
        lanes = pl.ds(chunk * HEAD_DIM, HEAD_DIM)
        for block in range(q_ref.shape[0] // SCALE_ROWS):
            rows = pl.ds(block * SCALE_ROWS, SCALE_ROWS)
            for stacked in range(2):
                out_ref[1 + stacked, rows, lanes] = decode(
                    fresh_ref[stacked, rows, lanes],
                    cached_ref[stacked, rows, lanes],
                    exps_ref[stacked, block, where_ref[NEAR] * per + chunk],
                )


def pack_own(split, where, exponents, queries, fresh_kv, cached_kv):
    tok, channels = queries.shape
    feat = channels // split
    out = jax.ShapeDtypeStruct((3, tok, feat), jnp.bfloat16)
    return call(
        functools.partial(own_kernel, feat // HEAD_DIM),
        "own",
        out,
        1,
        [
            pl.BlockSpec(memory_space=pltpu.SMEM),
            pl.BlockSpec((tok, feat), lambda i, w: (0, w[NEAR])),
            pl.BlockSpec((2, tok, feat), lambda i, w: (0, 0, w[NEAR])),
            pl.BlockSpec((2, tok, feat), lambda i, w: (0, w[PATCH], w[NEAR])),
        ],
        spec(out.shape),
    )(where, exponents, queries, fresh_kv, cached_kv)


def attend_kernel(split, part, where_ref, *refs):
    q_refs, kv_refs, out_ref = (refs[0], *refs[split - 1 : 0 : -1]), refs[:-1], refs[-1]
    factor = HEAD_DIM**-0.5 * math.log2(math.e)
    tok, feat = q_refs[0].shape[1:]
    count = out_ref.shape[1] // part[1]
    starts = [at * (tok // count) + part[0] for at in range(count)]
    for head in range(feat // HEAD_DIM):
        lanes = pl.ds(head * HEAD_DIM, HEAD_DIM)
        keys = jnp.concatenate([ref[1, :, lanes] for ref in kv_refs], axis=0)
        values = jnp.concatenate([ref[2, :, lanes] for ref in kv_refs], axis=0)
        values = jnp.concatenate([values, jnp.ones_like(values)], axis=1)
        for rel in range(split):
            rows = [q_refs[rel][0, start : start + part[1], lanes] for start in starts]
            query = jnp.concatenate(rows, axis=0) if len(rows) > 1 else rows[0]
            scores = lax.dot_general(
                query, keys, (((1,), (1,)), ((), ())), preferred_element_type=jnp.float32
            )
            peak = jnp.max(scores, axis=1, keepdims=True)
            expo = jnp.exp2((scores - peak) * factor).astype(jnp.bfloat16)
            mix = jnp.dot(expo, values, preferred_element_type=jnp.float32)
            mix = mix[:, :HEAD_DIM] / mix[:, HEAD_DIM:]
            out_ref[where_ref[NEAR] ^ rel, :, lanes] = mix.astype(jnp.bfloat16)


def attend(where, part, count, pieces, kv_pieces):
    split = len(pieces)
    _, tok, feat = pieces[0].shape
    out = jax.ShapeDtypeStruct((split, count * part[1], feat), jnp.bfloat16)
    return call(
        functools.partial(attend_kernel, split, part),
        "attend",
        out,
        1,
        [spec((3, tok, feat))] * len(kv_pieces),
        spec(out.shape),
        flops=ATTEND_FLOPS,
    )(where, *kv_pieces)


def project_kernel(split, n_slots, n_more, where_ref, *refs):
    slots, refs = refs[:n_slots], refs[n_slots:]
    more, weight_ref, refs = refs[:n_more], refs[n_more], refs[n_more + 1 :]
    outs, held_ref, acc_ref = refs[:-2], refs[-2], refs[-1]
    rows, feat = slots[0].shape
    n_sub, n_head = acc_ref.shape[3], acc_ref.shape[2]

    @pl.when(pl.program_id(0) == 0)
    def arrange():
        for at, slot in enumerate(slots):
            group, near = divmod(at, split)
            lane = (where_ref[NEAR] ^ near) * feat
            block = slot[...]
            if more and at == n_slots - 1:
                block = jnp.where(where_ref[INNER] == 1, block, more[0][...])
            held_ref[
                group * rows : (group + 1) * rows, pl.ds(pl.multiple_of(lane, HEAD_DIM), feat)
            ] = block

    acc = jnp.dot(held_ref[...], weight_ref[...], preferred_element_type=jnp.float32)
    acc_ref[...] = acc.reshape(acc_ref.shape)
    for sub in range(n_sub):
        for head in range(n_head):
            for at in range(n_slots):
                group, near = divmod(at, split)
                outs[sub][head, at] = acc_ref[
                    group, where_ref[NEAR] ^ near, where_ref[HEAD] ^ head, where_ref[SUB] ^ sub
                ].astype(jnp.bfloat16)


def project(split, where, slots, more, weight, n_head, n_sub):
    rows, feat = slots[0].shape
    n_patch = len(slots)
    total = rows * n_patch // split
    depth, cols = weight.shape
    wide = 640 if cols % 640 == 0 else cols
    piece = rows // (split * n_head * n_sub)
    return call(
        functools.partial(project_kernel, split, n_patch, len(more)),
        "project",
        [jax.ShapeDtypeStruct((n_head, n_patch, piece, cols), jnp.bfloat16)] * n_sub,
        cols // wide,
        [spec((rows, feat))] * (n_patch + len(more))
        + [pl.BlockSpec((depth, wide), lambda i, w: (0, i))],
        [pl.BlockSpec((n_head, n_patch, piece, wide), lambda i, w: (0, 0, 0, i))] * n_sub,
        [
            pltpu.VMEM((total, depth), jnp.bfloat16),
            pltpu.VMEM((n_patch // split, split, n_head, n_sub, piece, wide), jnp.float32),
        ],
        flops=PROJECT_FLOPS,
    )(where, *slots, *more, weight)


def mix_kernel(rels, where_ref, hidden_ref, gate_ref, *refs):
    blocks, out_ref = refs[:-1], refs[-1]
    piece, cols = blocks[0].shape
    for part in range(len(blocks) // len(rels)):
        rows = pl.ds(part * piece, piece)
        for at, rel in enumerate(rels):
            lanes = pl.ds(pl.multiple_of((where_ref[PATCH] ^ rel) * cols, HEAD_DIM), cols)
            mixed = hidden_ref[rows, lanes].astype(jnp.float32) + gate_ref[:, lanes] * blocks[
                part * len(rels) + at
            ][...].astype(jnp.float32)
            out_ref[rows, lanes] = mixed.astype(jnp.bfloat16)


def mix(where, hidden_in, attn_gate, blocks):
    rows, width = hidden_in.shape
    n_patch = len(blocks[0])
    piece, cols = blocks[0][0].shape
    if cols % HEAD_DIM:
        order = jnp.concatenate([jnp.stack(x) for x in blocks], axis=1)
        order = order[where[PATCH] ^ jnp.arange(n_patch)]
        projected = order.transpose(1, 0, 2).reshape(rows, width).astype(jnp.float32)
        return (hidden_in.astype(jnp.float32) + attn_gate * projected).astype(jnp.bfloat16)
    rels = [0, *range(n_patch - 1, 0, -1)]
    flat = [part[rel] for part in blocks for rel in rels]
    return call(
        functools.partial(mix_kernel, rels),
        "mix",
        jax.ShapeDtypeStruct((rows, width), jnp.bfloat16),
        1,
        [spec((rows, width)), spec((1, width))] + [spec((piece, cols))] * len(flat),
        spec((rows, width)),
    )(where, hidden_in, attn_gate[None], *flat)


def gather(parts, n_patch):
    if n_patch != 4:
        return [
            ([x] + [swap(x, "patch", n_patch, rel) for rel in range(1, n_patch)], [])
            for x in parts
        ]
    far = [swap(x, "patch", 4, 2) for x in parts]
    next_to = [swap(x, "patch", 4, 1) for x in parts]
    out = []
    for at, x in enumerate(parts):
        far[at], next_to[at], parts = lax.optimization_barrier((far[at], next_to[at], parts))
        middle = swap(parts[at], "patch", 4, 3, (1, 2))
        ends = lax.ppermute(far[at], "patch", [(1, 0), (2, 3)])
        if at + 1 < len(parts):
            ends, far[at + 1], next_to[at + 1] = lax.optimization_barrier(
                (ends, far[at + 1], next_to[at + 1])
            )
        out.append(([x, next_to[at], far[at], middle], [ends]))
    return out


def add_sub_kernel(n_sub, where_ref, *refs):
    terms, kept_ref, outs = refs[:n_sub], refs[n_sub], refs[n_sub + 1 :]
    for head in range(len(outs) + 1):
        total = terms[0][head].astype(jnp.float32)
        for term in terms[1:]:
            total += term[head].astype(jnp.float32)
        if head == 0:
            kept_ref[...] = total
        else:
            outs[head - 1][...] = total.astype(jnp.bfloat16)


def add_head_kernel(n_more, where_ref, kept_ref, *refs):
    for at, out in enumerate(refs[n_more:]):
        total = kept_ref[at]
        for term in refs[:n_more]:
            total += term[at].astype(jnp.float32)
        out[...] = total.astype(jnp.bfloat16)


def reduce_sub(sizes, where, terms):
    n_sub, n_head = sizes["sub"], sizes["head"]
    terms = [terms[0]] + [swap(terms[rel], "sub", n_sub, rel) for rel in range(1, n_sub)]
    shape = terms[0].shape[1:]
    return call(
        functools.partial(add_sub_kernel, n_sub),
        "add_sub",
        [jax.ShapeDtypeStruct(shape, jnp.float32)]
        + [jax.ShapeDtypeStruct(shape, jnp.bfloat16)] * (n_head - 1),
        1,
        [spec(terms[0].shape)] * n_sub,
        [spec(shape)] * n_head,
    )(where, *terms)


def reduce_head(sizes, where, sums):
    n_head = sizes["head"]
    shape = sums[0].shape
    sums = [sums[0]] + [swap(sums[rel], "head", n_head, rel) for rel in range(1, n_head)]
    return call(
        functools.partial(add_head_kernel, n_head - 1),
        "add_head",
        [jax.ShapeDtypeStruct(shape[1:], jnp.bfloat16)] * shape[0],
        1,
        [spec(shape)] * n_head,
        [spec(shape[1:])] * shape[0],
    )(where, *sums)


def sum_tail(sizes, where, pieces, kv_pieces, out_weight, hidden_in, attn_gate):
    n_patch, n_head, n_sub = sizes["patch"], sizes["head"], sizes["sub"]
    split, tok = len(pieces), pieces[0].shape[1]
    count = n_head * n_sub
    piece = tok // count
    parts = 2 if piece % 32 == 0 else 1
    attended = []
    for part in range(parts):
        rows = (part * (piece // parts), piece // parts)
        x = attend(where, rows, count, pieces, kv_pieces)
        attended.append(x.reshape(-1, x.shape[2]))
    slots = gather(attended, n_patch)
    blocks = []
    for part in range(parts):
        terms = project(split, where, *slots[part], out_weight, n_head, n_sub)
        total = reduce_head(sizes, where, reduce_sub(sizes, where, terms))
        blocks.append(
            [total[0]] + [swap(total[rel], "patch", n_patch, rel) for rel in range(1, n_patch)]
        )
    return mix(where, hidden_in, attn_gate, blocks)


def attend_half_kernel(half, where_ref, *refs):
    pieces, out = refs[:-1], refs[-1]
    factor = HEAD_DIM**-0.5 * math.log2(math.e)
    rows, feat = out.shape[1:]
    start = pl.multiple_of((where_ref[HEAD] ^ half) * rows, rows)
    for head in range(feat // HEAD_DIM):
        lanes = pl.ds(head * HEAD_DIM, HEAD_DIM)
        keys = jnp.concatenate([ref[1, :, lanes] for ref in pieces], axis=0)
        values = jnp.concatenate([ref[2, :, lanes] for ref in pieces], axis=0)
        values = jnp.concatenate([values, jnp.ones_like(values)], axis=1)
        for first in range(0, len(pieces), 2):
            query = [ref[0, pl.ds(start, rows), lanes] for ref in pieces[first : first + 2]]
            scores = lax.dot_general(
                jnp.concatenate(query, axis=0),
                keys,
                (((1,), (1,)), ((), ())),
                preferred_element_type=jnp.float32,
            )
            peak = jnp.max(scores, axis=1, keepdims=True)
            expo = jnp.exp2((scores - peak) * factor).astype(jnp.bfloat16)
            mix = jnp.dot(expo, values, preferred_element_type=jnp.float32)
            mix = (mix[:, :HEAD_DIM] / mix[:, HEAD_DIM:]).astype(jnp.bfloat16)
            for at in range(len(query)):
                block = mix[at * rows : (at + 1) * rows]
                out[where_ref[NEAR] ^ (first + at), :, lanes] = block


def attend_half(where, half, pieces):
    _, tok, feat = pieces[0].shape
    out = jax.ShapeDtypeStruct((len(pieces), tok // 2, feat), jnp.bfloat16)
    return call(
        functools.partial(attend_half_kernel, half),
        "attend",
        out,
        1,
        [spec((3, tok, feat))] * len(pieces),
        spec(out.shape),
        flops=HALF_FLOPS,
    )(where, *pieces).reshape(-1, feat)


def add_product_kernel(count, where_ref, *refs):
    total = refs[2 * count][...] if len(refs) > 2 * count + 1 else None
    for slot, weight in zip(refs[:count], refs[count : 2 * count]):
        term = jnp.dot(slot[...], weight[...], preferred_element_type=jnp.float32)
        total = term if total is None else total + term
    refs[-1][...] = total


def add_product(where, slots, weight, acc=None):
    rows, feat = next(iter(slots.values())).shape
    cols = weight.shape[1]
    wide = cols // 2
    whole = pl.BlockSpec((rows, wide), lambda i, w: (0, i))
    rels = list(slots)
    return call(
        functools.partial(add_product_kernel, len(rels)),
        "products",
        jax.ShapeDtypeStruct((rows, cols), jnp.float32),
        2,
        [spec((rows, feat))] * len(rels)
        + [pl.BlockSpec((feat, wide), lambda i, w, rel=rel: (w[NEAR] ^ rel, i)) for rel in rels]
        + ([] if acc is None else [whole]),
        whole,
        flops=ZERO_FLOPS if acc is None else 1,
    )(where, *slots.values(), *[weight] * len(rels), *([] if acc is None else [acc]))


def partner_place(where_ref, head):
    return (head + FETCHED * where_ref[GRP]) % 8


def first_kernel(where_ref, *refs):
    last, more, slots = refs[0], refs[1], refs[2:5]
    acc_ref, own_ref, fetched_ref, passed_ref, out_ref, held_ref = refs[5:]
    rows, feat = last.shape
    cut = fetched_ref.shape[0]

    def put(at, block):
        for head in range(2):
            there = partner_place(where_ref, 2 * (where_ref[NEAR] ^ at) + head)
            lanes = pl.ds(pl.multiple_of(there * HEAD_DIM, HEAD_DIM), HEAD_DIM)
            held_ref[:, lanes] = block[:, head * HEAD_DIM : (head + 1) * HEAD_DIM]

    @pl.when(pl.program_id(0) == 0)
    def arrange():
        for at, slot in zip((0, 2, 1), slots):
            put(at, slot[...])
        put(3, jnp.zeros((rows, feat), jnp.bfloat16))

    block = jnp.where(where_ref[INNER] == 1, last[...], more[...])
    acc = acc_ref[...]
    acc += jnp.dot(block, own_ref[...], preferred_element_type=jnp.float32)
    acc += jnp.dot(held_ref[:, :cut], fetched_ref[...], preferred_element_type=jnp.float32)
    acc += jnp.dot(held_ref[:, cut:], passed_ref[...], preferred_element_type=jnp.float32)
    out_ref[...] = acc


def first_product(where, last, more, slots, acc, weights):
    rows, feat = last.shape
    own, fetched, passed = weights
    wide = own.shape[1] // 2
    whole = pl.BlockSpec((rows, wide), lambda i, w: (0, i))
    return call(
        first_kernel,
        "first",
        jax.ShapeDtypeStruct(acc.shape, jnp.float32),
        2,
        [spec((rows, feat))] * 5
        + [whole, pl.BlockSpec((feat, wide), lambda i, w: (w[NEAR] ^ 3, i))]
        + [pl.BlockSpec((x.shape[0], wide), lambda i, w: (0, i)) for x in (fetched, passed)],
        whole,
        [pltpu.VMEM((rows, 4 * feat), jnp.bfloat16)],
    )(where, last, more, *slots, acc, own, fetched, passed)


def second_kernel(where_ref, slot, more, fetched_ref, passed_ref, acc_in, keep_ref, send_ref, acc_ref):
    weight = []
    for head in range(2):
        place = partner_place(where_ref, 2 * (where_ref[NEAR] ^ 3) + head)
        here = jnp.minimum(place, FETCHED - 1) * HEAD_DIM
        there = jnp.maximum(place - FETCHED, 0) * HEAD_DIM
        weight.append(
            jnp.where(
                place < FETCHED,
                fetched_ref[pl.ds(pl.multiple_of(here, HEAD_DIM), HEAD_DIM), :],
                passed_ref[pl.ds(pl.multiple_of(there, HEAD_DIM), HEAD_DIM), :],
            )
        )
    block = jnp.where(where_ref[INNER] == 1, slot[...], more[...])
    acc = acc_in[...] + jnp.dot(
        block, jnp.concatenate(weight, axis=0), preferred_element_type=jnp.float32
    )
    acc_ref[...] = acc.reshape(acc_ref.shape)
    for sub, out in enumerate((keep_ref, send_ref)):
        for at in range(4):
            out[at] = acc_ref[where_ref[NEAR] ^ at, where_ref[SUB] ^ sub].astype(jnp.bfloat16)


def second_product(where, chunk, slot, more, weights, acc):
    rows, feat = slot.shape
    cols = weights[0].shape[1]
    wide = cols // 2
    out = jax.ShapeDtypeStruct((4, rows // 8, wide), jnp.bfloat16)
    return call(
        second_kernel,
        "second",
        [out] * 2,
        1,
        [spec((rows, feat))] * 2
        + [pl.BlockSpec((x.shape[0], wide), lambda i, w: (0, chunk)) for x in weights]
        + [pl.BlockSpec((rows, wide), lambda i, w: (0, chunk))],
        [spec(out.shape)] * 2,
        [pltpu.VMEM((4, 2, rows // 8, wide), jnp.float32)],
    )(where, slot, more, *weights, acc)


def add_kernel(where_ref, keep_ref, term_ref, *outs):
    for at, out in enumerate(outs):
        total = keep_ref[at].astype(jnp.float32) + term_ref[at].astype(jnp.float32)
        out[...] = total.astype(jnp.bfloat16)


def add(where, keep, term):
    return call(
        add_kernel,
        "add",
        [jax.ShapeDtypeStruct(keep.shape[1:], jnp.bfloat16)] * keep.shape[0],
        1,
        [spec(keep.shape)] * 2,
        [spec(keep.shape[1:])] * keep.shape[0],
    )(where, keep, term)


def take_kernel(where_ref, weight_ref, out_ref):
    out_ref[...] = weight_ref[...]


def take_half(where, weight):
    rows, cols = weight.shape[0] // 2, weight.shape[1]
    return call(
        take_kernel,
        "take",
        jax.ShapeDtypeStruct((rows, cols), weight.dtype),
        2,
        [pl.BlockSpec((rows // 2, cols), lambda i, w: (2 * w[GRP] + i, 0))],
        pl.BlockSpec((rows // 2, cols), lambda i, w: (i, 0)),
    )(where, weight)


def share_tail(sizes, where, pieces, kv_pieces, out_weight, hidden_in, attn_gate):
    out_weight, where = lax.optimization_barrier((out_weight, where))
    fetched = swap(take_half(where, out_weight), "head", 2, 1)
    own, fetched = lax.optimization_barrier((pieces[0], fetched))
    pieces = [own, *pieces[1:]]
    passed = swap(fetched, "grp", 2, 1)

    pieces = [pieces[0], *pieces[:0:-1]]
    mine = attend_half(where, 0, pieces)
    where, mine = lax.optimization_barrier((where, mine))
    other = swap(attend_half(where, 1, pieces), "head", 2, 1)
    acc = add_product(where, {0: mine}, out_weight)
    other, acc = lax.optimization_barrier((other, acc))
    slots = []
    for at, x in enumerate((mine, other)):
        next_to, far = swap(x, "patch", 4, 1), swap(x, "patch", 4, 2)
        far, next_to, other, x = lax.optimization_barrier((far, next_to, other, x))
        if at == 1:
            acc = add_product(where, {2: slots[0][2], 1: slots[0][1]}, out_weight, acc)
            far, x, acc = lax.optimization_barrier((far, x, acc))
        middle = swap(x, "patch", 4, 3, (1, 2))
        ends = lax.ppermute(far, "patch", [(1, 0), (2, 3)])
        slots.append([x, next_to, far, middle, ends])
    weights = [out_weight, fetched, passed]
    partner = [slots[1][at] for at in (0, 2, 1)]
    acc = first_product(where, *slots[0][3:], partner, acc, weights)
    terms = [second_product(where, at, *slots[1][3:], [fetched, passed], acc) for at in range(2)]
    blocks = []
    for keep, send in terms:
        total = add(where, keep, swap(send, "sub", 2, 1))
        blocks.append([total[0]] + [swap(total[rel], "patch", 4, rel) for rel in range(3, 0, -1)])
    return mix_columns(where, hidden_in, attn_gate, blocks)


def mix_columns_kernel(where_ref, hidden_ref, gate_ref, *refs):
    blocks, out_ref = refs[:-1], refs[-1]
    cols = blocks[0].shape[1]
    for chunk in range(2):
        for at, rel in enumerate((0, 3, 2, 1)):
            start = (2 * (where_ref[PATCH] ^ rel) + chunk) * cols
            lanes = pl.ds(pl.multiple_of(start, HEAD_DIM), cols)
            mixed = hidden_ref[:, lanes].astype(jnp.float32) + gate_ref[:, lanes] * blocks[
                4 * chunk + at
            ][...].astype(jnp.float32)
            out_ref[:, lanes] = mixed.astype(jnp.bfloat16)


def mix_columns(where, hidden_in, attn_gate, blocks):
    rows, width = hidden_in.shape
    flat = [x for chunk in blocks for x in chunk]
    return call(
        mix_columns_kernel,
        "mix",
        jax.ShapeDtypeStruct((rows, width), jnp.bfloat16),
        2,
        [pl.BlockSpec((rows // 2, width), lambda i, w: (i, 0)), spec((1, width))]
        + [pl.BlockSpec((rows // 2, flat[0].shape[1]), lambda i, w: (i, 0))] * len(flat),
        pl.BlockSpec((rows // 2, width), lambda i, w: (i, 0)),
    )(where, hidden_in, attn_gate[None], *flat)


def body(sizes, queries, fresh_kv, cached_kv, exponents, out_weight, hidden_in, attn_gate):
    n_patch, n_head, n_sub = sizes["patch"], sizes["head"], sizes["sub"]
    tok, channels = queries.shape
    heads = channels // HEAD_DIM
    split = math.gcd(heads, n_patch)
    patch_at = lax.axis_index("patch")
    inner = (patch_at > 0) & (patch_at < n_patch - 1)
    where = jnp.stack(
        [
            patch_at,
            patch_at % split,
            lax.axis_index("head"),
            lax.axis_index("sub"),
            inner,
            lax.axis_index("grp"),
        ]
    ).astype(jnp.int32)

    arrays = (exponents, queries, fresh_kv, cached_kv)
    sent = pack(split, *arrays)
    arrived = {rel: swap(x, "patch", n_patch, rel) for rel, x in zip(send_order(split), sent)}
    where, sent = lax.optimization_barrier((where, sent))
    pieces = [pack_own(split, where, *arrays), *[arrived[rel] for rel in range(split - 1, 0, -1)]]
    kv_pieces = list(pieces)
    for rel in range(split, n_patch, split):
        kv_pieces += [swap(x, "patch", n_patch, rel) for x in pieces]

    tail = (sizes, where, pieces, kv_pieces, out_weight, hidden_in, attn_gate)
    if (sizes["grp"], n_head, split, n_patch) == (2, 2, 4, 4):
        return share_tail(*tail)
    return sum_tail(*tail)


def solution(mesh):
    in_specs = (
        P(("grp", "patch"), ("head", "sub")),
        P(None, ("grp", "patch"), ("head", "sub")),
        P(None, "grp", ("head", "sub")),
        P(None, ("grp", "patch"), ("head", "sub")),
        P(("head", "sub"), "patch"),
        P(("grp", "patch", "head", "sub"), None),
        P(),
    )
    out_specs = P(("grp", "patch", "head", "sub"), None)
    return jax.shard_map(
        functools.partial(body, dict(mesh.shape)),
        mesh=mesh,
        in_specs=in_specs,
        out_specs=out_specs,
        check_vma=False,
    )
```

```python
import functools
import math

import jax
import jax.numpy as jnp
from jax import lax
from jax.experimental import pallas as pl
from jax.experimental.pallas import tpu as pltpu
from jax.sharding import PartitionSpec as P

HEAD_DIM = 128
SCALE_ROWS = 128
SATURATION = 448.0
PACK_ROWS = 64
VMEM_BYTES = 32 * 1024 * 1024
PACK_VMEM_BYTES = 60 * 1024 * 1024
ATTEND_FLOPS = 1
PROJECT_FLOPS = 1
OWN_FLOPS = 1
FETCHED = 4
ZERO_FLOPS = 6_000_000_000
HALF_FLOPS = 1

PATCH, NEAR, HEAD, SUB, INNER, GRP = range(6)


def spec(shape):
    return pl.BlockSpec(shape, lambda i, w: (0,) * len(shape))


def call(kernel, name, out_shape, grid, in_specs, out_specs, scratch=(), flops=1, vmem=VMEM_BYTES):
    return pl.pallas_call(
        kernel,
        out_shape=out_shape,
        grid_spec=pltpu.PrefetchScalarGridSpec(
            num_scalar_prefetch=1,
            grid=(grid,),
            in_specs=in_specs,
            out_specs=out_specs,
            scratch_shapes=list(scratch),
        ),
        compiler_params=pltpu.CompilerParams(vmem_limit_bytes=vmem),
        cost_estimate=pl.CostEstimate(flops=flops, bytes_accessed=0, transcendentals=0),
        name=name,
    )


def swap(x, axes, count, mask, only=None):
    pairs = [(at, at ^ mask) for at in range(count) if only is None or at in only]
    return lax.ppermute(x, axes, pairs)


def decode(fresh, cached, exponent):
    power = jnp.full((1, HEAD_DIM), exponent.astype(jnp.float32))
    cached = cached.astype(jnp.float32)
    residual = fresh.astype(jnp.float32) - cached
    codes = jnp.clip(residual * jnp.exp2(-power), -SATURATION, SATURATION).astype(jnp.bfloat16)
    return (cached + codes.astype(jnp.float32) * jnp.exp2(power)).astype(jnp.bfloat16)


def pack_kernel(split, per, exps_ref, q_ref, fresh_ref, cached_ref, *refs):
    outs, bufs = refs[: split - 1], refs[split - 1 : 2 * split - 2]
    q_buf, fresh_buf, cached_buf, sems, out_sems = refs[2 * split - 2 :]
    patch = lax.axis_index("patch")
    near = lax.rem(patch, split)
    tok = q_buf.shape[0]
    copies, sent = [], []
    for block in range(tok // PACK_ROWS):
        rows = pl.ds(block * PACK_ROWS, PACK_ROWS)
        there = pl.ds(pl.multiple_of(patch * tok + block * PACK_ROWS, PACK_ROWS), PACK_ROWS)
        copies.append(
            [
                pltpu.make_async_copy(q_ref.at[rows], q_buf.at[rows], sems.at[block, 0]),
                pltpu.make_async_copy(fresh_ref.at[:, rows], fresh_buf.at[:, rows], sems.at[block, 1]),
                pltpu.make_async_copy(cached_ref.at[:, there], cached_buf.at[:, rows], sems.at[block, 2]),
            ]
        )
        for copy in copies[-1]:
            copy.start()
    for block in range(tok // PACK_ROWS):
        rows = pl.ds(block * PACK_ROWS, PACK_ROWS)
        for copy in copies[block]:
            copy.wait()
        for rel in range(split - 1, 0, -1):
            buf = bufs[split - 1 - rel]
            for chunk in range(per):
                head = (near ^ rel) * per + chunk
                lanes = pl.ds(pl.multiple_of(head * HEAD_DIM, HEAD_DIM), HEAD_DIM)
                here = pl.ds(chunk * HEAD_DIM, HEAD_DIM)
                buf[0, rows, here] = q_buf[rows, lanes]
                for stacked in range(2):
                    buf[1 + stacked, rows, here] = decode(
                        fresh_buf[stacked, rows, lanes],
                        cached_buf[stacked, rows, lanes],
                        exps_ref[stacked, block * PACK_ROWS // SCALE_ROWS, head],
                    )
            sent.append(
                pltpu.make_async_copy(
                    buf.at[:, rows],
                    outs[split - 1 - rel].at[:, rows],
                    out_sems.at[block, rel - 1],
                )
            )
            sent[-1].start()
    for copy in sent:
        copy.wait()


def pack(split, exponents, queries, fresh_kv, cached_kv):
    tok, channels = queries.shape
    feat = channels // split
    blocks = tok // PACK_ROWS
    hbm = pl.BlockSpec(memory_space=pltpu.HBM)
    return pl.pallas_call(
        functools.partial(pack_kernel, split, feat // HEAD_DIM),
        out_shape=[jax.ShapeDtypeStruct((3, tok, feat), jnp.bfloat16)] * (split - 1),
        in_specs=[pl.BlockSpec(memory_space=pltpu.SMEM), hbm, hbm, hbm],
        out_specs=[hbm] * (split - 1),
        scratch_shapes=[pltpu.VMEM((3, tok, feat), jnp.bfloat16)] * (split - 1)
        + [
            pltpu.VMEM((tok, channels), jnp.bfloat16),
            pltpu.VMEM((2, tok, channels), jnp.bfloat16),
            pltpu.VMEM((2, tok, channels), jnp.bfloat16),
            pltpu.SemaphoreType.DMA((blocks, 3)),
            pltpu.SemaphoreType.DMA((blocks, split - 1)),
        ],
        compiler_params=pltpu.CompilerParams(vmem_limit_bytes=PACK_VMEM_BYTES),
        name="pack",
    )(exponents, queries, fresh_kv, cached_kv)


def own_kernel(per, where_ref, exps_ref, q_ref, fresh_ref, cached_ref, out_ref):
    out_ref[0] = q_ref[...]
    for chunk in range(per):
        lanes = pl.ds(chunk * HEAD_DIM, HEAD_DIM)
        for block in range(q_ref.shape[0] // SCALE_ROWS):
            rows = pl.ds(block * SCALE_ROWS, SCALE_ROWS)
            for stacked in range(2):
                out_ref[1 + stacked, rows, lanes] = decode(
                    fresh_ref[stacked, rows, lanes],
                    cached_ref[stacked, rows, lanes],
                    exps_ref[stacked, block, where_ref[NEAR] * per + chunk],
                )


def pack_own(split, where, exponents, queries, fresh_kv, cached_kv):
    tok, channels = queries.shape
    feat = channels // split
    out = jax.ShapeDtypeStruct((3, tok, feat), jnp.bfloat16)
    return call(
        functools.partial(own_kernel, feat // HEAD_DIM),
        "own",
        out,
        1,
        [
            pl.BlockSpec(memory_space=pltpu.SMEM),
            pl.BlockSpec((tok, feat), lambda i, w: (0, w[NEAR])),
            pl.BlockSpec((2, tok, feat), lambda i, w: (0, 0, w[NEAR])),
            pl.BlockSpec((2, tok, feat), lambda i, w: (0, w[PATCH], w[NEAR])),
        ],
        spec(out.shape),
    )(where, exponents, queries, fresh_kv, cached_kv)


def attend_kernel(split, part, where_ref, *refs):
    q_refs, kv_refs, out_ref = (refs[0], *refs[split - 1 : 0 : -1]), refs[:-1], refs[-1]
    factor = HEAD_DIM**-0.5 * math.log2(math.e)
    tok, feat = q_refs[0].shape[1:]
    count = out_ref.shape[1] // part[1]
    starts = [at * (tok // count) + part[0] for at in range(count)]
    for head in range(feat // HEAD_DIM):
        lanes = pl.ds(head * HEAD_DIM, HEAD_DIM)
        keys = jnp.concatenate([ref[1, :, lanes] for ref in kv_refs], axis=0)
        values = jnp.concatenate([ref[2, :, lanes] for ref in kv_refs], axis=0)
        values = jnp.concatenate([values, jnp.ones_like(values)], axis=1)
        for rel in range(split):
            rows = [q_refs[rel][0, start : start + part[1], lanes] for start in starts]
            query = jnp.concatenate(rows, axis=0) if len(rows) > 1 else rows[0]
            scores = lax.dot_general(
                query, keys, (((1,), (1,)), ((), ())), preferred_element_type=jnp.float32
            )
            peak = jnp.max(scores, axis=1, keepdims=True)
            expo = jnp.exp2((scores - peak) * factor).astype(jnp.bfloat16)
            mix = jnp.dot(expo, values, preferred_element_type=jnp.float32)
            mix = mix[:, :HEAD_DIM] / mix[:, HEAD_DIM:]
            out_ref[where_ref[NEAR] ^ rel, :, lanes] = mix.astype(jnp.bfloat16)


def attend(where, part, count, pieces, kv_pieces):
    split = len(pieces)
    _, tok, feat = pieces[0].shape
    out = jax.ShapeDtypeStruct((split, count * part[1], feat), jnp.bfloat16)
    return call(
        functools.partial(attend_kernel, split, part),
        "attend",
        out,
        1,
        [spec((3, tok, feat))] * len(kv_pieces),
        spec(out.shape),
        flops=ATTEND_FLOPS,
    )(where, *kv_pieces)


def project_kernel(split, n_slots, n_more, where_ref, *refs):
    slots, refs = refs[:n_slots], refs[n_slots:]
    more, weight_ref, refs = refs[:n_more], refs[n_more], refs[n_more + 1 :]
    outs, held_ref, acc_ref = refs[:-2], refs[-2], refs[-1]
    rows, feat = slots[0].shape
    n_sub, n_head = acc_ref.shape[3], acc_ref.shape[2]

    @pl.when(pl.program_id(0) == 0)
    def arrange():
        for at, slot in enumerate(slots):
            group, near = divmod(at, split)
            lane = (where_ref[NEAR] ^ near) * feat
            block = slot[...]
            if more and at == n_slots - 1:
                block = jnp.where(where_ref[INNER] == 1, block, more[0][...])
            held_ref[
                group * rows : (group + 1) * rows, pl.ds(pl.multiple_of(lane, HEAD_DIM), feat)
            ] = block

    acc = jnp.dot(held_ref[...], weight_ref[...], preferred_element_type=jnp.float32)
    acc_ref[...] = acc.reshape(acc_ref.shape)
    for sub in range(n_sub):
        for head in range(n_head):
            for at in range(n_slots):
                group, near = divmod(at, split)
                outs[sub][head, at] = acc_ref[
                    group, where_ref[NEAR] ^ near, where_ref[HEAD] ^ head, where_ref[SUB] ^ sub
                ].astype(jnp.bfloat16)


def project(split, where, slots, more, weight, n_head, n_sub):
    rows, feat = slots[0].shape
    n_patch = len(slots)
    total = rows * n_patch // split
    depth, cols = weight.shape
    wide = 640 if cols % 640 == 0 else cols
    piece = rows // (split * n_head * n_sub)
    return call(
        functools.partial(project_kernel, split, n_patch, len(more)),
        "project",
        [jax.ShapeDtypeStruct((n_head, n_patch, piece, cols), jnp.bfloat16)] * n_sub,
        cols // wide,
        [spec((rows, feat))] * (n_patch + len(more))
        + [pl.BlockSpec((depth, wide), lambda i, w: (0, i))],
        [pl.BlockSpec((n_head, n_patch, piece, wide), lambda i, w: (0, 0, 0, i))] * n_sub,
        [
            pltpu.VMEM((total, depth), jnp.bfloat16),
            pltpu.VMEM((n_patch // split, split, n_head, n_sub, piece, wide), jnp.float32),
        ],
        flops=PROJECT_FLOPS,
    )(where, *slots, *more, weight)


def mix_kernel(rels, where_ref, hidden_ref, gate_ref, *refs):
    blocks, out_ref = refs[:-1], refs[-1]
    piece, cols = blocks[0].shape
    for part in range(len(blocks) // len(rels)):
        rows = pl.ds(part * piece, piece)
        for at, rel in enumerate(rels):
            lanes = pl.ds(pl.multiple_of((where_ref[PATCH] ^ rel) * cols, HEAD_DIM), cols)
            mixed = hidden_ref[rows, lanes].astype(jnp.float32) + gate_ref[:, lanes] * blocks[
                part * len(rels) + at
            ][...].astype(jnp.float32)
            out_ref[rows, lanes] = mixed.astype(jnp.bfloat16)


def mix(where, hidden_in, attn_gate, blocks):
    rows, width = hidden_in.shape
    n_patch = len(blocks[0])
    piece, cols = blocks[0][0].shape
    if cols % HEAD_DIM:
        order = jnp.concatenate([jnp.stack(x) for x in blocks], axis=1)
        order = order[where[PATCH] ^ jnp.arange(n_patch)]
        projected = order.transpose(1, 0, 2).reshape(rows, width).astype(jnp.float32)
        return (hidden_in.astype(jnp.float32) + attn_gate * projected).astype(jnp.bfloat16)
    rels = [0, *range(n_patch - 1, 0, -1)]
    flat = [part[rel] for part in blocks for rel in rels]
    return call(
        functools.partial(mix_kernel, rels),
        "mix",
        jax.ShapeDtypeStruct((rows, width), jnp.bfloat16),
        1,
        [spec((rows, width)), spec((1, width))] + [spec((piece, cols))] * len(flat),
        spec((rows, width)),
    )(where, hidden_in, attn_gate[None], *flat)


def gather(parts, n_patch):
    if n_patch != 4:
        return [
            ([x] + [swap(x, "patch", n_patch, rel) for rel in range(1, n_patch)], [])
            for x in parts
        ]
    far = [swap(x, "patch", 4, 2) for x in parts]
    next_to = [swap(x, "patch", 4, 1) for x in parts]
    out = []
    for at, x in enumerate(parts):
        far[at], next_to[at], parts = lax.optimization_barrier((far[at], next_to[at], parts))
        middle = swap(parts[at], "patch", 4, 3, (1, 2))
        ends = lax.ppermute(far[at], "patch", [(1, 0), (2, 3)])
        if at + 1 < len(parts):
            ends, far[at + 1], next_to[at + 1] = lax.optimization_barrier(
                (ends, far[at + 1], next_to[at + 1])
            )
        out.append(([x, next_to[at], far[at], middle], [ends]))
    return out


def add_sub_kernel(n_sub, where_ref, *refs):
    terms, kept_ref, outs = refs[:n_sub], refs[n_sub], refs[n_sub + 1 :]
    for head in range(len(outs) + 1):
        total = terms[0][head].astype(jnp.float32)
        for term in terms[1:]:
            total += term[head].astype(jnp.float32)
        if head == 0:
            kept_ref[...] = total
        else:
            outs[head - 1][...] = total.astype(jnp.bfloat16)


def add_head_kernel(n_more, where_ref, kept_ref, *refs):
    for at, out in enumerate(refs[n_more:]):
        total = kept_ref[at]
        for term in refs[:n_more]:
            total += term[at].astype(jnp.float32)
        out[...] = total.astype(jnp.bfloat16)


def reduce_sub(sizes, where, terms):
    n_sub, n_head = sizes["sub"], sizes["head"]
    terms = [terms[0]] + [swap(terms[rel], "sub", n_sub, rel) for rel in range(1, n_sub)]
    shape = terms[0].shape[1:]
    return call(
        functools.partial(add_sub_kernel, n_sub),
        "add_sub",
        [jax.ShapeDtypeStruct(shape, jnp.float32)]
        + [jax.ShapeDtypeStruct(shape, jnp.bfloat16)] * (n_head - 1),
        1,
        [spec(terms[0].shape)] * n_sub,
        [spec(shape)] * n_head,
    )(where, *terms)


def reduce_head(sizes, where, sums):
    n_head = sizes["head"]
    shape = sums[0].shape
    sums = [sums[0]] + [swap(sums[rel], "head", n_head, rel) for rel in range(1, n_head)]
    return call(
        functools.partial(add_head_kernel, n_head - 1),
        "add_head",
        [jax.ShapeDtypeStruct(shape[1:], jnp.bfloat16)] * shape[0],
        1,
        [spec(shape)] * n_head,
        [spec(shape[1:])] * shape[0],
    )(where, *sums)


def sum_tail(sizes, where, pieces, kv_pieces, out_weight, hidden_in, attn_gate):
    n_patch, n_head, n_sub = sizes["patch"], sizes["head"], sizes["sub"]
    split, tok = len(pieces), pieces[0].shape[1]
    count = n_head * n_sub
    piece = tok // count
    parts = 2 if piece % 32 == 0 else 1
    attended = []
    for part in range(parts):
        rows = (part * (piece // parts), piece // parts)
        x = attend(where, rows, count, pieces, kv_pieces)
        attended.append(x.reshape(-1, x.shape[2]))
    slots = gather(attended, n_patch)
    blocks = []
    for part in range(parts):
        terms = project(split, where, *slots[part], out_weight, n_head, n_sub)
        total = reduce_head(sizes, where, reduce_sub(sizes, where, terms))
        blocks.append(
            [total[0]] + [swap(total[rel], "patch", n_patch, rel) for rel in range(1, n_patch)]
        )
    return mix(where, hidden_in, attn_gate, blocks)


def attend_half_kernel(half, where_ref, *refs):
    pieces, out = refs[:-1], refs[-1]
    factor = HEAD_DIM**-0.5 * math.log2(math.e)
    rows, feat = out.shape[1:]
    start = pl.multiple_of((where_ref[HEAD] ^ half) * rows, rows)
    for head in range(feat // HEAD_DIM):
        lanes = pl.ds(head * HEAD_DIM, HEAD_DIM)
        keys = jnp.concatenate([ref[1, :, lanes] for ref in pieces], axis=0)
        values = jnp.concatenate([ref[2, :, lanes] for ref in pieces], axis=0)
        values = jnp.concatenate([values, jnp.ones_like(values)], axis=1)
        for first in range(0, len(pieces), 2):
            query = [ref[0, pl.ds(start, rows), lanes] for ref in pieces[first : first + 2]]
            scores = lax.dot_general(
                jnp.concatenate(query, axis=0),
                keys,
                (((1,), (1,)), ((), ())),
                preferred_element_type=jnp.float32,
            )
            peak = jnp.max(scores, axis=1, keepdims=True)
            expo = jnp.exp2((scores - peak) * factor).astype(jnp.bfloat16)
            mix = jnp.dot(expo, values, preferred_element_type=jnp.float32)
            mix = (mix[:, :HEAD_DIM] / mix[:, HEAD_DIM:]).astype(jnp.bfloat16)
            for at in range(len(query)):
                block = mix[at * rows : (at + 1) * rows]
                out[where_ref[NEAR] ^ (first + at), :, lanes] = block


def attend_half(where, half, pieces):
    _, tok, feat = pieces[0].shape
    out = jax.ShapeDtypeStruct((len(pieces), tok // 2, feat), jnp.bfloat16)
    return call(
        functools.partial(attend_half_kernel, half),
        "attend",
        out,
        1,
        [spec((3, tok, feat))] * len(pieces),
        spec(out.shape),
        flops=HALF_FLOPS,
    )(where, *pieces).reshape(-1, feat)


def add_product_kernel(count, where_ref, *refs):
    total = refs[2 * count][...] if len(refs) > 2 * count + 1 else None
    for slot, weight in zip(refs[:count], refs[count : 2 * count]):
        term = jnp.dot(slot[...], weight[...], preferred_element_type=jnp.float32)
        total = term if total is None else total + term
    refs[-1][...] = total


def add_product(where, slots, weight, acc=None):
    rows, feat = next(iter(slots.values())).shape
    cols = weight.shape[1]
    wide = cols // 2
    whole = pl.BlockSpec((rows, wide), lambda i, w: (0, i))
    rels = list(slots)
    return call(
        functools.partial(add_product_kernel, len(rels)),
        "products",
        jax.ShapeDtypeStruct((rows, cols), jnp.float32),
        2,
        [spec((rows, feat))] * len(rels)
        + [pl.BlockSpec((feat, wide), lambda i, w, rel=rel: (w[NEAR] ^ rel, i)) for rel in rels]
        + ([] if acc is None else [whole]),
        whole,
        flops=ZERO_FLOPS if acc is None else 1,
    )(where, *slots.values(), *[weight] * len(rels), *([] if acc is None else [acc]))


def partner_place(where_ref, head):
    return (head + FETCHED * where_ref[GRP]) % 8


def from_next(where_ref, up, down):
    return jnp.where(where_ref[PATCH] % 2 == 1, up[...], down[...])


def from_last(where_ref, up, down, ends):
    inner = jnp.where(where_ref[PATCH] % 2 == 1, down[...], up[...])
    return jnp.where(where_ref[INNER] == 1, inner, ends[...])


def first_kernel(where_ref, *refs):
    mine, (own, far, up, down), refs = refs[:3], refs[3:7], refs[7:]
    acc_ref, near_ref, last_ref, fetched_ref, passed_ref, out_ref, held_ref = refs
    rows, feat = own.shape
    cut = fetched_ref.shape[0]

    def put(at, block):
        for head in range(2):
            there = partner_place(where_ref, 2 * (where_ref[NEAR] ^ at) + head)
            lanes = pl.ds(pl.multiple_of(there * HEAD_DIM, HEAD_DIM), HEAD_DIM)
            held_ref[:, lanes] = block[:, head * HEAD_DIM : (head + 1) * HEAD_DIM]

    @pl.when(pl.program_id(0) == 0)
    def arrange():
        put(0, own[...])
        put(2, far[...])
        put(1, from_next(where_ref, up, down))
        put(3, jnp.zeros((rows, feat), jnp.bfloat16))

    block = jnp.concatenate(
        [from_next(where_ref, *mine[:2]), from_last(where_ref, *mine)], axis=1
    )
    weight = jnp.concatenate([near_ref[...], last_ref[...]], axis=0)
    acc = acc_ref[...]
    acc += jnp.dot(block, weight, preferred_element_type=jnp.float32)
    acc += jnp.dot(held_ref[:, :cut], fetched_ref[...], preferred_element_type=jnp.float32)
    acc += jnp.dot(held_ref[:, cut:], passed_ref[...], preferred_element_type=jnp.float32)
    out_ref[...] = acc


def first_product(where, mine, partner, acc, weights):
    rows, feat = mine[0].shape
    own, fetched, passed = weights
    wide = own.shape[1] // 2
    whole = pl.BlockSpec((rows, wide), lambda i, w: (0, i))
    return call(
        first_kernel,
        "first",
        jax.ShapeDtypeStruct(acc.shape, jnp.float32),
        2,
        [spec((rows, feat))] * 7
        + [whole]
        + [pl.BlockSpec((feat, wide), lambda i, w, at=at: (w[NEAR] ^ at, i)) for at in (1, 3)]
        + [pl.BlockSpec((x.shape[0], wide), lambda i, w: (0, i)) for x in (fetched, passed)],
        whole,
        [pltpu.VMEM((rows, 4 * feat), jnp.bfloat16)],
    )(where, *mine, *partner, acc, own, own, fetched, passed)


def second_kernel(where_ref, *refs):
    slots, refs = refs[:3], refs[3:]
    fetched_ref, passed_ref, acc_in, keep_ref, send_ref, acc_ref = refs
    weight = []
    for head in range(2):
        place = partner_place(where_ref, 2 * (where_ref[NEAR] ^ 3) + head)
        here = jnp.minimum(place, FETCHED - 1) * HEAD_DIM
        there = jnp.maximum(place - FETCHED, 0) * HEAD_DIM
        weight.append(
            jnp.where(
                place < FETCHED,
                fetched_ref[pl.ds(pl.multiple_of(here, HEAD_DIM), HEAD_DIM), :],
                passed_ref[pl.ds(pl.multiple_of(there, HEAD_DIM), HEAD_DIM), :],
            )
        )
    acc = acc_in[...] + jnp.dot(
        from_last(where_ref, *slots), jnp.concatenate(weight, axis=0), preferred_element_type=jnp.float32
    )
    acc_ref[...] = acc.reshape(acc_ref.shape)
    for sub, out in enumerate((keep_ref, send_ref)):
        for at in range(4):
            out[at] = acc_ref[where_ref[NEAR] ^ at, where_ref[SUB] ^ sub].astype(jnp.bfloat16)


def second_product(where, chunk, slots, weights, acc):
    rows, feat = slots[0].shape
    cols = weights[0].shape[1]
    wide = cols // 2
    out = jax.ShapeDtypeStruct((4, rows // 8, wide), jnp.bfloat16)
    return call(
        second_kernel,
        "second",
        [out] * 2,
        1,
        [spec((rows, feat))] * 3
        + [pl.BlockSpec((x.shape[0], wide), lambda i, w: (0, chunk)) for x in weights]
        + [pl.BlockSpec((rows, wide), lambda i, w: (0, chunk))],
        [spec(out.shape)] * 2,
        [pltpu.VMEM((4, 2, rows // 8, wide), jnp.float32)],
    )(where, *slots, *weights, acc)


def add_kernel(where_ref, keep_ref, term_ref, *outs):
    for at, out in enumerate(outs):
        total = keep_ref[at].astype(jnp.float32) + term_ref[at].astype(jnp.float32)
        out[...] = total.astype(jnp.bfloat16)


def add(where, keep, term):
    return call(
        add_kernel,
        "add",
        [jax.ShapeDtypeStruct(keep.shape[1:], jnp.bfloat16)] * keep.shape[0],
        1,
        [spec(keep.shape)] * 2,
        [spec(keep.shape[1:])] * keep.shape[0],
    )(where, keep, term)


def take_kernel(where_ref, weight_ref, out_ref):
    out_ref[...] = weight_ref[...]


def take_half(where, weight):
    rows, cols = weight.shape[0] // 2, weight.shape[1]
    return call(
        take_kernel,
        "take",
        jax.ShapeDtypeStruct((rows, cols), weight.dtype),
        2,
        [pl.BlockSpec((rows // 2, cols), lambda i, w: (2 * w[GRP] + i, 0))],
        pl.BlockSpec((rows // 2, cols), lambda i, w: (i, 0)),
    )(where, weight)


def share_tail(sizes, where, pieces, kv_pieces, out_weight, hidden_in, attn_gate):
    out_weight, where = lax.optimization_barrier((out_weight, where))
    fetched = swap(take_half(where, out_weight), "head", 2, 1)
    own, fetched = lax.optimization_barrier((pieces[0], fetched))
    pieces = [own, *pieces[1:]]
    passed = swap(fetched, "grp", 2, 1)

    pieces = [pieces[0], *pieces[:0:-1]]
    mine = attend_half(where, 0, pieces)
    where, mine = lax.optimization_barrier((where, mine))
    other = swap(attend_half(where, 1, pieces), "head", 2, 1)
    acc = add_product(where, {0: mine}, out_weight)
    other, acc = lax.optimization_barrier((other, acc))
    slots = []
    for at, x in enumerate((mine, other)):
        down = lax.ppermute(x, "patch", [(1, 0), (2, 1), (3, 2)])
        up = lax.ppermute(x, "patch", [(0, 1), (1, 2), (2, 3)])
        far = swap(x, "patch", 4, 2)
        down, up, far, other, x = lax.optimization_barrier((down, up, far, other, x))
        if at == 1:
            acc = add_product(where, {2: slots[0][1]}, out_weight, acc)
            far, x, acc = lax.optimization_barrier((far, x, acc))
        ends = lax.ppermute(far, "patch", [(1, 0), (2, 3)])
        slots.append([x, far, up, down, ends])
    weights = [out_weight, fetched, passed]
    acc = first_product(where, slots[0][2:], slots[1][:4], acc, weights)
    terms = [second_product(where, at, slots[1][2:], [fetched, passed], acc) for at in range(2)]
    blocks = []
    for keep, send in terms:
        total = add(where, keep, swap(send, "sub", 2, 1))
        blocks.append([total[0]] + [swap(total[rel], "patch", 4, rel) for rel in range(3, 0, -1)])
    return mix_columns(where, hidden_in, attn_gate, blocks)


def mix_columns_kernel(where_ref, hidden_ref, gate_ref, *refs):
    blocks, out_ref = refs[:-1], refs[-1]
    cols = blocks[0].shape[1]
    for chunk in range(2):
        for at, rel in enumerate((0, 3, 2, 1)):
            start = (2 * (where_ref[PATCH] ^ rel) + chunk) * cols
            lanes = pl.ds(pl.multiple_of(start, HEAD_DIM), cols)
            mixed = hidden_ref[:, lanes].astype(jnp.float32) + gate_ref[:, lanes] * blocks[
                4 * chunk + at
            ][...].astype(jnp.float32)
            out_ref[:, lanes] = mixed.astype(jnp.bfloat16)


def mix_columns(where, hidden_in, attn_gate, blocks):
    rows, width = hidden_in.shape
    flat = [x for chunk in blocks for x in chunk]
    return call(
        mix_columns_kernel,
        "mix",
        jax.ShapeDtypeStruct((rows, width), jnp.bfloat16),
        2,
        [pl.BlockSpec((rows // 2, width), lambda i, w: (i, 0)), spec((1, width))]
        + [pl.BlockSpec((rows // 2, flat[0].shape[1]), lambda i, w: (i, 0))] * len(flat),
        pl.BlockSpec((rows // 2, width), lambda i, w: (i, 0)),
    )(where, hidden_in, attn_gate[None], *flat)


def body(sizes, queries, fresh_kv, cached_kv, exponents, out_weight, hidden_in, attn_gate):
    n_patch, n_head, n_sub = sizes["patch"], sizes["head"], sizes["sub"]
    tok, channels = queries.shape
    heads = channels // HEAD_DIM
    split = math.gcd(heads, n_patch)
    patch_at = lax.axis_index("patch")
    inner = (patch_at > 0) & (patch_at < n_patch - 1)
    where = jnp.stack(
        [
            patch_at,
            patch_at % split,
            lax.axis_index("head"),
            lax.axis_index("sub"),
            inner,
            lax.axis_index("grp"),
        ]
    ).astype(jnp.int32)

    arrays = (exponents, queries, fresh_kv, cached_kv)
    sent = pack(split, *arrays)
    far_first = [
        swap(x, "patch", n_patch, split - 1 - at) for at, x in enumerate(sent)
    ]
    where, sent = lax.optimization_barrier((where, sent))
    pieces = [pack_own(split, where, *arrays), *far_first]
    kv_pieces = list(pieces)
    for rel in range(split, n_patch, split):
        kv_pieces += [swap(x, "patch", n_patch, rel) for x in pieces]

    tail = (sizes, where, pieces, kv_pieces, out_weight, hidden_in, attn_gate)
    if (sizes["grp"], n_head, split, n_patch) == (2, 2, 4, 4):
        return share_tail(*tail)
    return sum_tail(*tail)


def solution(mesh):
    in_specs = (
        P(("grp", "patch"), ("head", "sub")),
        P(None, ("grp", "patch"), ("head", "sub")),
        P(None, "grp", ("head", "sub")),
        P(None, ("grp", "patch"), ("head", "sub")),
        P(("head", "sub"), "patch"),
        P(("grp", "patch", "head", "sub"), None),
        P(),
    )
    out_specs = P(("grp", "patch", "head", "sub"), None)
    return jax.shard_map(
        functools.partial(body, dict(mesh.shape)),
        mesh=mesh,
        in_specs=in_specs,
        out_specs=out_specs,
        check_vma=False,
    )
```

```python
import functools
import math

import jax
import jax.numpy as jnp
from jax import lax
from jax.experimental import pallas as pl
from jax.experimental.pallas import tpu as pltpu
from jax.sharding import PartitionSpec as P

HEAD_DIM = 128
SCALE_ROWS = 128
SATURATION = 448.0
PACK_ROWS = 64
VMEM_BYTES = 32 * 1024 * 1024
PACK_VMEM_BYTES = 60 * 1024 * 1024
ATTEND_FLOPS = 1
PROJECT_FLOPS = 1
OWN_FLOPS = 1
FETCHED = 4
ZERO_FLOPS = 6_000_000_000
HALF_FLOPS = 1

PATCH, NEAR, HEAD, SUB, INNER, GRP = range(6)


def spec(shape):
    return pl.BlockSpec(shape, lambda i, w: (0,) * len(shape))


def call(kernel, name, out_shape, grid, in_specs, out_specs, scratch=(), flops=1, vmem=VMEM_BYTES):
    return pl.pallas_call(
        kernel,
        out_shape=out_shape,
        grid_spec=pltpu.PrefetchScalarGridSpec(
            num_scalar_prefetch=1,
            grid=(grid,),
            in_specs=in_specs,
            out_specs=out_specs,
            scratch_shapes=list(scratch),
        ),
        compiler_params=pltpu.CompilerParams(vmem_limit_bytes=vmem),
        cost_estimate=pl.CostEstimate(flops=flops, bytes_accessed=0, transcendentals=0),
        name=name,
    )


def swap(x, axes, count, mask, only=None):
    pairs = [(at, at ^ mask) for at in range(count) if only is None or at in only]
    return lax.ppermute(x, axes, pairs)


def decode(fresh, cached, exponent):
    power = jnp.full((1, HEAD_DIM), exponent.astype(jnp.float32))
    cached = cached.astype(jnp.float32)
    residual = fresh.astype(jnp.float32) - cached
    codes = jnp.clip(residual * jnp.exp2(-power), -SATURATION, SATURATION).astype(jnp.bfloat16)
    return (cached + codes.astype(jnp.float32) * jnp.exp2(power)).astype(jnp.bfloat16)


def pack_kernel(split, per, exps_ref, q_ref, fresh_ref, cached_ref, *refs):
    outs, bufs = refs[: split - 1], refs[split - 1 : 2 * split - 2]
    q_buf, fresh_buf, cached_buf, sems, out_sems = refs[2 * split - 2 :]
    patch = lax.axis_index("patch")
    near = lax.rem(patch, split)
    tok = q_buf.shape[0]
    copies, sent = [], []
    for block in range(tok // PACK_ROWS):
        rows = pl.ds(block * PACK_ROWS, PACK_ROWS)
        there = pl.ds(pl.multiple_of(patch * tok + block * PACK_ROWS, PACK_ROWS), PACK_ROWS)
        copies.append(
            [
                pltpu.make_async_copy(q_ref.at[rows], q_buf.at[rows], sems.at[block, 0]),
                pltpu.make_async_copy(fresh_ref.at[:, rows], fresh_buf.at[:, rows], sems.at[block, 1]),
                pltpu.make_async_copy(cached_ref.at[:, there], cached_buf.at[:, rows], sems.at[block, 2]),
            ]
        )
        for copy in copies[-1]:
            copy.start()
    for block in range(tok // PACK_ROWS):
        rows = pl.ds(block * PACK_ROWS, PACK_ROWS)
        for copy in copies[block]:
            copy.wait()
        for rel in range(split - 1, 0, -1):
            buf = bufs[split - 1 - rel]
            for chunk in range(per):
                head = (near ^ rel) * per + chunk
                lanes = pl.ds(pl.multiple_of(head * HEAD_DIM, HEAD_DIM), HEAD_DIM)
                here = pl.ds(chunk * HEAD_DIM, HEAD_DIM)
                buf[0, rows, here] = q_buf[rows, lanes]
                for stacked in range(2):
                    buf[1 + stacked, rows, here] = decode(
                        fresh_buf[stacked, rows, lanes],
                        cached_buf[stacked, rows, lanes],
                        exps_ref[stacked, block * PACK_ROWS // SCALE_ROWS, head],
                    )
            sent.append(
                pltpu.make_async_copy(
                    buf.at[:, rows],
                    outs[split - 1 - rel].at[:, rows],
                    out_sems.at[block, rel - 1],
                )
            )
            sent[-1].start()
    for copy in sent:
        copy.wait()


def pack(split, exponents, queries, fresh_kv, cached_kv):
    tok, channels = queries.shape
    feat = channels // split
    blocks = tok // PACK_ROWS
    hbm = pl.BlockSpec(memory_space=pltpu.HBM)
    return pl.pallas_call(
        functools.partial(pack_kernel, split, feat // HEAD_DIM),
        out_shape=[jax.ShapeDtypeStruct((3, tok, feat), jnp.bfloat16)] * (split - 1),
        in_specs=[pl.BlockSpec(memory_space=pltpu.SMEM), hbm, hbm, hbm],
        out_specs=[hbm] * (split - 1),
        scratch_shapes=[pltpu.VMEM((3, tok, feat), jnp.bfloat16)] * (split - 1)
        + [
            pltpu.VMEM((tok, channels), jnp.bfloat16),
            pltpu.VMEM((2, tok, channels), jnp.bfloat16),
            pltpu.VMEM((2, tok, channels), jnp.bfloat16),
            pltpu.SemaphoreType.DMA((blocks, 3)),
            pltpu.SemaphoreType.DMA((blocks, split - 1)),
        ],
        compiler_params=pltpu.CompilerParams(vmem_limit_bytes=PACK_VMEM_BYTES),
        name="pack",
    )(exponents, queries, fresh_kv, cached_kv)


def own_kernel(per, where_ref, exps_ref, q_ref, fresh_ref, cached_ref, out_ref):
    out_ref[0] = q_ref[...]
    for chunk in range(per):
        lanes = pl.ds(chunk * HEAD_DIM, HEAD_DIM)
        for block in range(q_ref.shape[0] // SCALE_ROWS):
            rows = pl.ds(block * SCALE_ROWS, SCALE_ROWS)
            for stacked in range(2):
                out_ref[1 + stacked, rows, lanes] = decode(
                    fresh_ref[stacked, rows, lanes],
                    cached_ref[stacked, rows, lanes],
                    exps_ref[stacked, block, where_ref[NEAR] * per + chunk],
                )


def pack_own(split, where, exponents, queries, fresh_kv, cached_kv):
    tok, channels = queries.shape
    feat = channels // split
    out = jax.ShapeDtypeStruct((3, tok, feat), jnp.bfloat16)
    return call(
        functools.partial(own_kernel, feat // HEAD_DIM),
        "own",
        out,
        1,
        [
            pl.BlockSpec(memory_space=pltpu.SMEM),
            pl.BlockSpec((tok, feat), lambda i, w: (0, w[NEAR])),
            pl.BlockSpec((2, tok, feat), lambda i, w: (0, 0, w[NEAR])),
            pl.BlockSpec((2, tok, feat), lambda i, w: (0, w[PATCH], w[NEAR])),
        ],
        spec(out.shape),
    )(where, exponents, queries, fresh_kv, cached_kv)


def attend_kernel(split, part, where_ref, *refs):
    q_refs, kv_refs, out_ref = (refs[0], *refs[split - 1 : 0 : -1]), refs[:-1], refs[-1]
    factor = HEAD_DIM**-0.5 * math.log2(math.e)
    tok, feat = q_refs[0].shape[1:]
    count = out_ref.shape[1] // part[1]
    starts = [at * (tok // count) + part[0] for at in range(count)]
    for head in range(feat // HEAD_DIM):
        lanes = pl.ds(head * HEAD_DIM, HEAD_DIM)
        keys = jnp.concatenate([ref[1, :, lanes] for ref in kv_refs], axis=0)
        values = jnp.concatenate([ref[2, :, lanes] for ref in kv_refs], axis=0)
        values = jnp.concatenate([values, jnp.ones_like(values)], axis=1)
        for rel in range(split):
            rows = [q_refs[rel][0, start : start + part[1], lanes] for start in starts]
            query = jnp.concatenate(rows, axis=0) if len(rows) > 1 else rows[0]
            scores = lax.dot_general(
                query, keys, (((1,), (1,)), ((), ())), preferred_element_type=jnp.float32
            )
            peak = jnp.max(scores, axis=1, keepdims=True)
            expo = jnp.exp2((scores - peak) * factor).astype(jnp.bfloat16)
            mix = jnp.dot(expo, values, preferred_element_type=jnp.float32)
            mix = mix[:, :HEAD_DIM] / mix[:, HEAD_DIM:]
            out_ref[where_ref[NEAR] ^ rel, :, lanes] = mix.astype(jnp.bfloat16)


def attend(where, part, count, pieces, kv_pieces):
    split = len(pieces)
    _, tok, feat = pieces[0].shape
    out = jax.ShapeDtypeStruct((split, count * part[1], feat), jnp.bfloat16)
    return call(
        functools.partial(attend_kernel, split, part),
        "attend",
        out,
        1,
        [spec((3, tok, feat))] * len(kv_pieces),
        spec(out.shape),
        flops=ATTEND_FLOPS,
    )(where, *kv_pieces)


def project_kernel(split, n_slots, n_more, where_ref, *refs):
    slots, refs = refs[:n_slots], refs[n_slots:]
    more, weight_ref, refs = refs[:n_more], refs[n_more], refs[n_more + 1 :]
    outs, held_ref, acc_ref = refs[:-2], refs[-2], refs[-1]
    rows, feat = slots[0].shape
    n_sub, n_head = acc_ref.shape[3], acc_ref.shape[2]

    @pl.when(pl.program_id(0) == 0)
    def arrange():
        for at, slot in enumerate(slots):
            group, near = divmod(at, split)
            lane = (where_ref[NEAR] ^ near) * feat
            block = slot[...]
            if more and at == n_slots - 1:
                block = jnp.where(where_ref[INNER] == 1, block, more[0][...])
            held_ref[
                group * rows : (group + 1) * rows, pl.ds(pl.multiple_of(lane, HEAD_DIM), feat)
            ] = block

    acc = jnp.dot(held_ref[...], weight_ref[...], preferred_element_type=jnp.float32)
    acc_ref[...] = acc.reshape(acc_ref.shape)
    for sub in range(n_sub):
        for head in range(n_head):
            for at in range(n_slots):
                group, near = divmod(at, split)
                outs[sub][head, at] = acc_ref[
                    group, where_ref[NEAR] ^ near, where_ref[HEAD] ^ head, where_ref[SUB] ^ sub
                ].astype(jnp.bfloat16)


def project(split, where, slots, more, weight, n_head, n_sub):
    rows, feat = slots[0].shape
    n_patch = len(slots)
    total = rows * n_patch // split
    depth, cols = weight.shape
    wide = 640 if cols % 640 == 0 else cols
    piece = rows // (split * n_head * n_sub)
    return call(
        functools.partial(project_kernel, split, n_patch, len(more)),
        "project",
        [jax.ShapeDtypeStruct((n_head, n_patch, piece, cols), jnp.bfloat16)] * n_sub,
        cols // wide,
        [spec((rows, feat))] * (n_patch + len(more))
        + [pl.BlockSpec((depth, wide), lambda i, w: (0, i))],
        [pl.BlockSpec((n_head, n_patch, piece, wide), lambda i, w: (0, 0, 0, i))] * n_sub,
        [
            pltpu.VMEM((total, depth), jnp.bfloat16),
            pltpu.VMEM((n_patch // split, split, n_head, n_sub, piece, wide), jnp.float32),
        ],
        flops=PROJECT_FLOPS,
    )(where, *slots, *more, weight)


def mix_kernel(rels, where_ref, hidden_ref, gate_ref, *refs):
    blocks, out_ref = refs[:-1], refs[-1]
    piece, cols = blocks[0].shape
    for part in range(len(blocks) // len(rels)):
        rows = pl.ds(part * piece, piece)
        for at, rel in enumerate(rels):
            lanes = pl.ds(pl.multiple_of((where_ref[PATCH] ^ rel) * cols, HEAD_DIM), cols)
            mixed = hidden_ref[rows, lanes].astype(jnp.float32) + gate_ref[:, lanes] * blocks[
                part * len(rels) + at
            ][...].astype(jnp.float32)
            out_ref[rows, lanes] = mixed.astype(jnp.bfloat16)


def mix(where, hidden_in, attn_gate, blocks):
    rows, width = hidden_in.shape
    n_patch = len(blocks[0])
    piece, cols = blocks[0][0].shape
    if cols % HEAD_DIM:
        order = jnp.concatenate([jnp.stack(x) for x in blocks], axis=1)
        order = order[where[PATCH] ^ jnp.arange(n_patch)]
        projected = order.transpose(1, 0, 2).reshape(rows, width).astype(jnp.float32)
        return (hidden_in.astype(jnp.float32) + attn_gate * projected).astype(jnp.bfloat16)
    rels = [0, *range(n_patch - 1, 0, -1)]
    flat = [part[rel] for part in blocks for rel in rels]
    return call(
        functools.partial(mix_kernel, rels),
        "mix",
        jax.ShapeDtypeStruct((rows, width), jnp.bfloat16),
        1,
        [spec((rows, width)), spec((1, width))] + [spec((piece, cols))] * len(flat),
        spec((rows, width)),
    )(where, hidden_in, attn_gate[None], *flat)


def gather(parts, n_patch):
    if n_patch != 4:
        return [
            ([x] + [swap(x, "patch", n_patch, rel) for rel in range(1, n_patch)], [])
            for x in parts
        ]
    far = [swap(x, "patch", 4, 2) for x in parts]
    next_to = [swap(x, "patch", 4, 1) for x in parts]
    out = []
    for at, x in enumerate(parts):
        far[at], next_to[at], parts = lax.optimization_barrier((far[at], next_to[at], parts))
        middle = swap(parts[at], "patch", 4, 3, (1, 2))
        ends = lax.ppermute(far[at], "patch", [(1, 0), (2, 3)])
        if at + 1 < len(parts):
            ends, far[at + 1], next_to[at + 1] = lax.optimization_barrier(
                (ends, far[at + 1], next_to[at + 1])
            )
        out.append(([x, next_to[at], far[at], middle], [ends]))
    return out


def add_sub_kernel(n_sub, where_ref, *refs):
    terms, kept_ref, outs = refs[:n_sub], refs[n_sub], refs[n_sub + 1 :]
    for head in range(len(outs) + 1):
        total = terms[0][head].astype(jnp.float32)
        for term in terms[1:]:
            total += term[head].astype(jnp.float32)
        if head == 0:
            kept_ref[...] = total
        else:
            outs[head - 1][...] = total.astype(jnp.bfloat16)


def add_head_kernel(n_more, where_ref, kept_ref, *refs):
    for at, out in enumerate(refs[n_more:]):
        total = kept_ref[at]
        for term in refs[:n_more]:
            total += term[at].astype(jnp.float32)
        out[...] = total.astype(jnp.bfloat16)


def reduce_sub(sizes, where, terms):
    n_sub, n_head = sizes["sub"], sizes["head"]
    terms = [terms[0]] + [swap(terms[rel], "sub", n_sub, rel) for rel in range(1, n_sub)]
    shape = terms[0].shape[1:]
    return call(
        functools.partial(add_sub_kernel, n_sub),
        "add_sub",
        [jax.ShapeDtypeStruct(shape, jnp.float32)]
        + [jax.ShapeDtypeStruct(shape, jnp.bfloat16)] * (n_head - 1),
        1,
        [spec(terms[0].shape)] * n_sub,
        [spec(shape)] * n_head,
    )(where, *terms)


def reduce_head(sizes, where, sums):
    n_head = sizes["head"]
    shape = sums[0].shape
    sums = [sums[0]] + [swap(sums[rel], "head", n_head, rel) for rel in range(1, n_head)]
    return call(
        functools.partial(add_head_kernel, n_head - 1),
        "add_head",
        [jax.ShapeDtypeStruct(shape[1:], jnp.bfloat16)] * shape[0],
        1,
        [spec(shape)] * n_head,
        [spec(shape[1:])] * shape[0],
    )(where, *sums)


def sum_tail(sizes, where, pieces, kv_pieces, out_weight, hidden_in, attn_gate):
    n_patch, n_head, n_sub = sizes["patch"], sizes["head"], sizes["sub"]
    split, tok = len(pieces), pieces[0].shape[1]
    count = n_head * n_sub
    piece = tok // count
    parts = 2 if piece % 32 == 0 else 1
    attended = []
    for part in range(parts):
        rows = (part * (piece // parts), piece // parts)
        x = attend(where, rows, count, pieces, kv_pieces)
        attended.append(x.reshape(-1, x.shape[2]))
    slots = gather(attended, n_patch)
    blocks = []
    for part in range(parts):
        terms = project(split, where, *slots[part], out_weight, n_head, n_sub)
        total = reduce_head(sizes, where, reduce_sub(sizes, where, terms))
        blocks.append(
            [total[0]] + [swap(total[rel], "patch", n_patch, rel) for rel in range(1, n_patch)]
        )
    return mix(where, hidden_in, attn_gate, blocks)


def attend_half_kernel(half, where_ref, *refs):
    pieces, out = refs[:-1], refs[-1]
    factor = HEAD_DIM**-0.5 * math.log2(math.e)
    rows, feat = out.shape[1:]
    start = pl.multiple_of((where_ref[HEAD] ^ half) * rows, rows)
    for head in range(feat // HEAD_DIM):
        lanes = pl.ds(head * HEAD_DIM, HEAD_DIM)
        keys = jnp.concatenate([ref[1, :, lanes] for ref in pieces], axis=0)
        values = jnp.concatenate([ref[2, :, lanes] for ref in pieces], axis=0)
        values = jnp.concatenate([values, jnp.ones_like(values)], axis=1)
        for first in range(0, len(pieces), 2):
            query = [ref[0, pl.ds(start, rows), lanes] for ref in pieces[first : first + 2]]
            scores = lax.dot_general(
                jnp.concatenate(query, axis=0),
                keys,
                (((1,), (1,)), ((), ())),
                preferred_element_type=jnp.float32,
            )
            peak = jnp.max(scores, axis=1, keepdims=True)
            expo = jnp.exp2((scores - peak) * factor).astype(jnp.bfloat16)
            mix = jnp.dot(expo, values, preferred_element_type=jnp.float32)
            mix = (mix[:, :HEAD_DIM] / mix[:, HEAD_DIM:]).astype(jnp.bfloat16)
            for at in range(len(query)):
                block = mix[at * rows : (at + 1) * rows]
                out[where_ref[NEAR] ^ (first + at), :, lanes] = block


def attend_half(where, half, pieces):
    _, tok, feat = pieces[0].shape
    out = jax.ShapeDtypeStruct((len(pieces), tok // 2, feat), jnp.bfloat16)
    return call(
        functools.partial(attend_half_kernel, half),
        "attend",
        out,
        1,
        [spec((3, tok, feat))] * len(pieces),
        spec(out.shape),
        flops=HALF_FLOPS,
    )(where, *pieces).reshape(-1, feat)


def add_product_kernel(count, where_ref, *refs):
    total = refs[2 * count][...] if len(refs) > 2 * count + 1 else None
    for slot, weight in zip(refs[:count], refs[count : 2 * count]):
        term = jnp.dot(slot[...], weight[...], preferred_element_type=jnp.float32)
        total = term if total is None else total + term
    refs[-1][...] = total


def add_product(where, slots, weight, acc=None):
    rows, feat = next(iter(slots.values())).shape
    cols = weight.shape[1]
    wide = cols // 2
    whole = pl.BlockSpec((rows, wide), lambda i, w: (0, i))
    rels = list(slots)
    return call(
        functools.partial(add_product_kernel, len(rels)),
        "products",
        jax.ShapeDtypeStruct((rows, cols), jnp.float32),
        2,
        [spec((rows, feat))] * len(rels)
        + [pl.BlockSpec((feat, wide), lambda i, w, rel=rel: (w[NEAR] ^ rel, i)) for rel in rels]
        + ([] if acc is None else [whole]),
        whole,
        flops=ZERO_FLOPS if acc is None else 1,
    )(where, *slots.values(), *[weight] * len(rels), *([] if acc is None else [acc]))


def partner_place(where_ref, head):
    return (head + FETCHED * where_ref[GRP]) % 8


def first_kernel(where_ref, *refs):
    last, more, slots = refs[0], refs[1], refs[2:5]
    acc_ref, own_ref, fetched_ref, passed_ref, out_ref, held_ref = refs[5:]
    rows, feat = last.shape
    cut = fetched_ref.shape[0]

    def put(at, block):
        for head in range(2):
            there = partner_place(where_ref, 2 * (where_ref[NEAR] ^ at) + head)
            lanes = pl.ds(pl.multiple_of(there * HEAD_DIM, HEAD_DIM), HEAD_DIM)
            held_ref[:, lanes] = block[:, head * HEAD_DIM : (head + 1) * HEAD_DIM]

    @pl.when(pl.program_id(0) == 0)
    def arrange():
        for at, slot in zip((0, 2, 1), slots):
            put(at, slot[...])
        put(3, jnp.zeros((rows, feat), jnp.bfloat16))

    block = jnp.where(where_ref[INNER] == 1, last[...], more[...])
    acc = acc_ref[...]
    acc += jnp.dot(block, own_ref[...], preferred_element_type=jnp.float32)
    acc += jnp.dot(held_ref[:, :cut], fetched_ref[...], preferred_element_type=jnp.float32)
    acc += jnp.dot(held_ref[:, cut:], passed_ref[...], preferred_element_type=jnp.float32)
    out_ref[...] = acc


def first_product(where, last, more, slots, acc, weights):
    rows, feat = last.shape
    own, fetched, passed = weights
    wide = own.shape[1] // 2
    whole = pl.BlockSpec((rows, wide), lambda i, w: (0, i))
    return call(
        first_kernel,
        "first",
        jax.ShapeDtypeStruct(acc.shape, jnp.float32),
        2,
        [spec((rows, feat))] * 5
        + [whole, pl.BlockSpec((feat, wide), lambda i, w: (w[NEAR] ^ 3, i))]
        + [pl.BlockSpec((x.shape[0], wide), lambda i, w: (0, i)) for x in (fetched, passed)],
        whole,
        [pltpu.VMEM((rows, 4 * feat), jnp.bfloat16)],
    )(where, last, more, *slots, acc, own, fetched, passed)


def second_kernel(where_ref, slot, more, fetched_ref, passed_ref, acc_in, keep_ref, send_ref, acc_ref):
    weight = []
    for head in range(2):
        place = partner_place(where_ref, 2 * (where_ref[NEAR] ^ 3) + head)
        here = jnp.minimum(place, FETCHED - 1) * HEAD_DIM
        there = jnp.maximum(place - FETCHED, 0) * HEAD_DIM
        weight.append(
            jnp.where(
                place < FETCHED,
                fetched_ref[pl.ds(pl.multiple_of(here, HEAD_DIM), HEAD_DIM), :],
                passed_ref[pl.ds(pl.multiple_of(there, HEAD_DIM), HEAD_DIM), :],
            )
        )
    block = jnp.where(where_ref[INNER] == 1, slot[...], more[...])
    acc = acc_in[...] + jnp.dot(
        block, jnp.concatenate(weight, axis=0), preferred_element_type=jnp.float32
    )
    acc_ref[...] = acc.reshape(acc_ref.shape)
    for sub, out in enumerate((keep_ref, send_ref)):
        for at in range(4):
            out[at] = acc_ref[where_ref[NEAR] ^ at, where_ref[SUB] ^ sub].astype(jnp.bfloat16)


def second_product(where, chunk, slot, more, weights, acc):
    rows, feat = slot.shape
    cols = weights[0].shape[1]
    wide = cols // 2
    out = jax.ShapeDtypeStruct((4, rows // 8, wide), jnp.bfloat16)
    return call(
        second_kernel,
        "second",
        [out] * 2,
        1,
        [spec((rows, feat))] * 2
        + [pl.BlockSpec((x.shape[0], wide), lambda i, w: (0, chunk)) for x in weights]
        + [pl.BlockSpec((rows, wide), lambda i, w: (0, chunk))],
        [spec(out.shape)] * 2,
        [pltpu.VMEM((4, 2, rows // 8, wide), jnp.float32)],
    )(where, slot, more, *weights, acc)


def add_kernel(where_ref, keep_ref, term_ref, *outs):
    for at, out in enumerate(outs):
        total = keep_ref[at].astype(jnp.float32) + term_ref[at].astype(jnp.float32)
        out[...] = total.astype(jnp.bfloat16)


def add(where, keep, term):
    return call(
        add_kernel,
        "add",
        [jax.ShapeDtypeStruct(keep.shape[1:], jnp.bfloat16)] * keep.shape[0],
        1,
        [spec(keep.shape)] * 2,
        [spec(keep.shape[1:])] * keep.shape[0],
    )(where, keep, term)


def take_kernel(where_ref, weight_ref, out_ref):
    out_ref[...] = weight_ref[...]


def take_half(where, weight):
    rows, cols = weight.shape[0] // 2, weight.shape[1]
    return call(
        take_kernel,
        "take",
        jax.ShapeDtypeStruct((rows, cols), weight.dtype),
        2,
        [pl.BlockSpec((rows // 2, cols), lambda i, w: (2 * w[GRP] + i, 0))],
        pl.BlockSpec((rows // 2, cols), lambda i, w: (i, 0)),
    )(where, weight)


def share_tail(sizes, where, pieces, kv_pieces, out_weight, hidden_in, attn_gate):
    out_weight, where = lax.optimization_barrier((out_weight, where))
    fetched = swap(take_half(where, out_weight), "head", 2, 1)
    own, fetched = lax.optimization_barrier((pieces[0], fetched))
    pieces = [own, *pieces[1:]]
    passed = swap(fetched, "grp", 2, 1)

    pieces = [pieces[0], *pieces[:0:-1]]
    mine = attend_half(where, 0, pieces)
    where, mine = lax.optimization_barrier((where, mine))
    other = swap(attend_half(where, 1, pieces), "head", 2, 1)
    acc = add_product(where, {0: mine}, out_weight)
    other, acc = lax.optimization_barrier((other, acc))
    slots = []
    for at, x in enumerate((mine, other)):
        next_to, far = swap(x, "patch", 4, 1), swap(x, "patch", 4, 2)
        next_to, far, other, x = lax.optimization_barrier((next_to, far, other, x))
        if at == 1:
            acc = add_product(where, {2: slots[0][2], 1: slots[0][1]}, out_weight, acc)
            far, x, acc = lax.optimization_barrier((far, x, acc))
        middle = swap(x, "patch", 4, 3, (1, 2))
        ends = lax.ppermute(far, "patch", [(1, 0), (2, 3)])
        slots.append([x, next_to, far, middle, ends])
    weights = [out_weight, fetched, passed]
    partner = [slots[1][at] for at in (0, 2, 1)]
    acc = first_product(where, *slots[0][3:], partner, acc, weights)
    terms = [second_product(where, at, *slots[1][3:], [fetched, passed], acc) for at in range(2)]
    blocks = []
    for keep, send in terms:
        total = add(where, keep, swap(send, "sub", 2, 1))
        blocks.append([total[0]] + [swap(total[rel], "patch", 4, rel) for rel in range(3, 0, -1)])
    return mix_columns(where, hidden_in, attn_gate, blocks)


def mix_columns_kernel(where_ref, hidden_ref, gate_ref, *refs):
    blocks, out_ref = refs[:-1], refs[-1]
    cols = blocks[0].shape[1]
    for chunk in range(2):
        for at, rel in enumerate((0, 3, 2, 1)):
            start = (2 * (where_ref[PATCH] ^ rel) + chunk) * cols
            lanes = pl.ds(pl.multiple_of(start, HEAD_DIM), cols)
            mixed = hidden_ref[:, lanes].astype(jnp.float32) + gate_ref[:, lanes] * blocks[
                4 * chunk + at
            ][...].astype(jnp.float32)
            out_ref[:, lanes] = mixed.astype(jnp.bfloat16)


def mix_columns(where, hidden_in, attn_gate, blocks):
    rows, width = hidden_in.shape
    flat = [x for chunk in blocks for x in chunk]
    return call(
        mix_columns_kernel,
        "mix",
        jax.ShapeDtypeStruct((rows, width), jnp.bfloat16),
        2,
        [pl.BlockSpec((rows // 2, width), lambda i, w: (i, 0)), spec((1, width))]
        + [pl.BlockSpec((rows // 2, flat[0].shape[1]), lambda i, w: (i, 0))] * len(flat),
        pl.BlockSpec((rows // 2, width), lambda i, w: (i, 0)),
    )(where, hidden_in, attn_gate[None], *flat)


def body(sizes, queries, fresh_kv, cached_kv, exponents, out_weight, hidden_in, attn_gate):
    n_patch, n_head, n_sub = sizes["patch"], sizes["head"], sizes["sub"]
    tok, channels = queries.shape
    heads = channels // HEAD_DIM
    split = math.gcd(heads, n_patch)
    patch_at = lax.axis_index("patch")
    inner = (patch_at > 0) & (patch_at < n_patch - 1)
    where = jnp.stack(
        [
            patch_at,
            patch_at % split,
            lax.axis_index("head"),
            lax.axis_index("sub"),
            inner,
            lax.axis_index("grp"),
        ]
    ).astype(jnp.int32)

    arrays = (exponents, queries, fresh_kv, cached_kv)
    sent = pack(split, *arrays)
    far_first = [
        swap(x, "patch", n_patch, split - 1 - at) for at, x in enumerate(sent)
    ]
    where, sent = lax.optimization_barrier((where, sent))
    pieces = [pack_own(split, where, *arrays), *far_first]
    kv_pieces = list(pieces)
    for rel in range(split, n_patch, split):
        kv_pieces += [swap(x, "patch", n_patch, rel) for x in pieces]

    tail = (sizes, where, pieces, kv_pieces, out_weight, hidden_in, attn_gate)
    if (sizes["grp"], n_head, split, n_patch) == (2, 2, 4, 4):
        return share_tail(*tail)
    return sum_tail(*tail)


def solution(mesh):
    in_specs = (
        P(("grp", "patch"), ("head", "sub")),
        P(None, ("grp", "patch"), ("head", "sub")),
        P(None, "grp", ("head", "sub")),
        P(None, ("grp", "patch"), ("head", "sub")),
        P(("head", "sub"), "patch"),
        P(("grp", "patch", "head", "sub"), None),
        P(),
    )
    out_specs = P(("grp", "patch", "head", "sub"), None)
    return jax.shard_map(
        functools.partial(body, dict(mesh.shape)),
        mesh=mesh,
        in_specs=in_specs,
        out_specs=out_specs,
        check_vma=False,
    )
```

```python
import functools
import math

import jax
import jax.numpy as jnp
from jax import lax
from jax.experimental import pallas as pl
from jax.experimental.pallas import tpu as pltpu
from jax.sharding import PartitionSpec as P

HEAD_DIM = 128
SCALE_ROWS = 128
SATURATION = 448.0
PACK_ROWS = 64
VMEM_BYTES = 32 * 1024 * 1024
PACK_VMEM_BYTES = 60 * 1024 * 1024
ATTEND_FLOPS = 1
PROJECT_FLOPS = 1
OWN_FLOPS = 1
FETCHED = 4
ZERO_FLOPS = 6_000_000_000
HALF_FLOPS = 1

PATCH, NEAR, HEAD, SUB, INNER, GRP = range(6)


def spec(shape):
    return pl.BlockSpec(shape, lambda i, w: (0,) * len(shape))


def call(kernel, name, out_shape, grid, in_specs, out_specs, scratch=(), flops=1, vmem=VMEM_BYTES):
    return pl.pallas_call(
        kernel,
        out_shape=out_shape,
        grid_spec=pltpu.PrefetchScalarGridSpec(
            num_scalar_prefetch=1,
            grid=(grid,),
            in_specs=in_specs,
            out_specs=out_specs,
            scratch_shapes=list(scratch),
        ),
        compiler_params=pltpu.CompilerParams(vmem_limit_bytes=vmem),
        cost_estimate=pl.CostEstimate(flops=flops, bytes_accessed=0, transcendentals=0),
        name=name,
    )


def swap(x, axes, count, mask, only=None):
    pairs = [(at, at ^ mask) for at in range(count) if only is None or at in only]
    return lax.ppermute(x, axes, pairs)


def decode(fresh, cached, exponent):
    power = jnp.full((1, HEAD_DIM), exponent.astype(jnp.float32))
    cached = cached.astype(jnp.float32)
    residual = fresh.astype(jnp.float32) - cached
    codes = jnp.clip(residual * jnp.exp2(-power), -SATURATION, SATURATION).astype(jnp.bfloat16)
    return (cached + codes.astype(jnp.float32) * jnp.exp2(power)).astype(jnp.bfloat16)


def pack_kernel(split, per, exps_ref, q_ref, fresh_ref, cached_ref, *refs):
    outs, bufs = refs[: split - 1], refs[split - 1 : 2 * split - 2]
    q_buf, fresh_buf, cached_buf, sems, out_sems = refs[2 * split - 2 :]
    patch = lax.axis_index("patch")
    near = lax.rem(patch, split)
    tok = q_buf.shape[0]
    copies, sent = [], []
    for block in range(tok // PACK_ROWS):
        rows = pl.ds(block * PACK_ROWS, PACK_ROWS)
        there = pl.ds(pl.multiple_of(patch * tok + block * PACK_ROWS, PACK_ROWS), PACK_ROWS)
        copies.append(
            [
                pltpu.make_async_copy(q_ref.at[rows], q_buf.at[rows], sems.at[block, 0]),
                pltpu.make_async_copy(fresh_ref.at[:, rows], fresh_buf.at[:, rows], sems.at[block, 1]),
                pltpu.make_async_copy(cached_ref.at[:, there], cached_buf.at[:, rows], sems.at[block, 2]),
            ]
        )
        for copy in copies[-1]:
            copy.start()
    for block in range(tok // PACK_ROWS):
        rows = pl.ds(block * PACK_ROWS, PACK_ROWS)
        for copy in copies[block]:
            copy.wait()
        for rel in range(split - 1, 0, -1):
            buf = bufs[split - 1 - rel]
            for chunk in range(per):
                head = (near ^ rel) * per + chunk
                lanes = pl.ds(pl.multiple_of(head * HEAD_DIM, HEAD_DIM), HEAD_DIM)
                here = pl.ds(chunk * HEAD_DIM, HEAD_DIM)
                buf[0, rows, here] = q_buf[rows, lanes]
                for stacked in range(2):
                    buf[1 + stacked, rows, here] = decode(
                        fresh_buf[stacked, rows, lanes],
                        cached_buf[stacked, rows, lanes],
                        exps_ref[stacked, block * PACK_ROWS // SCALE_ROWS, head],
                    )
            sent.append(
                pltpu.make_async_copy(
                    buf.at[:, rows],
                    outs[split - 1 - rel].at[:, rows],
                    out_sems.at[block, rel - 1],
                )
            )
            sent[-1].start()
    for copy in sent:
        copy.wait()


def pack(split, exponents, queries, fresh_kv, cached_kv):
    tok, channels = queries.shape
    feat = channels // split
    blocks = tok // PACK_ROWS
    hbm = pl.BlockSpec(memory_space=pltpu.HBM)
    return pl.pallas_call(
        functools.partial(pack_kernel, split, feat // HEAD_DIM),
        out_shape=[jax.ShapeDtypeStruct((3, tok, feat), jnp.bfloat16)] * (split - 1),
        in_specs=[pl.BlockSpec(memory_space=pltpu.SMEM), hbm, hbm, hbm],
        out_specs=[hbm] * (split - 1),
        scratch_shapes=[pltpu.VMEM((3, tok, feat), jnp.bfloat16)] * (split - 1)
        + [
            pltpu.VMEM((tok, channels), jnp.bfloat16),
            pltpu.VMEM((2, tok, channels), jnp.bfloat16),
            pltpu.VMEM((2, tok, channels), jnp.bfloat16),
            pltpu.SemaphoreType.DMA((blocks, 3)),
            pltpu.SemaphoreType.DMA((blocks, split - 1)),
        ],
        compiler_params=pltpu.CompilerParams(vmem_limit_bytes=PACK_VMEM_BYTES),
        name="pack",
    )(exponents, queries, fresh_kv, cached_kv)


def own_kernel(per, where_ref, exps_ref, q_ref, fresh_ref, cached_ref, out_ref):
    out_ref[0] = q_ref[...]
    for chunk in range(per):
        lanes = pl.ds(chunk * HEAD_DIM, HEAD_DIM)
        for block in range(q_ref.shape[0] // SCALE_ROWS):
            rows = pl.ds(block * SCALE_ROWS, SCALE_ROWS)
            for stacked in range(2):
                out_ref[1 + stacked, rows, lanes] = decode(
                    fresh_ref[stacked, rows, lanes],
                    cached_ref[stacked, rows, lanes],
                    exps_ref[stacked, block, where_ref[NEAR] * per + chunk],
                )


def pack_own(split, where, exponents, queries, fresh_kv, cached_kv):
    tok, channels = queries.shape
    feat = channels // split
    out = jax.ShapeDtypeStruct((3, tok, feat), jnp.bfloat16)
    return call(
        functools.partial(own_kernel, feat // HEAD_DIM),
        "own",
        out,
        1,
        [
            pl.BlockSpec(memory_space=pltpu.SMEM),
            pl.BlockSpec((tok, feat), lambda i, w: (0, w[NEAR])),
            pl.BlockSpec((2, tok, feat), lambda i, w: (0, 0, w[NEAR])),
            pl.BlockSpec((2, tok, feat), lambda i, w: (0, w[PATCH], w[NEAR])),
        ],
        spec(out.shape),
    )(where, exponents, queries, fresh_kv, cached_kv)


def attend_kernel(split, part, where_ref, *refs):
    q_refs, kv_refs, out_ref = (refs[0], *refs[split - 1 : 0 : -1]), refs[:-1], refs[-1]
    factor = HEAD_DIM**-0.5 * math.log2(math.e)
    tok, feat = q_refs[0].shape[1:]
    count = out_ref.shape[1] // part[1]
    starts = [at * (tok // count) + part[0] for at in range(count)]
    for head in range(feat // HEAD_DIM):
        lanes = pl.ds(head * HEAD_DIM, HEAD_DIM)
        keys = jnp.concatenate([ref[1, :, lanes] for ref in kv_refs], axis=0)
        values = jnp.concatenate([ref[2, :, lanes] for ref in kv_refs], axis=0)
        values = jnp.concatenate([values, jnp.ones_like(values)], axis=1)
        for rel in range(split):
            rows = [q_refs[rel][0, start : start + part[1], lanes] for start in starts]
            query = jnp.concatenate(rows, axis=0) if len(rows) > 1 else rows[0]
            scores = lax.dot_general(
                query, keys, (((1,), (1,)), ((), ())), preferred_element_type=jnp.float32
            )
            peak = jnp.max(scores, axis=1, keepdims=True)
            expo = jnp.exp2((scores - peak) * factor).astype(jnp.bfloat16)
            mix = jnp.dot(expo, values, preferred_element_type=jnp.float32)
            mix = mix[:, :HEAD_DIM] / mix[:, HEAD_DIM:]
            out_ref[where_ref[NEAR] ^ rel, :, lanes] = mix.astype(jnp.bfloat16)


def attend(where, part, count, pieces, kv_pieces):
    split = len(pieces)
    _, tok, feat = pieces[0].shape
    out = jax.ShapeDtypeStruct((split, count * part[1], feat), jnp.bfloat16)
    return call(
        functools.partial(attend_kernel, split, part),
        "attend",
        out,
        1,
        [spec((3, tok, feat))] * len(kv_pieces),
        spec(out.shape),
        flops=ATTEND_FLOPS,
    )(where, *kv_pieces)


def project_kernel(split, n_slots, n_more, where_ref, *refs):
    slots, refs = refs[:n_slots], refs[n_slots:]
    more, weight_ref, refs = refs[:n_more], refs[n_more], refs[n_more + 1 :]
    outs, held_ref, acc_ref = refs[:-2], refs[-2], refs[-1]
    rows, feat = slots[0].shape
    n_sub, n_head = acc_ref.shape[3], acc_ref.shape[2]

    @pl.when(pl.program_id(0) == 0)
    def arrange():
        for at, slot in enumerate(slots):
            group, near = divmod(at, split)
            lane = (where_ref[NEAR] ^ near) * feat
            block = slot[...]
            if more and at == n_slots - 1:
                block = jnp.where(where_ref[INNER] == 1, block, more[0][...])
            held_ref[
                group * rows : (group + 1) * rows, pl.ds(pl.multiple_of(lane, HEAD_DIM), feat)
            ] = block

    acc = jnp.dot(held_ref[...], weight_ref[...], preferred_element_type=jnp.float32)
    acc_ref[...] = acc.reshape(acc_ref.shape)
    for sub in range(n_sub):
        for head in range(n_head):
            for at in range(n_slots):
                group, near = divmod(at, split)
                outs[sub][head, at] = acc_ref[
                    group, where_ref[NEAR] ^ near, where_ref[HEAD] ^ head, where_ref[SUB] ^ sub
                ].astype(jnp.bfloat16)


def project(split, where, slots, more, weight, n_head, n_sub):
    rows, feat = slots[0].shape
    n_patch = len(slots)
    total = rows * n_patch // split
    depth, cols = weight.shape
    wide = 640 if cols % 640 == 0 else cols
    piece = rows // (split * n_head * n_sub)
    return call(
        functools.partial(project_kernel, split, n_patch, len(more)),
        "project",
        [jax.ShapeDtypeStruct((n_head, n_patch, piece, cols), jnp.bfloat16)] * n_sub,
        cols // wide,
        [spec((rows, feat))] * (n_patch + len(more))
        + [pl.BlockSpec((depth, wide), lambda i, w: (0, i))],
        [pl.BlockSpec((n_head, n_patch, piece, wide), lambda i, w: (0, 0, 0, i))] * n_sub,
        [
            pltpu.VMEM((total, depth), jnp.bfloat16),
            pltpu.VMEM((n_patch // split, split, n_head, n_sub, piece, wide), jnp.float32),
        ],
        flops=PROJECT_FLOPS,
    )(where, *slots, *more, weight)


def mix_kernel(rels, where_ref, hidden_ref, gate_ref, *refs):
    blocks, out_ref = refs[:-1], refs[-1]
    piece, cols = blocks[0].shape
    for part in range(len(blocks) // len(rels)):
        rows = pl.ds(part * piece, piece)
        for at, rel in enumerate(rels):
            lanes = pl.ds(pl.multiple_of((where_ref[PATCH] ^ rel) * cols, HEAD_DIM), cols)
            mixed = hidden_ref[rows, lanes].astype(jnp.float32) + gate_ref[:, lanes] * blocks[
                part * len(rels) + at
            ][...].astype(jnp.float32)
            out_ref[rows, lanes] = mixed.astype(jnp.bfloat16)


def mix(where, hidden_in, attn_gate, blocks):
    rows, width = hidden_in.shape
    n_patch = len(blocks[0])
    piece, cols = blocks[0][0].shape
    if cols % HEAD_DIM:
        order = jnp.concatenate([jnp.stack(x) for x in blocks], axis=1)
        order = order[where[PATCH] ^ jnp.arange(n_patch)]
        projected = order.transpose(1, 0, 2).reshape(rows, width).astype(jnp.float32)
        return (hidden_in.astype(jnp.float32) + attn_gate * projected).astype(jnp.bfloat16)
    rels = [0, *range(n_patch - 1, 0, -1)]
    flat = [part[rel] for part in blocks for rel in rels]
    return call(
        functools.partial(mix_kernel, rels),
        "mix",
        jax.ShapeDtypeStruct((rows, width), jnp.bfloat16),
        1,
        [spec((rows, width)), spec((1, width))] + [spec((piece, cols))] * len(flat),
        spec((rows, width)),
    )(where, hidden_in, attn_gate[None], *flat)


def gather(parts, n_patch):
    if n_patch != 4:
        return [
            ([x] + [swap(x, "patch", n_patch, rel) for rel in range(1, n_patch)], [])
            for x in parts
        ]
    far = [swap(x, "patch", 4, 2) for x in parts]
    next_to = [swap(x, "patch", 4, 1) for x in parts]
    out = []
    for at, x in enumerate(parts):
        far[at], next_to[at], parts = lax.optimization_barrier((far[at], next_to[at], parts))
        middle = swap(parts[at], "patch", 4, 3, (1, 2))
        ends = lax.ppermute(far[at], "patch", [(1, 0), (2, 3)])
        if at + 1 < len(parts):
            ends, far[at + 1], next_to[at + 1] = lax.optimization_barrier(
                (ends, far[at + 1], next_to[at + 1])
            )
        out.append(([x, next_to[at], far[at], middle], [ends]))
    return out


def add_sub_kernel(n_sub, where_ref, *refs):
    terms, kept_ref, outs = refs[:n_sub], refs[n_sub], refs[n_sub + 1 :]
    for head in range(len(outs) + 1):
        total = terms[0][head].astype(jnp.float32)
        for term in terms[1:]:
            total += term[head].astype(jnp.float32)
        if head == 0:
            kept_ref[...] = total
        else:
            outs[head - 1][...] = total.astype(jnp.bfloat16)


def add_head_kernel(n_more, where_ref, kept_ref, *refs):
    for at, out in enumerate(refs[n_more:]):
        total = kept_ref[at]
        for term in refs[:n_more]:
            total += term[at].astype(jnp.float32)
        out[...] = total.astype(jnp.bfloat16)


def reduce_sub(sizes, where, terms):
    n_sub, n_head = sizes["sub"], sizes["head"]
    terms = [terms[0]] + [swap(terms[rel], "sub", n_sub, rel) for rel in range(1, n_sub)]
    shape = terms[0].shape[1:]
    return call(
        functools.partial(add_sub_kernel, n_sub),
        "add_sub",
        [jax.ShapeDtypeStruct(shape, jnp.float32)]
        + [jax.ShapeDtypeStruct(shape, jnp.bfloat16)] * (n_head - 1),
        1,
        [spec(terms[0].shape)] * n_sub,
        [spec(shape)] * n_head,
    )(where, *terms)


def reduce_head(sizes, where, sums):
    n_head = sizes["head"]
    shape = sums[0].shape
    sums = [sums[0]] + [swap(sums[rel], "head", n_head, rel) for rel in range(1, n_head)]
    return call(
        functools.partial(add_head_kernel, n_head - 1),
        "add_head",
        [jax.ShapeDtypeStruct(shape[1:], jnp.bfloat16)] * shape[0],
        1,
        [spec(shape)] * n_head,
        [spec(shape[1:])] * shape[0],
    )(where, *sums)


def sum_tail(sizes, where, pieces, kv_pieces, out_weight, hidden_in, attn_gate):
    n_patch, n_head, n_sub = sizes["patch"], sizes["head"], sizes["sub"]
    split, tok = len(pieces), pieces[0].shape[1]
    count = n_head * n_sub
    piece = tok // count
    parts = 2 if piece % 32 == 0 else 1
    attended = []
    for part in range(parts):
        rows = (part * (piece // parts), piece // parts)
        x = attend(where, rows, count, pieces, kv_pieces)
        attended.append(x.reshape(-1, x.shape[2]))
    slots = gather(attended, n_patch)
    blocks = []
    for part in range(parts):
        terms = project(split, where, *slots[part], out_weight, n_head, n_sub)
        total = reduce_head(sizes, where, reduce_sub(sizes, where, terms))
        blocks.append(
            [total[0]] + [swap(total[rel], "patch", n_patch, rel) for rel in range(1, n_patch)]
        )
    return mix(where, hidden_in, attn_gate, blocks)


def attend_half_kernel(half, where_ref, *refs):
    pieces, out = refs[:-1], refs[-1]
    factor = HEAD_DIM**-0.5 * math.log2(math.e)
    rows, feat = out.shape[1:]
    start = pl.multiple_of((where_ref[HEAD] ^ half) * rows, rows)
    for head in range(feat // HEAD_DIM):
        lanes = pl.ds(head * HEAD_DIM, HEAD_DIM)
        keys = jnp.concatenate([ref[1, :, lanes] for ref in pieces], axis=0)
        values = jnp.concatenate([ref[2, :, lanes] for ref in pieces], axis=0)
        values = jnp.concatenate([values, jnp.ones_like(values)], axis=1)
        for first in range(0, len(pieces), 2):
            query = [ref[0, pl.ds(start, rows), lanes] for ref in pieces[first : first + 2]]
            scores = lax.dot_general(
                jnp.concatenate(query, axis=0),
                keys,
                (((1,), (1,)), ((), ())),
                preferred_element_type=jnp.float32,
            )
            peak = jnp.max(scores, axis=1, keepdims=True)
            expo = jnp.exp2((scores - peak) * factor).astype(jnp.bfloat16)
            mix = jnp.dot(expo, values, preferred_element_type=jnp.float32)
            mix = (mix[:, :HEAD_DIM] / mix[:, HEAD_DIM:]).astype(jnp.bfloat16)
            for at in range(len(query)):
                block = mix[at * rows : (at + 1) * rows]
                out[where_ref[NEAR] ^ (first + at), :, lanes] = block


def attend_half(where, half, pieces):
    _, tok, feat = pieces[0].shape
    out = jax.ShapeDtypeStruct((len(pieces), tok // 2, feat), jnp.bfloat16)
    return call(
        functools.partial(attend_half_kernel, half),
        "attend",
        out,
        1,
        [spec((3, tok, feat))] * len(pieces),
        spec(out.shape),
        flops=HALF_FLOPS,
    )(where, *pieces).reshape(-1, feat)


def add_product_kernel(count, where_ref, *refs):
    total = refs[2 * count][...] if len(refs) > 2 * count + 1 else None
    for slot, weight in zip(refs[:count], refs[count : 2 * count]):
        term = jnp.dot(slot[...], weight[...], preferred_element_type=jnp.float32)
        total = term if total is None else total + term
    refs[-1][...] = total


def add_product(where, slots, weight, acc=None):
    rows, feat = next(iter(slots.values())).shape
    cols = weight.shape[1]
    wide = cols // 2
    whole = pl.BlockSpec((rows, wide), lambda i, w: (0, i))
    rels = list(slots)
    return call(
        functools.partial(add_product_kernel, len(rels)),
        "products",
        jax.ShapeDtypeStruct((rows, cols), jnp.float32),
        2,
        [spec((rows, feat))] * len(rels)
        + [pl.BlockSpec((feat, wide), lambda i, w, rel=rel: (w[NEAR] ^ rel, i)) for rel in rels]
        + ([] if acc is None else [whole]),
        whole,
        flops=ZERO_FLOPS if acc is None else 1,
    )(where, *slots.values(), *[weight] * len(rels), *([] if acc is None else [acc]))


def partner_place(where_ref, head):
    return (head + FETCHED * where_ref[GRP]) % 8


def first_kernel(where_ref, *refs):
    last, more, slots = refs[0], refs[1], refs[2:5]
    acc_ref, own_ref, fetched_ref, passed_ref, out_ref, held_ref = refs[5:]
    rows, feat = last.shape
    cut = fetched_ref.shape[0]

    def put(at, block):
        for head in range(2):
            there = partner_place(where_ref, 2 * (where_ref[NEAR] ^ at) + head)
            lanes = pl.ds(pl.multiple_of(there * HEAD_DIM, HEAD_DIM), HEAD_DIM)
            held_ref[:, lanes] = block[:, head * HEAD_DIM : (head + 1) * HEAD_DIM]

    @pl.when(pl.program_id(0) == 0)
    def arrange():
        for at, slot in zip((0, 2, 1), slots):
            put(at, slot[...])
        put(3, jnp.zeros((rows, feat), jnp.bfloat16))

    block = jnp.where(where_ref[INNER] == 1, last[...], more[...])
    acc = acc_ref[...]
    acc += jnp.dot(block, own_ref[...], preferred_element_type=jnp.float32)
    acc += jnp.dot(held_ref[:, :cut], fetched_ref[...], preferred_element_type=jnp.float32)
    acc += jnp.dot(held_ref[:, cut:], passed_ref[...], preferred_element_type=jnp.float32)
    out_ref[...] = acc


def first_product(where, last, more, slots, acc, weights):
    rows, feat = last.shape
    own, fetched, passed = weights
    wide = own.shape[1] // 2
    whole = pl.BlockSpec((rows, wide), lambda i, w: (0, i))
    return call(
        first_kernel,
        "first",
        jax.ShapeDtypeStruct(acc.shape, jnp.float32),
        2,
        [spec((rows, feat))] * 5
        + [whole, pl.BlockSpec((feat, wide), lambda i, w: (w[NEAR] ^ 3, i))]
        + [pl.BlockSpec((x.shape[0], wide), lambda i, w: (0, i)) for x in (fetched, passed)],
        whole,
        [pltpu.VMEM((rows, 4 * feat), jnp.bfloat16)],
    )(where, last, more, *slots, acc, own, fetched, passed)


def second_kernel(where_ref, slot, more, fetched_ref, passed_ref, acc_in, keep_ref, send_ref, acc_ref):
    weight = []
    for head in range(2):
        place = partner_place(where_ref, 2 * (where_ref[NEAR] ^ 3) + head)
        here = jnp.minimum(place, FETCHED - 1) * HEAD_DIM
        there = jnp.maximum(place - FETCHED, 0) * HEAD_DIM
        weight.append(
            jnp.where(
                place < FETCHED,
                fetched_ref[pl.ds(pl.multiple_of(here, HEAD_DIM), HEAD_DIM), :],
                passed_ref[pl.ds(pl.multiple_of(there, HEAD_DIM), HEAD_DIM), :],
            )
        )
    block = jnp.where(where_ref[INNER] == 1, slot[...], more[...])
    acc = acc_in[...] + jnp.dot(
        block, jnp.concatenate(weight, axis=0), preferred_element_type=jnp.float32
    )
    acc_ref[...] = acc.reshape(acc_ref.shape)
    for sub, out in enumerate((keep_ref, send_ref)):
        for at in range(4):
            out[at] = acc_ref[where_ref[NEAR] ^ at, where_ref[SUB] ^ sub].astype(jnp.bfloat16)


def second_product(where, chunk, slot, more, weights, acc):
    rows, feat = slot.shape
    cols = weights[0].shape[1]
    wide = cols // 2
    out = jax.ShapeDtypeStruct((4, rows // 8, wide), jnp.bfloat16)
    return call(
        second_kernel,
        "second",
        [out] * 2,
        1,
        [spec((rows, feat))] * 2
        + [pl.BlockSpec((x.shape[0], wide), lambda i, w: (0, chunk)) for x in weights]
        + [pl.BlockSpec((rows, wide), lambda i, w: (0, chunk))],
        [spec(out.shape)] * 2,
        [pltpu.VMEM((4, 2, rows // 8, wide), jnp.float32)],
    )(where, slot, more, *weights, acc)


def add_kernel(where_ref, keep_ref, term_ref, *outs):
    for at, out in enumerate(outs):
        total = keep_ref[at].astype(jnp.float32) + term_ref[at].astype(jnp.float32)
        out[...] = total.astype(jnp.bfloat16)


def add(where, keep, term):
    return call(
        add_kernel,
        "add",
        [jax.ShapeDtypeStruct(keep.shape[1:], jnp.bfloat16)] * keep.shape[0],
        1,
        [spec(keep.shape)] * 2,
        [spec(keep.shape[1:])] * keep.shape[0],
    )(where, keep, term)


def take_kernel(where_ref, weight_ref, out_ref):
    out_ref[...] = weight_ref[...]


def take_half(where, weight):
    rows, cols = weight.shape[0] // 2, weight.shape[1]
    return call(
        take_kernel,
        "take",
        jax.ShapeDtypeStruct((rows, cols), weight.dtype),
        2,
        [pl.BlockSpec((rows // 2, cols), lambda i, w: (2 * w[GRP] + i, 0))],
        pl.BlockSpec((rows // 2, cols), lambda i, w: (i, 0)),
    )(where, weight)


def share_tail(sizes, where, pieces, kv_pieces, out_weight, hidden_in, attn_gate):
    out_weight, where = lax.optimization_barrier((out_weight, where))
    fetched = swap(take_half(where, out_weight), "head", 2, 1)
    own, fetched = lax.optimization_barrier((pieces[0], fetched))
    pieces = [own, *pieces[1:]]
    passed = swap(fetched, "grp", 2, 1)

    pieces = [pieces[0], *pieces[:0:-1]]
    mine = attend_half(where, 0, pieces)
    where, mine = lax.optimization_barrier((where, mine))
    other = swap(attend_half(where, 1, pieces), "head", 2, 1)
    acc = add_product(where, {0: mine}, out_weight)
    other, acc = lax.optimization_barrier((other, acc))
    slots, last = [], other
    for at, x in enumerate((mine, other)):
        next_to, far = swap(x, "patch", 4, 1), swap(x, "patch", 4, 2)
        next_to, far, other, x = lax.optimization_barrier((next_to, far, other, x))
        if at == 1:
            acc = add_product(where, {2: slots[0][2], 1: slots[0][1]}, out_weight, acc)
            far, x, acc = lax.optimization_barrier((far, x, acc))
        middle = swap((mine, last)[at], "patch", 4, 3, (1, 2))
        ends = lax.ppermute(far[at], "patch", [(1, 0), (2, 3)])
        if at + 1 < len(parts):
            ends, far[at + 1], next_to[at + 1] = lax.optimization_barrier(
                (ends, far[at + 1], next_to[at + 1])
            )
        out.append(([x, next_to[at], far[at], middle], [ends]))
    return out


def add_sub_kernel(n_sub, where_ref, *refs):
    terms, kept_ref, outs = refs[:n_sub], refs[n_sub], refs[n_sub + 1 :]
    for head in range(len(outs) + 1):
        total = terms[0][head].astype(jnp.float32)
        for term in terms[1:]:
            total += term[head].astype(jnp.float32)
        if head == 0:
            kept_ref[...] = total
        else:
            outs[head - 1][...] = total.astype(jnp.bfloat16)


def add_head_kernel(n_more, where_ref, kept_ref, *refs):
    for at, out in enumerate(refs[n_more:]):
        total = kept_ref[at]
        for term in refs[:n_more]:
            total += term[at].astype(jnp.float32)
        out[...] = total.astype(jnp.bfloat16)


def reduce_sub(sizes, where, terms):
    n_sub, n_head = sizes["sub"], sizes["head"]
    terms = [terms[0]] + [swap(terms[rel], "sub", n_sub, rel) for rel in range(1, n_sub)]
    shape = terms[0].shape[1:]
    return call(
        functools.partial(add_sub_kernel, n_sub),
        "add_sub",
        [jax.ShapeDtypeStruct(shape, jnp.float32)]
        + [jax.ShapeDtypeStruct(shape, jnp.bfloat16)] * (n_head - 1),
        1,
        [spec(terms[0].shape)] * n_sub,
        [spec(shape)] * n_head,
    )(where, *terms)


def reduce_head(sizes, where, sums):
    n_head = sizes["head"]
    shape = sums[0].shape
    sums = [sums[0]] + [swap(sums[rel], "head", n_head, rel) for rel in range(1, n_head)]
    return call(
        functools.partial(add_head_kernel, n_head - 1),
        "add_head",
        [jax.ShapeDtypeStruct(shape[1:], jnp.bfloat16)] * shape[0],
        1,
        [spec(shape)] * n_head,
        [spec(shape[1:])] * shape[0],
    )(where, *sums)


def sum_tail(sizes, where, pieces, kv_pieces, out_weight, hidden_in, attn_gate):
    n_patch, n_head, n_sub = sizes["patch"], sizes["head"], sizes["sub"]
    split, tok = len(pieces), pieces[0].shape[1]
    count = n_head * n_sub
    piece = tok // count
    parts = 2 if piece % 32 == 0 else 1
    attended = []
    for part in range(parts):
        rows = (part * (piece // parts), piece // parts)
        x = attend(where, rows, count, pieces, kv_pieces)
        attended.append(x.reshape(-1, x.shape[2]))
    slots = gather(attended, n_patch)
    blocks = []
    for part in range(parts):
        terms = project(split, where, *slots[part], out_weight, n_head, n_sub)
        total = reduce_head(sizes, where, reduce_sub(sizes, where, terms))
        blocks.append(
            [total[0]] + [swap(total[rel], "patch", n_patch, rel) for rel in range(1, n_patch)]
        )
    return mix(where, hidden_in, attn_gate, blocks)


def attend_half_kernel(half, where_ref, *refs):
    pieces, out = refs[:-1], refs[-1]
    factor = HEAD_DIM**-0.5 * math.log2(math.e)
    rows, feat = out.shape[1:]
    start = pl.multiple_of((where_ref[HEAD] ^ half) * rows, rows)
    for head in range(feat // HEAD_DIM):
        lanes = pl.ds(head * HEAD_DIM, HEAD_DIM)
        keys = jnp.concatenate([ref[1, :, lanes] for ref in pieces], axis=0)
        values = jnp.concatenate([ref[2, :, lanes] for ref in pieces], axis=0)
        values = jnp.concatenate([values, jnp.ones_like(values)], axis=1)
        for first in range(0, len(pieces), 2):
            query = [ref[0, pl.ds(start, rows), lanes] for ref in pieces[first : first + 2]]
            scores = lax.dot_general(
                jnp.concatenate(query, axis=0),
                keys,
                (((1,), (1,)), ((), ())),
                preferred_element_type=jnp.float32,
            )
            peak = jnp.max(scores, axis=1, keepdims=True)
            expo = jnp.exp2((scores - peak) * factor).astype(jnp.bfloat16)
            mix = jnp.dot(expo, values, preferred_element_type=jnp.float32)
            mix = (mix[:, :HEAD_DIM] / mix[:, HEAD_DIM:]).astype(jnp.bfloat16)
            for at in range(len(query)):
                block = mix[at * rows : (at + 1) * rows]
                out[where_ref[NEAR] ^ (first + at), :, lanes] = block


def attend_half(where, half, pieces):
    _, tok, feat = pieces[0].shape
    out = jax.ShapeDtypeStruct((len(pieces), tok // 2, feat), jnp.bfloat16)
    return call(
        functools.partial(attend_half_kernel, half),
        "attend",
        out,
        1,
        [spec((3, tok, feat))] * len(pieces),
        spec(out.shape),
        flops=HALF_FLOPS,
    )(where, *pieces).reshape(-1, feat)


def add_product_kernel(count, where_ref, *refs):
    total = refs[2 * count][...] if len(refs) > 2 * count + 1 else None
    for slot, weight in zip(refs[:count], refs[count : 2 * count]):
        term = jnp.dot(slot[...], weight[...], preferred_element_type=jnp.float32)
        total = term if total is None else total + term
    refs[-1][...] = total


def add_product(where, slots, weight, acc=None):
    rows, feat = next(iter(slots.values())).shape
    cols = weight.shape[1]
    wide = cols // 2
    whole = pl.BlockSpec((rows, wide), lambda i, w: (0, i))
    rels = list(slots)
    return call(
        functools.partial(add_product_kernel, len(rels)),
        "products",
        jax.ShapeDtypeStruct((rows, cols), jnp.float32),
        2,
        [spec((rows, feat))] * len(rels)
        + [pl.BlockSpec((feat, wide), lambda i, w, rel=rel: (w[NEAR] ^ rel, i)) for rel in rels]
        + ([] if acc is None else [whole]),
        whole,
        flops=ZERO_FLOPS if acc is None else 1,
    )(where, *slots.values(), *[weight] * len(rels), *([] if acc is None else [acc]))


def partner_place(where_ref, head):
    return (head + FETCHED * where_ref[GRP]) % 8


def first_kernel(where_ref, *refs):
    last, more, slots = refs[0], refs[1], refs[2:5]
    acc_ref, own_ref, fetched_ref, passed_ref, out_ref, held_ref = refs[5:]
    rows, feat = last.shape
    cut = fetched_ref.shape[0]

    def put(at, block):
        for head in range(2):
            there = partner_place(where_ref, 2 * (where_ref[NEAR] ^ at) + head)
            lanes = pl.ds(pl.multiple_of(there * HEAD_DIM, HEAD_DIM), HEAD_DIM)
            held_ref[:, lanes] = block[:, head * HEAD_DIM : (head + 1) * HEAD_DIM]

    @pl.when(pl.program_id(0) == 0)
    def arrange():
        for at, slot in zip((0, 2, 1), slots):
            put(at, slot[...])
        put(3, jnp.zeros((rows, feat), jnp.bfloat16))

    block = jnp.where(where_ref[INNER] == 1, last[...], more[...])
    acc = acc_ref[...]
    acc += jnp.dot(block, own_ref[...], preferred_element_type=jnp.float32)
    acc += jnp.dot(held_ref[:, :cut], fetched_ref[...], preferred_element_type=jnp.float32)
    acc += jnp.dot(held_ref[:, cut:], passed_ref[...], preferred_element_type=jnp.float32)
    out_ref[...] = acc


def first_product(where, last, more, slots, acc, weights):
    rows, feat = last.shape
    own, fetched, passed = weights
    wide = own.shape[1] // 2
    whole = pl.BlockSpec((rows, wide), lambda i, w: (0, i))
    return call(
        first_kernel,
        "first",
        jax.ShapeDtypeStruct(acc.shape, jnp.float32),
        2,
        [spec((rows, feat))] * 5
        + [whole, pl.BlockSpec((feat, wide), lambda i, w: (w[NEAR] ^ 3, i))]
        + [pl.BlockSpec((x.shape[0], wide), lambda i, w: (0, i)) for x in (fetched, passed)],
        whole,
        [pltpu.VMEM((rows, 4 * feat), jnp.bfloat16)],
    )(where, last, more, *slots, acc, own, fetched, passed)


def second_kernel(where_ref, slot, more, fetched_ref, passed_ref, acc_in, keep_ref, send_ref, acc_ref):
    weight = []
    for head in range(2):
        place = partner_place(where_ref, 2 * (where_ref[NEAR] ^ 3) + head)
        here = jnp.minimum(place, FETCHED - 1) * HEAD_DIM
        there = jnp.maximum(place - FETCHED, 0) * HEAD_DIM
        weight.append(
            jnp.where(
                place < FETCHED,
                fetched_ref[pl.ds(pl.multiple_of(here, HEAD_DIM), HEAD_DIM), :],
                passed_ref[pl.ds(pl.multiple_of(there, HEAD_DIM), HEAD_DIM), :],
            )
        )
    block = jnp.where(where_ref[INNER] == 1, slot[...], more[...])
    acc = acc_in[...] + jnp.dot(
        block, jnp.concatenate(weight, axis=0), preferred_element_type=jnp.float32
    )
    acc_ref[...] = acc.reshape(acc_ref.shape)
    for sub, out in enumerate((keep_ref, send_ref)):
        for at in range(4):
            out[at] = acc_ref[where_ref[NEAR] ^ at, where_ref[SUB] ^ sub].astype(jnp.bfloat16)


def second_product(where, chunk, slot, more, weights, acc):
    rows, feat = slot.shape
    cols = weights[0].shape[1]
    wide = cols // 2
    out = jax.ShapeDtypeStruct((4, rows // 8, wide), jnp.bfloat16)
    return call(
        second_kernel,
        "second",
        [out] * 2,
        1,
        [spec((rows, feat))] * 2
        + [pl.BlockSpec((x.shape[0], wide), lambda i, w: (0, chunk)) for x in weights]
        + [pl.BlockSpec((rows, wide), lambda i, w: (0, chunk))],
        [spec(out.shape)] * 2,
        [pltpu.VMEM((4, 2, rows // 8, wide), jnp.float32)],
    )(where, slot, more, *weights, acc)


def add_kernel(where_ref, keep_ref, term_ref, *outs):
    for at, out in enumerate(outs):
        total = keep_ref[at].astype(jnp.float32) + term_ref[at].astype(jnp.float32)
        out[...] = total.astype(jnp.bfloat16)


def add(where, keep, term):
    return call(
        add_kernel,
        "add",
        [jax.ShapeDtypeStruct(keep.shape[1:], jnp.bfloat16)] * keep.shape[0],
        1,
        [spec(keep.shape)] * 2,
        [spec(keep.shape[1:])] * keep.shape[0],
    )(where, keep, term)


def take_kernel(where_ref, weight_ref, out_ref):
    out_ref[...] = weight_ref[...]


def take_half(where, weight):
    rows, cols = weight.shape[0] // 2, weight.shape[1]
    return call(
        take_kernel,
        "take",
        jax.ShapeDtypeStruct((rows, cols), weight.dtype),
        2,
        [pl.BlockSpec((rows // 2, cols), lambda i, w: (2 * w[GRP] + i, 0))],
        pl.BlockSpec((rows // 2, cols), lambda i, w: (i, 0)),
    )(where, weight)


def share_tail(sizes, where, pieces, kv_pieces, out_weight, hidden_in, attn_gate):
    out_weight, where = lax.optimization_barrier((out_weight, where))
    fetched = swap(take_half(where, out_weight), "head", 2, 1)
    own, fetched = lax.optimization_barrier((pieces[0], fetched))
    pieces = [own, *pieces[1:]]
    passed = swap(fetched, "grp", 2, 1)

    pieces = [pieces[0], *pieces[:0:-1]]
    mine = attend_half(where, 0, pieces)
    where, mine = lax.optimization_barrier((where, mine))
    other = swap(attend_half(where, 1, pieces), "head", 2, 1)
    acc = add_product(where, {0: mine}, out_weight)
    other, acc = lax.optimization_barrier((other, acc))
    slots, last = [], other
    for at, x in enumerate((mine, other)):
        next_to, far = swap(x, "patch", 4, 1), swap(x, "patch", 4, 2)
        next_to, far, other, x = lax.optimization_barrier((next_to, far, other, x))
        if at == 1:
            acc = add_product(where, {2: slots[0][2], 1: slots[0][1]}, out_weight, acc)
            far, x, acc = lax.optimization_barrier((far, x, acc))
        if at == 0:
            middle = swap(x, "patch", 4, 3, (1, 2))
        else:
            middle = swap(last, "patch", 4, 3, (1, 2))
        ends = lax.ppermute(far, "patch", [(1, 0), (2, 3)])
        slots.append([x, next_to, far, middle, ends])
    weights = [out_weight, fetched, passed]
    partner = [slots[1][at] for at in (0, 2, 1)]
    acc = first_product(where, *slots[0][3:], partner, acc, weights)
    terms = [second_product(where, at, *slots[1][3:], [fetched, passed], acc) for at in range(2)]
    blocks = []
    for keep, send in terms:
        total = add(where, keep, swap(send, "sub", 2, 1))
        blocks.append([total[0]] + [swap(total[rel], "patch", 4, rel) for rel in range(3, 0, -1)])
    return mix_columns(where, hidden_in, attn_gate, blocks)


def mix_columns_kernel(where_ref, hidden_ref, gate_ref, *refs):
    blocks, out_ref = refs[:-1], refs[-1]
    cols = blocks[0].shape[1]
    for chunk in range(2):
        for at, rel in enumerate((0, 3, 2, 1)):
            start = (2 * (where_ref[PATCH] ^ rel) + chunk) * cols
            lanes = pl.ds(pl.multiple_of(start, HEAD_DIM), cols)
            mixed = hidden_ref[:, lanes].astype(jnp.float32) + gate_ref[:, lanes] * blocks[
                4 * chunk + at
            ][...].astype(jnp.float32)
            out_ref[:, lanes] = mixed.astype(jnp.bfloat16)


def mix_columns(where, hidden_in, attn_gate, blocks):
    rows, width = hidden_in.shape
    flat = [x for chunk in blocks for x in chunk]
    return call(
        mix_columns_kernel,
        "mix",
        jax.ShapeDtypeStruct((rows, width), jnp.bfloat16),
        2,
        [pl.BlockSpec((rows // 2, width), lambda i, w: (i, 0)), spec((1, width))]
        + [pl.BlockSpec((rows // 2, flat[0].shape[1]), lambda i, w: (i, 0))] * len(flat),
        pl.BlockSpec((rows // 2, width), lambda i, w: (i, 0)),
    )(where, hidden_in, attn_gate[None], *flat)


def body(sizes, queries, fresh_kv, cached_kv, exponents, out_weight, hidden_in, attn_gate):
    n_patch, n_head, n_sub = sizes["patch"], sizes["head"], sizes["sub"]
    tok, channels = queries.shape
    heads = channels // HEAD_DIM
    split = math.gcd(heads, n_patch)
    patch_at = lax.axis_index("patch")
    inner = (patch_at > 0) & (patch_at < n_patch - 1)
    where = jnp.stack(
        [
            patch_at,
            patch_at % split,
            lax.axis_index("head"),
            lax.axis_index("sub"),
            inner,
            lax.axis_index("grp"),
        ]
    ).astype(jnp.int32)

    arrays = (exponents, queries, fresh_kv, cached_kv)
    sent = pack(split, *arrays)
    far_first = [
        swap(x, "patch", n_patch, split - 1 - at) for at, x in enumerate(sent)
    ]
    where, sent = lax.optimization_barrier((where, sent))
    pieces = [pack_own(split, where, *arrays), *far_first]
    kv_pieces = list(pieces)
    for rel in range(split, n_patch, split):
        kv_pieces += [swap(x, "patch", n_patch, rel) for x in pieces]

    tail = (sizes, where, pieces, kv_pieces, out_weight, hidden_in, attn_gate)
    if (sizes["grp"], n_head, split, n_patch) == (2, 2, 4, 4):
        return share_tail(*tail)
    return sum_tail(*tail)


def solution(mesh):
    in_specs = (
        P(("grp", "patch"), ("head", "sub")),
        P(None, ("grp", "patch"), ("head", "sub")),
        P(None, "grp", ("head", "sub")),
        P(None, ("grp", "patch"), ("head", "sub")),
        P(("head", "sub"), "patch"),
        P(("grp", "patch", "head", "sub"), None),
        P(),
    )
    out_specs = P(("grp", "patch", "head", "sub"), None)
    return jax.shard_map(
        functools.partial(body, dict(mesh.shape)),
        mesh=mesh,
        in_specs=in_specs,
        out_specs=out_specs,
        check_vma=False,
    )
```
